32 devices in a mesh: groups: 2 (over y), shard: 4 (over z), cache: 2 (over x), pair: 2 (over core).
Axes of the slice: x: 2, y: 2, z: 4, core: 2. Of those that a mesh axis runs over, the one named last changes fastest.
Arguments:
- cand_items: int32 [4096], P(('groups', 'shard', 'cache', 'pair')), parts along dimension 0, may hold values from 0 to 1023, as said below
- reader_users: int32 [256], P(('groups', 'shard', 'cache', 'pair')), parts along dimension 0, may hold values from 0 to 511, as said below
- item_table: bfloat16 [1024, 3072], P(('shard', 'cache')), may hold values from -6 to 6
- user_states: bfloat16 [1024, 3072], P(('groups', 'shard')), parts along dimension 0, may hold values from -0.109375 to 0.109375
- pair_mats: bfloat16 [512, 64, 64], P('pair'), may hold values from -0.00390625 to 0.00390625
- pair_fields: int32 [512, 2], P('pair'), may hold values from 0 to 47, as said below
Outputs:
- score: float32 [4096], P(('groups', 'shard', 'cache', 'pair')), parts along dimension 0
The draws below stay inside these ranges and needn't reach their ends.
There are 2 independent parts, one for each index of `groups`. The reference program is written for one: setup_inputs(seed, part) draws one part's arguments, and reference() takes and returns one part's arrays. A program takes and returns all parts, laid end to end along the dimension named above; an argument that names none is the same for every part. Nothing has to cross between parts.
Inputs may be any that keep to these rules, and one draw needn't show every extreme that they name: `cand_items`: item ids; owner o holds ids o * 128 to (o + 1) * 128 - 1. The 128 candidates of one device name items of one owner at most 32 times, and one owner, the same for every device of the draw, exactly 32 times. `reader_users`: user ids; index s of shard holds ids s * 128 to (s + 1) * 128 - 1. The 8 users of one device lie in one such block at most 4 times, and one block, the same for every device of the draw, exactly 4 times. `pair_fields`: each row holds two field numbers a < b; no pair repeats.
All inputs are finite; a program needn't handle non-finite values.
Results may differ from the reference program's by a relative error of at most 0.0003.
Values may be sent and summed in bfloat16 or wider, within the bound.
No kernel may reach another device: no remote copies, remote signals or barrier semaphores. Data moves between devices by JAX's collectives and lax.ppermute only.
A program may use at most 64 MiB of HBM per device.

```python
import math
import jax
import jax.numpy as jnp
import numpy as np
from jax import lax

K = 64
FI = 48
LIST = 16
ROWS_DEV = 128
ITEM_OWN = 128
USER_SHARD = 128
OWNERS = 8
READERS_DEV = 8
CAP_ITEM = 32
CAP_USER = 4
CANDS = 2048
READERS = 128
ITEMS = 1024
USERS = 512
PAIRS = 512
N_PAIR = 2


def owned_ids(key, blocks, block_rows, owners, capacity, own_rows):
    hot_key, rest_key = jax.random.split(key)
    hottest = jax.random.randint(hot_key, (), 0, owners)

    def one_block(block_key):
        slot_key, order_key, within_key = jax.random.split(block_key, 3)
        others = jnp.arange((owners - 1) * capacity, dtype=jnp.int32) // capacity
        others = others + (others >= hottest).astype(jnp.int32)
        chosen = jax.random.permutation(slot_key, others)[:block_rows - capacity]
        owner_list = jnp.concatenate([jnp.full((capacity,), hottest, jnp.int32), chosen])
        owner_list = jax.random.permutation(order_key, owner_list)
        within = jax.random.randint(within_key, (block_rows,), 0, own_rows)
        return owner_list * own_rows + within
    return jax.vmap(one_block)(jax.random.split(rest_key, blocks)).reshape(-1).astype(jnp.int32)


def draw_cand_items(key, part):
    key = jax.random.fold_in(key, 11)
    return owned_ids(key, CANDS // ROWS_DEV, ROWS_DEV, OWNERS, CAP_ITEM, ITEM_OWN)


def draw_reader_users(key, part):
    key = jax.random.fold_in(key, 12)
    return owned_ids(key, READERS // READERS_DEV, READERS_DEV, USERS // USER_SHARD, CAP_USER, USER_SHARD)


def draw_pair_fields(key, part):
    key = jax.random.fold_in(key, 13)
    upper = np.triu_indices(FI, 1)
    table_all = jnp.asarray(np.stack([upper[0], upper[1]], axis=1), dtype=jnp.int32)
    picked = jax.random.permutation(key, table_all.shape[0])[:PAIRS]
    return jnp.take(table_all, picked, axis=0)


def levels(own_key, shape, shards, low, top_value):
    gain = 1.0
    for position, shards_of in shards:
        draws = jax.random.uniform(jax.random.fold_in(jax.random.fold_in(own_key, 6), position), (shards_of,), jnp.float32, low / len(shards), top_value / len(shards))
        gain = gain * jnp.repeat(jnp.exp(draws), shape[position] // shards_of).reshape((-1,) + (1,) * (len(shape) - 1 - position))
    return gain


def scatter_about(rng, extent, deviation, limit, pieces=(), held_as=jnp.bfloat16):
    loudness = levels(rng, extent, pieces, -0.22, 0.18) if pieces else 1.0
    drawn = jax.random.normal(rng, extent, jnp.float32) * deviation * loudness
    return jnp.minimum(jnp.maximum(drawn, -limit), limit).astype(held_as)


def setup_inputs(seed: int = 0, part: int = 0) -> dict:
    streams_of = jax.random.split(jax.random.key(seed), 7)
    own_keys = jax.random.split(jax.random.fold_in(streams_of[6], part), 7)
    cand_items = draw_cand_items(jax.random.fold_in(jax.random.fold_in(streams_of[6], part), 71), part)
    reader_users = draw_reader_users(jax.random.fold_in(jax.random.fold_in(streams_of[6], part), 71), part)
    item_table = scatter_about(streams_of[2], (ITEMS, FI * K), 1.0, 6.0, ((0, 8),))
    user_states = scatter_about(own_keys[3], (USERS, FI * K), (FI * K) ** -0.5, 0.109375, ((0, 4),))
    pair_mats = scatter_about(streams_of[4], (PAIRS, K, K), (K * K * PAIRS) ** -0.5, 0.00390625, ((0, 2),))
    pair_fields = draw_pair_fields(jax.random.fold_in(streams_of[6], 71), part)
    return dict(cand_items=cand_items, reader_users=reader_users, item_table=item_table, user_states=user_states, pair_mats=pair_mats, pair_fields=pair_fields)


def pair_total(embedded, pair_mats, pair_fields):
    row_count = embedded.shape[0]
    pair_count = pair_mats.shape[0]
    block_size = math.gcd(pair_count, 32)
    mats_blocked = pair_mats.reshape(pair_count // block_size, block_size, K, K)
    fields_blocked = pair_fields.reshape(pair_count // block_size, block_size, 2)

    def accumulate(running, inputs):
        mats_now, fields_now = inputs
        left_side = jnp.take(embedded, fields_now[:, 0], axis=1).astype(jnp.float32)
        right_side = jnp.take(embedded, fields_now[:, 1], axis=1).astype(jnp.float32)
        product = jnp.einsum("rpk,pkl->rpl", left_side, mats_now.astype(jnp.float32), precision=lax.Precision.HIGHEST)
        return running + jnp.sum(product * right_side, axis=(1, 2)), None

    result, leftover = lax.scan(accumulate, jnp.zeros((row_count,), jnp.float32), (mats_blocked, fields_blocked))
    return result


def reference(cand_items, reader_users, item_table, user_states, pair_mats, pair_fields):
    width = FI * K
    per_block = ROWS_DEV * N_PAIR
    blocks = cand_items.shape[0] // per_block
    readers_block = per_block // LIST
    items_blocked = cand_items.reshape(blocks, per_block)
    users_blocked = reader_users.reshape(blocks, readers_block)

    def score_block(inputs):
        items_now, users_now = inputs
        fetched = jnp.take(item_table, items_now, axis=0)
        states = jnp.take(user_states, users_now, axis=0).astype(jnp.float32)
        grouped = fetched.reshape(readers_block, LIST, width).astype(jnp.float32)
        linear = jnp.einsum("ulw,uw->ul", grouped, states, precision=lax.Precision.HIGHEST).reshape(per_block)
        return linear + pair_total(fetched.reshape(per_block, FI, K), pair_mats, pair_fields)

    return lax.map(score_block, (items_blocked, users_blocked)).reshape(-1)
```

```python
import functools

import jax
import jax.numpy as jnp
from jax import lax
from jax.experimental import pallas as pl
from jax.experimental.pallas import tpu as pltpu
from jax.sharding import PartitionSpec as P

K = 64
FI = 48
LANES = 128
VMEM_LIMIT = 48 * 1024 * 1024
NT = (((1,), (1,)), ((), ()))
TN = (((0,), (0,)), ((), ()))
NN = (((1,), (0,)), ((), ()))


def dot(a, b, dims, **kw):
    return lax.dot_general(a, b, dims, preferred_element_type=jnp.float32, **kw)


def iota(shape, dim):
    return lax.broadcasted_iota(jnp.int32, shape, dim)


def pair_kernel(fields, items, mats, out, mats_own, rows32, rows16, stacked, sem):
    count = mats_own.shape[2]
    first = pl.multiple_of(lax.axis_index("groups") * count, count)
    copy = pltpu.make_async_copy(mats.at[:, :, pl.ds(first, count)], mats_own, sem)
    copy.start()
    rows = items.shape[0]
    eye = (iota((LANES, LANES), 0) == iota((LANES, LANES), 1)).astype(jnp.bfloat16)
    for t in range(items.shape[1] // LANES):
        turned = dot(eye, items[:, t * LANES:(t + 1) * LANES], NT)
        rows32[t * LANES:(t + 1) * LANES, :] = turned
        rows16[t * LANES:(t + 1) * LANES, :] = turned.astype(jnp.bfloat16)
    copy.wait()
    eye_pairs = (iota((count, count), 0) == iota((count, count), 1)).astype(jnp.bfloat16)
    for k in range(K):
        both = jnp.concatenate([mats_own[k], mats_own[k]], axis=0)
        stacked[pl.ds(k, count, stride=K), :] = dot(eye_pairs, both, NT)

    def one(p, total):
        a = pl.multiple_of(fields[0, first + p] * K, K)
        b = pl.multiple_of(fields[1, first + p] * K, K)
        matrix = stacked[pl.ds(pl.multiple_of(p * K, K), K), :][:, :K].astype(jnp.bfloat16)
        moved = dot(matrix, rows16[pl.ds(b, K), :], NN)
        return total + moved * rows32[pl.ds(a, K), :]

    total = lax.fori_loop(0, count, one, jnp.zeros((K, rows), jnp.float32), unroll=8)
    line = jnp.sum(total, axis=0, keepdims=True)
    mine = iota(out.shape, 0) == lax.axis_index("cache")
    out[...] = jnp.where(mine, jnp.broadcast_to(line, out.shape), 0.0)


def pick_kernel(total, cap, *refs):
    users, (states, out) = refs[:total], refs[total:]
    own_rows = states.shape[0]
    me = lax.axis_index("shard")
    slots = out.shape[0]
    slot_index = iota((slots, own_rows), 0)
    row_index = iota((slots, own_rows), 1)
    chosen = jnp.zeros((slots, own_rows), jnp.float32)
    for j in range(total):
        taken = jnp.int32(0)
        source = lax.rem(me - j + total, total)
        for r in range(users[j].shape[0]):
            user = users[j][r]
            mine = user // own_rows == me
            slot = jnp.where(mine, source * cap + taken, -1)
            taken = taken + mine.astype(jnp.int32)
            chosen = jnp.where((slot_index == slot) & (row_index == user % own_rows), 1.0, chosen)
    out[...] = dot(chosen.astype(jnp.bfloat16), states[...], NN).astype(jnp.bfloat16)


def score_kernel(total, planes, parts, cap, *refs):
    users, refs = refs[:total], refs[total:]
    states, refs = refs[:total], refs[total:]
    cands, refs = refs[:total], refs[total:]
    items, refs = refs[:1 + (planes - 1) * parts], refs[1 + (planes - 1) * parts:]
    pairs, outs = refs[0], refs[1:]
    me = lax.axis_index("shard")
    plane = lax.axis_index("cache")
    core = lax.axis_index("pair")
    slots = states[0].shape[0]
    own_rows = items[0].shape[0]
    user_rows = slots_rows(users, total, cap, me)
    wanted = jnp.concatenate([ref[...] for ref in states], axis=0)
    blocks = []
    for q in range(planes):
        at = lax.rem(plane - q + planes, planes)
        base = (me * planes + at) * own_rows
        pair_row = pairs[pl.ds(at, 1), :]
        if q == 0:
            blocks.append((items[0], base, 0, pair_row))
        else:
            for h in range(parts):
                piece = own_rows // parts
                start = lax.rem(core - h + parts, parts) * piece
                blocks.append((items[1 + (q - 1) * parts + h], base + start, start, pair_row))
    linear = []
    for rows, base, start, pair_row in blocks:
        count = rows.shape[0]
        pick = iota((count, own_rows), 0) + start == iota((count, own_rows), 1)
        pair_column = jnp.sum(jnp.where(pick, pair_row, 0.0), axis=1, keepdims=True)
        linear.append((dot(rows[...], wanted, NT), base, pair_column))
    for j in range(total):
        width = cands[j].shape[1]
        readers = users[j].shape[0]
        lane = iota((1, width), 1) // (width // readers)
        slot_row = jnp.zeros((1, width), jnp.int32)
        for r in range(readers):
            slot_row = jnp.where(lane == r, user_rows[j][r], slot_row)
        spread = (iota((total * slots, width), 0) == slot_row).astype(jnp.float32)
        result = jnp.zeros((1, width), jnp.float32)
        for block, base, pair_column in linear:
            scores = dot(block, spread, NN, precision=lax.Precision.HIGHEST) + pair_column
            hit = iota(scores.shape, 0) + base == cands[j][...]
            result = result + jnp.sum(jnp.where(hit, scores, 0.0), axis=0, keepdims=True)
        outs[j][...] = result


def slots_rows(users, total, cap, me):
    result = []
    for j in range(total):
        source = lax.rem(me - j + total, total)
        holders = [users[j][r] // USER_ROWS[0] for r in range(users[j].shape[0])]
        line = []
        for r, holder in enumerate(holders):
            rank = jnp.int32(0)
            for earlier in holders[:r]:
                rank = rank + (earlier == holder).astype(jnp.int32)
            arrival = lax.rem(me - holder + total, total)
            line.append(arrival * (total * cap) + source * cap + rank)
        result.append(line)
    return result


USER_ROWS = [128]


def shift(x, axis, step):
    size = lax.axis_size(axis)
    return lax.ppermute(x, axis, [(s, (s + step) % size) for s in range(size)])


def body(cand_items, reader_users, item_table, user_states, pair_mats, pair_fields):
    total = lax.axis_size("shard")
    planes = lax.axis_size("cache")
    parts = lax.axis_size("pair")
    groups = lax.axis_size("groups")
    half = cand_items.shape[0]
    rows, width = item_table.shape
    readers = reader_users.shape[0]
    cap = 2 * ((readers + total - 1) // total)
    USER_ROWS[0] = user_states.shape[0]
    vmem = pl.BlockSpec(memory_space=pltpu.VMEM)
    smem = pl.BlockSpec(memory_space=pltpu.SMEM)
    anywhere = pl.BlockSpec(memory_space=pl.ANY)
    params = pltpu.CompilerParams(vmem_limit_bytes=VMEM_LIMIT)

    with jax.named_scope("ids"):
        users = [reader_users] + [shift(reader_users, "shard", j) for j in range(1, total)]
        cands = [cand_items] + [shift(cand_items, "shard", j) for j in range(1, total)]

    with jax.named_scope("item_rows"):
        piece = rows // parts
        mine = lax.dynamic_slice_in_dim(item_table, lax.axis_index("pair") * piece, piece, 0)
        items = [item_table]
        for q in range(1, planes):
            crossed = shift(mine, "cache", q)
            items.append(crossed)
            items.extend(shift(crossed, "pair", h) for h in range(1, parts))

    with jax.named_scope("pairs"):
        count = pair_mats.shape[0] // groups
        pair_scores = pl.pallas_call(
            pair_kernel,
            out_shape=jax.ShapeDtypeStruct((planes, rows), jnp.float32),
            in_specs=[smem, vmem, anywhere],
            out_specs=vmem,
            scratch_shapes=[
                pltpu.VMEM((K, K, count), jnp.bfloat16),
                pltpu.VMEM((width, rows), jnp.float32),
                pltpu.VMEM((width, rows), jnp.bfloat16),
                pltpu.VMEM((count * K, LANES), jnp.float32),
                pltpu.SemaphoreType.DMA,
            ],
            compiler_params=params,
            cost_estimate=pl.CostEstimate(flops=2 * count * K * K * rows * 16, bytes_accessed=2 * 1024 * 1024, transcendentals=0),
        )(pair_fields.T, item_table, jnp.transpose(pair_mats, (1, 2, 0)))
        pair_scores = lax.psum(pair_scores, ("groups", "cache", "pair"))

    with jax.named_scope("states"):
        picked = pl.pallas_call(
            functools.partial(pick_kernel, total, cap),
            out_shape=jax.ShapeDtypeStruct((total * cap, width), jnp.bfloat16),
            in_specs=[smem] * total + [vmem],
            out_specs=vmem,
            compiler_params=params,
            cost_estimate=pl.CostEstimate(flops=2 * total * cap * rows * width, bytes_accessed=1024 * 1024, transcendentals=0),
        )(*users, user_states)
        states = [picked] + [shift(picked, "shard", j) for j in range(1, total)]

    with jax.named_scope("scores"):
        outs = pl.pallas_call(
            functools.partial(score_kernel, total, planes, parts, cap),
            out_shape=[jax.ShapeDtypeStruct((1, half), jnp.float32)] * total,
            in_specs=[smem] * total + [vmem] * total + [vmem] * total + [vmem] * len(items) + [vmem],
            out_specs=[vmem] * total,
            compiler_params=params,
            cost_estimate=pl.CostEstimate(flops=2 * 64 * 256 * width, bytes_accessed=2 * 1024 * 1024, transcendentals=0),
        )(*users, *states, *[c.reshape(1, half) for c in cands], *items, pair_scores)

    with jax.named_scope("back"):
        result = outs[0]
        for j in range(1, total):
            result = result + shift(outs[j], "shard", -j)
    return result.reshape(half)


def solution(mesh):
    return jax.shard_map(
        body,
        mesh=mesh,
        in_specs=(
            P(("groups", "shard", "cache", "pair")),
            P(("groups", "shard", "cache", "pair")),
            P(("shard", "cache"), None),
            P(("groups", "shard"), None),
            P("pair", None, None),
            P("pair", None),
        ),
        out_specs=P(("groups", "shard", "cache", "pair")),
        check_vma=False,
    )
```

```python
import functools

import jax
import jax.numpy as jnp
from jax import lax
from jax.experimental import pallas as pl
from jax.experimental.pallas import tpu as pltpu
from jax.sharding import PartitionSpec as P

K = 64
FI = 48
LANES = 128
VMEM_LIMIT = 48 * 1024 * 1024
NT = (((1,), (1,)), ((), ()))
TN = (((0,), (0,)), ((), ()))
NN = (((1,), (0,)), ((), ()))


def dot(a, b, dims, **kw):
    return lax.dot_general(a, b, dims, preferred_element_type=jnp.float32, **kw)


def iota(shape, dim):
    return lax.broadcasted_iota(jnp.int32, shape, dim)


def pair_kernel(fields, items, mats, out, mats_own, rows32, rows16, stacked, sem):
    count = mats_own.shape[2]
    first = pl.multiple_of(lax.axis_index("groups") * count, count)
    copy = pltpu.make_async_copy(mats.at[:, :, pl.ds(first, count)], mats_own, sem)
    copy.start()
    rows = items.shape[0]
    eye = (iota((LANES, LANES), 0) == iota((LANES, LANES), 1)).astype(jnp.bfloat16)
    for t in range(items.shape[1] // LANES):
        turned = dot(eye, items[:, t * LANES:(t + 1) * LANES], NT)
        rows32[t * LANES:(t + 1) * LANES, :] = turned
        rows16[t * LANES:(t + 1) * LANES, :] = turned.astype(jnp.bfloat16)
    copy.wait()
    eye_pairs = (iota((count, count), 0) == iota((count, count), 1)).astype(jnp.bfloat16)
    for k in range(K):
        both = jnp.concatenate([mats_own[k], mats_own[k]], axis=0)
        stacked[pl.ds(k, count, stride=K), :] = dot(eye_pairs, both, NT)

    def one(p, total):
        a = pl.multiple_of(fields[0, first + p] * K, K)
        b = pl.multiple_of(fields[1, first + p] * K, K)
        matrix = stacked[pl.ds(pl.multiple_of(p * K, K), K), :][:, :K].astype(jnp.bfloat16)
        moved = dot(matrix, rows16[pl.ds(b, K), :], NN)
        return total + moved * rows32[pl.ds(a, K), :]

    total = lax.fori_loop(0, count, one, jnp.zeros((K, rows), jnp.float32), unroll=8)
    line = jnp.sum(total, axis=0, keepdims=True)
    mine = iota(out.shape, 0) == lax.axis_index("cache")
    out[...] = jnp.where(mine, jnp.broadcast_to(line, out.shape), 0.0)


def pick_kernel(cap, users, states, out):
    total, readers = users.shape
    own_rows = states.shape[0]
    me = lax.axis_index("shard")
    slots = out.shape[0]
    slot_index = iota((slots, own_rows), 0)
    row_index = iota((slots, own_rows), 1)

    def one(source, chosen):
        taken = jnp.int32(0)
        for r in range(readers):
            user = users[source, r]
            mine = user // own_rows == me
            slot = jnp.where(mine, source * cap + taken, -1)
            taken = taken + mine.astype(jnp.int32)
            chosen = jnp.where((slot_index == slot) & (row_index == user % own_rows), 1.0, chosen)
        return chosen

    chosen = lax.fori_loop(0, total, one, jnp.zeros((slots, own_rows), jnp.float32), unroll=total <= 8)
    out[...] = dot(chosen.astype(jnp.bfloat16), states[...], NN).astype(jnp.bfloat16)


def score_kernel(planes, parts, cap, user_rows, users, cands, states, pairs, *refs):
    items, out, linear = refs[:-2], refs[-2], refs[-1]
    total, readers = users.shape
    width = cands.shape[1]
    me = lax.axis_index("shard")
    plane = lax.axis_index("cache")
    core = lax.axis_index("pair")
    own_rows = items[0].shape[0]
    piece = own_rows // parts
    pair_sums = jnp.sum(pairs[...], axis=0)
    starts, pair_columns = [], []
    placed = 0
    for q in range(planes):
        at = lax.rem(plane - q + planes, planes)
        pair_row = jnp.sum(jnp.where(iota(pair_sums.shape, 0) == at, pair_sums, 0.0), axis=0, keepdims=True)
        for h in range(1 if q == 0 else parts):
            start = 0 if q == 0 else lax.rem(core - h + parts, parts) * piece
            rows = items[0 if q == 0 else 1 + (q - 1) * parts + h]
            count = rows.shape[0]
            linear[placed:placed + count, :] = dot(rows[...], states[...], NT)
            pick = iota((count, own_rows), 0) + start == iota((count, own_rows), 1)
            pair_columns.append(jnp.sum(jnp.where(pick, pair_row, 0.0), axis=1, keepdims=True))
            starts.append(iota((count, 1), 0) + (me * planes + at) * own_rows + start)
            placed += count
    pair_column = jnp.concatenate(pair_columns, axis=0)
    item_ids = jnp.concatenate(starts, axis=0)
    lane = iota((1, width), 1) // (width // readers)

    def one(source, carry):
        slot_row = jnp.zeros((1, width), jnp.int32)
        holders = [users[source, r] // user_rows for r in range(readers)]
        for r, holder in enumerate(holders):
            rank = jnp.int32(0)
            for earlier in holders[:r]:
                rank = rank + (earlier == holder).astype(jnp.int32)
            slot_row = jnp.where(lane == r, (holder * total + source) * cap + rank, slot_row)
        spread = (iota((states.shape[0], width), 0) == slot_row).astype(jnp.float32)
        scores = dot(linear[...], spread, NN, precision=lax.Precision.HIGHEST) + pair_column
        hit = item_ids == cands[pl.ds(source, 1), :]
        out[pl.ds(source, 1), :] = jnp.sum(jnp.where(hit, scores, 0.0), axis=0, keepdims=True)
        return carry

    lax.fori_loop(0, total, one, 0, unroll=total <= 8)


def shift(x, axis, step):
    size = lax.axis_size(axis)
    return lax.ppermute(x, axis, [(s, (s + step) % size) for s in range(size)])


def body(cand_items, reader_users, item_table, user_states, pair_mats, pair_fields):
    total = lax.axis_size("shard")
    planes = lax.axis_size("cache")
    parts = lax.axis_size("pair")
    groups = lax.axis_size("groups")
    half = cand_items.shape[0]
    rows, width = item_table.shape
    readers = reader_users.shape[0]
    cap = 2 * ((readers + total - 1) // total)
    vmem = pl.BlockSpec(memory_space=pltpu.VMEM)
    smem = pl.BlockSpec(memory_space=pltpu.SMEM)
    anywhere = pl.BlockSpec(memory_space=pl.ANY)
    params = pltpu.CompilerParams(vmem_limit_bytes=VMEM_LIMIT)

    with jax.named_scope("ids"):
        users = lax.all_gather(reader_users, "shard", axis=0)
        cands = lax.all_gather(cand_items, "shard", axis=0)

    with jax.named_scope("item_rows"):
        piece = rows // parts
        mine = lax.dynamic_slice_in_dim(item_table, lax.axis_index("pair") * piece, piece, 0)
        items = [item_table]
        for q in range(1, planes):
            crossed = shift(mine, "cache", q)
            items.append(crossed)
            items.extend(shift(crossed, "pair", h) for h in range(1, parts))

    with jax.named_scope("pairs"):
        count = pair_mats.shape[0] // groups
        pair_scores = pl.pallas_call(
            pair_kernel,
            out_shape=jax.ShapeDtypeStruct((planes, rows), jnp.float32),
            in_specs=[smem, vmem, anywhere],
            out_specs=vmem,
            scratch_shapes=[
                pltpu.VMEM((K, K, count), jnp.bfloat16),
                pltpu.VMEM((width, rows), jnp.float32),
                pltpu.VMEM((width, rows), jnp.bfloat16),
                pltpu.VMEM((count * K, LANES), jnp.float32),
                pltpu.SemaphoreType.DMA,
            ],
            compiler_params=params,
            cost_estimate=pl.CostEstimate(flops=2 * count * K * K * rows * 16, bytes_accessed=2 * 1024 * 1024, transcendentals=0),
        )(pair_fields.T, item_table, jnp.transpose(pair_mats, (1, 2, 0)))
        pair_scores = lax.all_gather(pair_scores, ("groups", "cache", "pair"), axis=0)

    with jax.named_scope("states"):
        picked = pl.pallas_call(
            functools.partial(pick_kernel, cap),
            out_shape=jax.ShapeDtypeStruct((total * cap, width), jnp.bfloat16),
            in_specs=[smem, vmem],
            out_specs=vmem,
            compiler_params=params,
            cost_estimate=pl.CostEstimate(flops=2 * total * cap * rows * width, bytes_accessed=1024 * 1024, transcendentals=0),
        )(users, user_states)
        states = lax.all_gather(picked, "shard", axis=0, tiled=True)

    with jax.named_scope("scores"):
        parted = pl.pallas_call(
            functools.partial(score_kernel, planes, parts, cap, user_states.shape[0]),
            out_shape=jax.ShapeDtypeStruct((total, half), jnp.float32),
            in_specs=[smem] + [vmem] * (3 + len(items)),
            out_specs=vmem,
            scratch_shapes=[pltpu.VMEM((planes * rows, total * total * cap), jnp.float32)],
            compiler_params=params,
            cost_estimate=pl.CostEstimate(flops=2 * 64 * 256 * width, bytes_accessed=2 * 1024 * 1024, transcendentals=0),
        )(users, cands, states, pair_scores, *items)

    with jax.named_scope("back"):
        result = lax.all_to_all(parted, "shard", split_axis=0, concat_axis=0, tiled=True)
        return jnp.sum(result, axis=0)


def solution(mesh):
    return jax.shard_map(
        body,
        mesh=mesh,
        in_specs=(
            P(("groups", "shard", "cache", "pair")),
            P(("groups", "shard", "cache", "pair")),
            P(("shard", "cache"), None),
            P(("groups", "shard"), None),
            P("pair", None, None),
            P("pair", None),
        ),
        out_specs=P(("groups", "shard", "cache", "pair")),
        check_vma=False,
    )
```

```python
import functools

import jax
import jax.numpy as jnp
from jax import lax
from jax.experimental import pallas as pl
from jax.experimental.pallas import tpu as pltpu
from jax.sharding import PartitionSpec as P

K = 64
LANES = 128
PITCH = 72
CODE = 128
VMEM_LIMIT = 40 * 1024 * 1024
NT = (((1,), (1,)), ((), ()))
NN = (((1,), (0,)), ((), ()))


def dot(a, b, dims, **kw):
    return lax.dot_general(a, b, dims, preferred_element_type=jnp.float32, **kw)


def iota(shape, dim):
    return lax.broadcasted_iota(jnp.int32, shape, dim)


def ring(index, size):
    return lax.rem(index + size, size)


def pick_kernel(total, cap, *refs):
    users, (own_users, cands, states_hbm, out, held, own, sems) = refs[:total - 1], refs[total - 1:]
    copies = [
        pltpu.make_async_copy(own_users, own, sems.at[0]),
        pltpu.make_async_copy(states_hbm, held, sems.at[1]),
    ]
    for copy in copies:
        copy.start()
    width = held.shape[1]
    code = cands[...]
    digits = jnp.where(iota((out.shape[0], code.shape[1]), 0) == 0, code // CODE, code % CODE)
    out[:, width:] = jnp.where(iota(digits.shape, 0) < 2, digits, 0).astype(jnp.float32).astype(jnp.bfloat16)
    copies[0].wait()
    own_rows = held.shape[0]
    me = lax.axis_index("shard")
    slots = out.shape[0]
    slot_index = iota((slots, own_rows), 0)
    row_index = iota((slots, own_rows), 1)
    chosen = jnp.zeros((slots, own_rows), jnp.float32)
    for j, line in enumerate((own,) + tuple(users)):
        source = ring(me - j, total)
        taken = jnp.int32(0)
        for r in range(line.shape[0]):
            user = line[r]
            mine = user // own_rows == me
            slot = jnp.where(mine, source * cap + taken, -1)
            taken = taken + mine.astype(jnp.int32)
            chosen = jnp.where((slot_index == slot) & (row_index == user % own_rows), 1.0, chosen)
    chosen = chosen.astype(jnp.bfloat16)
    copies[1].wait()
    out[:, :width] = dot(chosen, held[...], NN).astype(jnp.bfloat16)


def pair_kernel(fields_hbm, items_hbm, mats_hbm, picked, crossed, out, passed, fields, items, mats, rows32, rows16, stacked, sems):
    del picked, crossed, passed
    copies = [
        pltpu.make_async_copy(items_hbm, items, sems.at[0]),
        pltpu.make_async_copy(mats_hbm, mats, sems.at[1]),
        pltpu.make_async_copy(fields_hbm, fields, sems.at[2]),
    ]
    for copy in copies:
        copy.start()
    count = mats.shape[2]
    eye = (iota((LANES, LANES), 0) == iota((LANES, LANES), 1)).astype(jnp.bfloat16)
    copies[0].wait()
    for t in range(items.shape[1] // LANES):
        turned = dot(eye, items[:, t * LANES:(t + 1) * LANES], NT)
        rows32[t * LANES:(t + 1) * LANES, :] = turned
        rows16[t * LANES:(t + 1) * LANES, :] = turned.astype(jnp.bfloat16)
    eye_pairs = (iota((count, count), 0) == iota((count, count), 1)).astype(jnp.bfloat16)
    side = (iota((count, LANES), 0) % 2 == 0) == (iota((count, LANES), 1) < K)
    copies[1].wait()
    for k in range(K):
        both = jnp.concatenate([mats[k], mats[k]], axis=0)
        stacked[pl.ds(k, count, stride=PITCH), :] = jnp.where(side, dot(eye_pairs, both, NT), 0.0)
    copies[2].wait()

    def two(step, total):
        first = step * 2
        lefts, rights, mults = [], [], []
        for p in (first, first + 1):
            a = pl.multiple_of(fields[0, p] * K, K)
            b = pl.multiple_of(fields[1, p] * K, K)
            lefts.append(stacked[pl.ds(pl.multiple_of(p * PITCH, 8), K), :].astype(jnp.bfloat16))
            rights.append(rows16[pl.ds(b, K), :])
            mults.append(rows32[pl.ds(a, K), :])
        moved = dot(jnp.concatenate(lefts, axis=0), jnp.concatenate(rights, axis=0), NN)
        return total + moved * jnp.concatenate(mults, axis=0)

    total = lax.fori_loop(0, count // 2, two, jnp.zeros((2 * K, items.shape[0]), jnp.float32), unroll=16)
    out[...] = jnp.sum(total, axis=0, keepdims=True)


def score_kernel(total, planes, parts, cap, user_rows, *refs):
    users, refs = refs[:total], refs[total:]
    states, refs = refs[:total], refs[total:]
    pairs, refs = refs[:planes * parts], refs[planes * parts:]
    items, refs = refs[:1 + (planes - 1) * parts], refs[1 + (planes - 1) * parts:]
    outs, (asked, wanted, cands, linear, rows_out) = refs[:total], refs[total:]
    readers = users[0].shape[0]
    slots = states[0].shape[0]
    width = items[0].shape[1]
    half = outs[0].shape[1]
    me = lax.axis_index("shard")
    plane = lax.axis_index("cache")
    core = lax.axis_index("pair")
    for j in range(total):
        for r in range(readers):
            asked[j, r] = users[j][r]
        wanted[j * slots:(j + 1) * slots, :] = states[j][:, :width]
        digits = states[j][:, width:].astype(jnp.float32)
        place = iota(digits.shape, 0)
        weight = jnp.where(place == 0, float(CODE), jnp.where(place == 1, 1.0, 0.0))
        cands[j:j + 1, :] = jnp.sum(digits * weight, axis=0, keepdims=True).astype(jnp.int32)
    own_rows = items[0].shape[0]
    piece = own_rows // parts
    starts, pair_columns = [], []
    placed = 0
    for q in range(planes):
        at = ring(plane - q, planes)
        pair_row = sum(pairs[q * parts + h][...] for h in range(parts))
        for h in range(1 if q == 0 else parts):
            start = 0 if q == 0 else ring(core - h, parts) * piece
            rows = items[0 if q == 0 else 1 + (q - 1) * parts + h]
            count = rows.shape[0]
            linear[placed:placed + count, :] = dot(rows[...], wanted[...], NT)
            pick = iota((count, own_rows), 0) + start == iota((count, own_rows), 1)
            pair_columns.append(jnp.sum(jnp.where(pick, pair_row, 0.0), axis=1, keepdims=True))
            starts.append(iota((count, 1), 0) + (me * planes + at) * own_rows + start)
            placed += count
    pair_column = jnp.concatenate(pair_columns, axis=0)
    item_ids = jnp.concatenate(starts, axis=0)
    lane = iota((1, half), 1) // (half // readers)

    def one(j, carry):
        source = ring(me - j, total)
        slot_row = jnp.zeros((1, half), jnp.int32)
        holders = [asked[j, r] // user_rows for r in range(readers)]
        for r, holder in enumerate(holders):
            rank = jnp.int32(0)
            for earlier in holders[:r]:
                rank = rank + (earlier == holder).astype(jnp.int32)
            slot_row = jnp.where(lane == r, ring(me - holder, total) * slots + source * cap + rank, slot_row)
        spread = (iota((wanted.shape[0], half), 0) == slot_row).astype(jnp.float32)
        scores = dot(linear[...], spread, NN, precision=lax.Precision.HIGHEST) + pair_column
        hit = item_ids == cands[pl.ds(j, 1), :]
        rows_out[pl.ds(j, 1), :] = jnp.sum(jnp.where(hit, scores, 0.0), axis=0, keepdims=True)
        return carry

    lax.fori_loop(0, total, one, 0, unroll=total <= 8)
    for j in range(total):
        outs[j][...] = rows_out[j:j + 1, :]


def shift(x, axis, step):
    size = lax.axis_size(axis)
    return lax.ppermute(x, axis, [(s, (s + step) % size) for s in range(size)])


def body(cand_items, reader_users, item_table, user_states, pair_mats, pair_fields):
    total = lax.axis_size("shard")
    planes = lax.axis_size("cache")
    parts = lax.axis_size("pair")
    half = cand_items.shape[0]
    rows, width = item_table.shape
    readers = reader_users.shape[0]
    cap = 2 * ((readers + total - 1) // total)
    slots = -(-total * cap // 16) * 16
    count = pair_mats.shape[0]
    vmem = pl.BlockSpec(memory_space=pltpu.VMEM)
    smem = pl.BlockSpec(memory_space=pltpu.SMEM)
    hbm = pl.BlockSpec(memory_space=pltpu.HBM)
    anywhere = pl.BlockSpec(memory_space=pl.ANY)
    params = pltpu.CompilerParams(vmem_limit_bytes=VMEM_LIMIT)

    with jax.named_scope("ids"):
        others = [shift(reader_users, "shard", j) for j in range(1, total)]
        users = [reader_users] + others

    with jax.named_scope("item_rows"):
        piece = rows // parts
        mine = lax.dynamic_slice_in_dim(item_table, lax.axis_index("pair") * piece, piece, 0)
        crossed = [shift(mine, "cache", q) for q in range(1, planes)]

    with jax.named_scope("states"):
        picked = pl.pallas_call(
            functools.partial(pick_kernel, total, cap),
            out_shape=jax.ShapeDtypeStruct((slots, width + half), jnp.bfloat16),
            in_specs=[smem] * (total - 1) + [hbm, vmem, hbm],
            out_specs=vmem,
            scratch_shapes=[
                pltpu.VMEM(user_states.shape, jnp.bfloat16),
                pltpu.SMEM((readers,), jnp.int32),
                pltpu.SemaphoreType.DMA((2,)),
            ],
            compiler_params=params,
            cost_estimate=pl.CostEstimate(flops=2 * slots * rows * width, bytes_accessed=1024 * 1024, transcendentals=0),
        )(*others, reader_users, cand_items.reshape(1, half), user_states)
        states = [picked] + [shift(picked, "shard", j) for j in range(1, total)]

    with jax.named_scope("pairs"):
        pair_scores, passed = pl.pallas_call(
            pair_kernel,
            out_shape=(
                jax.ShapeDtypeStruct((1, rows), jnp.float32),
                jax.ShapeDtypeStruct(crossed[0].shape, crossed[0].dtype),
            ),
            in_specs=[hbm, hbm, hbm, anywhere, anywhere],
            out_specs=(vmem, anywhere),
            input_output_aliases={4: 1},
            scratch_shapes=[
                pltpu.SMEM((2, count), jnp.int32),
                pltpu.VMEM((rows, width), jnp.bfloat16),
                pltpu.VMEM((K, K, count), jnp.bfloat16),
                pltpu.VMEM((width, rows), jnp.float32),
                pltpu.VMEM((width, rows), jnp.bfloat16),
                pltpu.VMEM((count * PITCH, LANES), jnp.float32),
                pltpu.SemaphoreType.DMA((3,)),
            ],
            compiler_params=params,
            cost_estimate=pl.CostEstimate(flops=2 * count * K * K * rows * 16, bytes_accessed=4 * 1024 * 1024, transcendentals=0),
        )(pair_fields.T, item_table, jnp.transpose(pair_mats, (1, 2, 0)), picked, crossed[0])
        crossed[0] = passed
        items = [item_table]
        pairs = []
        for q in range(planes):
            moved = pair_scores if q == 0 else shift(pair_scores, "cache", q)
            pairs.append(moved)
            if q:
                items.append(crossed[q - 1])
            for h in range(1, parts):
                steps = [((c, d), ((c + q) % planes, (d + h) % parts)) for c in range(planes) for d in range(parts)]
                perm = [(c * parts + d, e * parts + f) for (c, d), (e, f) in steps]
                pairs.append(lax.ppermute(pair_scores, ("cache", "pair"), perm))
                if q:
                    items.append(shift(crossed[q - 1], "pair", h))

    with jax.named_scope("scores"):
        outs = pl.pallas_call(
            functools.partial(score_kernel, total, planes, parts, cap, user_states.shape[0]),
            out_shape=[jax.ShapeDtypeStruct((1, half), jnp.float32)] * total,
            in_specs=[smem] * total + [vmem] * (total + len(pairs) + len(items)),
            out_specs=[vmem] * total,
            scratch_shapes=[
                pltpu.SMEM((total, readers), jnp.int32),
                pltpu.VMEM((total * slots, width), jnp.bfloat16),
                pltpu.VMEM((-(-total // 8) * 8, half), jnp.int32),
                pltpu.VMEM((planes * rows, total * slots), jnp.float32),
                pltpu.VMEM((-(-total // 8) * 8, half), jnp.float32),
            ],
            compiler_params=params,
            cost_estimate=pl.CostEstimate(flops=2 * 64 * 256 * width, bytes_accessed=2 * 1024 * 1024, transcendentals=0),
        )(*users, *states, *pairs, *items)

    with jax.named_scope("back"):
        result = outs[0]
        for j in range(1, total):
            result = result + shift(outs[j], "shard", -j)
    return result.reshape(half)


def solution(mesh):
    return jax.shard_map(
        body,
        mesh=mesh,
        in_specs=(
            P(("groups", "shard", "cache", "pair")),
            P(("groups", "shard", "cache", "pair")),
            P(("shard", "cache"), None),
            P(("groups", "shard"), None),
            P("pair", None, None),
            P("pair", None),
        ),
        out_specs=P(("groups", "shard", "cache", "pair")),
        check_vma=False,
    )
```

```python
import functools

import jax
import jax.numpy as jnp
from jax import lax
from jax.experimental import pallas as pl
from jax.experimental.pallas import tpu as pltpu
from jax.sharding import PartitionSpec as P

K = 64
LANES = 128
PITCH = 72
CODE = 128
VMEM_LIMIT = 40 * 1024 * 1024
NT = (((1,), (1,)), ((), ()))
NN = (((1,), (0,)), ((), ()))


def dot(a, b, dims, **kw):
    return lax.dot_general(a, b, dims, preferred_element_type=jnp.float32, **kw)


def iota(shape, dim):
    return lax.broadcasted_iota(jnp.int32, shape, dim)


def ring(index, size):
    return lax.rem(index + size, size)


def pick_kernel(total, cap, *refs):
    users, (own_users, own_cands, states_hbm, out, held, own, cands, sems) = refs[:total - 1], refs[total - 1:]
    copies = [
        pltpu.make_async_copy(own_users, own, sems.at[0]),
        pltpu.make_async_copy(states_hbm, held, sems.at[1]),
        pltpu.make_async_copy(own_cands, cands, sems.at[2]),
    ]
    for copy in copies:
        copy.start()
    width = held.shape[1]
    copies[0].wait()
    own_rows = held.shape[0]
    me = lax.axis_index("shard")
    slots = out.shape[0]
    slot_index = iota((slots, own_rows), 0)
    row_index = iota((slots, own_rows), 1)
    chosen = jnp.zeros((slots, own_rows), jnp.float32)
    for j, line in enumerate((own,) + tuple(users)):
        source = ring(me - j, total)
        taken = jnp.int32(0)
        for r in range(line.shape[0]):
            user = line[r]
            mine = user // own_rows == me
            slot = jnp.where(mine, source * cap + taken, -1)
            taken = taken + mine.astype(jnp.int32)
            chosen = jnp.where((slot_index == slot) & (row_index == user % own_rows), 1.0, chosen)
    chosen = chosen.astype(jnp.bfloat16)
    copies[2].wait()
    code = cands[...]
    digits = jnp.where(iota((slots, code.shape[1]), 0) == 0, code // CODE, code % CODE)
    out[:, width:] = jnp.where(iota(digits.shape, 0) < 2, digits, 0).astype(jnp.float32).astype(jnp.bfloat16)
    copies[1].wait()
    out[:, :width] = dot(chosen, held[...], NN).astype(jnp.bfloat16)


def pair_kernel(fields_hbm, items_hbm, mats_hbm, picked, crossed, out, passed, fields, items, mats, rows32, rows16, stacked, sems):
    del picked, crossed, passed
    copies = [
        pltpu.make_async_copy(items_hbm, items, sems.at[0]),
        pltpu.make_async_copy(mats_hbm, mats, sems.at[1]),
        pltpu.make_async_copy(fields_hbm, fields, sems.at[2]),
    ]
    for copy in copies:
        copy.start()
    count = mats.shape[2]
    eye = (iota((LANES, LANES), 0) == iota((LANES, LANES), 1)).astype(jnp.bfloat16)
    copies[0].wait()
    for t in range(items.shape[1] // LANES):
        turned = dot(eye, items[:, t * LANES:(t + 1) * LANES], NT)
        rows32[t * LANES:(t + 1) * LANES, :] = turned
        rows16[t * LANES:(t + 1) * LANES, :] = turned.astype(jnp.bfloat16)
    eye_pairs = (iota((count, count), 0) == iota((count, count), 1)).astype(jnp.bfloat16)
    side = (iota((count, LANES), 0) % 2 == 0) == (iota((count, LANES), 1) < K)
    copies[1].wait()
    for k in range(K):
        both = jnp.concatenate([mats[k], mats[k]], axis=0)
        stacked[pl.ds(k, count, stride=PITCH), :] = jnp.where(side, dot(eye_pairs, both, NT), 0.0)
    copies[2].wait()

    def two(step, total):
        first = step * 2
        lefts, rights, mults = [], [], []
        for p in (first, first + 1):
            a = pl.multiple_of(fields[0, p] * K, K)
            b = pl.multiple_of(fields[1, p] * K, K)
            lefts.append(stacked[pl.ds(pl.multiple_of(p * PITCH, 8), K), :].astype(jnp.bfloat16))
            rights.append(rows16[pl.ds(b, K), :])
            mults.append(rows32[pl.ds(a, K), :])
        moved = dot(jnp.concatenate(lefts, axis=0), jnp.concatenate(rights, axis=0), NN)
        return total + moved * jnp.concatenate(mults, axis=0)

    total = lax.fori_loop(0, count // 2, two, jnp.zeros((2 * K, items.shape[0]), jnp.float32), unroll=16)
    mine = iota(out.shape, 0) == lax.axis_index("cache")
    out[...] = jnp.where(mine, jnp.sum(total, axis=0, keepdims=True), 0.0)


def score_kernel(total, planes, parts, cap, user_rows, *refs):
    users, refs = refs[:total], refs[total:]
    states, refs = refs[:total], refs[total:]
    pairs, refs = refs[0], refs[1:]
    items, refs = refs[:1 + (planes - 1) * parts], refs[1 + (planes - 1) * parts:]
    outs, (asked, wanted, cands, linear, rows_out) = refs[:total], refs[total:]
    readers = users[0].shape[0]
    slots = states[0].shape[0]
    width = items[0].shape[1]
    half = outs[0].shape[1]
    me = lax.axis_index("shard")
    plane = lax.axis_index("cache")
    core = lax.axis_index("pair")
    for j in range(total):
        for r in range(readers):
            asked[j, r] = users[j][r]
        wanted[j * slots:(j + 1) * slots, :] = states[j][:, :width]
        digits = states[j][:, width:].astype(jnp.float32)
        place = iota(digits.shape, 0)
        weight = jnp.where(place == 0, float(CODE), jnp.where(place == 1, 1.0, 0.0))
        cands[j:j + 1, :] = jnp.sum(digits * weight, axis=0, keepdims=True).astype(jnp.int32)
    own_rows = items[0].shape[0]
    piece = own_rows // parts
    starts, pair_columns = [], []
    placed = 0
    for q in range(planes):
        at = ring(plane - q, planes)
        pair_row = pairs[pl.ds(at, 1), :]
        for h in range(1 if q == 0 else parts):
            start = 0 if q == 0 else ring(core - h, parts) * piece
            rows = items[0 if q == 0 else 1 + (q - 1) * parts + h]
            count = rows.shape[0]
            linear[placed:placed + count, :] = dot(rows[...], wanted[...], NT)
            pick = iota((count, own_rows), 0) + start == iota((count, own_rows), 1)
            pair_columns.append(jnp.sum(jnp.where(pick, pair_row, 0.0), axis=1, keepdims=True))
            starts.append(iota((count, 1), 0) + (me * planes + at) * own_rows + start)
            placed += count
    pair_column = jnp.concatenate(pair_columns, axis=0)
    item_ids = jnp.concatenate(starts, axis=0)
    lane = iota((1, half), 1) // (half // readers)

    def one(j, carry):
        source = ring(me - j, total)
        slot_row = jnp.zeros((1, half), jnp.int32)
        holders = [asked[j, r] // user_rows for r in range(readers)]
        for r, holder in enumerate(holders):
            rank = jnp.int32(0)
            for earlier in holders[:r]:
                rank = rank + (earlier == holder).astype(jnp.int32)
            slot_row = jnp.where(lane == r, ring(me - holder, total) * slots + source * cap + rank, slot_row)
        spread = (iota((wanted.shape[0], half), 0) == slot_row).astype(jnp.float32)
        scores = dot(linear[...], spread, NN, precision=lax.Precision.HIGHEST) + pair_column
        hit = item_ids == cands[pl.ds(j, 1), :]
        rows_out[pl.ds(j, 1), :] = jnp.sum(jnp.where(hit, scores, 0.0), axis=0, keepdims=True)
        return carry

    lax.fori_loop(0, total, one, 0, unroll=total <= 8)
    for j in range(total):
        outs[j][...] = rows_out[j:j + 1, :]


def shift(x, axis, step):
    size = lax.axis_size(axis)
    return lax.ppermute(x, axis, [(s, (s + step) % size) for s in range(size)])


def body(cand_items, reader_users, item_table, user_states, pair_mats, pair_fields):
    total = lax.axis_size("shard")
    planes = lax.axis_size("cache")
    parts = lax.axis_size("pair")
    half = cand_items.shape[0]
    rows, width = item_table.shape
    readers = reader_users.shape[0]
    cap = 2 * ((readers + total - 1) // total)
    slots = -(-total * cap // 16) * 16
    count = pair_mats.shape[0]
    vmem = pl.BlockSpec(memory_space=pltpu.VMEM)
    smem = pl.BlockSpec(memory_space=pltpu.SMEM)
    hbm = pl.BlockSpec(memory_space=pltpu.HBM)
    anywhere = pl.BlockSpec(memory_space=pl.ANY)
    params = pltpu.CompilerParams(vmem_limit_bytes=VMEM_LIMIT)

    def in_hbm(x):
        return pltpu.with_memory_space_constraint(x, pltpu.HBM)

    with jax.named_scope("ids"):
        others = [shift(reader_users, "shard", j) for j in range(1, total)]
        users = [reader_users] + others

    with jax.named_scope("item_rows"):
        piece = rows // parts
        mine = lax.dynamic_slice_in_dim(item_table, lax.axis_index("pair") * piece, piece, 0)
        crossed = [shift(mine, "cache", q) for q in range(1, planes)]

    with jax.named_scope("states"):
        picked = pl.pallas_call(
            functools.partial(pick_kernel, total, cap),
            out_shape=jax.ShapeDtypeStruct((slots, width + half), jnp.bfloat16),
            in_specs=[smem] * (total - 1) + [hbm, hbm, hbm],
            out_specs=vmem,
            scratch_shapes=[
                pltpu.VMEM(user_states.shape, jnp.bfloat16),
                pltpu.SMEM((readers,), jnp.int32),
                pltpu.VMEM((1, half), jnp.int32),
                pltpu.SemaphoreType.DMA((3,)),
            ],
            compiler_params=params,
            cost_estimate=pl.CostEstimate(flops=2 * slots * rows * width, bytes_accessed=1024 * 1024, transcendentals=0),
        )(*others, in_hbm(reader_users), in_hbm(cand_items.reshape(1, half)), in_hbm(user_states))
        states = [picked] + [shift(picked, "shard", j) for j in range(1, total)]

    with jax.named_scope("pairs"):
        pair_scores, passed = pl.pallas_call(
            pair_kernel,
            out_shape=(
                jax.ShapeDtypeStruct((planes, rows), jnp.float32),
                jax.ShapeDtypeStruct(crossed[0].shape, crossed[0].dtype),
            ),
            in_specs=[hbm, hbm, hbm, anywhere, anywhere],
            out_specs=(vmem, anywhere),
            input_output_aliases={4: 1},
            scratch_shapes=[
                pltpu.SMEM((2, count), jnp.int32),
                pltpu.VMEM((rows, width), jnp.bfloat16),
                pltpu.VMEM((K, K, count), jnp.bfloat16),
                pltpu.VMEM((width, rows), jnp.float32),
                pltpu.VMEM((width, rows), jnp.bfloat16),
                pltpu.VMEM((count * PITCH, LANES), jnp.float32),
                pltpu.SemaphoreType.DMA((3,)),
            ],
            compiler_params=params,
            cost_estimate=pl.CostEstimate(flops=2 * count * K * K * rows * 16, bytes_accessed=4 * 1024 * 1024, transcendentals=0),
        )(in_hbm(pair_fields.T), in_hbm(item_table), in_hbm(jnp.transpose(pair_mats, (1, 2, 0))), picked, crossed[0])
        crossed[0] = passed
        pair_scores = lax.psum(pair_scores, ("cache", "pair"))
        items = [item_table]
        for piece_in in crossed:
            items += [piece_in] + [shift(piece_in, "pair", h) for h in range(1, parts)]

    with jax.named_scope("scores"):
        outs = pl.pallas_call(
            functools.partial(score_kernel, total, planes, parts, cap, user_states.shape[0]),
            out_shape=[jax.ShapeDtypeStruct((1, half), jnp.float32)] * total,
            in_specs=[smem] * total + [vmem] * (total + 1 + len(items)),
            out_specs=[vmem] * total,
            scratch_shapes=[
                pltpu.SMEM((total, readers), jnp.int32),
                pltpu.VMEM((total * slots, width), jnp.bfloat16),
                pltpu.VMEM((-(-total // 8) * 8, half), jnp.int32),
                pltpu.VMEM((planes * rows, total * slots), jnp.float32),
                pltpu.VMEM((-(-total // 8) * 8, half), jnp.float32),
            ],
            compiler_params=params,
            cost_estimate=pl.CostEstimate(flops=2 * 64 * 256 * width, bytes_accessed=2 * 1024 * 1024, transcendentals=0),
        )(*users, *states, pair_scores, *items)

    with jax.named_scope("back"):
        result = outs[0]
        for j in range(1, total):
            result = result + shift(outs[j], "shard", -j)
    return result.reshape(half)


def solution(mesh):
    return jax.shard_map(
        body,
        mesh=mesh,
        in_specs=(
            P(("groups", "shard", "cache", "pair")),
            P(("groups", "shard", "cache", "pair")),
            P(("shard", "cache"), None),
            P(("groups", "shard"), None),
            P("pair", None, None),
            P("pair", None),
        ),
        out_specs=P(("groups", "shard", "cache", "pair")),
        check_vma=False,
    )
```

```python
import functools

import jax
import jax.numpy as jnp
from jax import lax
from jax.experimental import pallas as pl
from jax.experimental.pallas import tpu as pltpu
from jax.sharding import PartitionSpec as P

K = 64
LANES = 128
PITCH = 72
CODE = 128
VMEM_LIMIT = 40 * 1024 * 1024
NT = (((1,), (1,)), ((), ()))
NN = (((1,), (0,)), ((), ()))


def dot(a, b, dims, **kw):
    return lax.dot_general(a, b, dims, preferred_element_type=jnp.float32, **kw)


def iota(shape, dim):
    return lax.broadcasted_iota(jnp.int32, shape, dim)


def ring(index, size):
    return lax.rem(index + size, size)


def pick_kernel(total, cap, *refs):
    users, (cands, states, later, out) = refs[:total], refs[total:]
    del later
    width = states.shape[1]
    own_rows = states.shape[0]
    me = lax.axis_index("shard")
    slots = out.shape[0]
    slot_index = iota((slots, own_rows), 0)
    row_index = iota((slots, own_rows), 1)
    chosen = jnp.zeros((slots, own_rows), jnp.float32)
    for j, line in enumerate(users):
        source = ring(me - j, total)
        taken = jnp.int32(0)
        for r in range(line.shape[0]):
            user = line[r]
            mine = user // own_rows == me
            slot = jnp.where(mine, source * cap + taken, -1)
            taken = taken + mine.astype(jnp.int32)
            chosen = jnp.where((slot_index == slot) & (row_index == user % own_rows), 1.0, chosen)
    code = cands[...]
    digits = jnp.where(iota((slots, code.shape[1]), 0) == 0, code // CODE, code % CODE)
    out[:, width:] = jnp.where(iota(digits.shape, 0) < 2, digits, 0).astype(jnp.float32).astype(jnp.bfloat16)
    out[:, :width] = dot(chosen.astype(jnp.bfloat16), states[...], NN).astype(jnp.bfloat16)


def pair_kernel(fields_hbm, items_hbm, mats_hbm, out, fields, items, mats, rows32, rows16, stacked, sems):
    copies = [
        pltpu.make_async_copy(items_hbm, items, sems.at[0]),
        pltpu.make_async_copy(mats_hbm, mats, sems.at[1]),
        pltpu.make_async_copy(fields_hbm, fields, sems.at[2]),
    ]
    for copy in copies:
        copy.start()
    count = mats.shape[2]
    eye = (iota((LANES, LANES), 0) == iota((LANES, LANES), 1)).astype(jnp.bfloat16)
    copies[0].wait()
    for t in range(items.shape[1] // LANES):
        turned = dot(eye, items[:, t * LANES:(t + 1) * LANES], NT)
        rows32[t * LANES:(t + 1) * LANES, :] = turned
        rows16[t * LANES:(t + 1) * LANES, :] = turned.astype(jnp.bfloat16)
    eye_pairs = (iota((count, count), 0) == iota((count, count), 1)).astype(jnp.bfloat16)
    side = (iota((count, LANES), 0) % 2 == 0) == (iota((count, LANES), 1) < K)
    copies[1].wait()
    for k in range(K):
        both = jnp.concatenate([mats[k], mats[k]], axis=0)
        stacked[pl.ds(k, count, stride=PITCH), :] = jnp.where(side, dot(eye_pairs, both, NT), 0.0)
    copies[2].wait()

    def two(step, total):
        first = step * 2
        lefts, rights, mults = [], [], []
        for p in (first, first + 1):
            a = pl.multiple_of(fields[0, p] * K, K)
            b = pl.multiple_of(fields[1, p] * K, K)
            lefts.append(stacked[pl.ds(pl.multiple_of(p * PITCH, 8), K), :].astype(jnp.bfloat16))
            rights.append(rows16[pl.ds(b, K), :])
            mults.append(rows32[pl.ds(a, K), :])
        moved = dot(jnp.concatenate(lefts, axis=0), jnp.concatenate(rights, axis=0), NN)
        return total + moved * jnp.concatenate(mults, axis=0)

    total = lax.fori_loop(0, count // 2, two, jnp.zeros((2 * K, items.shape[0]), jnp.float32), unroll=16)
    mine = iota(out.shape, 0) == lax.axis_index("cache")
    out[...] = jnp.where(mine, jnp.sum(total, axis=0, keepdims=True), 0.0)


def score_kernel(total, cap, user_rows, *refs):
    users, refs = refs[:total], refs[total:]
    states, refs = refs[:total], refs[total:]
    pairs, items, out, asked, wanted, cands, linear = refs
    readers = users[0].shape[0]
    slots = states[0].shape[0]
    count, width = items.shape
    half = out.shape[1]
    me = lax.axis_index("shard")
    for j in range(total):
        for r in range(readers):
            asked[j, r] = users[j][r]
        wanted[j * slots:(j + 1) * slots, :] = states[j][:, :width]
        digits = states[j][:, width:].astype(jnp.float32)
        place = iota(digits.shape, 0)
        weight = jnp.where(place == 0, float(CODE), jnp.where(place == 1, 1.0, 0.0))
        cands[j:j + 1, :] = jnp.sum(digits * weight, axis=0, keepdims=True).astype(jnp.int32)
    linear[...] = dot(items[...], wanted[...], NT)
    planes, own_rows = pairs.shape
    eye = iota((own_rows, own_rows), 0) == iota((own_rows, own_rows), 1)
    columns = [jnp.sum(jnp.where(eye, pairs[q:q + 1, :], 0.0), axis=1, keepdims=True) for q in range(planes)]
    pair_column = jnp.concatenate(columns, axis=0)
    item_ids = iota((count, 1), 0) + me * count
    lane = iota((1, half), 1) // (half // readers)

    def one(j, carry):
        source = ring(me - j, total)
        slot_row = jnp.zeros((1, half), jnp.int32)
        holders = [asked[j, r] // user_rows for r in range(readers)]
        for r, holder in enumerate(holders):
            rank = jnp.int32(0)
            for earlier in holders[:r]:
                rank = rank + (earlier == holder).astype(jnp.int32)
            slot_row = jnp.where(lane == r, ring(me - holder, total) * slots + source * cap + rank, slot_row)
        spread = (iota((wanted.shape[0], half), 0) == slot_row).astype(jnp.float32)
        scores = dot(linear[...], spread, NN, precision=lax.Precision.HIGHEST) + pair_column
        hit = item_ids == cands[pl.ds(j, 1), :]
        out[pl.ds(source, 1), :] = jnp.sum(jnp.where(hit, scores, 0.0), axis=0, keepdims=True)
        return carry

    lax.fori_loop(0, total, one, 0, unroll=total <= 8)


def shift(x, axis, step):
    size = lax.axis_size(axis)
    return lax.ppermute(x, axis, [(s, (s + step) % size) for s in range(size)])


def body(cand_items, reader_users, item_table, user_states, pair_mats, pair_fields):
    total = lax.axis_size("shard")
    planes = lax.axis_size("cache")
    half = cand_items.shape[0]
    rows, width = item_table.shape
    readers = reader_users.shape[0]
    cap = 2 * ((readers + total - 1) // total)
    slots = -(-total * cap // 16) * 16
    count = pair_mats.shape[0]
    vmem = pl.BlockSpec(memory_space=pltpu.VMEM)
    smem = pl.BlockSpec(memory_space=pltpu.SMEM)
    hbm = pl.BlockSpec(memory_space=pltpu.HBM)
    anywhere = pl.BlockSpec(memory_space=pl.ANY)
    params = pltpu.CompilerParams(vmem_limit_bytes=VMEM_LIMIT)

    def in_hbm(x):
        return pltpu.with_memory_space_constraint(x, pltpu.HBM)

    with jax.named_scope("ids"):
        others = [shift(reader_users, "shard", j) for j in range(1, total)]
        users = [reader_users] + others

    with jax.named_scope("item_rows"):
        items = lax.all_gather(item_table, "cache", axis=0, tiled=True)

    with jax.named_scope("pairs"):
        pair_parts = pl.pallas_call(
            pair_kernel,
            out_shape=jax.ShapeDtypeStruct((planes, rows), jnp.float32),
            in_specs=[hbm, hbm, hbm],
            out_specs=vmem,
            scratch_shapes=[
                pltpu.SMEM((2, count), jnp.int32),
                pltpu.VMEM((rows, width), jnp.bfloat16),
                pltpu.VMEM((K, K, count), jnp.bfloat16),
                pltpu.VMEM((width, rows), jnp.float32),
                pltpu.VMEM((width, rows), jnp.bfloat16),
                pltpu.VMEM((count * PITCH, LANES), jnp.float32),
                pltpu.SemaphoreType.DMA((3,)),
            ],
            compiler_params=params,
            cost_estimate=pl.CostEstimate(flops=2 * count * K * K * rows * 16, bytes_accessed=4 * 1024 * 1024, transcendentals=0),
        )(in_hbm(pair_fields.T), in_hbm(item_table), in_hbm(jnp.transpose(pair_mats, (1, 2, 0))))
        pair_scores = lax.psum(pair_parts, ("cache", "pair"))

    with jax.named_scope("states"):
        picked = pl.pallas_call(
            functools.partial(pick_kernel, total, cap),
            out_shape=jax.ShapeDtypeStruct((slots, width + half), jnp.bfloat16),
            in_specs=[smem] * total + [vmem, vmem, anywhere],
            out_specs=vmem,
            compiler_params=params,
            cost_estimate=pl.CostEstimate(flops=2 * slots * rows * width, bytes_accessed=1024 * 1024, transcendentals=0),
        )(*users, cand_items.reshape(1, half), user_states, pair_parts)
        states = [picked] + [shift(picked, "shard", j) for j in range(1, total)]

    with jax.named_scope("scores"):
        parted = pl.pallas_call(
            functools.partial(score_kernel, total, cap, user_states.shape[0]),
            out_shape=jax.ShapeDtypeStruct((total, half), jnp.float32),
            in_specs=[smem] * total + [vmem] * (total + 2),
            out_specs=vmem,
            scratch_shapes=[
                pltpu.SMEM((total, readers), jnp.int32),
                pltpu.VMEM((total * slots, width), jnp.bfloat16),
                pltpu.VMEM((-(-total // 8) * 8, half), jnp.int32),
                pltpu.VMEM((planes * rows, total * slots), jnp.float32),
            ],
            compiler_params=params,
            cost_estimate=pl.CostEstimate(flops=2 * 64 * 256 * width, bytes_accessed=2 * 1024 * 1024, transcendentals=0),
        )(*users, *states, pair_scores, items)

    with jax.named_scope("back"):
        return lax.psum_scatter(parted, "shard", scatter_dimension=0, tiled=True).reshape(half)


def solution(mesh):
    return jax.shard_map(
        body,
        mesh=mesh,
        in_specs=(
            P(("groups", "shard", "cache", "pair")),
            P(("groups", "shard", "cache", "pair")),
            P(("shard", "cache"), None),
            P(("groups", "shard"), None),
            P("pair", None, None),
            P("pair", None),
        ),
        out_specs=P(("groups", "shard", "cache", "pair")),
        check_vma=False,
    )
```

```python
import functools

import jax
import jax.numpy as jnp
from jax import lax
from jax.experimental import pallas as pl
from jax.experimental.pallas import tpu as pltpu
from jax.sharding import PartitionSpec as P

K = 64
LANES = 128
PITCH = 72
CODE = 128
VMEM_LIMIT = 40 * 1024 * 1024
NT = (((1,), (1,)), ((), ()))
NN = (((1,), (0,)), ((), ()))


def dot(a, b, dims, **kw):
    return lax.dot_general(a, b, dims, preferred_element_type=jnp.float32, **kw)


def iota(shape, dim):
    return lax.broadcasted_iota(jnp.int32, shape, dim)


def ring(index, size):
    return lax.rem(index + size, size)


def pick_kernel(total, cap, *refs):
    users, (own_cands, states_hbm, out, held, asked, cands, sems) = refs[:total], refs[total:]
    fetch = pltpu.make_async_copy(states_hbm, held, sems.at[total])
    digit_fetch = pltpu.make_async_copy(own_cands, cands, sems.at[total + 1])
    id_fetches = [pltpu.make_async_copy(users[j], asked.at[j], sems.at[j]) for j in range(total)]
    for copy in id_fetches + [fetch, digit_fetch]:
        copy.start()
    own_rows, width = held.shape
    me = lax.axis_index("shard")
    slots = out.shape[0]
    slot_index = iota((slots, own_rows), 0)
    row_index = iota((slots, own_rows), 1)
    chosen = jnp.zeros((slots, own_rows), jnp.float32)
    for copy in id_fetches:
        copy.wait()
    for j in range(total):
        source = ring(me - j, total)
        taken = jnp.int32(0)
        for r in range(asked.shape[1]):
            user = asked[j, r]
            mine = user // own_rows == me
            slot = jnp.where(mine, source * cap + taken, -1)
            taken = taken + mine.astype(jnp.int32)
            chosen = jnp.where((slot_index == slot) & (row_index == user % own_rows), 1.0, chosen)
    chosen = chosen.astype(jnp.bfloat16)
    digit_fetch.wait()
    code = cands[...]
    digits = jnp.where(iota((slots, code.shape[1]), 0) == 0, code // CODE, code % CODE)
    out[:, width:] = jnp.where(iota(digits.shape, 0) < 2, digits, 0).astype(jnp.float32).astype(jnp.bfloat16)
    fetch.wait()
    out[:, :width] = dot(chosen, held[...], NN).astype(jnp.bfloat16)


def slot_rows(asked, cap, slots, user_rows, half):
    total, readers = asked.shape
    me = lax.axis_index("shard")
    lane = iota((1, half), 1) // (half // readers)
    rows = []
    for j in range(total):
        source = ring(me - j, total)
        holders = [asked[j, r] // user_rows for r in range(readers)]
        row = jnp.zeros((1, half), jnp.int32)
        for r, holder in enumerate(holders):
            rank = jnp.int32(0)
            for earlier in holders[:r]:
                rank = rank + (earlier == holder).astype(jnp.int32)
            row = jnp.where(lane == r, ring(me - holder, total) * slots + source * cap + rank, row)
        rows.append(row)
    return rows


def pair_kernel(total, cap, slots, user_rows, *refs):
    users, refs = refs[:total], refs[total:]
    fields_hbm, items_hbm, mats_hbm, picked, out, places, asked, fields, items, mats, rows32, rows16, stacked, sems = refs
    del picked
    chunks = 4
    wide = items.shape[1] // chunks
    item_fetches = [
        pltpu.make_async_copy(items_hbm.at[:, pl.ds(t * wide, wide)], items.at[:, pl.ds(t * wide, wide)], sems.at[t])
        for t in range(chunks)
    ]
    mats_fetch = pltpu.make_async_copy(mats_hbm, mats, sems.at[chunks])
    fields_fetch = pltpu.make_async_copy(fields_hbm, fields, sems.at[chunks + 1])
    id_fetches = [pltpu.make_async_copy(users[j], asked.at[j], sems.at[chunks + 2 + j]) for j in range(total)]
    for copy in item_fetches + [mats_fetch, fields_fetch] + id_fetches:
        copy.start()
    count = mats.shape[2]
    eye = (iota((LANES, LANES), 0) == iota((LANES, LANES), 1)).astype(jnp.bfloat16)
    for t in range(items.shape[1] // LANES):
        if t * LANES % wide == 0:
            item_fetches[t * LANES // wide].wait()
        turned = dot(eye, items[:, t * LANES:(t + 1) * LANES], NT)
        rows32[t * LANES:(t + 1) * LANES, :] = turned
        rows16[t * LANES:(t + 1) * LANES, :] = turned.astype(jnp.bfloat16)
    eye_pairs = (iota((count, count), 0) == iota((count, count), 1)).astype(jnp.bfloat16)
    side = (iota((count, LANES), 0) % 2 == 0) == (iota((count, LANES), 1) < K)
    mats_fetch.wait()
    for k in range(K):
        both = jnp.concatenate([mats[k], mats[k]], axis=0)
        stacked[pl.ds(k, count, stride=PITCH), :] = jnp.where(side, dot(eye_pairs, both, NT), 0.0)
    fields_fetch.wait()

    def two(step, total):
        first = step * 2
        lefts, rights, mults = [], [], []
        for p in (first, first + 1):
            a = pl.multiple_of(fields[0, p] * K, K)
            b = pl.multiple_of(fields[1, p] * K, K)
            lefts.append(stacked[pl.ds(pl.multiple_of(p * PITCH, 8), K), :].astype(jnp.bfloat16))
            rights.append(rows16[pl.ds(b, K), :])
            mults.append(rows32[pl.ds(a, K), :])
        moved = dot(jnp.concatenate(lefts, axis=0), jnp.concatenate(rights, axis=0), NN)
        return total + moved * jnp.concatenate(mults, axis=0)

    sums = lax.fori_loop(0, count // 2, two, jnp.zeros((2 * K, items.shape[0]), jnp.float32), unroll=16)
    mine = iota(out.shape, 0) == lax.axis_index("cache")
    out[...] = jnp.where(mine, jnp.sum(sums, axis=0, keepdims=True), 0.0)
    for copy in id_fetches:
        copy.wait()
    for j, row in enumerate(slot_rows(asked, cap, slots, user_rows, places.shape[1])):
        places[j:j + 1, :] = row


def thirds(x):
    high = x.astype(jnp.bfloat16)
    rest = x - high.astype(jnp.float32)
    middle = rest.astype(jnp.bfloat16)
    return high, middle, (rest - middle.astype(jnp.float32)).astype(jnp.bfloat16)


def score_kernel(total, planes, *refs):
    states, refs = refs[:total], refs[total:]
    items, refs = refs[:planes], refs[planes:]
    places, pairs = refs[:2]
    outs, (wanted, cands, linear) = refs[2:2 + total], refs[2 + total:]
    slots = states[0].shape[0]
    own_rows, width = items[0].shape
    me = lax.axis_index("shard")
    plane = lax.axis_index("cache")
    count = total * slots
    for j in range(total):
        wanted[j * slots:(j + 1) * slots, :] = states[j][:, :width]
        digits = states[j][:, width:].astype(jnp.float32)
        place = iota(digits.shape, 0)
        weight = jnp.where(place == 0, float(CODE), jnp.where(place == 1, 1.0, 0.0))
        cands[j:j + 1, :] = jnp.sum(digits * weight, axis=0, keepdims=True).astype(jnp.int32)
    eye = iota((own_rows, own_rows), 0) == iota((own_rows, own_rows), 1)
    ids, columns = [], []
    for q in range(planes):
        at = ring(plane - q, planes)
        scores = dot(items[q][...], wanted[...], NT)
        for t, part in enumerate(thirds(scores)):
            linear[q * own_rows:(q + 1) * own_rows, t * count:(t + 1) * count] = part
        columns.append(jnp.sum(jnp.where(eye, pairs[pl.ds(at, 1), :], 0.0), axis=1, keepdims=True))
        ids.append(iota((own_rows, 1), 0) + (me * planes + at) * own_rows)
    pair_column = jnp.concatenate(columns, axis=0)
    item_ids = jnp.concatenate(ids, axis=0)
    for j in range(total):
        half = outs[j].shape[1]
        spread = (iota((count, half), 0) == places[j:j + 1, :]).astype(jnp.float32).astype(jnp.bfloat16)
        scores = dot(linear[...], jnp.concatenate([spread] * 3, axis=0), NN) + pair_column
        hit = item_ids == cands[j:j + 1, :]
        outs[j][...] = jnp.sum(jnp.where(hit, scores, 0.0), axis=0, keepdims=True)


def shift(x, axis, step):
    size = lax.axis_size(axis)
    return lax.ppermute(x, axis, [(s, (s + step) % size) for s in range(size)])


def body(cand_items, reader_users, item_table, user_states, pair_mats, pair_fields):
    total = lax.axis_size("shard")
    planes = lax.axis_size("cache")
    half = cand_items.shape[0]
    rows, width = item_table.shape
    readers = reader_users.shape[0]
    cap = 2 * ((readers + total - 1) // total)
    slots = -(-total * cap // 16) * 16
    count = pair_mats.shape[0]
    vmem = pl.BlockSpec(memory_space=pltpu.VMEM)
    hbm = pl.BlockSpec(memory_space=pltpu.HBM)
    anywhere = pl.BlockSpec(memory_space=pl.ANY)
    params = pltpu.CompilerParams(vmem_limit_bytes=VMEM_LIMIT)

    def in_hbm(x):
        return pltpu.with_memory_space_constraint(x, pltpu.HBM)

    with jax.named_scope("item_rows"):
        items = [item_table] + [shift(item_table, "cache", q) for q in range(1, planes)]

    with jax.named_scope("ids"):
        users = [in_hbm(reader_users)] + [shift(reader_users, "shard", j) for j in range(1, total)]

    with jax.named_scope("states"):
        picked = pl.pallas_call(
            functools.partial(pick_kernel, total, cap),
            out_shape=jax.ShapeDtypeStruct((slots, width + half), jnp.bfloat16),
            in_specs=[anywhere] * total + [hbm, hbm],
            out_specs=vmem,
            scratch_shapes=[
                pltpu.VMEM(user_states.shape, jnp.bfloat16),
                pltpu.SMEM((total, readers), jnp.int32),
                pltpu.VMEM((1, half), jnp.int32),
                pltpu.SemaphoreType.DMA((total + 2,)),
            ],
            compiler_params=params,
            cost_estimate=pl.CostEstimate(flops=2 * slots * rows * width, bytes_accessed=1024 * 1024, transcendentals=0),
        )(*users, in_hbm(cand_items.reshape(1, half)), in_hbm(user_states))
        states = [picked] + [shift(picked, "shard", j) for j in range(1, total)]

    with jax.named_scope("pairs"):
        pair_parts, places = pl.pallas_call(
            functools.partial(pair_kernel, total, cap, slots, user_states.shape[0]),
            out_shape=(
                jax.ShapeDtypeStruct((planes, rows), jnp.float32),
                jax.ShapeDtypeStruct((total, half), jnp.int32),
            ),
            in_specs=[anywhere] * total + [hbm, hbm, hbm, anywhere],
            out_specs=(vmem, vmem),
            scratch_shapes=[
                pltpu.SMEM((total, readers), jnp.int32),
                pltpu.SMEM((2, count), jnp.int32),
                pltpu.VMEM((rows, width), jnp.bfloat16),
                pltpu.VMEM((K, K, count), jnp.bfloat16),
                pltpu.VMEM((width, rows), jnp.float32),
                pltpu.VMEM((width, rows), jnp.bfloat16),
                pltpu.VMEM((count * PITCH, LANES), jnp.float32),
                pltpu.SemaphoreType.DMA((6 + total,)),
            ],
            compiler_params=params,
            cost_estimate=pl.CostEstimate(flops=2 * count * K * K * rows * 16, bytes_accessed=4 * 1024 * 1024, transcendentals=0),
        )(*users, in_hbm(pair_fields.T), in_hbm(item_table), in_hbm(jnp.transpose(pair_mats, (1, 2, 0))), picked)
        pair_scores = lax.psum(pair_parts, ("cache", "pair"))

    with jax.named_scope("scores"):
        outs = pl.pallas_call(
            functools.partial(score_kernel, total, planes),
            out_shape=[jax.ShapeDtypeStruct((1, half), jnp.float32)] * total,
            in_specs=[vmem] * (total + planes + 2),
            out_specs=[vmem] * total,
            scratch_shapes=[
                pltpu.VMEM((total * slots, width), jnp.bfloat16),
                pltpu.VMEM((-(-total // 8) * 8, half), jnp.int32),
                pltpu.VMEM((planes * rows, 3 * total * slots), jnp.bfloat16),
            ],
            compiler_params=params,
            cost_estimate=pl.CostEstimate(flops=2 * 64 * 256 * width, bytes_accessed=2 * 1024 * 1024, transcendentals=0),
        )(*states, *items, places, pair_scores)

    with jax.named_scope("back"):
        result = outs[0]
        for j in range(1, total):
            result = result + shift(outs[j], "shard", -j)
    return result.reshape(half)


def solution(mesh):
    return jax.shard_map(
        body,
        mesh=mesh,
        in_specs=(
            P(("groups", "shard", "cache", "pair")),
            P(("groups", "shard", "cache", "pair")),
            P(("shard", "cache"), None),
            P(("groups", "shard"), None),
            P("pair", None, None),
            P("pair", None),
        ),
        out_specs=P(("groups", "shard", "cache", "pair")),
        check_vma=False,
    )
```

```python
import functools

import jax
import jax.numpy as jnp
from jax import lax
from jax.experimental import pallas as pl
from jax.experimental.pallas import tpu as pltpu
from jax.sharding import PartitionSpec as P

K = 64
LANES = 128
PITCH = 72
CODE = 128
VMEM_LIMIT = 40 * 1024 * 1024
NT = (((1,), (1,)), ((), ()))
NN = (((1,), (0,)), ((), ()))


def dot(a, b, dims, **kw):
    return lax.dot_general(a, b, dims, preferred_element_type=jnp.float32, **kw)


def iota(shape, dim):
    return lax.broadcasted_iota(jnp.int32, shape, dim)


def ring(index, size):
    return lax.rem(index + size, size)


def pick_kernel(total, cap, *refs):
    users, (own_cands, states_hbm, out, held, asked, cands, sems) = refs[:total], refs[total:]
    fetch = pltpu.make_async_copy(states_hbm, held, sems.at[total])
    digit_fetch = pltpu.make_async_copy(own_cands, cands, sems.at[total + 1])
    id_fetches = [pltpu.make_async_copy(users[j], asked.at[j], sems.at[j]) for j in range(total)]
    for copy in id_fetches + [fetch, digit_fetch]:
        copy.start()
    own_rows, width = held.shape
    me = lax.axis_index("shard")
    slots = out.shape[0]
    slot_index = iota((slots, own_rows), 0)
    row_index = iota((slots, own_rows), 1)
    chosen = jnp.zeros((slots, own_rows), jnp.float32)
    for copy in id_fetches:
        copy.wait()
    for j in range(total):
        source = me ^ j
        taken = jnp.int32(0)
        for r in range(asked.shape[1]):
            user = asked[j, r]
            mine = user // own_rows == me
            slot = jnp.where(mine, source * cap + taken, -1)
            taken = taken + mine.astype(jnp.int32)
            chosen = jnp.where((slot_index == slot) & (row_index == user % own_rows), 1.0, chosen)
    chosen = chosen.astype(jnp.bfloat16)
    digit_fetch.wait()
    code = cands[...]
    digits = jnp.where(iota((slots, code.shape[1]), 0) == 0, code // CODE, code % CODE)
    out[:, width:] = jnp.where(iota(digits.shape, 0) < 2, digits, 0).astype(jnp.float32).astype(jnp.bfloat16)
    fetch.wait()
    out[:, :width] = dot(chosen, held[...], NN).astype(jnp.bfloat16)


def slot_rows(asked, cap, slots, user_rows, half):
    total, readers = asked.shape
    me = lax.axis_index("shard")
    lane = iota((1, half), 1) // (half // readers)
    rows = []
    for j in range(total):
        source = me ^ j
        holders = [asked[j, r] // user_rows for r in range(readers)]
        row = jnp.zeros((1, half), jnp.int32)
        for r, holder in enumerate(holders):
            rank = jnp.int32(0)
            for earlier in holders[:r]:
                rank = rank + (earlier == holder).astype(jnp.int32)
            row = jnp.where(lane == r, (me ^ holder) * slots + source * cap + rank, row)
        rows.append(row)
    return rows


def pair_kernel(total, cap, slots, user_rows, *refs):
    users, refs = refs[:total], refs[total:]
    fields_hbm, items_hbm, mats_hbm, picked, out, places, asked, fields, items, mats, rows32, rows16, stacked, sems = refs
    del picked
    chunks = 4
    wide = items.shape[1] // chunks
    item_fetches = [
        pltpu.make_async_copy(items_hbm.at[:, pl.ds(t * wide, wide)], items.at[:, pl.ds(t * wide, wide)], sems.at[t])
        for t in range(chunks)
    ]
    mats_fetch = pltpu.make_async_copy(mats_hbm, mats, sems.at[chunks])
    fields_fetch = pltpu.make_async_copy(fields_hbm, fields, sems.at[chunks + 1])
    id_fetches = [pltpu.make_async_copy(users[j], asked.at[j], sems.at[chunks + 2 + j]) for j in range(total)]
    for copy in item_fetches + [mats_fetch, fields_fetch] + id_fetches:
        copy.start()
    count = mats.shape[2]
    eye = (iota((LANES, LANES), 0) == iota((LANES, LANES), 1)).astype(jnp.bfloat16)
    for t in range(items.shape[1] // LANES):
        if t * LANES % wide == 0:
            item_fetches[t * LANES // wide].wait()
        turned = dot(eye, items[:, t * LANES:(t + 1) * LANES], NT)
        rows32[t * LANES:(t + 1) * LANES, :] = turned
        rows16[t * LANES:(t + 1) * LANES, :] = turned.astype(jnp.bfloat16)
    eye_pairs = (iota((count, count), 0) == iota((count, count), 1)).astype(jnp.bfloat16)
    side = (iota((count, LANES), 0) % 2 == 0) == (iota((count, LANES), 1) < K)
    mats_fetch.wait()
    for k in range(K):
        both = jnp.concatenate([mats[k], mats[k]], axis=0)
        stacked[pl.ds(k, count, stride=PITCH), :] = jnp.where(side, dot(eye_pairs, both, NT), 0.0)
    fields_fetch.wait()

    def two(step, total):
        first = step * 2
        lefts, rights, mults = [], [], []
        for p in (first, first + 1):
            a = pl.multiple_of(fields[0, p] * K, K)
            b = pl.multiple_of(fields[1, p] * K, K)
            lefts.append(stacked[pl.ds(pl.multiple_of(p * PITCH, 8), K), :].astype(jnp.bfloat16))
            rights.append(rows16[pl.ds(b, K), :])
            mults.append(rows32[pl.ds(a, K), :])
        moved = dot(jnp.concatenate(lefts, axis=0), jnp.concatenate(rights, axis=0), NN)
        return total + moved * jnp.concatenate(mults, axis=0)

    sums = lax.fori_loop(0, count // 2, two, jnp.zeros((2 * K, items.shape[0]), jnp.float32), unroll=16)
    mine = iota(out.shape, 0) == lax.axis_index("cache")
    out[...] = jnp.where(mine, jnp.sum(sums, axis=0, keepdims=True), 0.0)
    for copy in id_fetches:
        copy.wait()
    for j, row in enumerate(slot_rows(asked, cap, slots, user_rows, places.shape[1])):
        places[j:j + 1, :] = row


def thirds(x):
    high = x.astype(jnp.bfloat16)
    rest = x - high.astype(jnp.float32)
    middle = rest.astype(jnp.bfloat16)
    return high, middle, (rest - middle.astype(jnp.float32)).astype(jnp.bfloat16)


def score_kernel(total, planes, *refs):
    states, refs = refs[:total], refs[total:]
    items, refs = refs[:planes], refs[planes:]
    places, pairs = refs[:2]
    outs, (wanted, cands, linear) = refs[2:2 + total], refs[2 + total:]
    slots = states[0].shape[0]
    own_rows, width = items[0].shape
    me = lax.axis_index("shard")
    plane = lax.axis_index("cache")
    count = total * slots
    for j in range(total):
        wanted[j * slots:(j + 1) * slots, :] = states[j][:, :width]
        digits = states[j][:, width:].astype(jnp.float32)
        place = iota(digits.shape, 0)
        weight = jnp.where(place == 0, float(CODE), jnp.where(place == 1, 1.0, 0.0))
        cands[j:j + 1, :] = jnp.sum(digits * weight, axis=0, keepdims=True).astype(jnp.int32)
    eye = iota((own_rows, own_rows), 0) == iota((own_rows, own_rows), 1)
    ids, columns = [], []
    for q in range(planes):
        at = ring(plane - q, planes)
        scores = dot(items[q][...], wanted[...], NT)
        for t, part in enumerate(thirds(scores)):
            linear[q * own_rows:(q + 1) * own_rows, t * count:(t + 1) * count] = part
        columns.append(jnp.sum(jnp.where(eye, pairs[pl.ds(at, 1), :], 0.0), axis=1, keepdims=True))
        ids.append(iota((own_rows, 1), 0) + (me * planes + at) * own_rows)
    pair_column = jnp.concatenate(columns, axis=0)
    item_ids = jnp.concatenate(ids, axis=0)
    for j in range(total):
        half = outs[j].shape[1]
        spread = (iota((count, half), 0) == places[j:j + 1, :]).astype(jnp.float32).astype(jnp.bfloat16)
        scores = dot(linear[...], jnp.concatenate([spread] * 3, axis=0), NN) + pair_column
        hit = item_ids == cands[j:j + 1, :]
        outs[j][...] = jnp.sum(jnp.where(hit, scores, 0.0), axis=0, keepdims=True)


def shift(x, axis, step):
    size = lax.axis_size(axis)
    return lax.ppermute(x, axis, [(s, (s + step) % size) for s in range(size)])


def swap(x, axis, mask):
    return lax.ppermute(x, axis, [(s, s ^ mask) for s in range(lax.axis_size(axis))])


def body(cand_items, reader_users, item_table, user_states, pair_mats, pair_fields):
    total = lax.axis_size("shard")
    planes = lax.axis_size("cache")
    half = cand_items.shape[0]
    rows, width = item_table.shape
    readers = reader_users.shape[0]
    cap = 2 * ((readers + total - 1) // total)
    slots = -(-total * cap // 16) * 16
    count = pair_mats.shape[0]
    vmem = pl.BlockSpec(memory_space=pltpu.VMEM)
    hbm = pl.BlockSpec(memory_space=pltpu.HBM)
    anywhere = pl.BlockSpec(memory_space=pl.ANY)
    params = pltpu.CompilerParams(vmem_limit_bytes=VMEM_LIMIT)

    def in_hbm(x):
        return pltpu.with_memory_space_constraint(x, pltpu.HBM)

    with jax.named_scope("item_rows"):
        items = [item_table] + [shift(item_table, "cache", q) for q in range(1, planes)]

    with jax.named_scope("ids"):
        users = [in_hbm(reader_users)] + [swap(reader_users, "shard", j) for j in range(1, total)]

    with jax.named_scope("states"):
        picked = pl.pallas_call(
            functools.partial(pick_kernel, total, cap),
            out_shape=jax.ShapeDtypeStruct((slots, width + half), jnp.bfloat16),
            in_specs=[anywhere] * total + [hbm, hbm],
            out_specs=vmem,
            scratch_shapes=[
                pltpu.VMEM(user_states.shape, jnp.bfloat16),
                pltpu.SMEM((total, readers), jnp.int32),
                pltpu.VMEM((1, half), jnp.int32),
                pltpu.SemaphoreType.DMA((total + 2,)),
            ],
            compiler_params=params,
            cost_estimate=pl.CostEstimate(flops=2 * slots * rows * width, bytes_accessed=1024 * 1024, transcendentals=0),
        )(*users, in_hbm(cand_items.reshape(1, half)), in_hbm(user_states))
        states = [picked] + [swap(picked, "shard", j) for j in range(1, total)]

    with jax.named_scope("pairs"):
        pair_parts, places = pl.pallas_call(
            functools.partial(pair_kernel, total, cap, slots, user_states.shape[0]),
            out_shape=(
                jax.ShapeDtypeStruct((planes, rows), jnp.float32),
                jax.ShapeDtypeStruct((total, half), jnp.int32),
            ),
            in_specs=[anywhere] * total + [hbm, hbm, hbm, anywhere],
            out_specs=(vmem, vmem),
            scratch_shapes=[
                pltpu.SMEM((total, readers), jnp.int32),
                pltpu.SMEM((2, count), jnp.int32),
                pltpu.VMEM((rows, width), jnp.bfloat16),
                pltpu.VMEM((K, K, count), jnp.bfloat16),
                pltpu.VMEM((width, rows), jnp.float32),
                pltpu.VMEM((width, rows), jnp.bfloat16),
                pltpu.VMEM((count * PITCH, LANES), jnp.float32),
                pltpu.SemaphoreType.DMA((6 + total,)),
            ],
            compiler_params=params,
            cost_estimate=pl.CostEstimate(flops=2 * count * K * K * rows * 16, bytes_accessed=4 * 1024 * 1024, transcendentals=0),
        )(*users, in_hbm(pair_fields.T), in_hbm(item_table), in_hbm(jnp.transpose(pair_mats, (1, 2, 0))), picked)
        pair_scores = lax.psum(pair_parts, ("cache", "pair"))

    with jax.named_scope("scores"):
        outs = pl.pallas_call(
            functools.partial(score_kernel, total, planes),
            out_shape=[jax.ShapeDtypeStruct((1, half), jnp.float32)] * total,
            in_specs=[vmem] * (total + planes + 2),
            out_specs=[vmem] * total,
            scratch_shapes=[
                pltpu.VMEM((total * slots, width), jnp.bfloat16),
                pltpu.VMEM((-(-total // 8) * 8, half), jnp.int32),
                pltpu.VMEM((planes * rows, 3 * total * slots), jnp.bfloat16),
            ],
            compiler_params=params,
            cost_estimate=pl.CostEstimate(flops=2 * 64 * 256 * width, bytes_accessed=2 * 1024 * 1024, transcendentals=0),
        )(*states, *items, places, pair_scores)

    with jax.named_scope("back"):
        result = outs[0]
        for j in range(1, total):
            result = result + swap(outs[j], "shard", j)
    return result.reshape(half)


def solution(mesh):
    return jax.shard_map(
        body,
        mesh=mesh,
        in_specs=(
            P(("groups", "shard", "cache", "pair")),
            P(("groups", "shard", "cache", "pair")),
            P(("shard", "cache"), None),
            P(("groups", "shard"), None),
            P("pair", None, None),
            P("pair", None),
        ),
        out_specs=P(("groups", "shard", "cache", "pair")),
        check_vma=False,
    )
```

```python
import functools

import jax
import jax.numpy as jnp
from jax import lax
from jax.experimental import pallas as pl
from jax.experimental.pallas import tpu as pltpu
from jax.sharding import PartitionSpec as P

K = 64
LANES = 128
PITCH = 72
CODE = 128
VMEM_LIMIT = 40 * 1024 * 1024
NT = (((1,), (1,)), ((), ()))
NN = (((1,), (0,)), ((), ()))


def dot(a, b, dims, **kw):
    return lax.dot_general(a, b, dims, preferred_element_type=jnp.float32, **kw)


def iota(shape, dim):
    return lax.broadcasted_iota(jnp.int32, shape, dim)


def ring(index, size):
    return lax.rem(index + size, size)


def pick_kernel(total, cap, *refs):
    users, (own_cands, states_hbm, later, out, held, asked, cands, sems) = refs[:total], refs[total:]
    del later
    fetch = pltpu.make_async_copy(states_hbm, held, sems.at[total])
    digit_fetch = pltpu.make_async_copy(own_cands, cands, sems.at[total + 1])
    id_fetches = [pltpu.make_async_copy(users[j], asked.at[j], sems.at[j]) for j in range(total)]
    for copy in id_fetches + [fetch, digit_fetch]:
        copy.start()
    own_rows, width = held.shape
    me = lax.axis_index("shard")
    slots = out.shape[0]
    slot_index = iota((slots, own_rows), 0)
    row_index = iota((slots, own_rows), 1)
    chosen = jnp.zeros((slots, own_rows), jnp.float32)
    for copy in id_fetches:
        copy.wait()
    for j in range(total):
        source = ring(me - j, total)
        taken = jnp.int32(0)
        for r in range(asked.shape[1]):
            user = asked[j, r]
            mine = user // own_rows == me
            slot = jnp.where(mine, source * cap + taken, -1)
            taken = taken + mine.astype(jnp.int32)
            chosen = jnp.where((slot_index == slot) & (row_index == user % own_rows), 1.0, chosen)
    chosen = chosen.astype(jnp.bfloat16)
    digit_fetch.wait()
    code = cands[...]
    digits = jnp.where(iota((slots, code.shape[1]), 0) == 0, code // CODE, code % CODE)
    out[:, width:] = jnp.where(iota(digits.shape, 0) < 2, digits, 0).astype(jnp.float32).astype(jnp.bfloat16)
    fetch.wait()
    out[:, :width] = dot(chosen, held[...], NN).astype(jnp.bfloat16)


def slot_rows(asked, cap, slots, user_rows, half):
    total, readers = asked.shape
    me = lax.axis_index("shard")
    lane = iota((1, half), 1) // (half // readers)
    rows = []
    for j in range(total):
        source = ring(me - j, total)
        holders = [asked[j, r] // user_rows for r in range(readers)]
        row = jnp.zeros((1, half), jnp.int32)
        for r, holder in enumerate(holders):
            rank = jnp.int32(0)
            for earlier in holders[:r]:
                rank = rank + (earlier == holder).astype(jnp.int32)
            row = jnp.where(lane == r, ring(me - holder, total) * slots + source * cap + rank, row)
        rows.append(row)
    return rows


def turn_kernel(items_hbm, mats_hbm, rows32, rows16, mats, items, sems):
    chunks = sems.shape[0] - 1
    wide = items.shape[1] // chunks
    item_fetches = [
        pltpu.make_async_copy(items_hbm.at[:, pl.ds(t * wide, wide)], items.at[:, pl.ds(t * wide, wide)], sems.at[t])
        for t in range(chunks)
    ]
    mats_fetch = pltpu.make_async_copy(mats_hbm, mats, sems.at[chunks])
    for copy in item_fetches + [mats_fetch]:
        copy.start()
    eye = (iota((LANES, LANES), 0) == iota((LANES, LANES), 1)).astype(jnp.bfloat16)
    for t in range(items.shape[1] // LANES):
        if t * LANES % wide == 0:
            item_fetches[t * LANES // wide].wait()
        turned = dot(eye, items[:, t * LANES:(t + 1) * LANES], NT)
        rows32[t * LANES:(t + 1) * LANES, :] = turned
        rows16[t * LANES:(t + 1) * LANES, :] = turned.astype(jnp.bfloat16)
    mats_fetch.wait()


def pair_kernel(total, cap, slots, user_rows, *refs):
    users, refs = refs[:total], refs[total:]
    fields_hbm, rows32, rows16, mats, picked, out, places, asked, fields, stacked, sems = refs
    del picked
    fields_fetch = pltpu.make_async_copy(fields_hbm, fields, sems.at[total])
    id_fetches = [pltpu.make_async_copy(users[j], asked.at[j], sems.at[j]) for j in range(total)]
    for copy in [fields_fetch] + id_fetches:
        copy.start()
    count = mats.shape[2]
    eye_pairs = (iota((count, count), 0) == iota((count, count), 1)).astype(jnp.bfloat16)
    side = (iota((count, LANES), 0) % 2 == 0) == (iota((count, LANES), 1) < K)
    for k in range(0, K, 2):
        twice = jnp.concatenate([mats[k], mats[k], mats[k + 1], mats[k + 1]], axis=0)
        turned = dot(eye_pairs, twice, NT)
        stacked[pl.ds(k, count, stride=PITCH), :] = jnp.where(side, turned[:, :LANES], 0.0)
        stacked[pl.ds(k + 1, count, stride=PITCH), :] = jnp.where(side, turned[:, LANES:], 0.0)
    fields_fetch.wait()

    def two(step, total):
        first = step * 2
        lefts, rights, mults = [], [], []
        for p in (first, first + 1):
            a = pl.multiple_of(fields[0, p] * K, K)
            b = pl.multiple_of(fields[1, p] * K, K)
            lefts.append(stacked[pl.ds(pl.multiple_of(p * PITCH, 8), K), :].astype(jnp.bfloat16))
            rights.append(rows16[pl.ds(b, K), :])
            mults.append(rows32[pl.ds(a, K), :])
        moved = dot(jnp.concatenate(lefts, axis=0), jnp.concatenate(rights, axis=0), NN)
        return total + moved * jnp.concatenate(mults, axis=0)

    sums = lax.fori_loop(0, count // 2, two, jnp.zeros((2 * K, rows32.shape[1]), jnp.float32), unroll=16)
    mine = iota(out.shape, 0) == lax.axis_index("cache")
    out[...] = jnp.where(mine, jnp.sum(sums, axis=0, keepdims=True), 0.0)
    for copy in id_fetches:
        copy.wait()
    for j, row in enumerate(slot_rows(asked, cap, slots, user_rows, places.shape[1])):
        places[j:j + 1, :] = row


def thirds(x):
    high = x.astype(jnp.bfloat16)
    rest = x - high.astype(jnp.float32)
    middle = rest.astype(jnp.bfloat16)
    return high, middle, (rest - middle.astype(jnp.float32)).astype(jnp.bfloat16)


def score_kernel(total, planes, *refs):
    states, refs = refs[:total], refs[total:]
    items, refs = refs[:planes], refs[planes:]
    places, pairs = refs[:2]
    outs, (wanted, cands, linear) = refs[2:2 + total], refs[2 + total:]
    slots = states[0].shape[0]
    own_rows, width = items[0].shape
    me = lax.axis_index("shard")
    plane = lax.axis_index("cache")
    count = total * slots
    for j in range(total):
        wanted[j * slots:(j + 1) * slots, :] = states[j][:, :width]
        digits = states[j][:, width:].astype(jnp.float32)
        place = iota(digits.shape, 0)
        weight = jnp.where(place == 0, float(CODE), jnp.where(place == 1, 1.0, 0.0))
        cands[j:j + 1, :] = jnp.sum(digits * weight, axis=0, keepdims=True).astype(jnp.int32)
    eye = iota((own_rows, own_rows), 0) == iota((own_rows, own_rows), 1)
    ids, columns = [], []
    for q in range(planes):
        at = ring(plane - q, planes)
        scores = dot(items[q][...], wanted[...], NT)
        for t, part in enumerate(thirds(scores)):
            linear[q * own_rows:(q + 1) * own_rows, t * count:(t + 1) * count] = part
        columns.append(jnp.sum(jnp.where(eye, pairs[pl.ds(at, 1), :], 0.0), axis=1, keepdims=True))
        ids.append(iota((own_rows, 1), 0) + (me * planes + at) * own_rows)
    pair_column = jnp.concatenate(columns, axis=0)
    item_ids = jnp.concatenate(ids, axis=0)
    for j in range(total):
        half = outs[j].shape[1]
        spread = (iota((count, half), 0) == places[j:j + 1, :]).astype(jnp.float32).astype(jnp.bfloat16)
        scores = dot(linear[...], jnp.concatenate([spread] * 3, axis=0), NN) + pair_column
        hit = item_ids == cands[j:j + 1, :]
        outs[j][...] = jnp.sum(jnp.where(hit, scores, 0.0), axis=0, keepdims=True)


def shift(x, axis, step):
    size = lax.axis_size(axis)
    return lax.ppermute(x, axis, [(s, (s + step) % size) for s in range(size)])


def body(cand_items, reader_users, item_table, user_states, pair_mats, pair_fields):
    total = lax.axis_size("shard")
    planes = lax.axis_size("cache")
    half = cand_items.shape[0]
    rows, width = item_table.shape
    readers = reader_users.shape[0]
    cap = 2 * ((readers + total - 1) // total)
    slots = -(-total * cap // 16) * 16
    count = pair_mats.shape[0]
    vmem = pl.BlockSpec(memory_space=pltpu.VMEM)
    hbm = pl.BlockSpec(memory_space=pltpu.HBM)
    anywhere = pl.BlockSpec(memory_space=pl.ANY)
    params = pltpu.CompilerParams(vmem_limit_bytes=VMEM_LIMIT)

    def in_hbm(x):
        return pltpu.with_memory_space_constraint(x, pltpu.HBM)

    with jax.named_scope("item_rows"):
        items = [item_table] + [shift(item_table, "cache", q) for q in range(1, planes)]

    with jax.named_scope("ids"):
        users = [in_hbm(reader_users)] + [shift(reader_users, "shard", j) for j in range(1, total)]

    with jax.named_scope("turn"):
        turned = pl.pallas_call(
            turn_kernel,
            out_shape=(
                jax.ShapeDtypeStruct((width, rows), jnp.float32),
                jax.ShapeDtypeStruct((width, rows), jnp.bfloat16),
                jax.ShapeDtypeStruct((K, K, count), jnp.bfloat16),
            ),
            in_specs=[hbm, hbm],
            out_specs=(vmem, vmem, vmem),
            scratch_shapes=[pltpu.VMEM((rows, width), jnp.bfloat16), pltpu.SemaphoreType.DMA((5,))],
            compiler_params=params,
            cost_estimate=pl.CostEstimate(flops=2 * rows * rows * width * 16, bytes_accessed=8 * 1024 * 1024, transcendentals=0),
        )(in_hbm(item_table), in_hbm(jnp.transpose(pair_mats, (1, 2, 0))))

    with jax.named_scope("states"):
        picked = pl.pallas_call(
            functools.partial(pick_kernel, total, cap),
            out_shape=jax.ShapeDtypeStruct((slots, width + half), jnp.bfloat16),
            in_specs=[anywhere] * total + [hbm, hbm, anywhere],
            out_specs=vmem,
            scratch_shapes=[
                pltpu.VMEM(user_states.shape, jnp.bfloat16),
                pltpu.SMEM((total, readers), jnp.int32),
                pltpu.VMEM((1, half), jnp.int32),
                pltpu.SemaphoreType.DMA((total + 2,)),
            ],
            compiler_params=params,
            cost_estimate=pl.CostEstimate(flops=2 * slots * rows * width, bytes_accessed=1024 * 1024, transcendentals=0),
        )(*users, in_hbm(cand_items.reshape(1, half)), in_hbm(user_states), turned[1])
        states = [picked] + [shift(picked, "shard", j) for j in range(1, total)]

    with jax.named_scope("pairs"):
        pair_parts, places = pl.pallas_call(
            functools.partial(pair_kernel, total, cap, slots, user_states.shape[0]),
            out_shape=(
                jax.ShapeDtypeStruct((planes, rows), jnp.float32),
                jax.ShapeDtypeStruct((total, half), jnp.int32),
            ),
            in_specs=[anywhere] * total + [hbm, vmem, vmem, vmem, anywhere],
            out_specs=(vmem, vmem),
            scratch_shapes=[
                pltpu.SMEM((total, readers), jnp.int32),
                pltpu.SMEM((2, count), jnp.int32),
                pltpu.VMEM((count * PITCH, LANES), jnp.float32),
                pltpu.SemaphoreType.DMA((1 + total,)),
            ],
            compiler_params=params,
            cost_estimate=pl.CostEstimate(flops=2 * count * K * K * rows * 16, bytes_accessed=4 * 1024 * 1024, transcendentals=0),
        )(*users, in_hbm(pair_fields.T), *turned, picked)
        pair_scores = lax.psum(pair_parts, ("cache", "pair"))

    with jax.named_scope("scores"):
        outs = pl.pallas_call(
            functools.partial(score_kernel, total, planes),
            out_shape=[jax.ShapeDtypeStruct((1, half), jnp.float32)] * total,
            in_specs=[vmem] * (total + planes + 2),
            out_specs=[vmem] * total,
            scratch_shapes=[
                pltpu.VMEM((total * slots, width), jnp.bfloat16),
                pltpu.VMEM((-(-total // 8) * 8, half), jnp.int32),
                pltpu.VMEM((planes * rows, 3 * total * slots), jnp.bfloat16),
            ],
            compiler_params=params,
            cost_estimate=pl.CostEstimate(flops=2 * 64 * 256 * width, bytes_accessed=2 * 1024 * 1024, transcendentals=0),
        )(*states, *items, places, pair_scores)

    with jax.named_scope("back"):
        result = outs[0]
        for j in range(1, total):
            result = result + shift(outs[j], "shard", -j)
    return result.reshape(half)


def solution(mesh):
    return jax.shard_map(
        body,
        mesh=mesh,
        in_specs=(
            P(("groups", "shard", "cache", "pair")),
            P(("groups", "shard", "cache", "pair")),
            P(("shard", "cache"), None),
            P(("groups", "shard"), None),
            P("pair", None, None),
            P("pair", None),
        ),
        out_specs=P(("groups", "shard", "cache", "pair")),
        check_vma=False,
    )
```

```python
import functools

import jax
import jax.numpy as jnp
from jax import lax
from jax.experimental import pallas as pl
from jax.experimental.pallas import tpu as pltpu
from jax.sharding import PartitionSpec as P

K = 64
LANES = 128
PITCH = 72
CODE = 128
VMEM_LIMIT = 40 * 1024 * 1024
NT = (((1,), (1,)), ((), ()))
NN = (((1,), (0,)), ((), ()))


def dot(a, b, dims, **kw):
    return lax.dot_general(a, b, dims, preferred_element_type=jnp.float32, **kw)


def iota(shape, dim):
    return lax.broadcasted_iota(jnp.int32, shape, dim)


def ring(index, size):
    return lax.rem(index + size, size)


def pick_kernel(total, cap, *refs):
    users, (own_cands, held, out, asked, cands, sems) = refs[:total], refs[total:]
    digit_fetch = pltpu.make_async_copy(own_cands, cands, sems.at[total])
    id_fetches = [pltpu.make_async_copy(users[j], asked.at[j], sems.at[j]) for j in range(total)]
    for copy in id_fetches + [digit_fetch]:
        copy.start()
    own_rows, width = held.shape
    me = lax.axis_index("shard")
    slots = out.shape[0]
    slot_index = iota((slots, own_rows), 0)
    row_index = iota((slots, own_rows), 1)
    chosen = jnp.zeros((slots, own_rows), jnp.float32)
    for copy in id_fetches:
        copy.wait()
    for j in range(total):
        source = ring(me - j, total)
        taken = jnp.int32(0)
        for r in range(asked.shape[1]):
            user = asked[j, r]
            mine = user // own_rows == me
            slot = jnp.where(mine, source * cap + taken, -1)
            taken = taken + mine.astype(jnp.int32)
            chosen = jnp.where((slot_index == slot) & (row_index == user % own_rows), 1.0, chosen)
    chosen = chosen.astype(jnp.bfloat16)
    digit_fetch.wait()
    code = cands[...]
    digits = jnp.where(iota((slots, code.shape[1]), 0) == 0, code // CODE, code % CODE)
    out[:, width:] = jnp.where(iota(digits.shape, 0) < 2, digits, 0).astype(jnp.float32).astype(jnp.bfloat16)
    out[:, :width] = dot(chosen, held[...], NN).astype(jnp.bfloat16)


def slot_rows(asked, cap, slots, user_rows, half):
    total, readers = asked.shape
    me = lax.axis_index("shard")
    lane = iota((1, half), 1) // (half // readers)
    rows = []
    for j in range(total):
        source = ring(me - j, total)
        holders = [asked[j, r] // user_rows for r in range(readers)]
        row = jnp.zeros((1, half), jnp.int32)
        for r, holder in enumerate(holders):
            rank = jnp.int32(0)
            for earlier in holders[:r]:
                rank = rank + (earlier == holder).astype(jnp.int32)
            row = jnp.where(lane == r, ring(me - holder, total) * slots + source * cap + rank, row)
        rows.append(row)
    return rows


def turn_kernel(items_hbm, mats_hbm, states_hbm, rows32, rows16, mats, states, items, sems):
    chunks = sems.shape[0] - 2
    wide = items.shape[1] // chunks
    item_fetches = [
        pltpu.make_async_copy(items_hbm.at[:, pl.ds(t * wide, wide)], items.at[:, pl.ds(t * wide, wide)], sems.at[t])
        for t in range(chunks)
    ]
    mats_fetch = pltpu.make_async_copy(mats_hbm, mats, sems.at[chunks])
    states_fetch = pltpu.make_async_copy(states_hbm, states, sems.at[chunks + 1])
    for copy in item_fetches + [mats_fetch, states_fetch]:
        copy.start()
    eye = (iota((LANES, LANES), 0) == iota((LANES, LANES), 1)).astype(jnp.bfloat16)
    for t in range(items.shape[1] // LANES):
        if t * LANES % wide == 0:
            item_fetches[t * LANES // wide].wait()
        turned = dot(eye, items[:, t * LANES:(t + 1) * LANES], NT)
        rows32[t * LANES:(t + 1) * LANES, :] = turned
        rows16[t * LANES:(t + 1) * LANES, :] = turned.astype(jnp.bfloat16)
    mats_fetch.wait()
    states_fetch.wait()


def pair_kernel(total, cap, slots, user_rows, *refs):
    users, refs = refs[:total], refs[total:]
    fields_hbm, rows32, rows16, mats, picked, out, places, asked, fields, stacked, sems = refs
    del picked
    fields_fetch = pltpu.make_async_copy(fields_hbm, fields, sems.at[total])
    id_fetches = [pltpu.make_async_copy(users[j], asked.at[j], sems.at[j]) for j in range(total)]
    for copy in [fields_fetch] + id_fetches:
        copy.start()
    count = mats.shape[2]
    eye_pairs = (iota((count, count), 0) == iota((count, count), 1)).astype(jnp.bfloat16)
    side = (iota((count, LANES), 0) % 2 == 0) == (iota((count, LANES), 1) < K)
    for k in range(0, K, 2):
        twice = jnp.concatenate([mats[k], mats[k], mats[k + 1], mats[k + 1]], axis=0)
        turned = dot(eye_pairs, twice, NT)
        stacked[pl.ds(k, count, stride=PITCH), :] = jnp.where(side, turned[:, :LANES], 0.0)
        stacked[pl.ds(k + 1, count, stride=PITCH), :] = jnp.where(side, turned[:, LANES:], 0.0)
    fields_fetch.wait()

    def two(step, total):
        first = step * 2
        lefts, rights, mults = [], [], []
        for p in (first, first + 1):
            a = pl.multiple_of(fields[0, p] * K, K)
            b = pl.multiple_of(fields[1, p] * K, K)
            lefts.append(stacked[pl.ds(pl.multiple_of(p * PITCH, 8), K), :].astype(jnp.bfloat16))
            rights.append(rows16[pl.ds(b, K), :])
            mults.append(rows32[pl.ds(a, K), :])
        moved = dot(jnp.concatenate(lefts, axis=0), jnp.concatenate(rights, axis=0), NN)
        return total + moved * jnp.concatenate(mults, axis=0)

    sums = lax.fori_loop(0, count // 2, two, jnp.zeros((2 * K, rows32.shape[1]), jnp.float32), unroll=16)
    out[...] = jnp.sum(sums, axis=0, keepdims=True)
    for copy in id_fetches:
        copy.wait()
    for j, row in enumerate(slot_rows(asked, cap, slots, user_rows, places.shape[1])):
        places[j:j + 1, :] = row


def thirds(x):
    high = x.astype(jnp.bfloat16)
    rest = x - high.astype(jnp.float32)
    middle = rest.astype(jnp.bfloat16)
    return high, middle, (rest - middle.astype(jnp.float32)).astype(jnp.bfloat16)


def score_kernel(total, planes, parts, *refs):
    states, refs = refs[:total], refs[total:]
    items, refs = refs[:planes], refs[planes:]
    places, pairs, refs = refs[0], refs[1:1 + planes * parts], refs[1 + planes * parts:]
    outs, (wanted, cands, linear) = refs[:total], refs[total:]
    slots = states[0].shape[0]
    own_rows, width = items[0].shape
    me = lax.axis_index("shard")
    plane = lax.axis_index("cache")
    count = total * slots
    for j in range(total):
        wanted[j * slots:(j + 1) * slots, :] = states[j][:, :width]
        digits = states[j][:, width:].astype(jnp.float32)
        place = iota(digits.shape, 0)
        weight = jnp.where(place == 0, float(CODE), jnp.where(place == 1, 1.0, 0.0))
        cands[j:j + 1, :] = jnp.sum(digits * weight, axis=0, keepdims=True).astype(jnp.int32)
    eye = iota((own_rows, own_rows), 0) == iota((own_rows, own_rows), 1)
    ids, columns = [], []
    for q in range(planes):
        at = ring(plane - q, planes)
        scores = dot(items[q][...], wanted[...], NT)
        for t, part in enumerate(thirds(scores)):
            linear[q * own_rows:(q + 1) * own_rows, t * count:(t + 1) * count] = part
        row = sum(pairs[q * parts + h][...] for h in range(parts))
        columns.append(jnp.sum(jnp.where(eye, row, 0.0), axis=1, keepdims=True))
        ids.append(iota((own_rows, 1), 0) + (me * planes + at) * own_rows)
    pair_column = jnp.concatenate(columns, axis=0)
    item_ids = jnp.concatenate(ids, axis=0)
    for j in range(total):
        half = outs[j].shape[1]
        spread = (iota((count, half), 0) == places[j:j + 1, :]).astype(jnp.float32).astype(jnp.bfloat16)
        scores = dot(linear[...], jnp.concatenate([spread] * 3, axis=0), NN) + pair_column
        hit = item_ids == cands[j:j + 1, :]
        outs[j][...] = jnp.sum(jnp.where(hit, scores, 0.0), axis=0, keepdims=True)


def shift(x, axis, step):
    size = lax.axis_size(axis)
    return lax.ppermute(x, axis, [(s, (s + step) % size) for s in range(size)])


def body(cand_items, reader_users, item_table, user_states, pair_mats, pair_fields):
    total = lax.axis_size("shard")
    planes = lax.axis_size("cache")
    parts = lax.axis_size("pair")
    half = cand_items.shape[0]
    rows, width = item_table.shape
    readers = reader_users.shape[0]
    cap = 2 * ((readers + total - 1) // total)
    slots = -(-total * cap // 16) * 16
    count = pair_mats.shape[0]
    vmem = pl.BlockSpec(memory_space=pltpu.VMEM)
    hbm = pl.BlockSpec(memory_space=pltpu.HBM)
    anywhere = pl.BlockSpec(memory_space=pl.ANY)
    params = pltpu.CompilerParams(vmem_limit_bytes=VMEM_LIMIT)

    def in_hbm(x):
        return pltpu.with_memory_space_constraint(x, pltpu.HBM)

    with jax.named_scope("item_rows"):
        items = [item_table] + [shift(item_table, "cache", q) for q in range(1, planes)]

    with jax.named_scope("ids"):
        users = [in_hbm(reader_users)] + [shift(reader_users, "shard", j) for j in range(1, total)]

    with jax.named_scope("turn"):
        *turned, states_near = pl.pallas_call(
            turn_kernel,
            out_shape=(
                jax.ShapeDtypeStruct((width, rows), jnp.float32),
                jax.ShapeDtypeStruct((width, rows), jnp.bfloat16),
                jax.ShapeDtypeStruct((K, K, count), jnp.bfloat16),
                jax.ShapeDtypeStruct(user_states.shape, jnp.bfloat16),
            ),
            in_specs=[hbm, hbm, hbm],
            out_specs=(vmem, vmem, vmem, vmem),
            scratch_shapes=[pltpu.VMEM((rows, width), jnp.bfloat16), pltpu.SemaphoreType.DMA((6,))],
            compiler_params=params,
            cost_estimate=pl.CostEstimate(flops=2 * rows * rows * width * 16, bytes_accessed=8 * 1024 * 1024, transcendentals=0),
        )(in_hbm(item_table), in_hbm(jnp.transpose(pair_mats, (1, 2, 0))), in_hbm(user_states))

    with jax.named_scope("states"):
        picked = pl.pallas_call(
            functools.partial(pick_kernel, total, cap),
            out_shape=jax.ShapeDtypeStruct((slots, width + half), jnp.bfloat16),
            in_specs=[anywhere] * total + [hbm, vmem],
            out_specs=vmem,
            scratch_shapes=[
                pltpu.SMEM((total, readers), jnp.int32),
                pltpu.VMEM((1, half), jnp.int32),
                pltpu.SemaphoreType.DMA((total + 1,)),
            ],
            compiler_params=params,
            cost_estimate=pl.CostEstimate(flops=2 * slots * rows * width, bytes_accessed=1024 * 1024, transcendentals=0),
        )(*users, in_hbm(cand_items.reshape(1, half)), states_near)
        states = [picked] + [shift(picked, "shard", j) for j in range(1, total)]

    with jax.named_scope("pairs"):
        pair_parts, places = pl.pallas_call(
            functools.partial(pair_kernel, total, cap, slots, user_states.shape[0]),
            out_shape=(
                jax.ShapeDtypeStruct((1, rows), jnp.float32),
                jax.ShapeDtypeStruct((total, half), jnp.int32),
            ),
            in_specs=[anywhere] * total + [hbm, vmem, vmem, vmem, anywhere],
            out_specs=(vmem, vmem),
            scratch_shapes=[
                pltpu.SMEM((total, readers), jnp.int32),
                pltpu.SMEM((2, count), jnp.int32),
                pltpu.VMEM((count * PITCH, LANES), jnp.float32),
                pltpu.SemaphoreType.DMA((1 + total,)),
            ],
            compiler_params=params,
            cost_estimate=pl.CostEstimate(flops=2 * count * K * K * rows * 16, bytes_accessed=4 * 1024 * 1024, transcendentals=0),
        )(*users, in_hbm(pair_fields.T), *turned, picked)
        pair_scores, moved = [], 0
        for q in range(planes):
            for h in range(parts):
                perm = [
                    (c * parts + d, (c + q) % planes * parts + (d + h) % parts) for c in range(planes) for d in range(parts)
                ]
                source = pair_parts
                if 0 < moved < total:
                    source, states[moved] = lax.optimization_barrier((pair_parts, states[moved]))
                pair_scores.append(lax.ppermute(source, ("cache", "pair"), perm) if q or h else pair_parts)
                moved += q + h > 0

    with jax.named_scope("scores"):
        outs = pl.pallas_call(
            functools.partial(score_kernel, total, planes, parts),
            out_shape=[jax.ShapeDtypeStruct((1, half), jnp.float32)] * total,
            in_specs=[vmem] * (total + planes + 1 + planes * parts),
            out_specs=[vmem] * total,
            scratch_shapes=[
                pltpu.VMEM((total * slots, width), jnp.bfloat16),
                pltpu.VMEM((-(-total // 8) * 8, half), jnp.int32),
                pltpu.VMEM((planes * rows, 3 * total * slots), jnp.bfloat16),
            ],
            compiler_params=params,
            cost_estimate=pl.CostEstimate(flops=2 * 64 * 256 * width, bytes_accessed=2 * 1024 * 1024, transcendentals=0),
        )(*states, *items, places, *pair_scores)

    with jax.named_scope("back"):
        result = outs[0]
        for j in range(total - 1, 0, -1):
            result = result + shift(outs[j], "shard", -j)
    return result.reshape(half)


def solution(mesh):
    return jax.shard_map(
        body,
        mesh=mesh,
        in_specs=(
            P(("groups", "shard", "cache", "pair")),
            P(("groups", "shard", "cache", "pair")),
            P(("shard", "cache"), None),
            P(("groups", "shard"), None),
            P("pair", None, None),
            P("pair", None),
        ),
        out_specs=P(("groups", "shard", "cache", "pair")),
        check_vma=False,
    )
```

```python
import functools

import jax
import jax.numpy as jnp
from jax import lax
from jax.experimental import pallas as pl
from jax.experimental.pallas import tpu as pltpu
from jax.sharding import PartitionSpec as P

K = 64
LANES = 128
PITCH = 72
CODE = 128
VMEM_LIMIT = 40 * 1024 * 1024
NT = (((1,), (1,)), ((), ()))
NN = (((1,), (0,)), ((), ()))


def dot(a, b, dims, **kw):
    return lax.dot_general(a, b, dims, preferred_element_type=jnp.float32, **kw)


def iota(shape, dim):
    return lax.broadcasted_iota(jnp.int32, shape, dim)


def ring(index, size):
    return lax.rem(index + size, size)


def place_of(device, size):
    down = device % 2 == 0
    if isinstance(device, int):
        return (size - device // 2) % size if down else (device + 1) // 2
    return jnp.where(down, lax.rem(size - device // 2, size), (device + 1) // 2)


def pick_kernel(total, cap, *refs):
    users, (own_cands, held, out, asked, cands, sems) = refs[:total], refs[total:]
    digit_fetch = pltpu.make_async_copy(own_cands, cands, sems.at[total])
    id_fetches = [pltpu.make_async_copy(users[j], asked.at[j], sems.at[j]) for j in range(total)]
    for copy in id_fetches + [digit_fetch]:
        copy.start()
    own_rows, width = held.shape
    me = lax.axis_index("shard")
    place = place_of(me, total)
    slots = out.shape[0]
    slot_index = iota((slots, own_rows), 0)
    row_index = iota((slots, own_rows), 1)
    chosen = jnp.zeros((slots, own_rows), jnp.float32)
    for copy in id_fetches:
        copy.wait()
    for j in range(total):
        source = ring(place - j, total)
        taken = jnp.int32(0)
        for r in range(asked.shape[1]):
            user = asked[j, r]
            mine = user // own_rows == me
            slot = jnp.where(mine, source * cap + taken, -1)
            taken = taken + mine.astype(jnp.int32)
            chosen = jnp.where((slot_index == slot) & (row_index == user % own_rows), 1.0, chosen)
    chosen = chosen.astype(jnp.bfloat16)
    digit_fetch.wait()
    code = cands[...]
    digits = jnp.where(iota((slots, code.shape[1]), 0) == 0, code // CODE, code % CODE)
    out[:, width:] = jnp.where(iota(digits.shape, 0) < 2, digits, 0).astype(jnp.float32).astype(jnp.bfloat16)
    out[:, :width] = dot(chosen, held[...], NN).astype(jnp.bfloat16)


def slot_rows(asked, cap, slots, user_rows, half):
    total, readers = asked.shape
    me = place_of(lax.axis_index("shard"), total)
    lane = iota((1, half), 1) // (half // readers)
    rows = []
    for j in range(total):
        source = ring(me - j, total)
        holders = [asked[j, r] // user_rows for r in range(readers)]
        row = jnp.zeros((1, half), jnp.int32)
        for r, holder in enumerate(holders):
            rank = jnp.int32(0)
            for earlier in holders[:r]:
                rank = rank + (earlier == holder).astype(jnp.int32)
            arrival = ring(me - place_of(holder, total), total)
            row = jnp.where(lane == r, arrival * slots + source * cap + rank, row)
        rows.append(row)
    return rows


def turn_kernel(items_hbm, mats_hbm, states_hbm, rows32, rows16, mats, states, items, sems):
    chunks = sems.shape[0] - 2
    wide = items.shape[1] // chunks
    item_fetches = [
        pltpu.make_async_copy(items_hbm.at[:, pl.ds(t * wide, wide)], items.at[:, pl.ds(t * wide, wide)], sems.at[t])
        for t in range(chunks)
    ]
    mats_fetch = pltpu.make_async_copy(mats_hbm, mats, sems.at[chunks])
    states_fetch = pltpu.make_async_copy(states_hbm, states, sems.at[chunks + 1])
    for copy in item_fetches + [mats_fetch, states_fetch]:
        copy.start()
    eye = (iota((LANES, LANES), 0) == iota((LANES, LANES), 1)).astype(jnp.bfloat16)
    for t in range(items.shape[1] // LANES):
        if t * LANES % wide == 0:
            item_fetches[t * LANES // wide].wait()
        turned = dot(eye, items[:, t * LANES:(t + 1) * LANES], NT)
        rows32[t * LANES:(t + 1) * LANES, :] = turned
        rows16[t * LANES:(t + 1) * LANES, :] = turned.astype(jnp.bfloat16)
    mats_fetch.wait()
    states_fetch.wait()


def pair_kernel(total, cap, slots, user_rows, *refs):
    users, refs = refs[:total], refs[total:]
    fields_hbm, rows32, rows16, mats, picked, out, places, asked, fields, stacked, sems = refs
    del picked
    fields_fetch = pltpu.make_async_copy(fields_hbm, fields, sems.at[total])
    id_fetches = [pltpu.make_async_copy(users[j], asked.at[j], sems.at[j]) for j in range(total)]
    for copy in [fields_fetch] + id_fetches:
        copy.start()
    count = mats.shape[2]
    eye_pairs = (iota((count, count), 0) == iota((count, count), 1)).astype(jnp.bfloat16)
    side = (iota((count, LANES), 0) % 2 == 0) == (iota((count, LANES), 1) < K)
    for k in range(0, K, 2):
        twice = jnp.concatenate([mats[k], mats[k], mats[k + 1], mats[k + 1]], axis=0)
        turned = dot(eye_pairs, twice, NT)
        stacked[pl.ds(k, count, stride=PITCH), :] = jnp.where(side, turned[:, :LANES], 0.0)
        stacked[pl.ds(k + 1, count, stride=PITCH), :] = jnp.where(side, turned[:, LANES:], 0.0)
    fields_fetch.wait()

    def two(step, total):
        first = step * 2
        lefts, rights, mults = [], [], []
        for p in (first, first + 1):
            a = pl.multiple_of(fields[0, p] * K, K)
            b = pl.multiple_of(fields[1, p] * K, K)
            lefts.append(stacked[pl.ds(pl.multiple_of(p * PITCH, 8), K), :].astype(jnp.bfloat16))
            rights.append(rows16[pl.ds(b, K), :])
            mults.append(rows32[pl.ds(a, K), :])
        moved = dot(jnp.concatenate(lefts, axis=0), jnp.concatenate(rights, axis=0), NN)
        return total + moved * jnp.concatenate(mults, axis=0)

    sums = lax.fori_loop(0, count // 2, two, jnp.zeros((2 * K, rows32.shape[1]), jnp.float32), unroll=16)
    out[...] = jnp.sum(sums, axis=0, keepdims=True)
    for copy in id_fetches:
        copy.wait()
    for j, row in enumerate(slot_rows(asked, cap, slots, user_rows, places.shape[1])):
        places[j:j + 1, :] = row


def thirds(x):
    high = x.astype(jnp.bfloat16)
    rest = x - high.astype(jnp.float32)
    middle = rest.astype(jnp.bfloat16)
    return high, middle, (rest - middle.astype(jnp.float32)).astype(jnp.bfloat16)


def score_kernel(total, planes, parts, *refs):
    states, refs = refs[:total], refs[total:]
    items, refs = refs[:planes], refs[planes:]
    places, pairs, refs = refs[0], refs[1:1 + planes * parts], refs[1 + planes * parts:]
    outs, (wanted, cands, linear) = refs[:total], refs[total:]
    slots = states[0].shape[0]
    own_rows, width = items[0].shape
    me = lax.axis_index("shard")
    plane = lax.axis_index("cache")
    count = total * slots
    for j in range(total):
        wanted[j * slots:(j + 1) * slots, :] = states[j][:, :width]
        digits = states[j][:, width:].astype(jnp.float32)
        place = iota(digits.shape, 0)
        weight = jnp.where(place == 0, float(CODE), jnp.where(place == 1, 1.0, 0.0))
        cands[j:j + 1, :] = jnp.sum(digits * weight, axis=0, keepdims=True).astype(jnp.int32)
    eye = iota((own_rows, own_rows), 0) == iota((own_rows, own_rows), 1)
    ids, columns = [], []
    for q in range(planes):
        at = ring(plane - q, planes)
        scores = dot(items[q][...], wanted[...], NT)
        for t, part in enumerate(thirds(scores)):
            linear[q * own_rows:(q + 1) * own_rows, t * count:(t + 1) * count] = part
        row = sum(pairs[q * parts + h][...] for h in range(parts))
        columns.append(jnp.sum(jnp.where(eye, row, 0.0), axis=1, keepdims=True))
        ids.append(iota((own_rows, 1), 0) + (me * planes + at) * own_rows)
    pair_column = jnp.concatenate(columns, axis=0)
    item_ids = jnp.concatenate(ids, axis=0)
    for j in range(total):
        half = outs[j].shape[1]
        spread = (iota((count, half), 0) == places[j:j + 1, :]).astype(jnp.float32).astype(jnp.bfloat16)
        scores = dot(linear[...], jnp.concatenate([spread] * 3, axis=0), NN) + pair_column
        hit = item_ids == cands[j:j + 1, :]
        outs[j][...] = jnp.sum(jnp.where(hit, scores, 0.0), axis=0, keepdims=True)


def shift(x, axis, step):
    size = lax.axis_size(axis)
    return lax.ppermute(x, axis, [(s, (s + step) % size) for s in range(size)])


def along(x, step):
    total = lax.axis_size("shard")
    device_at = {place_of(s, total): s for s in range(total)}
    return lax.ppermute(x, "shard", [(device_at[p], device_at[(p + step) % total]) for p in range(total)])


def body(cand_items, reader_users, item_table, user_states, pair_mats, pair_fields):
    total = lax.axis_size("shard")
    planes = lax.axis_size("cache")
    parts = lax.axis_size("pair")
    half = cand_items.shape[0]
    rows, width = item_table.shape
    readers = reader_users.shape[0]
    cap = 2 * ((readers + total - 1) // total)
    slots = -(-total * cap // 16) * 16
    count = pair_mats.shape[0]
    vmem = pl.BlockSpec(memory_space=pltpu.VMEM)
    hbm = pl.BlockSpec(memory_space=pltpu.HBM)
    anywhere = pl.BlockSpec(memory_space=pl.ANY)
    params = pltpu.CompilerParams(vmem_limit_bytes=VMEM_LIMIT)

    def in_hbm(x):
        return pltpu.with_memory_space_constraint(x, pltpu.HBM)

    with jax.named_scope("item_rows"):
        items = [item_table] + [shift(item_table, "cache", q) for q in range(1, planes)]

    with jax.named_scope("ids"):
        users = [in_hbm(reader_users)] + [along(reader_users, j) for j in range(1, total)]

    with jax.named_scope("turn"):
        *turned, states_near = pl.pallas_call(
            turn_kernel,
            out_shape=(
                jax.ShapeDtypeStruct((width, rows), jnp.float32),
                jax.ShapeDtypeStruct((width, rows), jnp.bfloat16),
                jax.ShapeDtypeStruct((K, K, count), jnp.bfloat16),
                jax.ShapeDtypeStruct(user_states.shape, jnp.bfloat16),
            ),
            in_specs=[hbm, hbm, hbm],
            out_specs=(vmem, vmem, vmem, vmem),
            scratch_shapes=[pltpu.VMEM((rows, width), jnp.bfloat16), pltpu.SemaphoreType.DMA((6,))],
            compiler_params=params,
            cost_estimate=pl.CostEstimate(flops=2 * rows * rows * width * 16, bytes_accessed=8 * 1024 * 1024, transcendentals=0),
        )(in_hbm(item_table), in_hbm(jnp.transpose(pair_mats, (1, 2, 0))), in_hbm(user_states))

    with jax.named_scope("states"):
        picked = pl.pallas_call(
            functools.partial(pick_kernel, total, cap),
            out_shape=jax.ShapeDtypeStruct((slots, width + half), jnp.bfloat16),
            in_specs=[anywhere] * total + [hbm, vmem],
            out_specs=vmem,
            scratch_shapes=[
                pltpu.SMEM((total, readers), jnp.int32),
                pltpu.VMEM((1, half), jnp.int32),
                pltpu.SemaphoreType.DMA((total + 1,)),
            ],
            compiler_params=params,
            cost_estimate=pl.CostEstimate(flops=2 * slots * rows * width, bytes_accessed=1024 * 1024, transcendentals=0),
        )(*users, in_hbm(cand_items.reshape(1, half)), states_near)
        states = [picked] + [along(picked, j) for j in range(1, total)]

    with jax.named_scope("pairs"):
        pair_parts, places = pl.pallas_call(
            functools.partial(pair_kernel, total, cap, slots, user_states.shape[0]),
            out_shape=(
                jax.ShapeDtypeStruct((1, rows), jnp.float32),
                jax.ShapeDtypeStruct((total, half), jnp.int32),
            ),
            in_specs=[anywhere] * total + [hbm, vmem, vmem, vmem, anywhere],
            out_specs=(vmem, vmem),
            scratch_shapes=[
                pltpu.SMEM((total, readers), jnp.int32),
                pltpu.SMEM((2, count), jnp.int32),
                pltpu.VMEM((count * PITCH, LANES), jnp.float32),
                pltpu.SemaphoreType.DMA((1 + total,)),
            ],
            compiler_params=params,
            cost_estimate=pl.CostEstimate(flops=2 * count * K * K * rows * 16, bytes_accessed=4 * 1024 * 1024, transcendentals=0),
        )(*users, in_hbm(pair_fields.T), *turned, picked)
        pair_scores, moved = [], 0
        for q in range(planes):
            for h in range(parts):
                perm = [
                    (c * parts + d, (c + q) % planes * parts + (d + h) % parts) for c in range(planes) for d in range(parts)
                ]
                source = pair_parts
                if 0 < moved < total:
                    source, states[1] = lax.optimization_barrier((pair_parts, states[1]))
                pair_scores.append(lax.ppermute(source, ("cache", "pair"), perm) if q or h else pair_parts)
                moved += q + h > 0

    with jax.named_scope("scores"):
        outs = pl.pallas_call(
            functools.partial(score_kernel, total, planes, parts),
            out_shape=[jax.ShapeDtypeStruct((1, half), jnp.float32)] * total,
            in_specs=[vmem] * (total + planes + 1 + planes * parts),
            out_specs=[vmem] * total,
            scratch_shapes=[
                pltpu.VMEM((total * slots, width), jnp.bfloat16),
                pltpu.VMEM((-(-total // 8) * 8, half), jnp.int32),
                pltpu.VMEM((planes * rows, 3 * total * slots), jnp.bfloat16),
            ],
            compiler_params=params,
            cost_estimate=pl.CostEstimate(flops=2 * 64 * 256 * width, bytes_accessed=2 * 1024 * 1024, transcendentals=0),
        )(*states, *items, places, *pair_scores)

    with jax.named_scope("back"):
        result = outs[0]
        for j in range(total - 1, 0, -1):
            result = result + along(outs[j], -j)
    return result.reshape(half)


def solution(mesh):
    return jax.shard_map(
        body,
        mesh=mesh,
        in_specs=(
            P(("groups", "shard", "cache", "pair")),
            P(("groups", "shard", "cache", "pair")),
            P(("shard", "cache"), None),
            P(("groups", "shard"), None),
            P("pair", None, None),
            P("pair", None),
        ),
        out_specs=P(("groups", "shard", "cache", "pair")),
        check_vma=False,
    )
```

```python
import functools

import jax
import jax.numpy as jnp
from jax import lax
from jax.experimental import pallas as pl
from jax.experimental.pallas import tpu as pltpu
from jax.sharding import PartitionSpec as P

K = 64
LANES = 128
PITCH = 72
CODE_BITS = 7
VMEM_LIMIT = 40 * 1024 * 1024
NT = (((1,), (1,)), ((), ()))
NN = (((1,), (0,)), ((), ()))


def dot(a, b, dims, **kw):
    return lax.dot_general(a, b, dims, preferred_element_type=jnp.float32, **kw)


def iota(shape, dim):
    return lax.broadcasted_iota(jnp.int32, shape, dim)


def ring(index, size):
    return lax.rem(index + size, size)


def pick_kernel(total, cap, *refs):
    users, (digits, states, out) = refs[:total], refs[total:]
    own_rows, width = states.shape
    slots = out.shape[0]
    readers = users[0].shape[1]
    me = lax.axis_index("shard")
    first = me * own_rows
    across = iota((readers, readers), 1)
    down = iota((readers, readers), 0)
    chosen = jnp.zeros((slots, own_rows), jnp.float32)
    for j in range(total):
        row = users[j][...]
        column = jnp.sum(jnp.where(across == down, row, 0), axis=1, keepdims=True)
        mine = (column >= first) & (column < first + own_rows)
        rank = jnp.sum(jnp.where((down < across) & mine, 1, 0), axis=0, keepdims=True)
        held = (row >= first) & (row < first + own_rows)
        slot = jnp.where(held, ring(me - j, total) * cap + rank, -1)
        to_slot = (iota((slots, readers), 0) == slot).astype(jnp.float32).astype(jnp.bfloat16)
        from_row = (iota((readers, own_rows), 1) + first == column).astype(jnp.float32).astype(jnp.bfloat16)
        chosen = chosen + dot(to_slot, from_row, NN)
    out[:, width:] = digits[...]
    out[:, :width] = dot(chosen.astype(jnp.bfloat16), states[...], NN).astype(jnp.bfloat16)


def slot_rows(asked, cap, slots, user_rows, half):
    total, readers = asked.shape
    me = lax.axis_index("shard")
    lane = iota((1, half), 1) // (half // readers)
    rows = []
    for j in range(total):
        source = ring(me - j, total)
        holders = [asked[j, r] // user_rows for r in range(readers)]
        row = jnp.zeros((1, half), jnp.int32)
        for r, holder in enumerate(holders):
            rank = jnp.int32(0)
            for earlier in holders[:r]:
                rank = rank + (earlier == holder).astype(jnp.int32)
            row = jnp.where(lane == r, ring(me - holder, total) * slots + source * cap + rank, row)
        rows.append(row)
    return rows


def turn_kernel(items_hbm, mats_hbm, states_hbm, ids_hbm, cands_hbm, rows32, rows16, mats, states, ids, digits, items, cands, sems):
    chunks = sems.shape[0] - 4
    wide = items.shape[1] // chunks
    item_fetches = [
        pltpu.make_async_copy(items_hbm.at[:, pl.ds(t * wide, wide)], items.at[:, pl.ds(t * wide, wide)], sems.at[t])
        for t in range(chunks)
    ]
    mats_fetch = pltpu.make_async_copy(mats_hbm, mats, sems.at[chunks])
    states_fetch = pltpu.make_async_copy(states_hbm, states, sems.at[chunks + 1])
    ids_fetch = pltpu.make_async_copy(ids_hbm, ids, sems.at[chunks + 2])
    cands_fetch = pltpu.make_async_copy(cands_hbm, cands, sems.at[chunks + 3])
    for copy in item_fetches + [mats_fetch, states_fetch, ids_fetch, cands_fetch]:
        copy.start()
    eye = (iota((LANES, LANES), 0) == iota((LANES, LANES), 1)).astype(jnp.bfloat16)
    for t in range(items.shape[1] // LANES):
        if t * LANES % wide == 0:
            item_fetches[t * LANES // wide].wait()
        turned = dot(eye, items[:, t * LANES:(t + 1) * LANES], NT)
        rows32[t * LANES:(t + 1) * LANES, :] = turned
        rows16[t * LANES:(t + 1) * LANES, :] = turned.astype(jnp.bfloat16)
    cands_fetch.wait()
    code = jnp.broadcast_to(cands[...], digits.shape)
    place = iota(digits.shape, 0)
    digit = jnp.where(place == 0, code >> CODE_BITS, jnp.where(place == 1, code & ((1 << CODE_BITS) - 1), 0))
    digits[...] = digit.astype(jnp.float32).astype(jnp.bfloat16)
    ids_fetch.wait()
    mats_fetch.wait()
    states_fetch.wait()


def pair_kernel(total, cap, slots, user_rows, *refs):
    users, refs = refs[:total], refs[total:]
    fields_hbm, rows32, rows16, mats, picked, out, places, asked, fields, stacked, sems = refs
    del picked
    fields_fetch = pltpu.make_async_copy(fields_hbm, fields, sems.at[total])
    id_fetches = [pltpu.make_async_copy(users[j], asked.at[j], sems.at[j]) for j in range(total)]
    for copy in [fields_fetch] + id_fetches:
        copy.start()
    count = mats.shape[2]
    eye_pairs = (iota((count, count), 0) == iota((count, count), 1)).astype(jnp.bfloat16)
    side = (iota((count, LANES), 0) % 2 == 0) == (iota((count, LANES), 1) < K)
    for k in range(0, K, 2):
        twice = jnp.concatenate([mats[k], mats[k], mats[k + 1], mats[k + 1]], axis=0)
        turned = dot(eye_pairs, twice, NT)
        stacked[pl.ds(k, count, stride=PITCH), :] = jnp.where(side, turned[:, :LANES], 0.0)
        stacked[pl.ds(k + 1, count, stride=PITCH), :] = jnp.where(side, turned[:, LANES:], 0.0)
    fields_fetch.wait()

    def two(step, total):
        first = step * 2
        lefts, rights, mults = [], [], []
        for p in (first, first + 1):
            a = pl.multiple_of(fields[0, p] * K, K)
            b = pl.multiple_of(fields[1, p] * K, K)
            lefts.append(stacked[pl.ds(pl.multiple_of(p * PITCH, 8), K), :].astype(jnp.bfloat16))
            rights.append(rows16[pl.ds(b, K), :])
            mults.append(rows32[pl.ds(a, K), :])
        moved = dot(jnp.concatenate(lefts, axis=0), jnp.concatenate(rights, axis=0), NN)
        return total + moved * jnp.concatenate(mults, axis=0)

    sums = lax.fori_loop(0, count // 2, two, jnp.zeros((2 * K, rows32.shape[1]), jnp.float32), unroll=16)
    out[...] = jnp.sum(sums, axis=0, keepdims=True)
    for copy in id_fetches:
        copy.wait()
    for j, row in enumerate(slot_rows(asked, cap, slots, user_rows, places.shape[1])):
        places[j:j + 1, :] = row


def thirds(x):
    high = x.astype(jnp.bfloat16)
    rest = x - high.astype(jnp.float32)
    middle = rest.astype(jnp.bfloat16)
    return high, middle, (rest - middle.astype(jnp.float32)).astype(jnp.bfloat16)


def score_kernel(total, planes, parts, *refs):
    states, refs = refs[:total], refs[total:]
    items, refs = refs[:planes], refs[planes:]
    places, pairs, refs = refs[0], refs[1:1 + planes * parts], refs[1 + planes * parts:]
    outs, (wanted, cands, linear) = refs[:total], refs[total:]
    slots = states[0].shape[0]
    own_rows, width = items[0].shape
    me = lax.axis_index("shard")
    plane = lax.axis_index("cache")
    count = total * slots
    for j in range(total):
        wanted[j * slots:(j + 1) * slots, :] = states[j][:, :width]
        digits = states[j][:, width:].astype(jnp.float32)
        place = iota(digits.shape, 0)
        weight = jnp.where(place == 0, float(1 << CODE_BITS), jnp.where(place == 1, 1.0, 0.0))
        cands[j:j + 1, :] = jnp.sum(digits * weight, axis=0, keepdims=True).astype(jnp.int32)
    eye = iota((own_rows, own_rows), 0) == iota((own_rows, own_rows), 1)
    ids, columns = [], []
    for q in range(planes):
        at = ring(plane - q, planes)
        scores = dot(items[q][...], wanted[...], NT)
        for t, part in enumerate(thirds(scores)):
            linear[q * own_rows:(q + 1) * own_rows, t * count:(t + 1) * count] = part
        row = sum(pairs[q * parts + h][...] for h in range(parts))
        columns.append(jnp.sum(jnp.where(eye, row, 0.0), axis=1, keepdims=True))
        ids.append(iota((own_rows, 1), 0) + (me * planes + at) * own_rows)
    pair_column = jnp.concatenate(columns, axis=0)
    item_ids = jnp.concatenate(ids, axis=0)
    for j in range(total):
        half = outs[j].shape[1]
        spread = (iota((count, half), 0) == places[j:j + 1, :]).astype(jnp.float32).astype(jnp.bfloat16)
        scores = dot(linear[...], jnp.concatenate([spread] * 3, axis=0), NN) + pair_column
        hit = item_ids == cands[j:j + 1, :]
        outs[j][...] = jnp.sum(jnp.where(hit, scores, 0.0), axis=0, keepdims=True)


def shift(x, axis, step):
    size = lax.axis_size(axis)
    return lax.ppermute(x, axis, [(s, (s + step) % size) for s in range(size)])


def body(cand_items, reader_users, item_table, user_states, pair_mats, pair_fields):
    total = lax.axis_size("shard")
    planes = lax.axis_size("cache")
    parts = lax.axis_size("pair")
    half = cand_items.shape[0]
    rows, width = item_table.shape
    readers = reader_users.shape[0]
    cap = 2 * ((readers + total - 1) // total)
    slots = -(-total * cap // 16) * 16
    count = pair_mats.shape[0]
    vmem = pl.BlockSpec(memory_space=pltpu.VMEM)
    hbm = pl.BlockSpec(memory_space=pltpu.HBM)
    anywhere = pl.BlockSpec(memory_space=pl.ANY)
    params = pltpu.CompilerParams(vmem_limit_bytes=VMEM_LIMIT)

    def in_hbm(x):
        return pltpu.with_memory_space_constraint(x, pltpu.HBM)

    with jax.named_scope("item_rows"):
        items = [item_table] + [shift(item_table, "cache", q) for q in range(1, planes)]

    with jax.named_scope("ids"):
        users = [in_hbm(reader_users)] + [shift(reader_users, "shard", j) for j in range(1, total)]

    with jax.named_scope("turn"):
        *turned, states_near, own_ids, digits = pl.pallas_call(
            turn_kernel,
            out_shape=(
                jax.ShapeDtypeStruct((width, rows), jnp.float32),
                jax.ShapeDtypeStruct((width, rows), jnp.bfloat16),
                jax.ShapeDtypeStruct((K, K, count), jnp.bfloat16),
                jax.ShapeDtypeStruct(user_states.shape, jnp.bfloat16),
                jax.ShapeDtypeStruct((1, readers), jnp.int32),
                jax.ShapeDtypeStruct((slots, half), jnp.bfloat16),
            ),
            in_specs=[hbm] * 5,
            out_specs=(vmem,) * 6,
            scratch_shapes=[
                pltpu.VMEM((rows, width), jnp.bfloat16),
                pltpu.VMEM((1, half), jnp.int32),
                pltpu.SemaphoreType.DMA((8,)),
            ],
            compiler_params=params,
            cost_estimate=pl.CostEstimate(flops=2 * rows * rows * width * 16, bytes_accessed=8 * 1024 * 1024, transcendentals=0),
        )(
            in_hbm(item_table),
            in_hbm(jnp.transpose(pair_mats, (1, 2, 0))),
            in_hbm(user_states),
            in_hbm(reader_users.reshape(1, readers)),
            in_hbm(cand_items.reshape(1, half)),
        )

    with jax.named_scope("states"):
        picked = pl.pallas_call(
            functools.partial(pick_kernel, total, cap),
            out_shape=jax.ShapeDtypeStruct((slots, width + half), jnp.bfloat16),
            in_specs=[vmem] * (total + 2),
            out_specs=vmem,
            compiler_params=params,
            cost_estimate=pl.CostEstimate(flops=2 * slots * rows * width, bytes_accessed=1024 * 1024, transcendentals=0),
        )(own_ids, *[ids.reshape(1, readers) for ids in users[1:]], digits, states_near)
        states = [picked] + [shift(picked, "shard", j) for j in range(1, total)]

    with jax.named_scope("pairs"):
        pair_parts, places = pl.pallas_call(
            functools.partial(pair_kernel, total, cap, slots, user_states.shape[0]),
            out_shape=(
                jax.ShapeDtypeStruct((1, rows), jnp.float32),
                jax.ShapeDtypeStruct((total, half), jnp.int32),
            ),
            in_specs=[anywhere] * total + [hbm, vmem, vmem, vmem, anywhere],
            out_specs=(vmem, vmem),
            scratch_shapes=[
                pltpu.SMEM((total, readers), jnp.int32),
                pltpu.SMEM((2, count), jnp.int32),
                pltpu.VMEM((count * PITCH, LANES), jnp.float32),
                pltpu.SemaphoreType.DMA((1 + total,)),
            ],
            compiler_params=params,
            cost_estimate=pl.CostEstimate(flops=2 * count * K * K * rows * 16, bytes_accessed=4 * 1024 * 1024, transcendentals=0),
        )(*users, in_hbm(pair_fields.T), *turned, picked)
        pair_scores, moved = [], 0
        for q in range(planes):
            for h in range(parts):
                perm = [
                    (c * parts + d, (c + q) % planes * parts + (d + h) % parts) for c in range(planes) for d in range(parts)
                ]
                source = pair_parts
                if 0 < moved < total:
                    source, states[1] = lax.optimization_barrier((pair_parts, states[1]))
                pair_scores.append(lax.ppermute(source, ("cache", "pair"), perm) if q or h else pair_parts)
                moved += q + h > 0

    with jax.named_scope("scores"):
        outs = pl.pallas_call(
            functools.partial(score_kernel, total, planes, parts),
            out_shape=[jax.ShapeDtypeStruct((1, half), jnp.float32)] * total,
            in_specs=[vmem] * (total + planes + 1 + planes * parts),
            out_specs=[vmem] * total,
            scratch_shapes=[
                pltpu.VMEM((total * slots, width), jnp.bfloat16),
                pltpu.VMEM((-(-total // 8) * 8, half), jnp.int32),
                pltpu.VMEM((planes * rows, 3 * total * slots), jnp.bfloat16),
            ],
            compiler_params=params,
            cost_estimate=pl.CostEstimate(flops=2 * 64 * 256 * width, bytes_accessed=2 * 1024 * 1024, transcendentals=0),
        )(*states, *items, places, *pair_scores)

    with jax.named_scope("back"):
        result = outs[0]
        for j in range(total - 1, 0, -1):
            result = result + shift(outs[j], "shard", -j)
    return result.reshape(half)


def solution(mesh):
    return jax.shard_map(
        body,
        mesh=mesh,
        in_specs=(
            P(("groups", "shard", "cache", "pair")),
            P(("groups", "shard", "cache", "pair")),
            P(("shard", "cache"), None),
            P(("groups", "shard"), None),
            P("pair", None, None),
            P("pair", None),
        ),
        out_specs=P(("groups", "shard", "cache", "pair")),
        check_vma=False,
    )
```

```python
import functools

import jax
import jax.numpy as jnp
from jax import lax
from jax.experimental import pallas as pl
from jax.experimental.pallas import tpu as pltpu
from jax.sharding import PartitionSpec as P

K = 64
LANES = 128
PITCH = 72
CODE_BITS = 7
VMEM_LIMIT = 40 * 1024 * 1024
NT = (((1,), (1,)), ((), ()))
NN = (((1,), (0,)), ((), ()))


def dot(a, b, dims, **kw):
    return lax.dot_general(a, b, dims, preferred_element_type=jnp.float32, **kw)


def iota(shape, dim):
    return lax.broadcasted_iota(jnp.int32, shape, dim)


def ring(index, size):
    return lax.rem(index + size, size)


def pick_kernel(total, cap, *refs):
    users, (digits, states, out) = refs[:total], refs[total:]
    own_rows, width = states.shape
    slots = out.shape[0]
    readers = users[0].shape[1]
    me = lax.axis_index("shard")
    first = me * own_rows
    across = iota((readers, readers), 1)
    down = iota((readers, readers), 0)
    chosen = jnp.zeros((slots, own_rows), jnp.float32)
    for j in range(total):
        row = users[j][...]
        column = jnp.sum(jnp.where(across == down, row, 0), axis=1, keepdims=True)
        mine = (column >= first) & (column < first + own_rows)
        rank = jnp.sum(jnp.where((down < across) & mine, 1, 0), axis=0, keepdims=True)
        held = (row >= first) & (row < first + own_rows)
        slot = jnp.where(held, ring(me - j, total) * cap + rank, -1)
        to_slot = (iota((slots, readers), 0) == slot).astype(jnp.float32).astype(jnp.bfloat16)
        from_row = (iota((readers, own_rows), 1) + first == column).astype(jnp.float32).astype(jnp.bfloat16)
        chosen = chosen + dot(to_slot, from_row, NN)
    out[:, width:] = digits[...]
    out[:, :width] = dot(chosen.astype(jnp.bfloat16), states[...], NN).astype(jnp.bfloat16)


def slot_rows(asked, cap, slots, user_rows, half):
    total, readers = asked.shape
    me = lax.axis_index("shard")
    lane = iota((1, half), 1) // (half // readers)
    rows = []
    for j in range(total):
        source = ring(me - j, total)
        holders = [asked[j, r] // user_rows for r in range(readers)]
        row = jnp.zeros((1, half), jnp.int32)
        for r, holder in enumerate(holders):
            rank = jnp.int32(0)
            for earlier in holders[:r]:
                rank = rank + (earlier == holder).astype(jnp.int32)
            row = jnp.where(lane == r, ring(me - holder, total) * slots + source * cap + rank, row)
        rows.append(row)
    return rows


def turn_kernel(items_hbm, mats_hbm, states_hbm, ids_hbm, cands_hbm, rows32, rows16, mats, states, ids, digits, items, cands, sems):
    chunks = sems.shape[0] - 4
    wide = items.shape[1] // chunks
    item_fetches = [
        pltpu.make_async_copy(items_hbm.at[:, pl.ds(t * wide, wide)], items.at[:, pl.ds(t * wide, wide)], sems.at[t])
        for t in range(chunks)
    ]
    mats_fetch = pltpu.make_async_copy(mats_hbm, mats, sems.at[chunks])
    states_fetch = pltpu.make_async_copy(states_hbm, states, sems.at[chunks + 1])
    ids_fetch = pltpu.make_async_copy(ids_hbm, ids, sems.at[chunks + 2])
    cands_fetch = pltpu.make_async_copy(cands_hbm, cands, sems.at[chunks + 3])
    for copy in item_fetches + [mats_fetch, states_fetch, ids_fetch, cands_fetch]:
        copy.start()
    eye = (iota((LANES, LANES), 0) == iota((LANES, LANES), 1)).astype(jnp.bfloat16)
    for t in range(items.shape[1] // LANES):
        if t * LANES % wide == 0:
            item_fetches[t * LANES // wide].wait()
        turned = dot(eye, items[:, t * LANES:(t + 1) * LANES], NT)
        rows32[t * LANES:(t + 1) * LANES, :] = turned
        rows16[t * LANES:(t + 1) * LANES, :] = turned.astype(jnp.bfloat16)
    cands_fetch.wait()
    code = jnp.broadcast_to(cands[...], digits.shape)
    place = iota(digits.shape, 0)
    digit = jnp.where(place == 0, code >> CODE_BITS, jnp.where(place == 1, code & ((1 << CODE_BITS) - 1), 0))
    digits[...] = digit.astype(jnp.float32).astype(jnp.bfloat16)
    ids_fetch.wait()
    mats_fetch.wait()
    states_fetch.wait()


def pair_kernel(total, cap, slots, user_rows, *refs):
    users, refs = refs[:total], refs[total:]
    fields_hbm, rows32, rows16, mats, picked, out, places, asked, fields, stacked, sems = refs
    del picked
    fields_fetch = pltpu.make_async_copy(fields_hbm, fields, sems.at[total])
    id_fetches = [pltpu.make_async_copy(users[j], asked.at[j], sems.at[j]) for j in range(total)]
    for copy in [fields_fetch] + id_fetches:
        copy.start()
    count = mats.shape[2]
    eye_pairs = (iota((count, count), 0) == iota((count, count), 1)).astype(jnp.bfloat16)
    side = (iota((count, LANES), 0) % 2 == 0) == (iota((count, LANES), 1) < K)
    for k in range(0, K, 2):
        twice = jnp.concatenate([mats[k], mats[k], mats[k + 1], mats[k + 1]], axis=0)
        turned = dot(eye_pairs, twice, NT)
        stacked[pl.ds(k, count, stride=PITCH), :] = jnp.where(side, turned[:, :LANES], 0.0)
        stacked[pl.ds(k + 1, count, stride=PITCH), :] = jnp.where(side, turned[:, LANES:], 0.0)
    fields_fetch.wait()

    def two(step, total):
        first = step * 2
        lefts, rights, mults = [], [], []
        for p in (first, first + 1):
            a = pl.multiple_of(fields[0, p] * K, K)
            b = pl.multiple_of(fields[1, p] * K, K)
            lefts.append(stacked[pl.ds(pl.multiple_of(p * PITCH, 8), K), :].astype(jnp.bfloat16))
            rights.append(rows16[pl.ds(b, K), :])
            mults.append(rows32[pl.ds(a, K), :])
        moved = dot(jnp.concatenate(lefts, axis=0), jnp.concatenate(rights, axis=0), NN)
        return total + moved * jnp.concatenate(mults, axis=0)

    sums = lax.fori_loop(0, count // 2, two, jnp.zeros((2 * K, rows32.shape[1]), jnp.float32), unroll=16)
    out[...] = jnp.sum(sums, axis=0, keepdims=True)
    for copy in id_fetches:
        copy.wait()
    for j, row in enumerate(slot_rows(asked, cap, slots, user_rows, places.shape[1])):
        places[j:j + 1, :] = row


def thirds(x):
    high = x.astype(jnp.bfloat16)
    rest = x - high.astype(jnp.float32)
    middle = rest.astype(jnp.bfloat16)
    return high, middle, (rest - middle.astype(jnp.float32)).astype(jnp.bfloat16)


def score_kernel(total, planes, parts, *refs):
    states, refs = refs[:total], refs[total:]
    items, refs = refs[:planes], refs[planes:]
    places, pairs, refs = refs[0], refs[1:1 + planes * parts], refs[1 + planes * parts:]
    outs, (wanted, cands, linear) = refs[:total], refs[total:]
    slots = states[0].shape[0]
    own_rows, width = items[0].shape
    me = lax.axis_index("shard")
    plane = lax.axis_index("cache")
    count = total * slots
    for j in range(total):
        wanted[j * slots:(j + 1) * slots, :] = states[j][:, :width]
        digits = states[j][:, width:].astype(jnp.float32)
        place = iota(digits.shape, 0)
        weight = jnp.where(place == 0, float(1 << CODE_BITS), jnp.where(place == 1, 1.0, 0.0))
        cands[j:j + 1, :] = jnp.sum(digits * weight, axis=0, keepdims=True).astype(jnp.int32)
    eye = iota((own_rows, own_rows), 0) == iota((own_rows, own_rows), 1)
    ids, columns = [], []
    for q in range(planes):
        at = ring(plane - q, planes)
        scores = dot(items[q][...], wanted[...], NT)
        for t, part in enumerate(thirds(scores)):
            linear[q * own_rows:(q + 1) * own_rows, t * count:(t + 1) * count] = part
        row = sum(pairs[q * parts + h][...] for h in range(parts))
        columns.append(jnp.sum(jnp.where(eye, row, 0.0), axis=1, keepdims=True))
        ids.append(iota((own_rows, 1), 0) + (me * planes + at) * own_rows)
    pair_column = jnp.concatenate(columns, axis=0)
    item_ids = jnp.concatenate(ids, axis=0)
    for j in range(total):
        half = outs[j].shape[1]
        spread = (iota((count, half), 0) == places[j:j + 1, :]).astype(jnp.float32).astype(jnp.bfloat16)
        scores = dot(linear[...], jnp.concatenate([spread] * 3, axis=0), NN) + pair_column
        hit = item_ids == cands[j:j + 1, :]
        outs[j][...] = jnp.sum(jnp.where(hit, scores, 0.0), axis=0, keepdims=True)


def shift(x, axis, step):
    size = lax.axis_size(axis)
    return lax.ppermute(x, axis, [(s, (s + step) % size) for s in range(size)])


def body(cand_items, reader_users, item_table, user_states, pair_mats, pair_fields):
    total = lax.axis_size("shard")
    planes = lax.axis_size("cache")
    parts = lax.axis_size("pair")
    half = cand_items.shape[0]
    rows, width = item_table.shape
    readers = reader_users.shape[0]
    cap = 2 * ((readers + total - 1) // total)
    slots = -(-total * cap // 16) * 16
    count = pair_mats.shape[0]
    vmem = pl.BlockSpec(memory_space=pltpu.VMEM)
    hbm = pl.BlockSpec(memory_space=pltpu.HBM)
    anywhere = pl.BlockSpec(memory_space=pl.ANY)
    params = pltpu.CompilerParams(vmem_limit_bytes=VMEM_LIMIT)

    def in_hbm(x):
        return pltpu.with_memory_space_constraint(x, pltpu.HBM)

    with jax.named_scope("item_rows"):
        items = [item_table] + [shift(item_table, "cache", q) for q in range(1, planes)]

    with jax.named_scope("ids"):
        users = [in_hbm(reader_users)] + [shift(reader_users, "shard", j) for j in range(1, total)]

    with jax.named_scope("turn"):
        *turned, states_near, own_ids, digits = pl.pallas_call(
            turn_kernel,
            out_shape=(
                jax.ShapeDtypeStruct((width, rows), jnp.float32),
                jax.ShapeDtypeStruct((width, rows), jnp.bfloat16),
                jax.ShapeDtypeStruct((K, K, count), jnp.bfloat16),
                jax.ShapeDtypeStruct(user_states.shape, jnp.bfloat16),
                jax.ShapeDtypeStruct((1, readers), jnp.int32),
                jax.ShapeDtypeStruct((slots, half), jnp.bfloat16),
            ),
            in_specs=[hbm] * 5,
            out_specs=(vmem,) * 6,
            scratch_shapes=[
                pltpu.VMEM((rows, width), jnp.bfloat16),
                pltpu.VMEM((1, half), jnp.int32),
                pltpu.SemaphoreType.DMA((8,)),
            ],
            compiler_params=params,
            cost_estimate=pl.CostEstimate(flops=2 * rows * rows * width * 16, bytes_accessed=8 * 1024 * 1024, transcendentals=0),
        )(
            in_hbm(item_table),
            in_hbm(jnp.transpose(pair_mats, (1, 2, 0))),
            in_hbm(user_states),
            in_hbm(reader_users.reshape(1, readers)),
            in_hbm(cand_items.reshape(1, half)),
        )

    with jax.named_scope("states"):
        picked = pl.pallas_call(
            functools.partial(pick_kernel, total, cap),
            out_shape=jax.ShapeDtypeStruct((slots, width + half), jnp.bfloat16),
            in_specs=[vmem] * (total + 2),
            out_specs=vmem,
            compiler_params=params,
            cost_estimate=pl.CostEstimate(flops=2 * slots * rows * width, bytes_accessed=1024 * 1024, transcendentals=0),
        )(own_ids, *[ids.reshape(1, readers) for ids in users[1:]], digits, states_near)
        states = [picked] + [shift(picked, "shard", j) for j in range(1, total)]

    with jax.named_scope("pairs"):
        pair_parts, places = pl.pallas_call(
            functools.partial(pair_kernel, total, cap, slots, user_states.shape[0]),
            out_shape=(
                jax.ShapeDtypeStruct((1, rows), jnp.float32),
                jax.ShapeDtypeStruct((total, half), jnp.int32),
            ),
            in_specs=[anywhere] * total + [hbm, vmem, vmem, vmem, anywhere],
            out_specs=(vmem, vmem),
            scratch_shapes=[
                pltpu.SMEM((total, readers), jnp.int32),
                pltpu.SMEM((2, count), jnp.int32),
                pltpu.VMEM((count * PITCH, LANES), jnp.float32),
                pltpu.SemaphoreType.DMA((1 + total,)),
            ],
            compiler_params=params,
            cost_estimate=pl.CostEstimate(flops=2 * count * K * K * rows * 16, bytes_accessed=4 * 1024 * 1024, transcendentals=0),
        )(*users, in_hbm(pair_fields.T), *turned, picked)
        pair_scores = {(0, 0): pair_parts}
        for q, h in [(q, h) for q in range(planes - 1, -1, -1) for h in range(parts) if q or h]:
            perm = [
                (c * parts + d, (c + q) % planes * parts + (d + h) % parts) for c in range(planes) for d in range(parts)
            ]
            source, after = pair_parts, {1: 3, 2: 2}.get(len(pair_scores) - 1, 0)
            if after:
                source, states[after] = lax.optimization_barrier((pair_parts, states[after]))
            pair_scores[q, h] = lax.ppermute(source, ("cache", "pair"), perm)
        pair_scores = [pair_scores[q, h] for q in range(planes) for h in range(parts)]

    with jax.named_scope("scores"):
        outs = pl.pallas_call(
            functools.partial(score_kernel, total, planes, parts),
            out_shape=[jax.ShapeDtypeStruct((1, half), jnp.float32)] * total,
            in_specs=[vmem] * (total + planes + 1 + planes * parts),
            out_specs=[vmem] * total,
            scratch_shapes=[
                pltpu.VMEM((total * slots, width), jnp.bfloat16),
                pltpu.VMEM((-(-total // 8) * 8, half), jnp.int32),
                pltpu.VMEM((planes * rows, 3 * total * slots), jnp.bfloat16),
            ],
            compiler_params=params,
            cost_estimate=pl.CostEstimate(flops=2 * 64 * 256 * width, bytes_accessed=2 * 1024 * 1024, transcendentals=0),
        )(*states, *items, places, *pair_scores)

    with jax.named_scope("back"):
        result = outs[0]
        for j in range(total - 1, 0, -1):
            result = result + shift(outs[j], "shard", -j)
    return result.reshape(half)


def solution(mesh):
    return jax.shard_map(
        body,
        mesh=mesh,
        in_specs=(
            P(("groups", "shard", "cache", "pair")),
            P(("groups", "shard", "cache", "pair")),
            P(("shard", "cache"), None),
            P(("groups", "shard"), None),
            P("pair", None, None),
            P("pair", None),
        ),
        out_specs=P(("groups", "shard", "cache", "pair")),
        check_vma=False,
    )
```

```python
import functools

import jax
import jax.numpy as jnp
from jax import lax
from jax.experimental import pallas as pl
from jax.experimental.pallas import tpu as pltpu
from jax.sharding import PartitionSpec as P

K = 64
LANES = 128
PITCH = 72
CODE_BITS = 7
VMEM_LIMIT = 40 * 1024 * 1024
NT = (((1,), (1,)), ((), ()))
NN = (((1,), (0,)), ((), ()))


def dot(a, b, dims, **kw):
    return lax.dot_general(a, b, dims, preferred_element_type=jnp.float32, **kw)


def iota(shape, dim):
    return lax.broadcasted_iota(jnp.int32, shape, dim)


def ring(index, size):
    return lax.rem(index + size, size)


def pick_kernel(total, cap, *refs):
    users, (digits, states, out) = refs[:total], refs[total:]
    own_rows, width = states.shape
    slots = out.shape[0]
    readers = users[0].shape[1]
    me = lax.axis_index("shard")
    first = me * own_rows
    across = iota((readers, readers), 1)
    down = iota((readers, readers), 0)
    chosen = jnp.zeros((slots, own_rows), jnp.float32)
    for j in range(total):
        row = users[j][...]
        column = jnp.sum(jnp.where(across == down, row, 0), axis=1, keepdims=True)
        mine = (column >= first) & (column < first + own_rows)
        rank = jnp.sum(jnp.where((down < across) & mine, 1, 0), axis=0, keepdims=True)
        held = (row >= first) & (row < first + own_rows)
        slot = jnp.where(held, ring(me - j, total) * cap + rank, -1)
        to_slot = (iota((slots, readers), 0) == slot).astype(jnp.float32).astype(jnp.bfloat16)
        from_row = (iota((readers, own_rows), 1) + first == column).astype(jnp.float32).astype(jnp.bfloat16)
        chosen = chosen + dot(to_slot, from_row, NN)
    out[:, width:] = digits[...]
    out[:, :width] = dot(chosen.astype(jnp.bfloat16), states[...], NN).astype(jnp.bfloat16)


def slot_rows(asked, cap, slots, user_rows, half):
    total, readers = asked.shape
    me = lax.axis_index("shard")
    lane = iota((1, half), 1) // (half // readers)
    rows = []
    for j in range(total):
        source = ring(me - j, total)
        holders = [asked[j, r] // user_rows for r in range(readers)]
        row = jnp.zeros((1, half), jnp.int32)
        for r, holder in enumerate(holders):
            rank = jnp.int32(0)
            for earlier in holders[:r]:
                rank = rank + (earlier == holder).astype(jnp.int32)
            row = jnp.where(lane == r, ring(me - holder, total) * slots + source * cap + rank, row)
        rows.append(row)
    return rows


def turn_kernel(items_hbm, mats_hbm, states_hbm, ids_hbm, cands_hbm, rows32, rows16, mats, states, ids, digits, items, cands, sems):
    chunks = sems.shape[0] - 4
    wide = items.shape[1] // chunks
    item_fetches = [
        pltpu.make_async_copy(items_hbm.at[:, pl.ds(t * wide, wide)], items.at[:, pl.ds(t * wide, wide)], sems.at[t])
        for t in range(chunks)
    ]
    mats_fetch = pltpu.make_async_copy(mats_hbm, mats, sems.at[chunks])
    states_fetch = pltpu.make_async_copy(states_hbm, states, sems.at[chunks + 1])
    ids_fetch = pltpu.make_async_copy(ids_hbm, ids, sems.at[chunks + 2])
    cands_fetch = pltpu.make_async_copy(cands_hbm, cands, sems.at[chunks + 3])
    for copy in item_fetches + [mats_fetch, states_fetch, ids_fetch, cands_fetch]:
        copy.start()
    eye = (iota((LANES, LANES), 0) == iota((LANES, LANES), 1)).astype(jnp.bfloat16)
    for t in range(items.shape[1] // LANES):
        if t * LANES % wide == 0:
            item_fetches[t * LANES // wide].wait()
        turned = dot(eye, items[:, t * LANES:(t + 1) * LANES], NT)
        rows32[t * LANES:(t + 1) * LANES, :] = turned
        rows16[t * LANES:(t + 1) * LANES, :] = turned.astype(jnp.bfloat16)
    cands_fetch.wait()
    code = jnp.broadcast_to(cands[...], digits.shape)
    place = iota(digits.shape, 0)
    digit = jnp.where(place == 0, code >> CODE_BITS, jnp.where(place == 1, code & ((1 << CODE_BITS) - 1), 0))
    digits[...] = digit.astype(jnp.float32).astype(jnp.bfloat16)
    ids_fetch.wait()
    mats_fetch.wait()
    states_fetch.wait()


def pair_kernel(total, cap, slots, user_rows, *refs):
    users, refs = refs[:total], refs[total:]
    fields_hbm, rows32, rows16, mats, picked, out, places, asked, fields, stacked, sems = refs
    del picked
    fields_fetch = pltpu.make_async_copy(fields_hbm, fields, sems.at[total])
    id_fetches = [pltpu.make_async_copy(users[j], asked.at[j], sems.at[j]) for j in range(total)]
    for copy in [fields_fetch] + id_fetches:
        copy.start()
    count = mats.shape[2]
    eye_pairs = (iota((count, count), 0) == iota((count, count), 1)).astype(jnp.bfloat16)
    side = (iota((count, LANES), 0) % 2 == 0) == (iota((count, LANES), 1) < K)
    for k in range(0, K, 2):
        twice = jnp.concatenate([mats[k], mats[k], mats[k + 1], mats[k + 1]], axis=0)
        turned = dot(eye_pairs, twice, NT)
        stacked[pl.ds(k, count, stride=PITCH), :] = jnp.where(side, turned[:, :LANES], 0.0)
        stacked[pl.ds(k + 1, count, stride=PITCH), :] = jnp.where(side, turned[:, LANES:], 0.0)
    fields_fetch.wait()

    def two(step, total):
        first = step * 2
        lefts, rights, mults = [], [], []
        for p in (first, first + 1):
            a = pl.multiple_of(fields[0, p] * K, K)
            b = pl.multiple_of(fields[1, p] * K, K)
            lefts.append(stacked[pl.ds(pl.multiple_of(p * PITCH, 8), K), :].astype(jnp.bfloat16))
            rights.append(rows16[pl.ds(b, K), :])
            mults.append(rows32[pl.ds(a, K), :])
        moved = dot(jnp.concatenate(lefts, axis=0), jnp.concatenate(rights, axis=0), NN)
        return total + moved * jnp.concatenate(mults, axis=0)

    sums = lax.fori_loop(0, count // 2, two, jnp.zeros((2 * K, rows32.shape[1]), jnp.float32), unroll=16)
    out[...] = jnp.sum(sums, axis=0, keepdims=True)
    for copy in id_fetches:
        copy.wait()
    for j, row in enumerate(slot_rows(asked, cap, slots, user_rows, places.shape[1])):
        places[j:j + 1, :] = row


def thirds(x):
    high = x.astype(jnp.bfloat16)
    rest = x - high.astype(jnp.float32)
    middle = rest.astype(jnp.bfloat16)
    return high, middle, (rest - middle.astype(jnp.float32)).astype(jnp.bfloat16)


def score_kernel(total, planes, parts, *refs):
    states, refs = refs[:1] + refs[total - 1:0:-1], refs[total:]
    items, refs = refs[:planes], refs[planes:]
    places, pairs, refs = refs[0], refs[1:1 + planes * parts], refs[1 + planes * parts:]
    outs, (wanted, cands, linear) = refs[:total], refs[total:]
    slots = states[0].shape[0]
    own_rows, width = items[0].shape
    me = lax.axis_index("shard")
    plane = lax.axis_index("cache")
    count = total * slots
    for j in range(total):
        wanted[j * slots:(j + 1) * slots, :] = states[j][:, :width]
        digits = states[j][:, width:].astype(jnp.float32)
        place = iota(digits.shape, 0)
        weight = jnp.where(place == 0, float(1 << CODE_BITS), jnp.where(place == 1, 1.0, 0.0))
        cands[j:j + 1, :] = jnp.sum(digits * weight, axis=0, keepdims=True).astype(jnp.int32)
    eye = iota((own_rows, own_rows), 0) == iota((own_rows, own_rows), 1)
    ids, columns = [], []
    for q in range(planes):
        at = ring(plane - q, planes)
        scores = dot(items[q][...], wanted[...], NT)
        for t, part in enumerate(thirds(scores)):
            linear[q * own_rows:(q + 1) * own_rows, t * count:(t + 1) * count] = part
        row = sum(pairs[q * parts + h][...] for h in range(parts))
        columns.append(jnp.sum(jnp.where(eye, row, 0.0), axis=1, keepdims=True))
        ids.append(iota((own_rows, 1), 0) + (me * planes + at) * own_rows)
    pair_column = jnp.concatenate(columns, axis=0)
    item_ids = jnp.concatenate(ids, axis=0)
    for j in range(total):
        half = outs[j].shape[1]
        spread = (iota((count, half), 0) == places[j:j + 1, :]).astype(jnp.float32).astype(jnp.bfloat16)
        scores = dot(linear[...], jnp.concatenate([spread] * 3, axis=0), NN) + pair_column
        hit = item_ids == cands[j:j + 1, :]
        outs[j][...] = jnp.sum(jnp.where(hit, scores, 0.0), axis=0, keepdims=True)


def shift(x, axis, step):
    size = lax.axis_size(axis)
    return lax.ppermute(x, axis, [(s, (s + step) % size) for s in range(size)])


def body(cand_items, reader_users, item_table, user_states, pair_mats, pair_fields):
    total = lax.axis_size("shard")
    planes = lax.axis_size("cache")
    parts = lax.axis_size("pair")
    half = cand_items.shape[0]
    rows, width = item_table.shape
    readers = reader_users.shape[0]
    cap = 2 * ((readers + total - 1) // total)
    slots = -(-total * cap // 16) * 16
    count = pair_mats.shape[0]
    vmem = pl.BlockSpec(memory_space=pltpu.VMEM)
    hbm = pl.BlockSpec(memory_space=pltpu.HBM)
    anywhere = pl.BlockSpec(memory_space=pl.ANY)
    params = pltpu.CompilerParams(vmem_limit_bytes=VMEM_LIMIT)

    def in_hbm(x):
        return pltpu.with_memory_space_constraint(x, pltpu.HBM)

    with jax.named_scope("item_rows"):
        items = [item_table] + [shift(item_table, "cache", q) for q in range(1, planes)]

    with jax.named_scope("ids"):
        users = [in_hbm(reader_users)] + [shift(reader_users, "shard", j) for j in range(1, total)]

    with jax.named_scope("turn"):
        *turned, states_near, own_ids, digits = pl.pallas_call(
            turn_kernel,
            out_shape=(
                jax.ShapeDtypeStruct((width, rows), jnp.float32),
                jax.ShapeDtypeStruct((width, rows), jnp.bfloat16),
                jax.ShapeDtypeStruct((K, K, count), jnp.bfloat16),
                jax.ShapeDtypeStruct(user_states.shape, jnp.bfloat16),
                jax.ShapeDtypeStruct((1, readers), jnp.int32),
                jax.ShapeDtypeStruct((slots, half), jnp.bfloat16),
            ),
            in_specs=[hbm] * 5,
            out_specs=(vmem,) * 6,
            scratch_shapes=[
                pltpu.VMEM((rows, width), jnp.bfloat16),
                pltpu.VMEM((1, half), jnp.int32),
                pltpu.SemaphoreType.DMA((8,)),
            ],
            compiler_params=params,
            cost_estimate=pl.CostEstimate(flops=2 * rows * rows * width * 16, bytes_accessed=8 * 1024 * 1024, transcendentals=0),
        )(
            in_hbm(item_table),
            in_hbm(jnp.transpose(pair_mats, (1, 2, 0))),
            in_hbm(user_states),
            in_hbm(reader_users.reshape(1, readers)),
            in_hbm(cand_items.reshape(1, half)),
        )

    with jax.named_scope("states"):
        picked = pl.pallas_call(
            functools.partial(pick_kernel, total, cap),
            out_shape=jax.ShapeDtypeStruct((slots, width + half), jnp.bfloat16),
            in_specs=[vmem] * (total + 2),
            out_specs=vmem,
            compiler_params=params,
            cost_estimate=pl.CostEstimate(flops=2 * slots * rows * width, bytes_accessed=1024 * 1024, transcendentals=0),
        )(own_ids, *[ids.reshape(1, readers) for ids in users[1:]], digits, states_near)
        states = [picked] + [shift(picked, "shard", j) for j in range(1, total)]

    with jax.named_scope("pairs"):
        pair_parts, places = pl.pallas_call(
            functools.partial(pair_kernel, total, cap, slots, user_states.shape[0]),
            out_shape=(
                jax.ShapeDtypeStruct((1, rows), jnp.float32),
                jax.ShapeDtypeStruct((total, half), jnp.int32),
            ),
            in_specs=[anywhere] * total + [hbm, vmem, vmem, vmem, anywhere],
            out_specs=(vmem, vmem),
            scratch_shapes=[
                pltpu.SMEM((total, readers), jnp.int32),
                pltpu.SMEM((2, count), jnp.int32),
                pltpu.VMEM((count * PITCH, LANES), jnp.float32),
                pltpu.SemaphoreType.DMA((1 + total,)),
            ],
            compiler_params=params,
            cost_estimate=pl.CostEstimate(flops=2 * count * K * K * rows * 16, bytes_accessed=4 * 1024 * 1024, transcendentals=0),
        )(*users, in_hbm(pair_fields.T), *turned, picked)
        pair_scores = {(0, 0): pair_parts}
        for q, h in [(q, h) for q in range(planes - 1, -1, -1) for h in range(parts) if q or h]:
            perm = [
                (c * parts + d, (c + q) % planes * parts + (d + h) % parts) for c in range(planes) for d in range(parts)
            ]
            source, after = pair_parts, {1: 1, 2: 2}.get(len(pair_scores) - 1, 0)
            if after:
                source, states[after] = lax.optimization_barrier((pair_parts, states[after]))
            pair_scores[q, h] = lax.ppermute(source, ("cache", "pair"), perm)
        pair_scores = [pair_scores[q, h] for q in range(planes) for h in range(parts)]

    with jax.named_scope("scores"):
        outs = pl.pallas_call(
            functools.partial(score_kernel, total, planes, parts),
            out_shape=[jax.ShapeDtypeStruct((1, half), jnp.float32)] * total,
            in_specs=[vmem] * (total + planes + 1 + planes * parts),
            out_specs=[vmem] * total,
            scratch_shapes=[
                pltpu.VMEM((total * slots, width), jnp.bfloat16),
                pltpu.VMEM((-(-total // 8) * 8, half), jnp.int32),
                pltpu.VMEM((planes * rows, 3 * total * slots), jnp.bfloat16),
            ],
            compiler_params=params,
            cost_estimate=pl.CostEstimate(flops=2 * 64 * 256 * width, bytes_accessed=2 * 1024 * 1024, transcendentals=0),
        )(picked, *states[:0:-1], *items, places, *pair_scores)

    with jax.named_scope("back"):
        result = outs[0]
        for j in range(total - 1, 0, -1):
            result = result + shift(outs[j], "shard", -j)
    return result.reshape(half)


def solution(mesh):
    return jax.shard_map(
        body,
        mesh=mesh,
        in_specs=(
            P(("groups", "shard", "cache", "pair")),
            P(("groups", "shard", "cache", "pair")),
            P(("shard", "cache"), None),
            P(("groups", "shard"), None),
            P("pair", None, None),
            P("pair", None),
        ),
        out_specs=P(("groups", "shard", "cache", "pair")),
        check_vma=False,
    )
```

```python
import functools

import jax
import jax.numpy as jnp
from jax import lax
from jax.experimental import pallas as pl
from jax.experimental.pallas import tpu as pltpu
from jax.sharding import PartitionSpec as P

K = 64
LANES = 128
PITCH = 72
CODE_BITS = 7
VMEM_LIMIT = 40 * 1024 * 1024
NT = (((1,), (1,)), ((), ()))
NN = (((1,), (0,)), ((), ()))


def dot(a, b, dims, **kw):
    return lax.dot_general(a, b, dims, preferred_element_type=jnp.float32, **kw)


def iota(shape, dim):
    return lax.broadcasted_iota(jnp.int32, shape, dim)


def ring(index, size):
    return lax.rem(index + size, size)


def pick_kernel(total, cap, *refs):
    users, (digits, states, out) = refs[:total], refs[total:]
    own_rows, width = states.shape
    slots = out.shape[0]
    readers = users[0].shape[1]
    me = lax.axis_index("shard")
    first = me * own_rows
    across = iota((readers, readers), 1)
    down = iota((readers, readers), 0)
    chosen = jnp.zeros((slots, own_rows), jnp.float32)
    for j in range(total):
        row = users[j][...]
        column = jnp.sum(jnp.where(across == down, row, 0), axis=1, keepdims=True)
        mine = (column >= first) & (column < first + own_rows)
        rank = jnp.sum(jnp.where((down < across) & mine, 1, 0), axis=0, keepdims=True)
        held = (row >= first) & (row < first + own_rows)
        slot = jnp.where(held, ring(me - j, total) * cap + rank, -1)
        to_slot = (iota((slots, readers), 0) == slot).astype(jnp.float32).astype(jnp.bfloat16)
        from_row = (iota((readers, own_rows), 1) + first == column).astype(jnp.float32).astype(jnp.bfloat16)
        chosen = chosen + dot(to_slot, from_row, NN)
    out[:, width:] = digits[...]
    out[:, :width] = dot(chosen.astype(jnp.bfloat16), states[...], NN).astype(jnp.bfloat16)


def slot_rows(asked, cap, slots, user_rows, half):
    total, readers = asked.shape
    me = lax.axis_index("shard")
    lane = iota((1, half), 1) // (half // readers)
    rows = []
    for j in range(total):
        source = ring(me - j, total)
        holders = [asked[j, r] // user_rows for r in range(readers)]
        row = jnp.zeros((1, half), jnp.int32)
        for r, holder in enumerate(holders):
            rank = jnp.int32(0)
            for earlier in holders[:r]:
                rank = rank + (earlier == holder).astype(jnp.int32)
            row = jnp.where(lane == r, ring(me - holder, total) * slots + source * cap + rank, row)
        rows.append(row)
    return rows


def turn_kernel(items_hbm, mats_hbm, states_hbm, ids_hbm, cands_hbm, rows32, rows16, mats, states, ids, digits, items, cands, sems):
    chunks = sems.shape[0] - 4
    wide = items.shape[1] // chunks
    item_fetches = [
        pltpu.make_async_copy(items_hbm.at[:, pl.ds(t * wide, wide)], items.at[:, pl.ds(t * wide, wide)], sems.at[t])
        for t in range(chunks)
    ]
    mats_fetch = pltpu.make_async_copy(mats_hbm, mats, sems.at[chunks])
    states_fetch = pltpu.make_async_copy(states_hbm, states, sems.at[chunks + 1])
    ids_fetch = pltpu.make_async_copy(ids_hbm, ids, sems.at[chunks + 2])
    cands_fetch = pltpu.make_async_copy(cands_hbm, cands, sems.at[chunks + 3])
    for copy in item_fetches + [mats_fetch, states_fetch, ids_fetch, cands_fetch]:
        copy.start()
    eye = (iota((LANES, LANES), 0) == iota((LANES, LANES), 1)).astype(jnp.bfloat16)
    for t in range(items.shape[1] // LANES):
        if t * LANES % wide == 0:
            item_fetches[t * LANES // wide].wait()
        turned = dot(eye, items[:, t * LANES:(t + 1) * LANES], NT)
        rows32[t * LANES:(t + 1) * LANES, :] = turned
        rows16[t * LANES:(t + 1) * LANES, :] = turned.astype(jnp.bfloat16)
    cands_fetch.wait()
    code = jnp.broadcast_to(cands[...], digits.shape)
    place = iota(digits.shape, 0)
    digit = jnp.where(place == 0, code >> CODE_BITS, jnp.where(place == 1, code & ((1 << CODE_BITS) - 1), 0))
    digits[...] = digit.astype(jnp.float32).astype(jnp.bfloat16)
    ids_fetch.wait()
    mats_fetch.wait()
    states_fetch.wait()


def pair_kernel(total, cap, slots, user_rows, *refs):
    users, refs = refs[:total], refs[total:]
    fields_hbm, rows32, rows16, mats, picked, out, places, asked, fields, stacked, sems = refs
    del picked
    fields_fetch = pltpu.make_async_copy(fields_hbm, fields, sems.at[total])
    id_fetches = [pltpu.make_async_copy(users[j], asked.at[j], sems.at[j]) for j in range(total)]
    for copy in [fields_fetch] + id_fetches:
        copy.start()
    count = mats.shape[2]
    eye_pairs = (iota((count, count), 0) == iota((count, count), 1)).astype(jnp.bfloat16)
    side = (iota((count, LANES), 0) % 2 == 0) == (iota((count, LANES), 1) < K)
    for k in range(0, K, 2):
        twice = jnp.concatenate([mats[k], mats[k], mats[k + 1], mats[k + 1]], axis=0)
        turned = dot(eye_pairs, twice, NT)
        stacked[pl.ds(k, count, stride=PITCH), :] = jnp.where(side, turned[:, :LANES], 0.0)
        stacked[pl.ds(k + 1, count, stride=PITCH), :] = jnp.where(side, turned[:, LANES:], 0.0)
    fields_fetch.wait()

    def two(step, total):
        first = step * 2
        lefts, rights, mults = [], [], []
        for p in (first, first + 1):
            a = pl.multiple_of(fields[0, p] * K, K)
            b = pl.multiple_of(fields[1, p] * K, K)
            lefts.append(stacked[pl.ds(pl.multiple_of(p * PITCH, 8), K), :].astype(jnp.bfloat16))
            rights.append(rows16[pl.ds(b, K), :])
            mults.append(rows32[pl.ds(a, K), :])
        moved = dot(jnp.concatenate(lefts, axis=0), jnp.concatenate(rights, axis=0), NN)
        return total + moved * jnp.concatenate(mults, axis=0)

    sums = lax.fori_loop(0, count // 2, two, jnp.zeros((2 * K, rows32.shape[1]), jnp.float32), unroll=16)
    out[...] = jnp.sum(sums, axis=0, keepdims=True)
    for copy in id_fetches:
        copy.wait()
    for j, row in enumerate(slot_rows(asked, cap, slots, user_rows, places.shape[1])):
        places[j:j + 1, :] = row


def thirds(x):
    high = x.astype(jnp.bfloat16)
    rest = x - high.astype(jnp.float32)
    middle = rest.astype(jnp.bfloat16)
    return high, middle, (rest - middle.astype(jnp.float32)).astype(jnp.bfloat16)


def linear_kernel(total, planes, *refs):
    states, refs = refs[:total], refs[total:]
    items, (places, out, hits, wanted, linear) = refs[:planes], refs[planes:]
    slots = states[0].shape[0]
    own_rows, width = items[0].shape
    half = out.shape[1]
    me = lax.axis_index("shard")
    plane = lax.axis_index("cache")
    count = total * slots
    cands = []
    for j in range(total):
        wanted[j * slots:(j + 1) * slots, :] = states[j][:, :width]
        digits = states[j][:, width:].astype(jnp.float32)
        place = iota(digits.shape, 0)
        weight = jnp.where(place == 0, float(1 << CODE_BITS), jnp.where(place == 1, 1.0, 0.0))
        cands.append(jnp.sum(digits * weight, axis=0, keepdims=True).astype(jnp.int32))

    for q, rows in enumerate(items):
        for t, part in enumerate(thirds(dot(rows[...], wanted[...], NT))):
            linear[q * own_rows:(q + 1) * own_rows, t * count:(t + 1) * count] = part
    ids = [iota((own_rows, 1), 0) + (me * planes + ring(plane - q, planes)) * own_rows for q in range(planes)]
    item_ids = jnp.concatenate(ids, axis=0)
    for j in range(total):
        spread = (iota((count, half), 0) == places[j:j + 1, :]).astype(jnp.float32).astype(jnp.bfloat16)
        scores = dot(linear[...], jnp.concatenate([spread] * 3, axis=0), NN)
        hit = item_ids == cands[j]
        out[j:j + 1, :] = jnp.sum(jnp.where(hit, scores, 0.0), axis=0, keepdims=True)
        hits[:, j * half:(j + 1) * half] = hit.astype(jnp.float32).astype(jnp.bfloat16)


def score_kernel(total, planes, parts, *refs):
    pairs, (linear, hits), outs = refs[:planes * parts], refs[planes * parts:planes * parts + 2], refs[planes * parts + 2:]
    half = linear.shape[1]
    sums = [sum(pairs[q * parts + h][...] for h in range(parts)) for q in range(planes)]
    row = jnp.concatenate(sums, axis=1)
    pieces = jnp.zeros((16, row.shape[1]), jnp.float32)
    for t, part in enumerate(thirds(row)):
        pieces = jnp.where(iota(pieces.shape, 0) == t, part.astype(jnp.float32), pieces)
    added = jnp.sum(dot(pieces.astype(jnp.bfloat16), hits[...], NN), axis=0, keepdims=True)
    for j in range(total):
        outs[j][...] = linear[j:j + 1, :] + added[:, j * half:(j + 1) * half]


def shift(x, axis, step):
    size = lax.axis_size(axis)
    return lax.ppermute(x, axis, [(s, (s + step) % size) for s in range(size)])


def body(cand_items, reader_users, item_table, user_states, pair_mats, pair_fields):
    total = lax.axis_size("shard")
    planes = lax.axis_size("cache")
    parts = lax.axis_size("pair")
    half = cand_items.shape[0]
    rows, width = item_table.shape
    readers = reader_users.shape[0]
    cap = 2 * ((readers + total - 1) // total)
    slots = -(-total * cap // 16) * 16
    count = pair_mats.shape[0]
    vmem = pl.BlockSpec(memory_space=pltpu.VMEM)
    hbm = pl.BlockSpec(memory_space=pltpu.HBM)
    anywhere = pl.BlockSpec(memory_space=pl.ANY)
    params = pltpu.CompilerParams(vmem_limit_bytes=VMEM_LIMIT)

    def in_hbm(x):
        return pltpu.with_memory_space_constraint(x, pltpu.HBM)

    with jax.named_scope("item_rows"):
        items = [item_table] + [shift(item_table, "cache", q) for q in range(1, planes)]

    with jax.named_scope("ids"):
        users = [in_hbm(reader_users)] + [shift(reader_users, "shard", j) for j in range(1, total)]

    with jax.named_scope("turn"):
        *turned, states_near, own_ids, digits = pl.pallas_call(
            turn_kernel,
            out_shape=(
                jax.ShapeDtypeStruct((width, rows), jnp.float32),
                jax.ShapeDtypeStruct((width, rows), jnp.bfloat16),
                jax.ShapeDtypeStruct((K, K, count), jnp.bfloat16),
                jax.ShapeDtypeStruct(user_states.shape, jnp.bfloat16),
                jax.ShapeDtypeStruct((1, readers), jnp.int32),
                jax.ShapeDtypeStruct((slots, half), jnp.bfloat16),
            ),
            in_specs=[hbm] * 5,
            out_specs=(vmem,) * 6,
            scratch_shapes=[
                pltpu.VMEM((rows, width), jnp.bfloat16),
                pltpu.VMEM((1, half), jnp.int32),
                pltpu.SemaphoreType.DMA((8,)),
            ],
            compiler_params=params,
            cost_estimate=pl.CostEstimate(flops=2 * rows * rows * width * 16, bytes_accessed=8 * 1024 * 1024, transcendentals=0),
        )(
            in_hbm(item_table),
            in_hbm(jnp.transpose(pair_mats, (1, 2, 0))),
            in_hbm(user_states),
            in_hbm(reader_users.reshape(1, readers)),
            in_hbm(cand_items.reshape(1, half)),
        )

    with jax.named_scope("states"):
        picked = pl.pallas_call(
            functools.partial(pick_kernel, total, cap),
            out_shape=jax.ShapeDtypeStruct((slots, width + half), jnp.bfloat16),
            in_specs=[vmem] * (total + 2),
            out_specs=vmem,
            compiler_params=params,
            cost_estimate=pl.CostEstimate(flops=2 * slots * rows * width, bytes_accessed=1024 * 1024, transcendentals=0),
        )(own_ids, *[ids.reshape(1, readers) for ids in users[1:]], digits, states_near)
        states = [picked] + [shift(picked, "shard", j) for j in range(1, total)]

    with jax.named_scope("pairs"):
        pair_parts, places = pl.pallas_call(
            functools.partial(pair_kernel, total, cap, slots, user_states.shape[0]),
            out_shape=(
                jax.ShapeDtypeStruct((1, rows), jnp.float32),
                jax.ShapeDtypeStruct((total, half), jnp.int32),
            ),
            in_specs=[anywhere] * total + [hbm, vmem, vmem, vmem, anywhere],
            out_specs=(vmem, vmem),
            scratch_shapes=[
                pltpu.SMEM((total, readers), jnp.int32),
                pltpu.SMEM((2, count), jnp.int32),
                pltpu.VMEM((count * PITCH, LANES), jnp.float32),
                pltpu.SemaphoreType.DMA((1 + total,)),
            ],
            compiler_params=params,
            cost_estimate=pl.CostEstimate(flops=2 * count * K * K * rows * 16, bytes_accessed=4 * 1024 * 1024, transcendentals=0),
        )(*users, in_hbm(pair_fields.T), *turned, picked)
        pair_scores = {(0, 0): pair_parts}
        steps = [(q, h) for q in range(planes - 1, -1, -1) for h in range(parts) if q or h]
        for q, h in sorted(steps, key=lambda step: bool(step[0] and step[1])):
            perm = [
                (c * parts + d, (c + q) % planes * parts + (d + h) % parts) for c in range(planes) for d in range(parts)
            ]
            source, after = pair_parts, {1: 2, 2: 1}.get(len(pair_scores) - 1, 0)
            if after:
                source, states[after] = lax.optimization_barrier((pair_parts, states[after]))
            pair_scores[q, h] = lax.ppermute(source, ("cache", "pair"), perm)
        pair_scores = [pair_scores[q, h] for q in range(planes) for h in range(parts)]

    with jax.named_scope("scores"):
        linear, hits = pl.pallas_call(
            functools.partial(linear_kernel, total, planes),
            out_shape=(
                jax.ShapeDtypeStruct((total, half), jnp.float32),
                jax.ShapeDtypeStruct((planes * rows, total * half), jnp.bfloat16),
            ),
            in_specs=[vmem] * (total + len(items) + 1),
            out_specs=(vmem, vmem),
            scratch_shapes=[
                pltpu.VMEM((total * slots, width), jnp.bfloat16),
                pltpu.VMEM((planes * rows, 3 * total * slots), jnp.bfloat16),
            ],
            compiler_params=params,
            cost_estimate=pl.CostEstimate(flops=2 * 64 * 256 * width, bytes_accessed=2 * 1024 * 1024, transcendentals=0),
        )(*states, *items, places)
        outs = pl.pallas_call(
            functools.partial(score_kernel, total, planes, parts),
            out_shape=[jax.ShapeDtypeStruct((1, half), jnp.float32)] * total,
            in_specs=[vmem] * (planes * parts + 2),
            out_specs=[vmem] * total,
            compiler_params=params,
            cost_estimate=pl.CostEstimate(flops=2 * 16 * 256 * 512, bytes_accessed=512 * 1024, transcendentals=0),
        )(*pair_scores, linear, hits)

    with jax.named_scope("back"):
        result = outs[0]
        for j in range(1, total):
            result = result + shift(outs[j], "shard", -j)
    return result.reshape(half)


def solution(mesh):
    return jax.shard_map(
        body,
        mesh=mesh,
        in_specs=(
            P(("groups", "shard", "cache", "pair")),
            P(("groups", "shard", "cache", "pair")),
            P(("shard", "cache"), None),
            P(("groups", "shard"), None),
            P("pair", None, None),
            P("pair", None),
        ),
        out_specs=P(("groups", "shard", "cache", "pair")),
        check_vma=False,
    )
```

```python
import functools

import jax
import jax.numpy as jnp
from jax import lax
from jax.experimental import pallas as pl
from jax.experimental.pallas import tpu as pltpu
from jax.sharding import PartitionSpec as P

K = 64
LANES = 128
PITCH = 72
CODE_BITS = 7
VMEM_LIMIT = 40 * 1024 * 1024
NT = (((1,), (1,)), ((), ()))
NN = (((1,), (0,)), ((), ()))


def dot(a, b, dims, **kw):
    return lax.dot_general(a, b, dims, preferred_element_type=jnp.float32, **kw)


def iota(shape, dim):
    return lax.broadcasted_iota(jnp.int32, shape, dim)


def ring(index, size):
    return lax.rem(index + size, size)


def pick_kernel(total, cap, *refs):
    users, (digits, states, out) = refs[:total], refs[total:]
    own_rows, width = states.shape
    slots = out.shape[0]
    readers = users[0].shape[1]
    me = lax.axis_index("shard")
    first = me * own_rows
    across = iota((readers, readers), 1)
    down = iota((readers, readers), 0)
    chosen = jnp.zeros((slots, own_rows), jnp.float32)
    for j in range(total):
        row = users[j][...]
        column = jnp.sum(jnp.where(across == down, row, 0), axis=1, keepdims=True)
        mine = (column >= first) & (column < first + own_rows)
        rank = jnp.sum(jnp.where((down < across) & mine, 1, 0), axis=0, keepdims=True)
        held = (row >= first) & (row < first + own_rows)
        slot = jnp.where(held, ring(me - j, total) * cap + rank, -1)
        to_slot = (iota((slots, readers), 0) == slot).astype(jnp.float32).astype(jnp.bfloat16)
        from_row = (iota((readers, own_rows), 1) + first == column).astype(jnp.float32).astype(jnp.bfloat16)
        chosen = chosen + dot(to_slot, from_row, NN)
    out[:, width:] = digits[...]
    out[:, :width] = dot(chosen.astype(jnp.bfloat16), states[...], NN).astype(jnp.bfloat16)


def slot_rows(asked, cap, slots, user_rows, half):
    total, readers = asked.shape
    me = lax.axis_index("shard")
    lane = iota((1, half), 1) // (half // readers)
    rows = []
    for j in range(total):
        source = ring(me - j, total)
        holders = [asked[j, r] // user_rows for r in range(readers)]
        row = jnp.zeros((1, half), jnp.int32)
        for r, holder in enumerate(holders):
            rank = jnp.int32(0)
            for earlier in holders[:r]:
                rank = rank + (earlier == holder).astype(jnp.int32)
            row = jnp.where(lane == r, ring(me - holder, total) * slots + source * cap + rank, row)
        rows.append(row)
    return rows


def turn_kernel(items_hbm, mats_hbm, states_hbm, ids_hbm, cands_hbm, rows32, rows16, mats, states, ids, digits, items, cands, sems):
    chunks = sems.shape[0] - 4
    wide = items.shape[1] // chunks
    item_fetches = [
        pltpu.make_async_copy(items_hbm.at[:, pl.ds(t * wide, wide)], items.at[:, pl.ds(t * wide, wide)], sems.at[t])
        for t in range(chunks)
    ]
    mats_fetch = pltpu.make_async_copy(mats_hbm, mats, sems.at[chunks])
    states_fetch = pltpu.make_async_copy(states_hbm, states, sems.at[chunks + 1])
    ids_fetch = pltpu.make_async_copy(ids_hbm, ids, sems.at[chunks + 2])
    cands_fetch = pltpu.make_async_copy(cands_hbm, cands, sems.at[chunks + 3])
    for copy in item_fetches + [mats_fetch, states_fetch, ids_fetch, cands_fetch]:
        copy.start()
    eye = (iota((LANES, LANES), 0) == iota((LANES, LANES), 1)).astype(jnp.bfloat16)
    for t in range(items.shape[1] // LANES):
        if t * LANES % wide == 0:
            item_fetches[t * LANES // wide].wait()
        turned = dot(eye, items[:, t * LANES:(t + 1) * LANES], NT)
        rows32[t * LANES:(t + 1) * LANES, :] = turned
        rows16[t * LANES:(t + 1) * LANES, :] = turned.astype(jnp.bfloat16)
    cands_fetch.wait()
    code = jnp.broadcast_to(cands[...], digits.shape)
    place = iota(digits.shape, 0)
    digit = jnp.where(place == 0, code >> CODE_BITS, jnp.where(place == 1, code & ((1 << CODE_BITS) - 1), 0))
    digits[...] = digit.astype(jnp.float32).astype(jnp.bfloat16)
    ids_fetch.wait()
    mats_fetch.wait()
    states_fetch.wait()


def pair_kernel(total, cap, slots, user_rows, *refs):
    users, refs = refs[:total], refs[total:]
    fields_hbm, rows32, rows16, mats, picked, out, places, asked, fields, stacked, sems = refs
    del picked
    fields_fetch = pltpu.make_async_copy(fields_hbm, fields, sems.at[total])
    id_fetches = [pltpu.make_async_copy(users[j], asked.at[j], sems.at[j]) for j in range(total)]
    for copy in [fields_fetch] + id_fetches:
        copy.start()
    count = mats.shape[2]
    eye_pairs = (iota((count, count), 0) == iota((count, count), 1)).astype(jnp.bfloat16)
    side = (iota((count, LANES), 0) % 2 == 0) == (iota((count, LANES), 1) < K)
    for k in range(0, K, 2):
        twice = jnp.concatenate([mats[k], mats[k], mats[k + 1], mats[k + 1]], axis=0)
        turned = dot(eye_pairs, twice, NT)
        stacked[pl.ds(k, count, stride=PITCH), :] = jnp.where(side, turned[:, :LANES], 0.0)
        stacked[pl.ds(k + 1, count, stride=PITCH), :] = jnp.where(side, turned[:, LANES:], 0.0)
    fields_fetch.wait()

    def two(step, total):
        first = step * 2
        lefts, rights, mults = [], [], []
        for p in (first, first + 1):
            a = pl.multiple_of(fields[0, p] * K, K)
            b = pl.multiple_of(fields[1, p] * K, K)
            lefts.append(stacked[pl.ds(pl.multiple_of(p * PITCH, 8), K), :].astype(jnp.bfloat16))
            rights.append(rows16[pl.ds(b, K), :])
            mults.append(rows32[pl.ds(a, K), :])
        moved = dot(jnp.concatenate(lefts, axis=0), jnp.concatenate(rights, axis=0), NN)
        return total + moved * jnp.concatenate(mults, axis=0)

    sums = lax.fori_loop(0, count // 2, two, jnp.zeros((2 * K, rows32.shape[1]), jnp.float32), unroll=16)
    out[...] = jnp.sum(sums, axis=0, keepdims=True)
    for copy in id_fetches:
        copy.wait()
    for j, row in enumerate(slot_rows(asked, cap, slots, user_rows, places.shape[1])):
        places[j:j + 1, :] = row


def thirds(x):
    high = x.astype(jnp.bfloat16)
    rest = x - high.astype(jnp.float32)
    middle = rest.astype(jnp.bfloat16)
    return high, middle, (rest - middle.astype(jnp.float32)).astype(jnp.bfloat16)


def linear_kernel(total, planes, parts, *refs):
    states, refs = refs[:total], refs[total:]
    own_items, refs = refs[0], refs[1:]
    crossed, refs = refs[:(planes - 1) * parts], refs[(planes - 1) * parts:]
    places, out, hits, wanted, linear = refs
    slots = states[0].shape[0]
    own_rows, width = own_items.shape
    half = out.shape[1]
    me = lax.axis_index("shard")
    plane = lax.axis_index("cache")
    core = lax.axis_index("pair")
    count = total * slots
    cands = []
    for j in range(total):
        wanted[j * slots:(j + 1) * slots, :] = states[j][:, :width]
        digits = states[j][:, width:].astype(jnp.float32)
        place = iota(digits.shape, 0)
        weight = jnp.where(place == 0, float(1 << CODE_BITS), jnp.where(place == 1, 1.0, 0.0))
        cands.append(jnp.sum(digits * weight, axis=0, keepdims=True).astype(jnp.int32))

    def fill(q, rows):
        for t, part in enumerate(thirds(dot(rows[...], wanted[...], NT))):
            linear[q * own_rows:(q + 1) * own_rows, t * count:(t + 1) * count] = part

    fill(0, own_items)
    for h in range(parts):
        @pl.when(core == h)
        def _():
            for q in range(1, planes):
                fill(q, crossed[(q - 1) * parts + h])

    ids = [iota((own_rows, 1), 0) + (me * planes + ring(plane - q, planes)) * own_rows for q in range(planes)]
    item_ids = jnp.concatenate(ids, axis=0)
    for j in range(total):
        spread = (iota((count, half), 0) == places[j:j + 1, :]).astype(jnp.float32).astype(jnp.bfloat16)
        scores = dot(linear[...], jnp.concatenate([spread] * 3, axis=0), NN)
        hit = item_ids == cands[j]
        out[j:j + 1, :] = jnp.sum(jnp.where(hit, scores, 0.0), axis=0, keepdims=True)
        hits[:, j * half:(j + 1) * half] = hit.astype(jnp.float32).astype(jnp.bfloat16)


def score_kernel(total, planes, parts, *refs):
    pairs, (linear, hits), outs = refs[:planes * parts], refs[planes * parts:planes * parts + 2], refs[planes * parts + 2:]
    half = linear.shape[1]
    sums = [sum(pairs[q * parts + h][...] for h in range(parts)) for q in range(planes)]
    row = jnp.concatenate(sums, axis=1)
    pieces = jnp.zeros((16, row.shape[1]), jnp.float32)
    for t, part in enumerate(thirds(row)):
        pieces = jnp.where(iota(pieces.shape, 0) == t, part.astype(jnp.float32), pieces)
    added = jnp.sum(dot(pieces.astype(jnp.bfloat16), hits[...], NN), axis=0, keepdims=True)
    for j in range(total):
        outs[j][...] = linear[j:j + 1, :] + added[:, j * half:(j + 1) * half]


def shift(x, axis, step):
    size = lax.axis_size(axis)
    return lax.ppermute(x, axis, [(s, (s + step) % size) for s in range(size)])


def body(cand_items, reader_users, item_table, user_states, pair_mats, pair_fields):
    total = lax.axis_size("shard")
    planes = lax.axis_size("cache")
    parts = lax.axis_size("pair")
    half = cand_items.shape[0]
    rows, width = item_table.shape
    readers = reader_users.shape[0]
    cap = 2 * ((readers + total - 1) // total)
    slots = -(-total * cap // 16) * 16
    count = pair_mats.shape[0]
    vmem = pl.BlockSpec(memory_space=pltpu.VMEM)
    hbm = pl.BlockSpec(memory_space=pltpu.HBM)
    anywhere = pl.BlockSpec(memory_space=pl.ANY)
    params = pltpu.CompilerParams(vmem_limit_bytes=VMEM_LIMIT)

    def in_hbm(x):
        return pltpu.with_memory_space_constraint(x, pltpu.HBM)

    with jax.named_scope("item_rows"):
        items = [item_table]
        for q in range(1, planes):
            perm = [(c * parts, (c + q) % planes * parts) for c in range(planes)]
            items.append(lax.ppermute(item_table, ("cache", "pair"), perm))

    with jax.named_scope("ids"):
        users = [in_hbm(reader_users)] + [shift(reader_users, "shard", j) for j in range(1, total)]

    with jax.named_scope("turn"):
        *turned, states_near, own_ids, digits = pl.pallas_call(
            turn_kernel,
            out_shape=(
                jax.ShapeDtypeStruct((width, rows), jnp.float32),
                jax.ShapeDtypeStruct((width, rows), jnp.bfloat16),
                jax.ShapeDtypeStruct((K, K, count), jnp.bfloat16),
                jax.ShapeDtypeStruct(user_states.shape, jnp.bfloat16),
                jax.ShapeDtypeStruct((1, readers), jnp.int32),
                jax.ShapeDtypeStruct((slots, half), jnp.bfloat16),
            ),
            in_specs=[hbm] * 5,
            out_specs=(vmem,) * 6,
            scratch_shapes=[
                pltpu.VMEM((rows, width), jnp.bfloat16),
                pltpu.VMEM((1, half), jnp.int32),
                pltpu.SemaphoreType.DMA((8,)),
            ],
            compiler_params=params,
            cost_estimate=pl.CostEstimate(flops=2 * rows * rows * width * 16, bytes_accessed=8 * 1024 * 1024, transcendentals=0),
        )(
            in_hbm(item_table),
            in_hbm(jnp.transpose(pair_mats, (1, 2, 0))),
            in_hbm(user_states),
            in_hbm(reader_users.reshape(1, readers)),
            in_hbm(cand_items.reshape(1, half)),
        )

    with jax.named_scope("states"):
        picked = pl.pallas_call(
            functools.partial(pick_kernel, total, cap),
            out_shape=jax.ShapeDtypeStruct((slots, width + half), jnp.bfloat16),
            in_specs=[vmem] * (total + 2),
            out_specs=vmem,
            compiler_params=params,
            cost_estimate=pl.CostEstimate(flops=2 * slots * rows * width, bytes_accessed=1024 * 1024, transcendentals=0),
        )(own_ids, *[ids.reshape(1, readers) for ids in users[1:]], digits, states_near)
        states = [picked] + [shift(picked, "shard", j) for j in range(1, total)]
        crossed, items = items[1:], items[:1]
        for rows_in in crossed:
            rows_in, _ = lax.optimization_barrier((rows_in, picked))
            items += [rows_in] + [lax.ppermute(rows_in, "pair", [(0, h)]) for h in range(1, parts)]

    with jax.named_scope("pairs"):
        pair_parts, places = pl.pallas_call(
            functools.partial(pair_kernel, total, cap, slots, user_states.shape[0]),
            out_shape=(
                jax.ShapeDtypeStruct((1, rows), jnp.float32),
                jax.ShapeDtypeStruct((total, half), jnp.int32),
            ),
            in_specs=[anywhere] * total + [hbm, vmem, vmem, vmem, anywhere],
            out_specs=(vmem, vmem),
            scratch_shapes=[
                pltpu.SMEM((total, readers), jnp.int32),
                pltpu.SMEM((2, count), jnp.int32),
                pltpu.VMEM((count * PITCH, LANES), jnp.float32),
                pltpu.SemaphoreType.DMA((1 + total,)),
            ],
            compiler_params=params,
            cost_estimate=pl.CostEstimate(flops=2 * count * K * K * rows * 16, bytes_accessed=4 * 1024 * 1024, transcendentals=0),
        )(*users, in_hbm(pair_fields.T), *turned, picked)
        pair_scores = {(0, 0): pair_parts}
        steps = [(q, h) for q in range(planes - 1, -1, -1) for h in range(parts) if q or h]
        for q, h in sorted(steps, key=lambda step: bool(step[0] and step[1])):
            perm = [
                (c * parts + d, (c + q) % planes * parts + (d + h) % parts) for c in range(planes) for d in range(parts)
            ]
            source, after = pair_parts, {1: 1, 2: 2}.get(len(pair_scores) - 1, 0)
            if after:
                source, states[after] = lax.optimization_barrier((pair_parts, states[after]))
            pair_scores[q, h] = lax.ppermute(source, ("cache", "pair"), perm)
        pair_scores = [pair_scores[q, h] for q in range(planes) for h in range(parts)]

    with jax.named_scope("scores"):
        linear, hits = pl.pallas_call(
            functools.partial(linear_kernel, total, planes, parts),
            out_shape=(
                jax.ShapeDtypeStruct((total, half), jnp.float32),
                jax.ShapeDtypeStruct((planes * rows, total * half), jnp.bfloat16),
            ),
            in_specs=[vmem] * (total + len(items) + 1),
            out_specs=(vmem, vmem),
            scratch_shapes=[
                pltpu.VMEM((total * slots, width), jnp.bfloat16),
                pltpu.VMEM((planes * rows, 3 * total * slots), jnp.bfloat16),
            ],
            compiler_params=params,
            cost_estimate=pl.CostEstimate(flops=2 * 64 * 256 * width, bytes_accessed=2 * 1024 * 1024, transcendentals=0),
        )(*states, *items, places)
        outs = pl.pallas_call(
            functools.partial(score_kernel, total, planes, parts),
            out_shape=[jax.ShapeDtypeStruct((1, half), jnp.float32)] * total,
            in_specs=[vmem] * (planes * parts + 2),
            out_specs=[vmem] * total,
            compiler_params=params,
            cost_estimate=pl.CostEstimate(flops=2 * 16 * 256 * 512, bytes_accessed=512 * 1024, transcendentals=0),
        )(*pair_scores, linear, hits)

    with jax.named_scope("back"):
        result = outs[0]
        for j in range(1, total):
            result = result + shift(outs[j], "shard", -j)
    return result.reshape(half)


def solution(mesh):
    return jax.shard_map(
        body,
        mesh=mesh,
        in_specs=(
            P(("groups", "shard", "cache", "pair")),
            P(("groups", "shard", "cache", "pair")),
            P(("shard", "cache"), None),
            P(("groups", "shard"), None),
            P("pair", None, None),
            P("pair", None),
        ),
        out_specs=P(("groups", "shard", "cache", "pair")),
        check_vma=False,
    )
```

```python
import functools

import jax
import jax.numpy as jnp
from jax import lax
from jax.experimental import pallas as pl
from jax.experimental.pallas import tpu as pltpu
from jax.sharding import PartitionSpec as P

K = 64
LANES = 128
PITCH = 72
CODE_BITS = 7
VMEM_LIMIT = 40 * 1024 * 1024
NT = (((1,), (1,)), ((), ()))
NN = (((1,), (0,)), ((), ()))


def dot(a, b, dims, **kw):
    return lax.dot_general(a, b, dims, preferred_element_type=jnp.float32, **kw)


def iota(shape, dim):
    return lax.broadcasted_iota(jnp.int32, shape, dim)


def ring(index, size):
    return lax.rem(index + size, size)


def pick_kernel(total, cap, *refs):
    users, (digits, states, out) = refs[:total], refs[total:]
    own_rows, width = states.shape
    slots = out.shape[0]
    readers = users[0].shape[1]
    me = lax.axis_index("shard")
    first = me * own_rows
    across = iota((readers, readers), 1)
    down = iota((readers, readers), 0)
    chosen = jnp.zeros((slots, own_rows), jnp.float32)
    for j in range(total):
        row = users[j][...]
        column = jnp.sum(jnp.where(across == down, row, 0), axis=1, keepdims=True)
        mine = (column >= first) & (column < first + own_rows)
        rank = jnp.sum(jnp.where((down < across) & mine, 1, 0), axis=0, keepdims=True)
        held = (row >= first) & (row < first + own_rows)
        slot = jnp.where(held, ring(me - j, total) * cap + rank, -1)
        to_slot = (iota((slots, readers), 0) == slot).astype(jnp.float32).astype(jnp.bfloat16)
        from_row = (iota((readers, own_rows), 1) + first == column).astype(jnp.float32).astype(jnp.bfloat16)
        chosen = chosen + dot(to_slot, from_row, NN)
    out[:, width:] = digits[...]
    out[:, :width] = dot(chosen.astype(jnp.bfloat16), states[...], NN).astype(jnp.bfloat16)


def slot_rows(asked, cap, slots, user_rows, half):
    total, readers = asked.shape
    me = lax.axis_index("shard")
    lane = iota((1, half), 1) // (half // readers)
    rows = []
    for j in range(total):
        source = ring(me - j, total)
        holders = [asked[j, r] // user_rows for r in range(readers)]
        row = jnp.zeros((1, half), jnp.int32)
        for r, holder in enumerate(holders):
            rank = jnp.int32(0)
            for earlier in holders[:r]:
                rank = rank + (earlier == holder).astype(jnp.int32)
            row = jnp.where(lane == r, ring(me - holder, total) * slots + source * cap + rank, row)
        rows.append(row)
    return rows


def turn_kernel(items_hbm, mats_hbm, states_hbm, ids_hbm, cands_hbm, rows32, rows16, mats, states, ids, digits, items, cands, sems):
    chunks = sems.shape[0] - 4
    wide = items.shape[1] // chunks
    item_fetches = [
        pltpu.make_async_copy(items_hbm.at[:, pl.ds(t * wide, wide)], items.at[:, pl.ds(t * wide, wide)], sems.at[t])
        for t in range(chunks)
    ]
    mats_fetch = pltpu.make_async_copy(mats_hbm, mats, sems.at[chunks])
    states_fetch = pltpu.make_async_copy(states_hbm, states, sems.at[chunks + 1])
    ids_fetch = pltpu.make_async_copy(ids_hbm, ids, sems.at[chunks + 2])
    cands_fetch = pltpu.make_async_copy(cands_hbm, cands, sems.at[chunks + 3])
    for copy in item_fetches + [mats_fetch, states_fetch, ids_fetch, cands_fetch]:
        copy.start()
    eye = (iota((LANES, LANES), 0) == iota((LANES, LANES), 1)).astype(jnp.bfloat16)
    for t in range(items.shape[1] // LANES):
        if t * LANES % wide == 0:
            item_fetches[t * LANES // wide].wait()
        turned = dot(eye, items[:, t * LANES:(t + 1) * LANES], NT)
        rows32[t * LANES:(t + 1) * LANES, :] = turned
        rows16[t * LANES:(t + 1) * LANES, :] = turned.astype(jnp.bfloat16)
    cands_fetch.wait()
    code = jnp.broadcast_to(cands[...], digits.shape)
    place = iota(digits.shape, 0)
    digit = jnp.where(place == 0, code >> CODE_BITS, jnp.where(place == 1, code & ((1 << CODE_BITS) - 1), 0))
    digits[...] = digit.astype(jnp.float32).astype(jnp.bfloat16)
    ids_fetch.wait()
    mats_fetch.wait()
    states_fetch.wait()


def pair_kernel(total, cap, slots, user_rows, *refs):
    users, refs = refs[:total], refs[total:]
    fields_hbm, rows32, rows16, mats, picked, out, places, asked, fields, stacked, sems = refs
    del picked
    fields_fetch = pltpu.make_async_copy(fields_hbm, fields, sems.at[total])
    id_fetches = [pltpu.make_async_copy(users[j], asked.at[j], sems.at[j]) for j in range(total)]
    for copy in [fields_fetch] + id_fetches:
        copy.start()
    count = mats.shape[2]
    eye_pairs = (iota((count, count), 0) == iota((count, count), 1)).astype(jnp.bfloat16)
    side = (iota((count, LANES), 0) % 2 == 0) == (iota((count, LANES), 1) < K)
    for k in range(0, K, 2):
        twice = jnp.concatenate([mats[k], mats[k], mats[k + 1], mats[k + 1]], axis=0)
        turned = dot(eye_pairs, twice, NT)
        stacked[pl.ds(k, count, stride=PITCH), :] = jnp.where(side, turned[:, :LANES], 0.0)
        stacked[pl.ds(k + 1, count, stride=PITCH), :] = jnp.where(side, turned[:, LANES:], 0.0)
    fields_fetch.wait()

    def two(step, total):
        first = step * 2
        lefts, rights, mults = [], [], []
        for p in (first, first + 1):
            a = pl.multiple_of(fields[0, p] * K, K)
            b = pl.multiple_of(fields[1, p] * K, K)
            lefts.append(stacked[pl.ds(pl.multiple_of(p * PITCH, 8), K), :].astype(jnp.bfloat16))
            rights.append(rows16[pl.ds(b, K), :])
            mults.append(rows32[pl.ds(a, K), :])
        moved = dot(jnp.concatenate(lefts, axis=0), jnp.concatenate(rights, axis=0), NN)
        return total + moved * jnp.concatenate(mults, axis=0)

    sums = lax.fori_loop(0, count // 2, two, jnp.zeros((2 * K, rows32.shape[1]), jnp.float32), unroll=16)
    out[...] = jnp.sum(sums, axis=0, keepdims=True)
    for copy in id_fetches:
        copy.wait()
    for j, row in enumerate(slot_rows(asked, cap, slots, user_rows, places.shape[1])):
        places[j:j + 1, :] = row


def thirds(x):
    high = x.astype(jnp.bfloat16)
    rest = x - high.astype(jnp.float32)
    middle = rest.astype(jnp.bfloat16)
    return high, middle, (rest - middle.astype(jnp.float32)).astype(jnp.bfloat16)


def linear_kernel(total, planes, *refs):
    states, refs = refs[:total], refs[total:]
    items, (places, out, hits, wanted, linear) = refs[:planes], refs[planes:]
    slots = states[0].shape[0]
    own_rows, width = items[0].shape
    half = out.shape[1]
    me = lax.axis_index("shard")
    plane = lax.axis_index("cache")
    count = total * slots
    cands = []
    for j in range(total):
        wanted[j * slots:(j + 1) * slots, :] = states[j][:, :width]
        digits = states[j][:, width:].astype(jnp.float32)
        place = iota(digits.shape, 0)
        weight = jnp.where(place == 0, float(1 << CODE_BITS), jnp.where(place == 1, 1.0, 0.0))
        cands.append(jnp.sum(digits * weight, axis=0, keepdims=True).astype(jnp.int32))

    for q, rows in enumerate(items):
        for t, part in enumerate(thirds(dot(rows[...], wanted[...], NT))):
            linear[q * own_rows:(q + 1) * own_rows, t * count:(t + 1) * count] = part
    ids = [iota((own_rows, 1), 0) + (me * planes + ring(plane - q, planes)) * own_rows for q in range(planes)]
    item_ids = jnp.concatenate(ids, axis=0)
    for j in range(total):
        spread = (iota((count, half), 0) == places[j:j + 1, :]).astype(jnp.float32).astype(jnp.bfloat16)
        scores = dot(linear[...], jnp.concatenate([spread] * 3, axis=0), NN)
        hit = item_ids == cands[j]
        out[j:j + 1, :] = jnp.sum(jnp.where(hit, scores, 0.0), axis=0, keepdims=True)
        hits[:, j * half:(j + 1) * half] = hit.astype(jnp.float32).astype(jnp.bfloat16)


def score_kernel(total, planes, parts, *refs):
    pairs, (linear, hits), outs = refs[:planes * parts], refs[planes * parts:planes * parts + 2], refs[planes * parts + 2:]
    half = linear.shape[1]
    sums = [sum(pairs[q * parts + h][...] for h in range(parts)) for q in range(planes)]
    row = jnp.concatenate(sums, axis=1)
    pieces = jnp.zeros((16, row.shape[1]), jnp.float32)
    for t, part in enumerate(thirds(row)):
        pieces = jnp.where(iota(pieces.shape, 0) == t, part.astype(jnp.float32), pieces)
    added = jnp.sum(dot(pieces.astype(jnp.bfloat16), hits[...], NN), axis=0, keepdims=True)
    for j in range(total):
        outs[j][...] = linear[j:j + 1, :] + added[:, j * half:(j + 1) * half]


def shift(x, axis, step):
    size = lax.axis_size(axis)
    return lax.ppermute(x, axis, [(s, (s + step) % size) for s in range(size)])


def body(cand_items, reader_users, item_table, user_states, pair_mats, pair_fields):
    total = lax.axis_size("shard")
    planes = lax.axis_size("cache")
    parts = lax.axis_size("pair")
    half = cand_items.shape[0]
    rows, width = item_table.shape
    readers = reader_users.shape[0]
    cap = 2 * ((readers + total - 1) // total)
    slots = -(-total * cap // 16) * 16
    count = pair_mats.shape[0]
    vmem = pl.BlockSpec(memory_space=pltpu.VMEM)
    hbm = pl.BlockSpec(memory_space=pltpu.HBM)
    anywhere = pl.BlockSpec(memory_space=pl.ANY)
    params = pltpu.CompilerParams(vmem_limit_bytes=VMEM_LIMIT)

    def in_hbm(x):
        return pltpu.with_memory_space_constraint(x, pltpu.HBM)

    with jax.named_scope("item_rows"):
        items = [item_table] + [shift(item_table, "cache", q) for q in range(1, planes)]

    with jax.named_scope("ids"):
        users = [in_hbm(reader_users)] + [shift(reader_users, "shard", j) for j in range(1, total)]

    with jax.named_scope("turn"):
        *turned, states_near, own_ids, digits = pl.pallas_call(
            turn_kernel,
            out_shape=(
                jax.ShapeDtypeStruct((width, rows), jnp.float32),
                jax.ShapeDtypeStruct((width, rows), jnp.bfloat16),
                jax.ShapeDtypeStruct((K, K, count), jnp.bfloat16),
                jax.ShapeDtypeStruct(user_states.shape, jnp.bfloat16),
                jax.ShapeDtypeStruct((1, readers), jnp.int32),
                jax.ShapeDtypeStruct((slots, half), jnp.bfloat16),
            ),
            in_specs=[hbm] * 5,
            out_specs=(vmem,) * 6,
            scratch_shapes=[
                pltpu.VMEM((rows, width), jnp.bfloat16),
                pltpu.VMEM((1, half), jnp.int32),
                pltpu.SemaphoreType.DMA((8,)),
            ],
            compiler_params=params,
            cost_estimate=pl.CostEstimate(flops=2 * rows * rows * width * 16, bytes_accessed=8 * 1024 * 1024, transcendentals=0),
        )(
            in_hbm(item_table),
            in_hbm(jnp.transpose(pair_mats, (1, 2, 0))),
            in_hbm(user_states),
            in_hbm(reader_users.reshape(1, readers)),
            in_hbm(cand_items.reshape(1, half)),
        )

    with jax.named_scope("states"):
        picked = pl.pallas_call(
            functools.partial(pick_kernel, total, cap),
            out_shape=jax.ShapeDtypeStruct((slots, width + half), jnp.bfloat16),
            in_specs=[vmem] * (total + 2),
            out_specs=vmem,
            compiler_params=params,
            cost_estimate=pl.CostEstimate(flops=2 * slots * rows * width, bytes_accessed=1024 * 1024, transcendentals=0),
        )(own_ids, *[ids.reshape(1, readers) for ids in users[1:]], digits, states_near)
        states = [picked] + [shift(picked, "shard", j) for j in range(1, total)]

    with jax.named_scope("pairs"):
        pair_parts, places = pl.pallas_call(
            functools.partial(pair_kernel, total, cap, slots, user_states.shape[0]),
            out_shape=(
                jax.ShapeDtypeStruct((1, rows), jnp.float32),
                jax.ShapeDtypeStruct((total, half), jnp.int32),
            ),
            in_specs=[anywhere] * total + [hbm, vmem, vmem, vmem, anywhere],
            out_specs=(vmem, vmem),
            scratch_shapes=[
                pltpu.SMEM((total, readers), jnp.int32),
                pltpu.SMEM((2, count), jnp.int32),
                pltpu.VMEM((count * PITCH, LANES), jnp.float32),
                pltpu.SemaphoreType.DMA((1 + total,)),
            ],
            compiler_params=params,
            cost_estimate=pl.CostEstimate(flops=2 * count * K * K * rows * 16, bytes_accessed=4 * 1024 * 1024, transcendentals=0),
        )(*users, in_hbm(pair_fields.T), *turned, picked)
        pair_scores = {(0, 0): pair_parts}
        steps = [(q, h) for q in range(planes - 1, -1, -1) for h in range(parts) if q or h]
        for q, h in sorted(steps, key=lambda step: bool(step[0] and step[1])):
            perm = [
                (c * parts + d, (c + q) % planes * parts + (d + h) % parts) for c in range(planes) for d in range(parts)
            ]
            source, after = pair_parts, {1: 1, 2: 2}.get(len(pair_scores) - 1, 0)
            if after:
                source, states[after] = lax.optimization_barrier((pair_parts, states[after]))
            pair_scores[q, h] = lax.ppermute(source, ("cache", "pair"), perm)
        pair_scores = [pair_scores[q, h] for q in range(planes) for h in range(parts)]

    with jax.named_scope("scores"):
        linear, hits = pl.pallas_call(
            functools.partial(linear_kernel, total, planes),
            out_shape=(
                jax.ShapeDtypeStruct((total, half), jnp.float32),
                jax.ShapeDtypeStruct((planes * rows, total * half), jnp.bfloat16),
            ),
            in_specs=[vmem] * (total + len(items) + 1),
            out_specs=(vmem, vmem),
            scratch_shapes=[
                pltpu.VMEM((total * slots, width), jnp.bfloat16),
                pltpu.VMEM((planes * rows, 3 * total * slots), jnp.bfloat16),
            ],
            compiler_params=params,
            cost_estimate=pl.CostEstimate(flops=2 * 64 * 256 * width, bytes_accessed=2 * 1024 * 1024, transcendentals=0),
        )(*states, *items, places)
        outs = pl.pallas_call(
            functools.partial(score_kernel, total, planes, parts),
            out_shape=[jax.ShapeDtypeStruct((1, half), jnp.float32)] * total,
            in_specs=[vmem] * (planes * parts + 2),
            out_specs=[vmem] * total,
            compiler_params=params,
            cost_estimate=pl.CostEstimate(flops=2 * 16 * 256 * 512, bytes_accessed=512 * 1024, transcendentals=0),
        )(*pair_scores, linear, hits)

    with jax.named_scope("back"):
        result = outs[0]
        for j in range(1, total):
            result = result + shift(outs[j], "shard", -j)
    return result.reshape(half)


def solution(mesh):
    return jax.shard_map(
        body,
        mesh=mesh,
        in_specs=(
            P(("groups", "shard", "cache", "pair")),
            P(("groups", "shard", "cache", "pair")),
            P(("shard", "cache"), None),
            P(("groups", "shard"), None),
            P("pair", None, None),
            P("pair", None),
        ),
        out_specs=P(("groups", "shard", "cache", "pair")),
        check_vma=False,
    )
```

```python
import functools

import jax
import jax.numpy as jnp
from jax import lax
from jax.experimental import pallas as pl
from jax.experimental.pallas import tpu as pltpu
from jax.sharding import PartitionSpec as P

K = 64
LANES = 128
PITCH = 72
CODE_BITS = 7
VMEM_LIMIT = 40 * 1024 * 1024
NT = (((1,), (1,)), ((), ()))
NN = (((1,), (0,)), ((), ()))


def dot(a, b, dims, **kw):
    return lax.dot_general(a, b, dims, preferred_element_type=jnp.float32, **kw)


def iota(shape, dim):
    return lax.broadcasted_iota(jnp.int32, shape, dim)


def ring(index, size):
    return lax.rem(index + size, size)


def pick_kernel(total, cap, *refs):
    users, (digits, states, out) = refs[:total], refs[total:]
    own_rows, width = states.shape
    slots = out.shape[0]
    readers = users[0].shape[1]
    me = lax.axis_index("shard")
    first = me * own_rows
    across = iota((readers, readers), 1)
    down = iota((readers, readers), 0)
    chosen = jnp.zeros((slots, own_rows), jnp.float32)
    for j in range(total):
        row = users[j][...]
        column = jnp.sum(jnp.where(across == down, row, 0), axis=1, keepdims=True)
        mine = (column >= first) & (column < first + own_rows)
        rank = jnp.sum(jnp.where((down < across) & mine, 1, 0), axis=0, keepdims=True)
        held = (row >= first) & (row < first + own_rows)
        slot = jnp.where(held, ring(me - j, total) * cap + rank, -1)
        to_slot = (iota((slots, readers), 0) == slot).astype(jnp.float32).astype(jnp.bfloat16)
        from_row = (iota((readers, own_rows), 1) + first == column).astype(jnp.float32).astype(jnp.bfloat16)
        chosen = chosen + dot(to_slot, from_row, NN)
    out[:, width:] = digits[...]
    out[:, :width] = dot(chosen.astype(jnp.bfloat16), states[...], NN).astype(jnp.bfloat16)


def slot_rows(asked, cap, slots, user_rows, half):
    total, readers = asked.shape
    me = lax.axis_index("shard")
    lane = iota((1, half), 1) // (half // readers)
    rows = []
    for j in range(total):
        source = ring(me - j, total)
        holders = [asked[j, r] // user_rows for r in range(readers)]
        row = jnp.zeros((1, half), jnp.int32)
        for r, holder in enumerate(holders):
            rank = jnp.int32(0)
            for earlier in holders[:r]:
                rank = rank + (earlier == holder).astype(jnp.int32)
            row = jnp.where(lane == r, ring(me - holder, total) * slots + source * cap + rank, row)
        rows.append(row)
    return rows


def turn_kernel(items_hbm, mats_hbm, states_hbm, ids_hbm, cands_hbm, rows32, rows16, mats, states, ids, digits, items, cands, sems):
    chunks = sems.shape[0] - 4
    wide = items.shape[1] // chunks
    item_fetches = [
        pltpu.make_async_copy(items_hbm.at[:, pl.ds(t * wide, wide)], items.at[:, pl.ds(t * wide, wide)], sems.at[t])
        for t in range(chunks)
    ]
    mats_fetch = pltpu.make_async_copy(mats_hbm, mats, sems.at[chunks])
    states_fetch = pltpu.make_async_copy(states_hbm, states, sems.at[chunks + 1])
    ids_fetch = pltpu.make_async_copy(ids_hbm, ids, sems.at[chunks + 2])
    cands_fetch = pltpu.make_async_copy(cands_hbm, cands, sems.at[chunks + 3])
    for copy in item_fetches + [mats_fetch, states_fetch, ids_fetch, cands_fetch]:
        copy.start()
    eye = (iota((LANES, LANES), 0) == iota((LANES, LANES), 1)).astype(jnp.bfloat16)
    for t in range(items.shape[1] // LANES):
        if t * LANES % wide == 0:
            item_fetches[t * LANES // wide].wait()
        turned = dot(eye, items[:, t * LANES:(t + 1) * LANES], NT)
        rows32[t * LANES:(t + 1) * LANES, :] = turned
        rows16[t * LANES:(t + 1) * LANES, :] = turned.astype(jnp.bfloat16)
    cands_fetch.wait()
    code = jnp.broadcast_to(cands[...], digits.shape)
    place = iota(digits.shape, 0)
    digit = jnp.where(place == 0, code >> CODE_BITS, jnp.where(place == 1, code & ((1 << CODE_BITS) - 1), 0))
    digits[...] = digit.astype(jnp.float32).astype(jnp.bfloat16)
    ids_fetch.wait()
    mats_fetch.wait()
    states_fetch.wait()


def pair_kernel(total, cap, slots, user_rows, *refs):
    users, refs = refs[:total], refs[total:]
    fields_hbm, rows32, rows16, mats, picked, out, places, asked, fields, stacked, sems = refs
    del picked
    fields_fetch = pltpu.make_async_copy(fields_hbm, fields, sems.at[total])
    id_fetches = [pltpu.make_async_copy(users[j], asked.at[j], sems.at[j]) for j in range(total)]
    for copy in [fields_fetch] + id_fetches:
        copy.start()
    pairs = mats.shape[2]
    steps = pairs // 2
    eye = (iota((steps, steps), 0) == iota((steps, steps), 1)).astype(jnp.bfloat16)
    for k in range(0, K, 2):
        sides = [mats[at, :, part * steps:(part + 1) * steps] for at in (k, k + 1) for part in range(2)]
        turned = dot(eye, jnp.concatenate(sides, axis=0), NT)
        stacked[pl.ds(k, steps, stride=PITCH), :] = turned[:, :LANES]
        stacked[pl.ds(k + 1, steps, stride=PITCH), :] = turned[:, LANES:]
    fields_fetch.wait()
    items = rows32.shape[1]
    blank = jnp.zeros((K, items), jnp.bfloat16)

    def two(p, total):
        fields_of = [(pl.multiple_of(fields[0, q] * K, K), pl.multiple_of(fields[1, q] * K, K)) for q in (p, p + steps)]
        left = stacked[pl.ds(pl.multiple_of(p * PITCH, 8), K), :].astype(jnp.bfloat16)
        first, second = [rows16[pl.ds(b, K), :] for _, b in fields_of]
        right = jnp.concatenate(
            [jnp.concatenate([first, blank], axis=1), jnp.concatenate([blank, second], axis=1)], axis=0
        )
        return total + dot(left, right, NN) * jnp.concatenate([rows32[pl.ds(a, K), :] for a, _ in fields_of], axis=1)

    sums = lax.fori_loop(0, steps, two, jnp.zeros((K, 2 * items), jnp.float32), unroll=16)
    line = jnp.sum(sums, axis=0, keepdims=True)
    out[...] = line[:, :items] + line[:, items:]
    for copy in id_fetches:
        copy.wait()
    for j, row in enumerate(slot_rows(asked, cap, slots, user_rows, places.shape[1])):
        places[j:j + 1, :] = row


def thirds(x):
    high = x.astype(jnp.bfloat16)
    rest = x - high.astype(jnp.float32)
    middle = rest.astype(jnp.bfloat16)
    return high, middle, (rest - middle.astype(jnp.float32)).astype(jnp.bfloat16)


def linear_kernel(total, planes, *refs):
    states, refs = refs[:total], refs[total:]
    items, (places, out, hits, wanted, linear) = refs[:planes], refs[planes:]
    slots = states[0].shape[0]
    own_rows, width = items[0].shape
    half = out.shape[1]
    me = lax.axis_index("shard")
    plane = lax.axis_index("cache")
    count = total * slots
    cands = []
    for j in range(total):
        wanted[j * slots:(j + 1) * slots, :] = states[j][:, :width]
        digits = states[j][:, width:].astype(jnp.float32)
        place = iota(digits.shape, 0)
        weight = jnp.where(place == 0, float(1 << CODE_BITS), jnp.where(place == 1, 1.0, 0.0))
        cands.append(jnp.sum(digits * weight, axis=0, keepdims=True).astype(jnp.int32))

    for q, rows in enumerate(items):
        for t, part in enumerate(thirds(dot(rows[...], wanted[...], NT))):
            linear[q * own_rows:(q + 1) * own_rows, t * count:(t + 1) * count] = part
    ids = [iota((own_rows, 1), 0) + (me * planes + ring(plane - q, planes)) * own_rows for q in range(planes)]
    item_ids = jnp.concatenate(ids, axis=0)
    for j in range(total):
        spread = (iota((count, half), 0) == places[j:j + 1, :]).astype(jnp.float32).astype(jnp.bfloat16)
        scores = dot(linear[...], jnp.concatenate([spread] * 3, axis=0), NN)
        hit = item_ids == cands[j]
        out[j:j + 1, :] = jnp.sum(jnp.where(hit, scores, 0.0), axis=0, keepdims=True)
        hits[:, j * half:(j + 1) * half] = hit.astype(jnp.float32).astype(jnp.bfloat16)


def score_kernel(total, planes, parts, *refs):
    pairs, (linear, hits), outs = refs[:planes * parts], refs[planes * parts:planes * parts + 2], refs[planes * parts + 2:]
    half = linear.shape[1]
    sums = [sum(pairs[q * parts + h][...] for h in range(parts)) for q in range(planes)]
    row = jnp.concatenate(sums, axis=1)
    pieces = jnp.zeros((16, row.shape[1]), jnp.float32)
    for t, part in enumerate(thirds(row)):
        pieces = jnp.where(iota(pieces.shape, 0) == t, part.astype(jnp.float32), pieces)
    added = jnp.sum(dot(pieces.astype(jnp.bfloat16), hits[...], NN), axis=0, keepdims=True)
    for j in range(total):
        outs[j][...] = linear[j:j + 1, :] + added[:, j * half:(j + 1) * half]


def shift(x, axis, step):
    size = lax.axis_size(axis)
    return lax.ppermute(x, axis, [(s, (s + step) % size) for s in range(size)])


def body(cand_items, reader_users, item_table, user_states, pair_mats, pair_fields):
    total = lax.axis_size("shard")
    planes = lax.axis_size("cache")
    parts = lax.axis_size("pair")
    half = cand_items.shape[0]
    rows, width = item_table.shape
    readers = reader_users.shape[0]
    cap = 2 * ((readers + total - 1) // total)
    slots = -(-total * cap // 16) * 16
    count = pair_mats.shape[0]
    vmem = pl.BlockSpec(memory_space=pltpu.VMEM)
    hbm = pl.BlockSpec(memory_space=pltpu.HBM)
    anywhere = pl.BlockSpec(memory_space=pl.ANY)
    params = pltpu.CompilerParams(vmem_limit_bytes=VMEM_LIMIT)

    def in_hbm(x):
        return pltpu.with_memory_space_constraint(x, pltpu.HBM)

    with jax.named_scope("item_rows"):
        items = [item_table] + [shift(item_table, "cache", q) for q in range(1, planes)]

    with jax.named_scope("ids"):
        users = [in_hbm(reader_users)] + [shift(reader_users, "shard", j) for j in range(1, total)]

    with jax.named_scope("turn"):
        *turned, states_near, own_ids, digits = pl.pallas_call(
            turn_kernel,
            out_shape=(
                jax.ShapeDtypeStruct((width, rows), jnp.float32),
                jax.ShapeDtypeStruct((width, rows), jnp.bfloat16),
                jax.ShapeDtypeStruct((K, K, count), jnp.bfloat16),
                jax.ShapeDtypeStruct(user_states.shape, jnp.bfloat16),
                jax.ShapeDtypeStruct((1, readers), jnp.int32),
                jax.ShapeDtypeStruct((slots, half), jnp.bfloat16),
            ),
            in_specs=[hbm] * 5,
            out_specs=(vmem,) * 6,
            scratch_shapes=[
                pltpu.VMEM((rows, width), jnp.bfloat16),
                pltpu.VMEM((1, half), jnp.int32),
                pltpu.SemaphoreType.DMA((8,)),
            ],
            compiler_params=params,
            cost_estimate=pl.CostEstimate(flops=2 * rows * rows * width * 16, bytes_accessed=8 * 1024 * 1024, transcendentals=0),
        )(
            in_hbm(item_table),
            in_hbm(jnp.transpose(pair_mats, (1, 2, 0))),
            in_hbm(user_states),
            in_hbm(reader_users.reshape(1, readers)),
            in_hbm(cand_items.reshape(1, half)),
        )

    with jax.named_scope("states"):
        picked = pl.pallas_call(
            functools.partial(pick_kernel, total, cap),
            out_shape=jax.ShapeDtypeStruct((slots, width + half), jnp.bfloat16),
            in_specs=[vmem] * (total + 2),
            out_specs=vmem,
            compiler_params=params,
            cost_estimate=pl.CostEstimate(flops=2 * slots * rows * width, bytes_accessed=1024 * 1024, transcendentals=0),
        )(own_ids, *[ids.reshape(1, readers) for ids in users[1:]], digits, states_near)
        states = [picked] + [shift(picked, "shard", j) for j in range(1, total)]

    with jax.named_scope("pairs"):
        pair_parts, places = pl.pallas_call(
            functools.partial(pair_kernel, total, cap, slots, user_states.shape[0]),
            out_shape=(
                jax.ShapeDtypeStruct((1, rows), jnp.float32),
                jax.ShapeDtypeStruct((total, half), jnp.int32),
            ),
            in_specs=[anywhere] * total + [hbm, vmem, vmem, vmem, anywhere],
            out_specs=(vmem, vmem),
            scratch_shapes=[
                pltpu.SMEM((total, readers), jnp.int32),
                pltpu.SMEM((2, count), jnp.int32),
                pltpu.VMEM((count // 2 * PITCH, LANES), jnp.float32),
                pltpu.SemaphoreType.DMA((1 + total,)),
            ],
            compiler_params=params,
            cost_estimate=pl.CostEstimate(flops=2 * count * K * K * rows * 16, bytes_accessed=4 * 1024 * 1024, transcendentals=0),
        )(*users, in_hbm(pair_fields.T), *turned, picked)
        pair_scores = {(0, 0): pair_parts}
        steps = [(q, h) for q in range(planes - 1, -1, -1) for h in range(parts) if q or h]
        for q, h in sorted(steps, key=lambda step: bool(step[0] and step[1])):
            perm = [
                (c * parts + d, (c + q) % planes * parts + (d + h) % parts) for c in range(planes) for d in range(parts)
            ]
            source, after = pair_parts, {1: 1, 2: 2}.get(len(pair_scores) - 1, 0)
            if after:
                source, states[after] = lax.optimization_barrier((pair_parts, states[after]))
            pair_scores[q, h] = lax.ppermute(source, ("cache", "pair"), perm)
        pair_scores = [pair_scores[q, h] for q in range(planes) for h in range(parts)]

    with jax.named_scope("scores"):
        linear, hits = pl.pallas_call(
            functools.partial(linear_kernel, total, planes),
            out_shape=(
                jax.ShapeDtypeStruct((total, half), jnp.float32),
                jax.ShapeDtypeStruct((planes * rows, total * half), jnp.bfloat16),
            ),
            in_specs=[vmem] * (total + len(items) + 1),
            out_specs=(vmem, vmem),
            scratch_shapes=[
                pltpu.VMEM((total * slots, width), jnp.bfloat16),
                pltpu.VMEM((planes * rows, 3 * total * slots), jnp.bfloat16),
            ],
            compiler_params=params,
            cost_estimate=pl.CostEstimate(flops=2 * 64 * 256 * width, bytes_accessed=2 * 1024 * 1024, transcendentals=0),
        )(*states, *items, places)
        outs = pl.pallas_call(
            functools.partial(score_kernel, total, planes, parts),
            out_shape=[jax.ShapeDtypeStruct((1, half), jnp.float32)] * total,
            in_specs=[vmem] * (planes * parts + 2),
            out_specs=[vmem] * total,
            compiler_params=params,
            cost_estimate=pl.CostEstimate(flops=2 * 16 * 256 * 512, bytes_accessed=512 * 1024, transcendentals=0),
        )(*pair_scores, linear, hits)

    with jax.named_scope("back"):
        result = outs[0]
        for j in range(1, total):
            result = result + shift(outs[j], "shard", -j)
    return result.reshape(half)


def solution(mesh):
    return jax.shard_map(
        body,
        mesh=mesh,
        in_specs=(
            P(("groups", "shard", "cache", "pair")),
            P(("groups", "shard", "cache", "pair")),
            P(("shard", "cache"), None),
            P(("groups", "shard"), None),
            P("pair", None, None),
            P("pair", None),
        ),
        out_specs=P(("groups", "shard", "cache", "pair")),
        check_vma=False,
    )
```

```python
import functools

import jax
import jax.numpy as jnp
from jax import lax
from jax.experimental import pallas as pl
from jax.experimental.pallas import tpu as pltpu
from jax.sharding import PartitionSpec as P

K = 64
LANES = 128
PITCH = 72
CODE_BITS = 7
VMEM_LIMIT = 40 * 1024 * 1024
NT = (((1,), (1,)), ((), ()))
NN = (((1,), (0,)), ((), ()))


def dot(a, b, dims, **kw):
    return lax.dot_general(a, b, dims, preferred_element_type=jnp.float32, **kw)


def iota(shape, dim):
    return lax.broadcasted_iota(jnp.int32, shape, dim)


def ring(index, size):
    return lax.rem(index + size, size)


def pick_kernel(total, cap, *refs):
    users, (digits, states, out) = refs[:total], refs[total:]
    own_rows, width = states.shape
    slots = out.shape[0]
    readers = users[0].shape[1]
    me = lax.axis_index("shard")
    first = me * own_rows
    across = iota((readers, readers), 1)
    down = iota((readers, readers), 0)
    chosen = jnp.zeros((slots, own_rows), jnp.float32)
    for j in range(total):
        row = users[j][...]
        column = jnp.sum(jnp.where(across == down, row, 0), axis=1, keepdims=True)
        mine = (column >= first) & (column < first + own_rows)
        rank = jnp.sum(jnp.where((down < across) & mine, 1, 0), axis=0, keepdims=True)
        held = (row >= first) & (row < first + own_rows)
        slot = jnp.where(held, ring(me - j, total) * cap + rank, -1)
        to_slot = (iota((slots, readers), 0) == slot).astype(jnp.float32).astype(jnp.bfloat16)
        from_row = (iota((readers, own_rows), 1) + first == column).astype(jnp.float32).astype(jnp.bfloat16)
        chosen = chosen + dot(to_slot, from_row, NN)
    out[:, width:] = digits[...]
    out[:, :width] = dot(chosen.astype(jnp.bfloat16), states[...], NN).astype(jnp.bfloat16)


def slot_rows(asked, cap, slots, user_rows, half):
    total, readers = asked.shape
    me = lax.axis_index("shard")
    lane = iota((1, half), 1) // (half // readers)
    rows = []
    for j in range(total):
        source = ring(me - j, total)
        holders = [asked[j, r] // user_rows for r in range(readers)]
        row = jnp.zeros((1, half), jnp.int32)
        for r, holder in enumerate(holders):
            rank = jnp.int32(0)
            for earlier in holders[:r]:
                rank = rank + (earlier == holder).astype(jnp.int32)
            row = jnp.where(lane == r, ring(me - holder, total) * slots + source * cap + rank, row)
        rows.append(row)
    return rows


def turn_kernel(items_hbm, mats_hbm, states_hbm, ids_hbm, cands_hbm, rows32, rows16, mats, states, ids, digits, items, cands, sems):
    chunks = sems.shape[0] - 4
    wide = items.shape[1] // chunks
    item_fetches = [
        pltpu.make_async_copy(items_hbm.at[:, pl.ds(t * wide, wide)], items.at[:, pl.ds(t * wide, wide)], sems.at[t])
        for t in range(chunks)
    ]
    mats_fetch = pltpu.make_async_copy(mats_hbm, mats, sems.at[chunks])
    states_fetch = pltpu.make_async_copy(states_hbm, states, sems.at[chunks + 1])
    ids_fetch = pltpu.make_async_copy(ids_hbm, ids, sems.at[chunks + 2])
    cands_fetch = pltpu.make_async_copy(cands_hbm, cands, sems.at[chunks + 3])
    for copy in item_fetches + [mats_fetch, states_fetch, ids_fetch, cands_fetch]:
        copy.start()
    eye = (iota((LANES, LANES), 0) == iota((LANES, LANES), 1)).astype(jnp.bfloat16)
    for t in range(items.shape[1] // LANES):
        if t * LANES % wide == 0:
            item_fetches[t * LANES // wide].wait()
        turned = dot(eye, items[:, t * LANES:(t + 1) * LANES], NT)
        rows32[t * LANES:(t + 1) * LANES, :] = turned
        rows16[t * LANES:(t + 1) * LANES, :] = turned.astype(jnp.bfloat16)
    cands_fetch.wait()
    code = jnp.broadcast_to(cands[...], digits.shape)
    place = iota(digits.shape, 0)
    digit = jnp.where(place == 0, code >> CODE_BITS, jnp.where(place == 1, code & ((1 << CODE_BITS) - 1), 0))
    digits[...] = digit.astype(jnp.float32).astype(jnp.bfloat16)
    ids_fetch.wait()
    mats_fetch.wait()
    states_fetch.wait()


def pair_kernel(total, cap, slots, user_rows, *refs):
    users, refs = refs[:total], refs[total:]
    fields_hbm, rows32, rows16, mats, picked, out, places, asked, fields, stacked, sems = refs
    del picked
    fields_fetch = pltpu.make_async_copy(fields_hbm, fields, sems.at[total])
    id_fetches = [pltpu.make_async_copy(users[j], asked.at[j], sems.at[j]) for j in range(total)]
    for copy in [fields_fetch] + id_fetches:
        copy.start()
    pairs = mats.shape[2]
    steps = pairs // 2
    eye = (iota((steps, steps), 0) == iota((steps, steps), 1)).astype(jnp.bfloat16)
    for k in range(0, K, 2):
        sides = [mats[at, :, part * steps:(part + 1) * steps] for at in (k, k + 1) for part in range(2)]
        turned = dot(eye, jnp.concatenate(sides, axis=0), NT)
        stacked[pl.ds(k, steps, stride=PITCH), :] = turned[:, :LANES]
        stacked[pl.ds(k + 1, steps, stride=PITCH), :] = turned[:, LANES:]
    fields_fetch.wait()
    items = rows32.shape[1]
    blank = jnp.zeros((K, items), jnp.bfloat16)

    def two(p, total):
        fields_of = [(pl.multiple_of(fields[0, q] * K, K), pl.multiple_of(fields[1, q] * K, K)) for q in (p, p + steps)]
        left = stacked[pl.ds(pl.multiple_of(p * PITCH, 8), K), :].astype(jnp.bfloat16)
        first, second = [rows16[pl.ds(b, K), :] for _, b in fields_of]
        right = jnp.concatenate(
            [jnp.concatenate([first, blank], axis=1), jnp.concatenate([blank, second], axis=1)], axis=0
        )
        return total + dot(left, right, NN) * jnp.concatenate([rows32[pl.ds(a, K), :] for a, _ in fields_of], axis=1)

    sums = lax.fori_loop(0, steps, two, jnp.zeros((K, 2 * items), jnp.float32), unroll=16)
    line = jnp.sum(sums, axis=0, keepdims=True)
    out[...] = line[:, :items] + line[:, items:]
    for copy in id_fetches:
        copy.wait()
    for j, row in enumerate(slot_rows(asked, cap, slots, user_rows, places.shape[1])):
        places[j:j + 1, :] = row


def thirds(x):
    high = x.astype(jnp.bfloat16)
    rest = x - high.astype(jnp.float32)
    middle = rest.astype(jnp.bfloat16)
    return high, middle, (rest - middle.astype(jnp.float32)).astype(jnp.bfloat16)


def linear_kernel(total, planes, *refs):
    states, refs = refs[:total], refs[total:]
    items, (places, out, hits, wanted, linear) = refs[:planes], refs[planes:]
    slots = states[0].shape[0]
    own_rows, width = items[0].shape
    half = out.shape[1]
    me = lax.axis_index("shard")
    plane = lax.axis_index("cache")
    count = total * slots
    cands = []
    for j in range(total):
        wanted[j * slots:(j + 1) * slots, :] = states[j][:, :width]
        digits = states[j][:, width:].astype(jnp.float32)
        place = iota(digits.shape, 0)
        weight = jnp.where(place == 0, float(1 << CODE_BITS), jnp.where(place == 1, 1.0, 0.0))
        cands.append(jnp.sum(digits * weight, axis=0, keepdims=True).astype(jnp.int32))

    for q, rows in enumerate(items):
        for t, part in enumerate(thirds(dot(rows[...], wanted[...], NT))):
            linear[q * own_rows:(q + 1) * own_rows, t * count:(t + 1) * count] = part
    ids = [iota((own_rows, 1), 0) + (me * planes + ring(plane - q, planes)) * own_rows for q in range(planes)]
    item_ids = jnp.concatenate(ids, axis=0)
    for j in range(total):
        spread = (iota((count, half), 0) == places[j:j + 1, :]).astype(jnp.float32).astype(jnp.bfloat16)
        scores = dot(linear[...], jnp.concatenate([spread] * 3, axis=0), NN)
        hit = item_ids == cands[j]
        out[j:j + 1, :] = jnp.sum(jnp.where(hit, scores, 0.0), axis=0, keepdims=True)
        hits[:, j * half:(j + 1) * half] = hit.astype(jnp.float32).astype(jnp.bfloat16)


def score_kernel(total, planes, parts, *refs):
    pairs, (linear, hits), outs = refs[:planes * parts], refs[planes * parts:planes * parts + 2], refs[planes * parts + 2:]
    half = linear.shape[1]
    sums = [sum(pairs[q * parts + h][...] for h in range(parts)) for q in range(planes)]
    row = jnp.concatenate(sums, axis=1)
    pieces = jnp.zeros((16, row.shape[1]), jnp.float32)
    for t, part in enumerate(thirds(row)):
        pieces = jnp.where(iota(pieces.shape, 0) == t, part.astype(jnp.float32), pieces)
    added = jnp.sum(dot(pieces.astype(jnp.bfloat16), hits[...], NN), axis=0, keepdims=True)
    for j in range(total):
        outs[j][...] = linear[j:j + 1, :] + added[:, j * half:(j + 1) * half]


def shift(x, axis, step):
    size = lax.axis_size(axis)
    return lax.ppermute(x, axis, [(s, (s + step) % size) for s in range(size)])


def body(cand_items, reader_users, item_table, user_states, pair_mats, pair_fields):
    total = lax.axis_size("shard")
    planes = lax.axis_size("cache")
    parts = lax.axis_size("pair")
    half = cand_items.shape[0]
    rows, width = item_table.shape
    readers = reader_users.shape[0]
    cap = 2 * ((readers + total - 1) // total)
    slots = -(-total * cap // 16) * 16
    count = pair_mats.shape[0]
    vmem = pl.BlockSpec(memory_space=pltpu.VMEM)
    hbm = pl.BlockSpec(memory_space=pltpu.HBM)
    anywhere = pl.BlockSpec(memory_space=pl.ANY)
    params = pltpu.CompilerParams(vmem_limit_bytes=VMEM_LIMIT)

    def in_hbm(x):
        return pltpu.with_memory_space_constraint(x, pltpu.HBM)

    with jax.named_scope("item_rows"):
        items = [item_table] + [shift(item_table, "cache", q) for q in range(1, planes)]

    with jax.named_scope("ids"):
        users = [in_hbm(reader_users)] + [shift(reader_users, "shard", j) for j in range(1, total)]

    with jax.named_scope("turn"):
        *turned, states_near, own_ids, digits = pl.pallas_call(
            turn_kernel,
            out_shape=(
                jax.ShapeDtypeStruct((width, rows), jnp.float32),
                jax.ShapeDtypeStruct((width, rows), jnp.bfloat16),
                jax.ShapeDtypeStruct((K, K, count), jnp.bfloat16),
                jax.ShapeDtypeStruct(user_states.shape, jnp.bfloat16),
                jax.ShapeDtypeStruct((1, readers), jnp.int32),
                jax.ShapeDtypeStruct((slots, half), jnp.bfloat16),
            ),
            in_specs=[hbm] * 5,
            out_specs=(vmem,) * 6,
            scratch_shapes=[
                pltpu.VMEM((rows, width), jnp.bfloat16),
                pltpu.VMEM((1, half), jnp.int32),
                pltpu.SemaphoreType.DMA((8,)),
            ],
            compiler_params=params,
            cost_estimate=pl.CostEstimate(flops=2 * rows * rows * width * 16, bytes_accessed=8 * 1024 * 1024, transcendentals=0),
        )(
            in_hbm(item_table),
            in_hbm(jnp.transpose(pair_mats, (1, 2, 0))),
            in_hbm(user_states),
            in_hbm(reader_users.reshape(1, readers)),
            in_hbm(cand_items.reshape(1, half)),
        )

    with jax.named_scope("states"):
        picked = pl.pallas_call(
            functools.partial(pick_kernel, total, cap),
            out_shape=jax.ShapeDtypeStruct((slots, width + half), jnp.bfloat16),
            in_specs=[vmem] * (total + 2),
            out_specs=vmem,
            compiler_params=params,
            cost_estimate=pl.CostEstimate(flops=2 * slots * rows * width, bytes_accessed=1024 * 1024, transcendentals=0),
        )(own_ids, *[ids.reshape(1, readers) for ids in users[1:]], digits, states_near)
        states = [picked] + [shift(picked, "shard", j) for j in range(1, total)]

    with jax.named_scope("pairs"):
        pair_parts, places = pl.pallas_call(
            functools.partial(pair_kernel, total, cap, slots, user_states.shape[0]),
            out_shape=(
                jax.ShapeDtypeStruct((1, rows), jnp.float32),
                jax.ShapeDtypeStruct((total, half), jnp.int32),
            ),
            in_specs=[anywhere] * total + [hbm, vmem, vmem, vmem, anywhere],
            out_specs=(vmem, vmem),
            scratch_shapes=[
                pltpu.SMEM((total, readers), jnp.int32),
                pltpu.SMEM((2, count), jnp.int32),
                pltpu.VMEM((count // 2 * PITCH, LANES), jnp.float32),
                pltpu.SemaphoreType.DMA((1 + total,)),
            ],
            compiler_params=params,
            cost_estimate=pl.CostEstimate(flops=2 * count * K * K * rows * 16, bytes_accessed=4 * 1024 * 1024, transcendentals=0),
        )(*users, in_hbm(pair_fields.T), *turned, picked)
        pair_scores = {(0, 0): pair_parts}
        steps = [(q, h) for q in range(planes) for h in range(parts) if q or h]
        for q, h in steps:
            perm = [
                (c * parts + d, (c + q) % planes * parts + (d + h) % parts) for c in range(planes) for d in range(parts)
            ]
            source = pair_parts
            if len(pair_scores) == 2:
                source, states[1] = lax.optimization_barrier((pair_parts, states[1]))
            if len(pair_scores) == 3:
                source, pair_scores[0, 1] = lax.optimization_barrier((pair_parts, pair_scores[0, 1]))
            pair_scores[q, h] = lax.ppermute(source, ("cache", "pair"), perm)
        pair_scores = [pair_scores[q, h] for q in range(planes) for h in range(parts)]

    with jax.named_scope("scores"):
        linear, hits = pl.pallas_call(
            functools.partial(linear_kernel, total, planes),
            out_shape=(
                jax.ShapeDtypeStruct((total, half), jnp.float32),
                jax.ShapeDtypeStruct((planes * rows, total * half), jnp.bfloat16),
            ),
            in_specs=[vmem] * (total + len(items) + 1),
            out_specs=(vmem, vmem),
            scratch_shapes=[
                pltpu.VMEM((total * slots, width), jnp.bfloat16),
                pltpu.VMEM((planes * rows, 3 * total * slots), jnp.bfloat16),
            ],
            compiler_params=params,
            cost_estimate=pl.CostEstimate(flops=2 * 64 * 256 * width, bytes_accessed=2 * 1024 * 1024, transcendentals=0),
        )(*states, *items, places)
        outs = pl.pallas_call(
            functools.partial(score_kernel, total, planes, parts),
            out_shape=[jax.ShapeDtypeStruct((1, half), jnp.float32)] * total,
            in_specs=[vmem] * (planes * parts + 2),
            out_specs=[vmem] * total,
            compiler_params=params,
            cost_estimate=pl.CostEstimate(flops=2 * 16 * 256 * 512, bytes_accessed=512 * 1024, transcendentals=0),
        )(*pair_scores, linear, hits)

    with jax.named_scope("back"):
        result = outs[0]
        for j in range(1, total):
            result = result + shift(outs[j], "shard", -j)
    return result.reshape(half)


def solution(mesh):
    return jax.shard_map(
        body,
        mesh=mesh,
        in_specs=(
            P(("groups", "shard", "cache", "pair")),
            P(("groups", "shard", "cache", "pair")),
            P(("shard", "cache"), None),
            P(("groups", "shard"), None),
            P("pair", None, None),
            P("pair", None),
        ),
        out_specs=P(("groups", "shard", "cache", "pair")),
        check_vma=False,
    )
```

```python
import functools

import jax
import jax.numpy as jnp
from jax import lax
from jax.experimental import pallas as pl
from jax.experimental.pallas import tpu as pltpu
from jax.sharding import PartitionSpec as P

K = 64
LANES = 128
PITCH = 72
CODE_BITS = 7
VMEM_LIMIT = 40 * 1024 * 1024
NT = (((1,), (1,)), ((), ()))
NN = (((1,), (0,)), ((), ()))


def dot(a, b, dims, **kw):
    return lax.dot_general(a, b, dims, preferred_element_type=jnp.float32, **kw)


def iota(shape, dim):
    return lax.broadcasted_iota(jnp.int32, shape, dim)


def ring(index, size):
    return lax.rem(index + size, size)


def pick_kernel(total, cap, *refs):
    users, (digits, states, out) = refs[:total], refs[total:]
    own_rows, width = states.shape
    slots = out.shape[0]
    readers = users[0].shape[1]
    me = lax.axis_index("shard")
    first = me * own_rows
    across = iota((readers, readers), 1)
    down = iota((readers, readers), 0)
    chosen = jnp.zeros((slots, own_rows), jnp.float32)
    for j in range(total):
        row = users[j][...]
        column = jnp.sum(jnp.where(across == down, row, 0), axis=1, keepdims=True)
        mine = (column >= first) & (column < first + own_rows)
        rank = jnp.sum(jnp.where((down < across) & mine, 1, 0), axis=0, keepdims=True)
        held = (row >= first) & (row < first + own_rows)
        slot = jnp.where(held, ring(me - j, total) * cap + rank, -1)
        to_slot = (iota((slots, readers), 0) == slot).astype(jnp.float32).astype(jnp.bfloat16)
        from_row = (iota((readers, own_rows), 1) + first == column).astype(jnp.float32).astype(jnp.bfloat16)
        chosen = chosen + dot(to_slot, from_row, NN)
    out[:, width:] = digits[...]
    out[:, :width] = dot(chosen.astype(jnp.bfloat16), states[...], NN).astype(jnp.bfloat16)


def slot_rows(asked, cap, slots, user_rows, half):
    total, readers = asked.shape
    me = lax.axis_index("shard")
    lane = iota((1, half), 1) // (half // readers)
    rows = []
    for j in range(total):
        source = ring(me - j, total)
        holders = [asked[j, r] // user_rows for r in range(readers)]
        row = jnp.zeros((1, half), jnp.int32)
        for r, holder in enumerate(holders):
            rank = jnp.int32(0)
            for earlier in holders[:r]:
                rank = rank + (earlier == holder).astype(jnp.int32)
            row = jnp.where(lane == r, ring(me - holder, total) * slots + source * cap + rank, row)
        rows.append(row)
    return rows


def turn_kernel(items_hbm, mats_hbm, states_hbm, ids_hbm, cands_hbm, rows32, rows16, mats, states, ids, digits, items, cands, sems):
    chunks = sems.shape[0] - 4
    wide = items.shape[1] // chunks
    item_fetches = [
        pltpu.make_async_copy(items_hbm.at[:, pl.ds(t * wide, wide)], items.at[:, pl.ds(t * wide, wide)], sems.at[t])
        for t in range(chunks)
    ]
    mats_fetch = pltpu.make_async_copy(mats_hbm, mats, sems.at[chunks])
    states_fetch = pltpu.make_async_copy(states_hbm, states, sems.at[chunks + 1])
    ids_fetch = pltpu.make_async_copy(ids_hbm, ids, sems.at[chunks + 2])
    cands_fetch = pltpu.make_async_copy(cands_hbm, cands, sems.at[chunks + 3])
    for copy in item_fetches + [mats_fetch, states_fetch, ids_fetch, cands_fetch]:
        copy.start()
    eye = (iota((LANES, LANES), 0) == iota((LANES, LANES), 1)).astype(jnp.bfloat16)
    for t in range(items.shape[1] // LANES):
        if t * LANES % wide == 0:
            item_fetches[t * LANES // wide].wait()
        turned = dot(eye, items[:, t * LANES:(t + 1) * LANES], NT)
        rows32[t * LANES:(t + 1) * LANES, :] = turned
        rows16[t * LANES:(t + 1) * LANES, :] = turned.astype(jnp.bfloat16)
    cands_fetch.wait()
    code = jnp.broadcast_to(cands[...], digits.shape)
    place = iota(digits.shape, 0)
    digit = jnp.where(place == 0, code >> CODE_BITS, jnp.where(place == 1, code & ((1 << CODE_BITS) - 1), 0))
    digits[...] = digit.astype(jnp.float32).astype(jnp.bfloat16)
    ids_fetch.wait()
    mats_fetch.wait()
    states_fetch.wait()


def pair_kernel(total, cap, slots, user_rows, *refs):
    users, refs = refs[:total], refs[total:]
    fields_hbm, rows32, rows16, mats, picked, out, places, asked, fields, stacked, sems = refs
    del picked
    fields_fetch = pltpu.make_async_copy(fields_hbm, fields, sems.at[total])
    id_fetches = [pltpu.make_async_copy(users[j], asked.at[j], sems.at[j]) for j in range(total)]
    for copy in [fields_fetch] + id_fetches:
        copy.start()
    pairs = mats.shape[2]
    steps = pairs // 2
    eye = (iota((steps, steps), 0) == iota((steps, steps), 1)).astype(jnp.bfloat16)
    for k in range(0, K, 2):
        sides = [mats[at, :, part * steps:(part + 1) * steps] for at in (k, k + 1) for part in range(2)]
        turned = dot(eye, jnp.concatenate(sides, axis=0), NT)
        stacked[pl.ds(k, steps, stride=PITCH), :] = turned[:, :LANES]
        stacked[pl.ds(k + 1, steps, stride=PITCH), :] = turned[:, LANES:]
    fields_fetch.wait()
    items = rows32.shape[1]
    blank = jnp.zeros((K, items), jnp.bfloat16)

    def two(p, total):
        fields_of = [(pl.multiple_of(fields[0, q] * K, K), pl.multiple_of(fields[1, q] * K, K)) for q in (p, p + steps)]
        left = stacked[pl.ds(pl.multiple_of(p * PITCH, 8), K), :].astype(jnp.bfloat16)
        first, second = [rows16[pl.ds(b, K), :] for _, b in fields_of]
        right = jnp.concatenate(
            [jnp.concatenate([first, blank], axis=1), jnp.concatenate([blank, second], axis=1)], axis=0
        )
        return total + dot(left, right, NN) * jnp.concatenate([rows32[pl.ds(a, K), :] for a, _ in fields_of], axis=1)

    sums = lax.fori_loop(0, steps, two, jnp.zeros((K, 2 * items), jnp.float32), unroll=16)
    line = jnp.sum(sums, axis=0, keepdims=True)
    out[...] = line[:, :items] + line[:, items:]
    for copy in id_fetches:
        copy.wait()
    for j, row in enumerate(slot_rows(asked, cap, slots, user_rows, places.shape[1])):
        places[j:j + 1, :] = row


def thirds(x):
    high = x.astype(jnp.bfloat16)
    rest = x - high.astype(jnp.float32)
    middle = rest.astype(jnp.bfloat16)
    return high, middle, (rest - middle.astype(jnp.float32)).astype(jnp.bfloat16)


def linear_kernel(total, planes, *refs):
    states, refs = refs[:total], refs[total:]
    items, (places, out, hits, wanted, linear) = refs[:planes], refs[planes:]
    slots = states[0].shape[0]
    own_rows, width = items[0].shape
    half = out.shape[1]
    me = lax.axis_index("shard")
    plane = lax.axis_index("cache")
    count = total * slots
    cands = []
    for j in range(total):
        wanted[j * slots:(j + 1) * slots, :] = states[j][:, :width]
        digits = states[j][:, width:].astype(jnp.float32)
        place = iota(digits.shape, 0)
        weight = jnp.where(place == 0, float(1 << CODE_BITS), jnp.where(place == 1, 1.0, 0.0))
        cands.append(jnp.sum(digits * weight, axis=0, keepdims=True).astype(jnp.int32))

    for q, rows in enumerate(items):
        for t, part in enumerate(thirds(dot(rows[...], wanted[...], NT))):
            linear[q * own_rows:(q + 1) * own_rows, t * count:(t + 1) * count] = part
    ids = [iota((own_rows, 1), 0) + (me * planes + ring(plane - q, planes)) * own_rows for q in range(planes)]
    item_ids = jnp.concatenate(ids, axis=0)
    for j in range(total):
        spread = (iota((count, half), 0) == places[j:j + 1, :]).astype(jnp.float32).astype(jnp.bfloat16)
        scores = dot(linear[...], jnp.concatenate([spread] * 3, axis=0), NN)
        hit = item_ids == cands[j]
        out[j:j + 1, :] = jnp.sum(jnp.where(hit, scores, 0.0), axis=0, keepdims=True)
        hits[:, j * half:(j + 1) * half] = hit.astype(jnp.float32).astype(jnp.bfloat16)


def score_kernel(total, planes, parts, *refs):
    pairs, (linear, hits), outs = refs[:planes * parts], refs[planes * parts:planes * parts + 2], refs[planes * parts + 2:]
    half = linear.shape[1]
    sums = [sum(pairs[(h + 1) * planes - 1 - q][...] for h in range(parts)) for q in range(planes)]
    row = jnp.concatenate(sums, axis=1)
    pieces = jnp.zeros((16, row.shape[1]), jnp.float32)
    for t, part in enumerate(thirds(row)):
        pieces = jnp.where(iota(pieces.shape, 0) == t, part.astype(jnp.float32), pieces)
    added = jnp.sum(dot(pieces.astype(jnp.bfloat16), hits[...], NN), axis=0, keepdims=True)
    for j in range(total):
        outs[j][...] = linear[j:j + 1, :] + added[:, j * half:(j + 1) * half]


def shift(x, axis, step):
    size = lax.axis_size(axis)
    return lax.ppermute(x, axis, [(s, (s + step) % size) for s in range(size)])


def body(cand_items, reader_users, item_table, user_states, pair_mats, pair_fields):
    total = lax.axis_size("shard")
    planes = lax.axis_size("cache")
    parts = lax.axis_size("pair")
    half = cand_items.shape[0]
    rows, width = item_table.shape
    readers = reader_users.shape[0]
    cap = 2 * ((readers + total - 1) // total)
    slots = -(-total * cap // 16) * 16
    count = pair_mats.shape[0]
    vmem = pl.BlockSpec(memory_space=pltpu.VMEM)
    hbm = pl.BlockSpec(memory_space=pltpu.HBM)
    anywhere = pl.BlockSpec(memory_space=pl.ANY)
    params = pltpu.CompilerParams(vmem_limit_bytes=VMEM_LIMIT)

    def in_hbm(x):
        return pltpu.with_memory_space_constraint(x, pltpu.HBM)

    with jax.named_scope("item_rows"):
        items = [item_table] + [shift(item_table, "cache", q) for q in range(1, planes)]

    with jax.named_scope("ids"):
        users = [in_hbm(reader_users)] + [shift(reader_users, "shard", j) for j in range(1, total)]

    with jax.named_scope("turn"):
        *turned, states_near, own_ids, digits = pl.pallas_call(
            turn_kernel,
            out_shape=(
                jax.ShapeDtypeStruct((width, rows), jnp.float32),
                jax.ShapeDtypeStruct((width, rows), jnp.bfloat16),
                jax.ShapeDtypeStruct((K, K, count), jnp.bfloat16),
                jax.ShapeDtypeStruct(user_states.shape, jnp.bfloat16),
                jax.ShapeDtypeStruct((1, readers), jnp.int32),
                jax.ShapeDtypeStruct((slots, half), jnp.bfloat16),
            ),
            in_specs=[hbm] * 5,
            out_specs=(vmem,) * 6,
            scratch_shapes=[
                pltpu.VMEM((rows, width), jnp.bfloat16),
                pltpu.VMEM((1, half), jnp.int32),
                pltpu.SemaphoreType.DMA((8,)),
            ],
            compiler_params=params,
            cost_estimate=pl.CostEstimate(flops=2 * rows * rows * width * 16, bytes_accessed=8 * 1024 * 1024, transcendentals=0),
        )(
            in_hbm(item_table),
            in_hbm(jnp.transpose(pair_mats, (1, 2, 0))),
            in_hbm(user_states),
            in_hbm(reader_users.reshape(1, readers)),
            in_hbm(cand_items.reshape(1, half)),
        )

    with jax.named_scope("states"):
        picked = pl.pallas_call(
            functools.partial(pick_kernel, total, cap),
            out_shape=jax.ShapeDtypeStruct((slots, width + half), jnp.bfloat16),
            in_specs=[vmem] * (total + 2),
            out_specs=vmem,
            compiler_params=params,
            cost_estimate=pl.CostEstimate(flops=2 * slots * rows * width, bytes_accessed=1024 * 1024, transcendentals=0),
        )(own_ids, *[ids.reshape(1, readers) for ids in users[1:]], digits, states_near)
        states = [picked] + [shift(picked, "shard", j) for j in range(1, total)]

    with jax.named_scope("pairs"):
        pair_parts, places = pl.pallas_call(
            functools.partial(pair_kernel, total, cap, slots, user_states.shape[0]),
            out_shape=(
                jax.ShapeDtypeStruct((1, rows), jnp.float32),
                jax.ShapeDtypeStruct((total, half), jnp.int32),
            ),
            in_specs=[anywhere] * total + [hbm, vmem, vmem, vmem, anywhere],
            out_specs=(vmem, vmem),
            scratch_shapes=[
                pltpu.SMEM((total, readers), jnp.int32),
                pltpu.SMEM((2, count), jnp.int32),
                pltpu.VMEM((count // 2 * PITCH, LANES), jnp.float32),
                pltpu.SemaphoreType.DMA((1 + total,)),
            ],
            compiler_params=params,
            cost_estimate=pl.CostEstimate(flops=2 * count * K * K * rows * 16, bytes_accessed=4 * 1024 * 1024, transcendentals=0),
        )(*users, in_hbm(pair_fields.T), *turned, picked)
        pair_scores = {(0, 0): pair_parts}
        steps = [(q, h) for q in range(planes - 1, -1, -1) for h in range(parts) if q or h]
        for q, h in steps:
            perm = [
                (c * parts + d, (c + q) % planes * parts + (d + h) % parts) for c in range(planes) for d in range(parts)
            ]
            source, after = pair_parts, {1: 1, 2: 2}.get(len(pair_scores) - 1, 0)
            if after:
                source, states[after] = lax.optimization_barrier((pair_parts, states[after]))
            pair_scores[q, h] = lax.ppermute(source, ("cache", "pair"), perm)
        pair_scores = [pair_scores[q, h] for h in range(parts) for q in range(planes - 1, -1, -1)]

    with jax.named_scope("scores"):
        linear, hits = pl.pallas_call(
            functools.partial(linear_kernel, total, planes),
            out_shape=(
                jax.ShapeDtypeStruct((total, half), jnp.float32),
                jax.ShapeDtypeStruct((planes * rows, total * half), jnp.bfloat16),
            ),
            in_specs=[vmem] * (total + len(items) + 1),
            out_specs=(vmem, vmem),
            scratch_shapes=[
                pltpu.VMEM((total * slots, width), jnp.bfloat16),
                pltpu.VMEM((planes * rows, 3 * total * slots), jnp.bfloat16),
            ],
            compiler_params=params,
            cost_estimate=pl.CostEstimate(flops=2 * 64 * 256 * width, bytes_accessed=2 * 1024 * 1024, transcendentals=0),
        )(*states, *items, places)
        outs = pl.pallas_call(
            functools.partial(score_kernel, total, planes, parts),
            out_shape=[jax.ShapeDtypeStruct((1, half), jnp.float32)] * total,
            in_specs=[vmem] * (planes * parts + 2),
            out_specs=[vmem] * total,
            compiler_params=params,
            cost_estimate=pl.CostEstimate(flops=2 * 16 * 256 * 512, bytes_accessed=512 * 1024, transcendentals=0),
        )(*pair_scores, linear, hits)

    with jax.named_scope("back"):
        result = outs[0]
        for j in range(1, total):
            result = result + shift(outs[j], "shard", -j)
    return result.reshape(half)


def solution(mesh):
    return jax.shard_map(
        body,
        mesh=mesh,
        in_specs=(
            P(("groups", "shard", "cache", "pair")),
            P(("groups", "shard", "cache", "pair")),
            P(("shard", "cache"), None),
            P(("groups", "shard"), None),
            P("pair", None, None),
            P("pair", None),
        ),
        out_specs=P(("groups", "shard", "cache", "pair")),
        check_vma=False,
    )
```

```python
import functools

import jax
import jax.numpy as jnp
from jax import lax
from jax.experimental import pallas as pl
from jax.experimental.pallas import tpu as pltpu
from jax.sharding import PartitionSpec as P

K = 64
LANES = 128
PITCH = 72
CODE_BITS = 7
VMEM_LIMIT = 40 * 1024 * 1024
NT = (((1,), (1,)), ((), ()))
NN = (((1,), (0,)), ((), ()))


def dot(a, b, dims, **kw):
    return lax.dot_general(a, b, dims, preferred_element_type=jnp.float32, **kw)


def iota(shape, dim):
    return lax.broadcasted_iota(jnp.int32, shape, dim)


def ring(index, size):
    return lax.rem(index + size, size)


def pick_kernel(total, cap, *refs):
    users, (digits, states, out) = refs[:total], refs[total:]
    own_rows, width = states.shape
    slots = out.shape[0]
    readers = users[0].shape[1]
    me = lax.axis_index("shard")
    first = me * own_rows
    across = iota((readers, readers), 1)
    down = iota((readers, readers), 0)
    chosen = jnp.zeros((slots, own_rows), jnp.float32)
    for j in range(total):
        row = users[j][...]
        column = jnp.sum(jnp.where(across == down, row, 0), axis=1, keepdims=True)
        mine = (column >= first) & (column < first + own_rows)
        rank = jnp.sum(jnp.where((down < across) & mine, 1, 0), axis=0, keepdims=True)
        held = (row >= first) & (row < first + own_rows)
        slot = jnp.where(held, ring(me - j, total) * cap + rank, -1)
        to_slot = (iota((slots, readers), 0) == slot).astype(jnp.float32).astype(jnp.bfloat16)
        from_row = (iota((readers, own_rows), 1) + first == column).astype(jnp.float32).astype(jnp.bfloat16)
        chosen = chosen + dot(to_slot, from_row, NN)
    out[:, width:] = digits[...]
    out[:, :width] = dot(chosen.astype(jnp.bfloat16), states[...], NN).astype(jnp.bfloat16)


def slot_rows(asked, cap, slots, user_rows, half):
    total, readers = asked.shape
    me = lax.axis_index("shard")
    lane = iota((1, half), 1) // (half // readers)
    rows = []
    for j in range(total):
        source = ring(me - j, total)
        holders = [asked[j, r] // user_rows for r in range(readers)]
        row = jnp.zeros((1, half), jnp.int32)
        for r, holder in enumerate(holders):
            rank = jnp.int32(0)
            for earlier in holders[:r]:
                rank = rank + (earlier == holder).astype(jnp.int32)
            row = jnp.where(lane == r, ring(me - holder, total) * slots + source * cap + rank, row)
        rows.append(row)
    return rows


def turn_kernel(items_hbm, mats_hbm, states_hbm, ids_hbm, cands_hbm, rows32, rows16, mats, states, ids, digits, items, cands, sems):
    chunks = sems.shape[0] - 4
    wide = items.shape[1] // chunks
    item_fetches = [
        pltpu.make_async_copy(items_hbm.at[:, pl.ds(t * wide, wide)], items.at[:, pl.ds(t * wide, wide)], sems.at[t])
        for t in range(chunks)
    ]
    mats_fetch = pltpu.make_async_copy(mats_hbm, mats, sems.at[chunks])
    states_fetch = pltpu.make_async_copy(states_hbm, states, sems.at[chunks + 1])
    ids_fetch = pltpu.make_async_copy(ids_hbm, ids, sems.at[chunks + 2])
    cands_fetch = pltpu.make_async_copy(cands_hbm, cands, sems.at[chunks + 3])
    for copy in item_fetches + [mats_fetch, states_fetch, ids_fetch, cands_fetch]:
        copy.start()
    eye = (iota((LANES, LANES), 0) == iota((LANES, LANES), 1)).astype(jnp.bfloat16)
    for t in range(items.shape[1] // LANES):
        if t * LANES % wide == 0:
            item_fetches[t * LANES // wide].wait()
        turned = dot(eye, items[:, t * LANES:(t + 1) * LANES], NT)
        rows32[t * LANES:(t + 1) * LANES, :] = turned
        rows16[t * LANES:(t + 1) * LANES, :] = turned.astype(jnp.bfloat16)
    cands_fetch.wait()
    code = jnp.broadcast_to(cands[...], digits.shape)
    place = iota(digits.shape, 0)
    digit = jnp.where(place == 0, code >> CODE_BITS, jnp.where(place == 1, code & ((1 << CODE_BITS) - 1), 0))
    digits[...] = digit.astype(jnp.float32).astype(jnp.bfloat16)
    ids_fetch.wait()
    mats_fetch.wait()
    states_fetch.wait()


def pair_kernel(total, cap, slots, user_rows, *refs):
    users, refs = refs[:total], refs[total:]
    fields_hbm, rows32, rows16, mats, picked, out, places, asked, fields, stacked, sems = refs
    del picked
    fields_fetch = pltpu.make_async_copy(fields_hbm, fields, sems.at[total])
    id_fetches = [pltpu.make_async_copy(users[j], asked.at[j], sems.at[j]) for j in range(total)]
    for copy in [fields_fetch] + id_fetches:
        copy.start()
    pairs = mats.shape[2]
    steps = pairs // 2
    eye = (iota((steps, steps), 0) == iota((steps, steps), 1)).astype(jnp.bfloat16)
    for k in range(0, K, 2):
        sides = [mats[at, :, part * steps:(part + 1) * steps] for at in (k, k + 1) for part in range(2)]
        turned = dot(eye, jnp.concatenate(sides, axis=0), NT)
        stacked[pl.ds(k, steps, stride=PITCH), :] = turned[:, :LANES]
        stacked[pl.ds(k + 1, steps, stride=PITCH), :] = turned[:, LANES:]
    fields_fetch.wait()
    items = rows32.shape[1]
    blank = jnp.zeros((K, items), jnp.bfloat16)

    def two(p, total):
        fields_of = [(pl.multiple_of(fields[0, q] * K, K), pl.multiple_of(fields[1, q] * K, K)) for q in (p, p + steps)]
        left = stacked[pl.ds(pl.multiple_of(p * PITCH, 8), K), :].astype(jnp.bfloat16)
        first, second = [rows16[pl.ds(b, K), :] for _, b in fields_of]
        right = jnp.concatenate(
            [jnp.concatenate([first, blank], axis=1), jnp.concatenate([blank, second], axis=1)], axis=0
        )
        return total + dot(left, right, NN) * jnp.concatenate([rows32[pl.ds(a, K), :] for a, _ in fields_of], axis=1)

    sums = lax.fori_loop(0, steps, two, jnp.zeros((K, 2 * items), jnp.float32), unroll=16)
    line = jnp.sum(sums, axis=0, keepdims=True)
    out[...] = line[:, :items] + line[:, items:]
    for copy in id_fetches:
        copy.wait()
    for j, row in enumerate(slot_rows(asked, cap, slots, user_rows, places.shape[1])):
        places[j:j + 1, :] = row


def thirds(x):
    high = x.astype(jnp.bfloat16)
    rest = x - high.astype(jnp.float32)
    middle = rest.astype(jnp.bfloat16)
    return high, middle, (rest - middle.astype(jnp.float32)).astype(jnp.bfloat16)


def linear_kernel(total, planes, *refs):
    states, refs = refs[:total], refs[total:]
    items, (places, out, hits, wanted, linear) = refs[:planes], refs[planes:]
    slots = states[0].shape[0]
    own_rows, width = items[0].shape
    half = out.shape[1]
    me = lax.axis_index("shard")
    plane = lax.axis_index("cache")
    count = total * slots
    cands = []
    for j in range(total):
        wanted[j * slots:(j + 1) * slots, :] = states[j][:, :width]
        digits = states[j][:, width:].astype(jnp.float32)
        place = iota(digits.shape, 0)
        weight = jnp.where(place == 0, float(1 << CODE_BITS), jnp.where(place == 1, 1.0, 0.0))
        cands.append(jnp.sum(digits * weight, axis=0, keepdims=True).astype(jnp.int32))

    for q, rows in enumerate(items):
        for t, part in enumerate(thirds(dot(rows[...], wanted[...], NT))):
            linear[q * own_rows:(q + 1) * own_rows, t * count:(t + 1) * count] = part
    ids = [iota((own_rows, 1), 0) + (me * planes + ring(plane - q, planes)) * own_rows for q in range(planes)]
    item_ids = jnp.concatenate(ids, axis=0)
    for j in range(total):
        spread = (iota((count, half), 0) == places[j:j + 1, :]).astype(jnp.float32).astype(jnp.bfloat16)
        scores = dot(linear[...], jnp.concatenate([spread] * 3, axis=0), NN)
        hit = item_ids == cands[j]
        out[j:j + 1, :] = jnp.sum(jnp.where(hit, scores, 0.0), axis=0, keepdims=True)
        hits[:, j * half:(j + 1) * half] = hit.astype(jnp.float32).astype(jnp.bfloat16)


def score_kernel(total, planes, parts, *refs):
    pairs, (linear, hits, stays, goes, rows) = refs[:planes * parts], refs[planes * parts:]
    half = linear.shape[1]
    sums = [sum(pairs[(h + 1) * planes - 1 - q][...] for h in range(parts)) for q in range(planes)]
    row = jnp.concatenate(sums, axis=1)
    pieces = jnp.zeros((16, row.shape[1]), jnp.float32)
    for t, part in enumerate(thirds(row)):
        pieces = jnp.where(iota(pieces.shape, 0) == t, part.astype(jnp.float32), pieces)
    added = jnp.sum(dot(pieces.astype(jnp.bfloat16), hits[...], NN), axis=0, keepdims=True)
    for j in range(total):
        rows[j:j + 1, :] = linear[j:j + 1, :] + added[:, j * half:(j + 1) * half]
    me = lax.axis_index("shard")
    for mask in range(total):
        target = stays if mask < total // 2 else goes
        at = mask % (total // 2)
        target[at:at + 1, :] = rows[pl.ds(ring(me - (me ^ mask), total), 1), :]


def halve_kernel(held, came, stays, goes):
    count = stays.shape[0]
    stays[...] = held[:count, :] + came[:count, :]
    goes[...] = held[count:, :] + came[count:, :]


def shift(x, axis, step):
    size = lax.axis_size(axis)
    return lax.ppermute(x, axis, [(s, (s + step) % size) for s in range(size)])


def swap(x, axis, mask):
    return lax.ppermute(x, axis, [(s, s ^ mask) for s in range(lax.axis_size(axis))])


def body(cand_items, reader_users, item_table, user_states, pair_mats, pair_fields):
    total = lax.axis_size("shard")
    planes = lax.axis_size("cache")
    parts = lax.axis_size("pair")
    half = cand_items.shape[0]
    rows, width = item_table.shape
    readers = reader_users.shape[0]
    cap = 2 * ((readers + total - 1) // total)
    slots = -(-total * cap // 16) * 16
    count = pair_mats.shape[0]
    vmem = pl.BlockSpec(memory_space=pltpu.VMEM)
    hbm = pl.BlockSpec(memory_space=pltpu.HBM)
    anywhere = pl.BlockSpec(memory_space=pl.ANY)
    params = pltpu.CompilerParams(vmem_limit_bytes=VMEM_LIMIT)

    def in_hbm(x):
        return pltpu.with_memory_space_constraint(x, pltpu.HBM)

    with jax.named_scope("item_rows"):
        items = [item_table] + [shift(item_table, "cache", q) for q in range(1, planes)]

    with jax.named_scope("ids"):
        users = [in_hbm(reader_users)] + [shift(reader_users, "shard", j) for j in range(1, total)]

    with jax.named_scope("turn"):
        *turned, states_near, own_ids, digits = pl.pallas_call(
            turn_kernel,
            out_shape=(
                jax.ShapeDtypeStruct((width, rows), jnp.float32),
                jax.ShapeDtypeStruct((width, rows), jnp.bfloat16),
                jax.ShapeDtypeStruct((K, K, count), jnp.bfloat16),
                jax.ShapeDtypeStruct(user_states.shape, jnp.bfloat16),
                jax.ShapeDtypeStruct((1, readers), jnp.int32),
                jax.ShapeDtypeStruct((slots, half), jnp.bfloat16),
            ),
            in_specs=[hbm] * 5,
            out_specs=(vmem,) * 6,
            scratch_shapes=[
                pltpu.VMEM((rows, width), jnp.bfloat16),
                pltpu.VMEM((1, half), jnp.int32),
                pltpu.SemaphoreType.DMA((8,)),
            ],
            compiler_params=params,
            cost_estimate=pl.CostEstimate(flops=2 * rows * rows * width * 16, bytes_accessed=8 * 1024 * 1024, transcendentals=0),
        )(
            in_hbm(item_table),
            in_hbm(jnp.transpose(pair_mats, (1, 2, 0))),
            in_hbm(user_states),
            in_hbm(reader_users.reshape(1, readers)),
            in_hbm(cand_items.reshape(1, half)),
        )

    with jax.named_scope("states"):
        picked = pl.pallas_call(
            functools.partial(pick_kernel, total, cap),
            out_shape=jax.ShapeDtypeStruct((slots, width + half), jnp.bfloat16),
            in_specs=[vmem] * (total + 2),
            out_specs=vmem,
            compiler_params=params,
            cost_estimate=pl.CostEstimate(flops=2 * slots * rows * width, bytes_accessed=1024 * 1024, transcendentals=0),
        )(own_ids, *[ids.reshape(1, readers) for ids in users[1:]], digits, states_near)
        states = [picked] + [shift(picked, "shard", j) for j in range(1, total)]

    with jax.named_scope("pairs"):
        pair_parts, places = pl.pallas_call(
            functools.partial(pair_kernel, total, cap, slots, user_states.shape[0]),
            out_shape=(
                jax.ShapeDtypeStruct((1, rows), jnp.float32),
                jax.ShapeDtypeStruct((total, half), jnp.int32),
            ),
            in_specs=[anywhere] * total + [hbm, vmem, vmem, vmem, anywhere],
            out_specs=(vmem, vmem),
            scratch_shapes=[
                pltpu.SMEM((total, readers), jnp.int32),
                pltpu.SMEM((2, count), jnp.int32),
                pltpu.VMEM((count // 2 * PITCH, LANES), jnp.float32),
                pltpu.SemaphoreType.DMA((1 + total,)),
            ],
            compiler_params=params,
            cost_estimate=pl.CostEstimate(flops=2 * count * K * K * rows * 16, bytes_accessed=4 * 1024 * 1024, transcendentals=0),
        )(*users, in_hbm(pair_fields.T), *turned, picked)
        pair_scores = {(0, 0): pair_parts}
        steps = [(q, h) for q in range(planes - 1, -1, -1) for h in range(parts) if q or h]
        for q, h in steps:
            perm = [
                (c * parts + d, (c + q) % planes * parts + (d + h) % parts) for c in range(planes) for d in range(parts)
            ]
            source, after = pair_parts, {1: 1, 2: 2}.get(len(pair_scores) - 1, 0)
            if after:
                source, states[after] = lax.optimization_barrier((pair_parts, states[after]))
            pair_scores[q, h] = lax.ppermute(source, ("cache", "pair"), perm)
        pair_scores = [pair_scores[q, h] for h in range(parts) for q in range(planes - 1, -1, -1)]

    with jax.named_scope("scores"):
        linear, hits = pl.pallas_call(
            functools.partial(linear_kernel, total, planes),
            out_shape=(
                jax.ShapeDtypeStruct((total, half), jnp.float32),
                jax.ShapeDtypeStruct((planes * rows, total * half), jnp.bfloat16),
            ),
            in_specs=[vmem] * (total + len(items) + 1),
            out_specs=(vmem, vmem),
            scratch_shapes=[
                pltpu.VMEM((total * slots, width), jnp.bfloat16),
                pltpu.VMEM((planes * rows, 3 * total * slots), jnp.bfloat16),
            ],
            compiler_params=params,
            cost_estimate=pl.CostEstimate(flops=2 * 64 * 256 * width, bytes_accessed=2 * 1024 * 1024, transcendentals=0),
        )(*states, *items, places)
        cut = [jax.ShapeDtypeStruct((total // 2, half), jnp.float32)] * 2
        stays, goes = pl.pallas_call(
            functools.partial(score_kernel, total, planes, parts),
            out_shape=cut,
            in_specs=[vmem] * (planes * parts + 2),
            out_specs=[vmem] * 2,
            scratch_shapes=[pltpu.VMEM((-(-total // 8) * 8, half), jnp.float32)],
            compiler_params=params,
            cost_estimate=pl.CostEstimate(flops=2 * 16 * 256 * 512, bytes_accessed=512 * 1024, transcendentals=0),
        )(*pair_scores, linear, hits)

    with jax.named_scope("back"):
        mask = total // 2
        while mask > 1:
            came = swap(goes, "shard", mask)
            mask //= 2
            stays, goes = pl.pallas_call(
                halve_kernel,
                out_shape=[jax.ShapeDtypeStruct((mask, half), jnp.float32)] * 2,
                in_specs=[vmem] * 2,
                out_specs=[vmem] * 2,
                compiler_params=params,
            )(stays, came)
        return (stays + swap(goes, "shard", mask)).reshape(half)


def solution(mesh):
    return jax.shard_map(
        body,
        mesh=mesh,
        in_specs=(
            P(("groups", "shard", "cache", "pair")),
            P(("groups", "shard", "cache", "pair")),
            P(("shard", "cache"), None),
            P(("groups", "shard"), None),
            P("pair", None, None),
            P("pair", None),
        ),
        out_specs=P(("groups", "shard", "cache", "pair")),
        check_vma=False,
    )
```

```python
import functools

import jax
import jax.numpy as jnp
from jax import lax
from jax.experimental import pallas as pl
from jax.experimental.pallas import tpu as pltpu
from jax.sharding import PartitionSpec as P

K = 64
LANES = 128
PITCH = 72
CODE_BITS = 7
VMEM_LIMIT = 40 * 1024 * 1024
NT = (((1,), (1,)), ((), ()))
NN = (((1,), (0,)), ((), ()))


def dot(a, b, dims, **kw):
    return lax.dot_general(a, b, dims, preferred_element_type=jnp.float32, **kw)


def iota(shape, dim):
    return lax.broadcasted_iota(jnp.int32, shape, dim)


def ring(index, size):
    return lax.rem(index + size, size)


def pick_kernel(total, cap, *refs):
    users, (digits, states, out) = refs[:total], refs[total:]
    own_rows, width = states.shape
    slots = out.shape[0]
    readers = users[0].shape[1]
    me = lax.axis_index("shard")
    first = me * own_rows
    across = iota((readers, readers), 1)
    down = iota((readers, readers), 0)
    chosen = jnp.zeros((slots, own_rows), jnp.float32)
    for j in range(total):
        row = users[j][...]
        column = jnp.sum(jnp.where(across == down, row, 0), axis=1, keepdims=True)
        mine = (column >= first) & (column < first + own_rows)
        rank = jnp.sum(jnp.where((down < across) & mine, 1, 0), axis=0, keepdims=True)
        held = (row >= first) & (row < first + own_rows)
        slot = jnp.where(held, ring(me - j, total) * cap + rank, -1)
        to_slot = (iota((slots, readers), 0) == slot).astype(jnp.float32).astype(jnp.bfloat16)
        from_row = (iota((readers, own_rows), 1) + first == column).astype(jnp.float32).astype(jnp.bfloat16)
        chosen = chosen + dot(to_slot, from_row, NN)
    out[:, width:] = digits[...]
    out[:, :width] = dot(chosen.astype(jnp.bfloat16), states[...], NN).astype(jnp.bfloat16)


def slot_rows(asked, cap, slots, user_rows, half):
    total, readers = asked.shape
    me = lax.axis_index("shard")
    lane = iota((1, half), 1) // (half // readers)
    rows = []
    for j in range(total):
        source = ring(me - j, total)
        holders = [asked[j, r] // user_rows for r in range(readers)]
        row = jnp.zeros((1, half), jnp.int32)
        for r, holder in enumerate(holders):
            rank = jnp.int32(0)
            for earlier in holders[:r]:
                rank = rank + (earlier == holder).astype(jnp.int32)
            row = jnp.where(lane == r, ring(me - holder, total) * slots + source * cap + rank, row)
        rows.append(row)
    return rows


def turn_kernel(items_hbm, mats_hbm, states_hbm, ids_hbm, cands_hbm, rows32, rows16, mats, states, ids, digits, items, cands, sems):
    chunks = sems.shape[0] - 4
    wide = items.shape[1] // chunks
    item_fetches = [
        pltpu.make_async_copy(items_hbm.at[:, pl.ds(t * wide, wide)], items.at[:, pl.ds(t * wide, wide)], sems.at[t])
        for t in range(chunks)
    ]
    mats_fetch = pltpu.make_async_copy(mats_hbm, mats, sems.at[chunks])
    states_fetch = pltpu.make_async_copy(states_hbm, states, sems.at[chunks + 1])
    ids_fetch = pltpu.make_async_copy(ids_hbm, ids, sems.at[chunks + 2])
    cands_fetch = pltpu.make_async_copy(cands_hbm, cands, sems.at[chunks + 3])
    for copy in item_fetches + [mats_fetch, states_fetch, ids_fetch, cands_fetch]:
        copy.start()
    eye = (iota((LANES, LANES), 0) == iota((LANES, LANES), 1)).astype(jnp.bfloat16)
    for t in range(items.shape[1] // LANES):
        if t * LANES % wide == 0:
            item_fetches[t * LANES // wide].wait()
        turned = dot(eye, items[:, t * LANES:(t + 1) * LANES], NT)
        rows32[t * LANES:(t + 1) * LANES, :] = turned
        rows16[t * LANES:(t + 1) * LANES, :] = turned.astype(jnp.bfloat16)
    cands_fetch.wait()
    code = jnp.broadcast_to(cands[...], digits.shape)
    place = iota(digits.shape, 0)
    digit = jnp.where(place == 0, code >> CODE_BITS, jnp.where(place == 1, code & ((1 << CODE_BITS) - 1), 0))
    digits[...] = digit.astype(jnp.float32).astype(jnp.bfloat16)
    ids_fetch.wait()
    mats_fetch.wait()
    states_fetch.wait()


def pair_kernel(total, cap, slots, user_rows, *refs):
    users, refs = refs[:total], refs[total:]
    fields_hbm, rows32, rows16, mats, picked, out, places, asked, fields, stacked, sems = refs
    del picked
    fields_fetch = pltpu.make_async_copy(fields_hbm, fields, sems.at[total])
    id_fetches = [pltpu.make_async_copy(users[j], asked.at[j], sems.at[j]) for j in range(total)]
    for copy in [fields_fetch] + id_fetches:
        copy.start()
    pairs = mats.shape[2]
    steps = pairs // 2
    eye = (iota((steps, steps), 0) == iota((steps, steps), 1)).astype(jnp.bfloat16)
    for k in range(0, K, 2):
        sides = [mats[at, :, part * steps:(part + 1) * steps] for at in (k, k + 1) for part in range(2)]
        turned = dot(eye, jnp.concatenate(sides, axis=0), NT)
        stacked[pl.ds(k, steps, stride=PITCH), :] = turned[:, :LANES]
        stacked[pl.ds(k + 1, steps, stride=PITCH), :] = turned[:, LANES:]
    fields_fetch.wait()
    items = rows32.shape[1]
    blank = jnp.zeros((K, items), jnp.bfloat16)

    def two(p, total):
        fields_of = [(pl.multiple_of(fields[0, q] * K, K), pl.multiple_of(fields[1, q] * K, K)) for q in (p, p + steps)]
        left = stacked[pl.ds(pl.multiple_of(p * PITCH, 8), K), :].astype(jnp.bfloat16)
        first, second = [rows16[pl.ds(b, K), :] for _, b in fields_of]
        right = jnp.concatenate(
            [jnp.concatenate([first, blank], axis=1), jnp.concatenate([blank, second], axis=1)], axis=0
        )
        return total + dot(left, right, NN) * jnp.concatenate([rows32[pl.ds(a, K), :] for a, _ in fields_of], axis=1)

    sums = lax.fori_loop(0, steps, two, jnp.zeros((K, 2 * items), jnp.float32), unroll=16)
    line = jnp.sum(sums, axis=0, keepdims=True)
    out[...] = line[:, :items] + line[:, items:]
    for copy in id_fetches:
        copy.wait()
    for j, row in enumerate(slot_rows(asked, cap, slots, user_rows, places.shape[1])):
        places[j:j + 1, :] = row


def thirds(x):
    high = x.astype(jnp.bfloat16)
    rest = x - high.astype(jnp.float32)
    middle = rest.astype(jnp.bfloat16)
    return high, middle, (rest - middle.astype(jnp.float32)).astype(jnp.bfloat16)


def linear_kernel(total, planes, *refs):
    states, refs = refs[:total], refs[total:]
    items, (places, out, hits, wanted, linear) = refs[:planes], refs[planes:]
    slots = states[0].shape[0]
    own_rows, width = items[0].shape
    half = out.shape[1]
    me = lax.axis_index("shard")
    plane = lax.axis_index("cache")
    count = total * slots
    cands = []
    for j in range(total):
        wanted[j * slots:(j + 1) * slots, :] = states[j][:, :width]
        digits = states[j][:, width:].astype(jnp.float32)
        place = iota(digits.shape, 0)
        weight = jnp.where(place == 0, float(1 << CODE_BITS), jnp.where(place == 1, 1.0, 0.0))
        cands.append(jnp.sum(digits * weight, axis=0, keepdims=True).astype(jnp.int32))

    for q, rows in enumerate(items):
        for t, part in enumerate(thirds(dot(rows[...], wanted[...], NT))):
            linear[q * own_rows:(q + 1) * own_rows, t * count:(t + 1) * count] = part
    ids = [iota((own_rows, 1), 0) + (me * planes + ring(plane - q, planes)) * own_rows for q in range(planes)]
    item_ids = jnp.concatenate(ids, axis=0)
    for j in range(total):
        spread = (iota((count, half), 0) == places[j:j + 1, :]).astype(jnp.float32).astype(jnp.bfloat16)
        scores = dot(linear[...], jnp.concatenate([spread] * 3, axis=0), NN)
        hit = item_ids == cands[j]
        out[j:j + 1, :] = jnp.sum(jnp.where(hit, scores, 0.0), axis=0, keepdims=True)
        hits[:, j * half:(j + 1) * half] = hit.astype(jnp.float32).astype(jnp.bfloat16)


def score_kernel(total, planes, parts, *refs):
    pairs, (linear, hits), refs = refs[:planes * parts], refs[planes * parts:planes * parts + 2], refs[planes * parts + 2:]
    outs, rows = refs[:total], refs[total]
    half = linear.shape[1]
    sums = [sum(pairs[(h + 1) * planes - 1 - q][...] for h in range(parts)) for q in range(planes)]
    row = jnp.concatenate(sums, axis=1)
    pieces = jnp.zeros((16, row.shape[1]), jnp.float32)
    for t, part in enumerate(thirds(row)):
        pieces = jnp.where(iota(pieces.shape, 0) == t, part.astype(jnp.float32), pieces)
    added = jnp.sum(dot(pieces.astype(jnp.bfloat16), hits[...], NN), axis=0, keepdims=True)
    for j in range(total):
        rows[j:j + 1, :] = linear[j:j + 1, :] + added[:, j * half:(j + 1) * half]
    me = lax.axis_index("shard")
    for mask in range(total):
        outs[mask][...] = rows[pl.ds(ring(me - (me ^ mask), total), 1), :]


def shift(x, axis, step):
    size = lax.axis_size(axis)
    return lax.ppermute(x, axis, [(s, (s + step) % size) for s in range(size)])


def swap(x, axis, mask):
    return lax.ppermute(x, axis, [(s, s ^ mask) for s in range(lax.axis_size(axis))])


def body(cand_items, reader_users, item_table, user_states, pair_mats, pair_fields):
    total = lax.axis_size("shard")
    planes = lax.axis_size("cache")
    parts = lax.axis_size("pair")
    half = cand_items.shape[0]
    rows, width = item_table.shape
    readers = reader_users.shape[0]
    cap = 2 * ((readers + total - 1) // total)
    slots = -(-total * cap // 16) * 16
    count = pair_mats.shape[0]
    vmem = pl.BlockSpec(memory_space=pltpu.VMEM)
    hbm = pl.BlockSpec(memory_space=pltpu.HBM)
    anywhere = pl.BlockSpec(memory_space=pl.ANY)
    params = pltpu.CompilerParams(vmem_limit_bytes=VMEM_LIMIT)

    def in_hbm(x):
        return pltpu.with_memory_space_constraint(x, pltpu.HBM)

    with jax.named_scope("item_rows"):
        items = [item_table] + [shift(item_table, "cache", q) for q in range(1, planes)]

    with jax.named_scope("ids"):
        users = [in_hbm(reader_users)] + [shift(reader_users, "shard", j) for j in range(1, total)]

    with jax.named_scope("turn"):
        *turned, states_near, own_ids, digits = pl.pallas_call(
            turn_kernel,
            out_shape=(
                jax.ShapeDtypeStruct((width, rows), jnp.float32),
                jax.ShapeDtypeStruct((width, rows), jnp.bfloat16),
                jax.ShapeDtypeStruct((K, K, count), jnp.bfloat16),
                jax.ShapeDtypeStruct(user_states.shape, jnp.bfloat16),
                jax.ShapeDtypeStruct((1, readers), jnp.int32),
                jax.ShapeDtypeStruct((slots, half), jnp.bfloat16),
            ),
            in_specs=[hbm] * 5,
            out_specs=(vmem,) * 6,
            scratch_shapes=[
                pltpu.VMEM((rows, width), jnp.bfloat16),
                pltpu.VMEM((1, half), jnp.int32),
                pltpu.SemaphoreType.DMA((8,)),
            ],
            compiler_params=params,
            cost_estimate=pl.CostEstimate(flops=2 * rows * rows * width * 16, bytes_accessed=8 * 1024 * 1024, transcendentals=0),
        )(
            in_hbm(item_table),
            in_hbm(jnp.transpose(pair_mats, (1, 2, 0))),
            in_hbm(user_states),
            in_hbm(reader_users.reshape(1, readers)),
            in_hbm(cand_items.reshape(1, half)),
        )

    with jax.named_scope("states"):
        picked = pl.pallas_call(
            functools.partial(pick_kernel, total, cap),
            out_shape=jax.ShapeDtypeStruct((slots, width + half), jnp.bfloat16),
            in_specs=[vmem] * (total + 2),
            out_specs=vmem,
            compiler_params=params,
            cost_estimate=pl.CostEstimate(flops=2 * slots * rows * width, bytes_accessed=1024 * 1024, transcendentals=0),
        )(own_ids, *[ids.reshape(1, readers) for ids in users[1:]], digits, states_near)
        states = [picked] + [shift(picked, "shard", j) for j in range(1, total)]

    with jax.named_scope("pairs"):
        pair_parts, places = pl.pallas_call(
            functools.partial(pair_kernel, total, cap, slots, user_states.shape[0]),
            out_shape=(
                jax.ShapeDtypeStruct((1, rows), jnp.float32),
                jax.ShapeDtypeStruct((total, half), jnp.int32),
            ),
            in_specs=[anywhere] * total + [hbm, vmem, vmem, vmem, anywhere],
            out_specs=(vmem, vmem),
            scratch_shapes=[
                pltpu.SMEM((total, readers), jnp.int32),
                pltpu.SMEM((2, count), jnp.int32),
                pltpu.VMEM((count // 2 * PITCH, LANES), jnp.float32),
                pltpu.SemaphoreType.DMA((1 + total,)),
            ],
            compiler_params=params,
            cost_estimate=pl.CostEstimate(flops=2 * count * K * K * rows * 16, bytes_accessed=4 * 1024 * 1024, transcendentals=0),
        )(*users, in_hbm(pair_fields.T), *turned, picked)
        pair_scores = {(0, 0): pair_parts}
        steps = [(q, h) for q in range(planes - 1, -1, -1) for h in range(parts) if q or h]
        for q, h in steps:
            perm = [
                (c * parts + d, (c + q) % planes * parts + (d + h) % parts) for c in range(planes) for d in range(parts)
            ]
            source, after = pair_parts, {1: 1, 2: 2}.get(len(pair_scores) - 1, 0)
            if after:
                source, states[after] = lax.optimization_barrier((pair_parts, states[after]))
            pair_scores[q, h] = lax.ppermute(source, ("cache", "pair"), perm)
        pair_scores = [pair_scores[q, h] for h in range(parts) for q in range(planes - 1, -1, -1)]

    with jax.named_scope("scores"):
        linear, hits = pl.pallas_call(
            functools.partial(linear_kernel, total, planes),
            out_shape=(
                jax.ShapeDtypeStruct((total, half), jnp.float32),
                jax.ShapeDtypeStruct((planes * rows, total * half), jnp.bfloat16),
            ),
            in_specs=[vmem] * (total + len(items) + 1),
            out_specs=(vmem, vmem),
            scratch_shapes=[
                pltpu.VMEM((total * slots, width), jnp.bfloat16),
                pltpu.VMEM((planes * rows, 3 * total * slots), jnp.bfloat16),
            ],
            compiler_params=params,
            cost_estimate=pl.CostEstimate(flops=2 * 64 * 256 * width, bytes_accessed=2 * 1024 * 1024, transcendentals=0),
        )(*states, *items, places)
        outs = pl.pallas_call(
            functools.partial(score_kernel, total, planes, parts),
            out_shape=[jax.ShapeDtypeStruct((1, half), jnp.float32)] * total,
            in_specs=[vmem] * (planes * parts + 2),
            out_specs=[vmem] * total,
            scratch_shapes=[pltpu.VMEM((-(-total // 8) * 8, half), jnp.float32)],
            compiler_params=params,
            cost_estimate=pl.CostEstimate(flops=2 * 16 * 256 * 512, bytes_accessed=512 * 1024, transcendentals=0),
        )(*pair_scores, linear, hits)

    with jax.named_scope("back"):
        result = outs[0]
        for j in range(1, total):
            result = result + swap(outs[j], "shard", j)
    return result.reshape(half)


def solution(mesh):
    return jax.shard_map(
        body,
        mesh=mesh,
        in_specs=(
            P(("groups", "shard", "cache", "pair")),
            P(("groups", "shard", "cache", "pair")),
            P(("shard", "cache"), None),
            P(("groups", "shard"), None),
            P("pair", None, None),
            P("pair", None),
        ),
        out_specs=P(("groups", "shard", "cache", "pair")),
        check_vma=False,
    )
```

```python
import functools

import jax
import jax.numpy as jnp
from jax import lax
from jax.experimental import pallas as pl
from jax.experimental.pallas import tpu as pltpu
from jax.sharding import PartitionSpec as P

K = 64
LANES = 128
PITCH = 72
CODE_BITS = 7
VMEM_LIMIT = 40 * 1024 * 1024
NT = (((1,), (1,)), ((), ()))
NN = (((1,), (0,)), ((), ()))


def dot(a, b, dims, **kw):
    return lax.dot_general(a, b, dims, preferred_element_type=jnp.float32, **kw)


def iota(shape, dim):
    return lax.broadcasted_iota(jnp.int32, shape, dim)


def ring(index, size):
    return lax.rem(index + size, size)


def pick_kernel(total, cap, *refs):
    users, (digits, states, out) = refs[:total], refs[total:]
    own_rows, width = states.shape
    slots = out.shape[0]
    readers = users[0].shape[1]
    me = lax.axis_index("shard")
    first = me * own_rows
    across = iota((readers, readers), 1)
    down = iota((readers, readers), 0)
    chosen = jnp.zeros((slots, own_rows), jnp.float32)
    for j in range(total):
        row = users[j][...]
        column = jnp.sum(jnp.where(across == down, row, 0), axis=1, keepdims=True)
        mine = (column >= first) & (column < first + own_rows)
        rank = jnp.sum(jnp.where((down < across) & mine, 1, 0), axis=0, keepdims=True)
        held = (row >= first) & (row < first + own_rows)
        slot = jnp.where(held, ring(me - j, total) * cap + rank, -1)
        to_slot = (iota((slots, readers), 0) == slot).astype(jnp.float32).astype(jnp.bfloat16)
        from_row = (iota((readers, own_rows), 1) + first == column).astype(jnp.float32).astype(jnp.bfloat16)
        chosen = chosen + dot(to_slot, from_row, NN)
    out[:, width:] = digits[...]
    out[:, :width] = dot(chosen.astype(jnp.bfloat16), states[...], NN).astype(jnp.bfloat16)


def turn_kernel(items_hbm, mats_hbm, states_hbm, ids_hbm, cands_hbm, rows32, rows16, mats, states, ids, digits, items, cands, sems):
    chunks = sems.shape[0] - 4
    wide = items.shape[1] // chunks
    item_fetches = [
        pltpu.make_async_copy(items_hbm.at[:, pl.ds(t * wide, wide)], items.at[:, pl.ds(t * wide, wide)], sems.at[t])
        for t in range(chunks)
    ]
    mats_fetch = pltpu.make_async_copy(mats_hbm, mats, sems.at[chunks])
    states_fetch = pltpu.make_async_copy(states_hbm, states, sems.at[chunks + 1])
    ids_fetch = pltpu.make_async_copy(ids_hbm, ids, sems.at[chunks + 2])
    cands_fetch = pltpu.make_async_copy(cands_hbm, cands, sems.at[chunks + 3])
    for copy in item_fetches + [mats_fetch, states_fetch, ids_fetch, cands_fetch]:
        copy.start()
    eye = (iota((LANES, LANES), 0) == iota((LANES, LANES), 1)).astype(jnp.bfloat16)
    for t in range(items.shape[1] // LANES):
        if t * LANES % wide == 0:
            item_fetches[t * LANES // wide].wait()
        turned = dot(eye, items[:, t * LANES:(t + 1) * LANES], NT)
        rows32[t * LANES:(t + 1) * LANES, :] = turned
        rows16[t * LANES:(t + 1) * LANES, :] = turned.astype(jnp.bfloat16)
    cands_fetch.wait()
    code = jnp.broadcast_to(cands[...], digits.shape)
    place = iota(digits.shape, 0)
    digit = jnp.where(place == 0, code >> CODE_BITS, jnp.where(place == 1, code & ((1 << CODE_BITS) - 1), 0))
    digits[...] = digit.astype(jnp.float32).astype(jnp.bfloat16)
    ids_fetch.wait()
    mats_fetch.wait()
    states_fetch.wait()


def pair_kernel(fields_hbm, rows32, rows16, mats, picked, out, fields, stacked, sem):
    del picked
    fields_fetch = pltpu.make_async_copy(fields_hbm, fields, sem)
    fields_fetch.start()
    pairs = mats.shape[2]
    steps = pairs // 2
    eye = (iota((steps, steps), 0) == iota((steps, steps), 1)).astype(jnp.bfloat16)
    for k in range(0, K, 2):
        sides = [mats[at, :, part * steps:(part + 1) * steps] for at in (k, k + 1) for part in range(2)]
        turned = dot(eye, jnp.concatenate(sides, axis=0), NT)
        stacked[pl.ds(k, steps, stride=PITCH), :] = turned[:, :LANES]
        stacked[pl.ds(k + 1, steps, stride=PITCH), :] = turned[:, LANES:]
    fields_fetch.wait()
    items = rows32.shape[1]
    blank = jnp.zeros((K, items), jnp.bfloat16)

    def two(p, total):
        fields_of = [(pl.multiple_of(fields[0, q] * K, K), pl.multiple_of(fields[1, q] * K, K)) for q in (p, p + steps)]
        left = stacked[pl.ds(pl.multiple_of(p * PITCH, 8), K), :].astype(jnp.bfloat16)
        first, second = [rows16[pl.ds(b, K), :] for _, b in fields_of]
        right = jnp.concatenate(
            [jnp.concatenate([first, blank], axis=1), jnp.concatenate([blank, second], axis=1)], axis=0
        )
        return total + dot(left, right, NN) * jnp.concatenate([rows32[pl.ds(a, K), :] for a, _ in fields_of], axis=1)

    sums = lax.fori_loop(0, steps, two, jnp.zeros((K, 2 * items), jnp.float32), unroll=32)
    line = jnp.sum(sums, axis=0, keepdims=True)
    out[...] = line[:, :items] + line[:, items:]


def thirds(x):
    high = x.astype(jnp.bfloat16)
    rest = x - high.astype(jnp.float32)
    middle = rest.astype(jnp.bfloat16)
    return high, middle, (rest - middle.astype(jnp.float32)).astype(jnp.bfloat16)


def linear_kernel(total, planes, cap, user_rows, *refs):
    states, refs = refs[:total], refs[total:]
    items, refs = refs[:planes], refs[planes:]
    users, (out, hits, wanted, linear) = refs[:total], refs[total:]
    slots = states[0].shape[0]
    own_rows, width = items[0].shape
    half = out.shape[1]
    me = lax.axis_index("shard")
    plane = lax.axis_index("cache")
    count = total * slots
    cands = []
    for j in range(total):
        wanted[j * slots:(j + 1) * slots, :] = states[j][:, :width]
        digits = states[j][:, width:].astype(jnp.float32)
        place = iota(digits.shape, 0)
        weight = jnp.where(place == 0, float(1 << CODE_BITS), jnp.where(place == 1, 1.0, 0.0))
        cands.append(jnp.sum(digits * weight, axis=0, keepdims=True).astype(jnp.int32))

    for q, rows in enumerate(items):
        for t, part in enumerate(thirds(dot(rows[...], wanted[...], NT))):
            linear[q * own_rows:(q + 1) * own_rows, t * count:(t + 1) * count] = part
    ids = [iota((own_rows, 1), 0) + (me * planes + ring(plane - q, planes)) * own_rows for q in range(planes)]
    item_ids = jnp.concatenate(ids, axis=0)
    readers = users[0].shape[1]
    across = iota((readers, readers), 1)
    down = iota((readers, readers), 0)
    asks = (iota((readers, half), 1) // (half // readers) == iota((readers, half), 0)).astype(jnp.float32).astype(jnp.bfloat16)
    for j in range(total):
        holder = users[j][...] >> (user_rows.bit_length() - 1)
        column = jnp.sum(jnp.where(across == down, holder, 0), axis=1, keepdims=True)
        rank = jnp.sum(jnp.where((down < across) & (column == holder), 1, 0), axis=0, keepdims=True)
        arrival = jnp.where(holder > me, me - holder + total, me - holder)
        slot = arrival * slots + ring(me - j, total) * cap + rank
        at_slot = (iota((count, readers), 0) == slot).astype(jnp.float32).astype(jnp.bfloat16)
        spread = dot(at_slot, asks, NN).astype(jnp.bfloat16)
        scores = dot(linear[...], jnp.concatenate([spread] * 3, axis=0), NN)
        hit = item_ids == cands[j]
        out[j:j + 1, :] = jnp.sum(jnp.where(hit, scores, 0.0), axis=0, keepdims=True)
        hits[:, j * half:(j + 1) * half] = hit.astype(jnp.float32).astype(jnp.bfloat16)


def score_kernel(total, planes, parts, *refs):
    pairs, (linear, hits), outs = refs[:planes * parts], refs[planes * parts:planes * parts + 2], refs[planes * parts + 2:]
    half = linear.shape[1]
    sums = [sum(pairs[(h + 1) * planes - 1 - q][...] for h in range(parts)) for q in range(planes)]
    row = jnp.concatenate(sums, axis=1)
    pieces = jnp.zeros((16, row.shape[1]), jnp.float32)
    for t, part in enumerate(thirds(row)):
        pieces = jnp.where(iota(pieces.shape, 0) == t, part.astype(jnp.float32), pieces)
    added = jnp.sum(dot(pieces.astype(jnp.bfloat16), hits[...], NN), axis=0, keepdims=True)
    for j in range(total):
        outs[j][...] = linear[j:j + 1, :] + added[:, j * half:(j + 1) * half]


def shift(x, axis, step):
    size = lax.axis_size(axis)
    return lax.ppermute(x, axis, [(s, (s + step) % size) for s in range(size)])


def body(cand_items, reader_users, item_table, user_states, pair_mats, pair_fields):
    total = lax.axis_size("shard")
    planes = lax.axis_size("cache")
    parts = lax.axis_size("pair")
    half = cand_items.shape[0]
    rows, width = item_table.shape
    readers = reader_users.shape[0]
    cap = 2 * ((readers + total - 1) // total)
    slots = -(-total * cap // 16) * 16
    count = pair_mats.shape[0]
    vmem = pl.BlockSpec(memory_space=pltpu.VMEM)
    hbm = pl.BlockSpec(memory_space=pltpu.HBM)
    anywhere = pl.BlockSpec(memory_space=pl.ANY)
    params = pltpu.CompilerParams(vmem_limit_bytes=VMEM_LIMIT)

    def in_hbm(x):
        return pltpu.with_memory_space_constraint(x, pltpu.HBM)

    with jax.named_scope("item_rows"):
        items = [item_table] + [shift(item_table, "cache", q) for q in range(1, planes)]

    with jax.named_scope("ids"):
        users = [shift(reader_users, "shard", j) for j in range(1, total)]

    with jax.named_scope("turn"):
        *turned, states_near, own_ids, digits = pl.pallas_call(
            turn_kernel,
            out_shape=(
                jax.ShapeDtypeStruct((width, rows), jnp.float32),
                jax.ShapeDtypeStruct((width, rows), jnp.bfloat16),
                jax.ShapeDtypeStruct((K, K, count), jnp.bfloat16),
                jax.ShapeDtypeStruct(user_states.shape, jnp.bfloat16),
                jax.ShapeDtypeStruct((1, readers), jnp.int32),
                jax.ShapeDtypeStruct((slots, half), jnp.bfloat16),
            ),
            in_specs=[hbm] * 5,
            out_specs=(vmem,) * 6,
            scratch_shapes=[
                pltpu.VMEM((rows, width), jnp.bfloat16),
                pltpu.VMEM((1, half), jnp.int32),
                pltpu.SemaphoreType.DMA((8,)),
            ],
            compiler_params=params,
            cost_estimate=pl.CostEstimate(flops=2 * rows * rows * width * 16, bytes_accessed=8 * 1024 * 1024, transcendentals=0),
        )(
            in_hbm(item_table),
            in_hbm(jnp.transpose(pair_mats, (1, 2, 0))),
            in_hbm(user_states),
            in_hbm(reader_users.reshape(1, readers)),
            in_hbm(cand_items.reshape(1, half)),
        )

    with jax.named_scope("states"):
        users_near = [own_ids] + [ids.reshape(1, readers) for ids in users]
        picked = pl.pallas_call(
            functools.partial(pick_kernel, total, cap),
            out_shape=jax.ShapeDtypeStruct((slots, width + half), jnp.bfloat16),
            in_specs=[vmem] * (total + 2),
            out_specs=vmem,
            compiler_params=params,
            cost_estimate=pl.CostEstimate(flops=2 * slots * rows * width, bytes_accessed=1024 * 1024, transcendentals=0),
        )(*users_near, digits, states_near)
        states = [picked] + [shift(picked, "shard", j) for j in range(1, total)]

    with jax.named_scope("pairs"):
        pair_parts = pl.pallas_call(
            pair_kernel,
            out_shape=jax.ShapeDtypeStruct((1, rows), jnp.float32),
            in_specs=[hbm, vmem, vmem, vmem, anywhere],
            out_specs=vmem,
            scratch_shapes=[
                pltpu.SMEM((2, count), jnp.int32),
                pltpu.VMEM((count // 2 * PITCH + K, LANES), jnp.float32),
                pltpu.SemaphoreType.DMA,
            ],
            compiler_params=params,
            cost_estimate=pl.CostEstimate(flops=2 * count * K * K * rows * 16, bytes_accessed=4 * 1024 * 1024, transcendentals=0),
        )(in_hbm(pair_fields.T), *turned, picked)
        pair_scores = {(0, 0): pair_parts}
        steps = [(q, h) for q in range(planes - 1, -1, -1) for h in range(parts) if q or h]
        for q, h in steps:
            perm = [
                (c * parts + d, (c + q) % planes * parts + (d + h) % parts) for c in range(planes) for d in range(parts)
            ]
            source, after = pair_parts, {1: 1, 2: 2}.get(len(pair_scores) - 1, 0)
            if after:
                source, states[after] = lax.optimization_barrier((pair_parts, states[after]))
            pair_scores[q, h] = lax.ppermute(source, ("cache", "pair"), perm)
        pair_scores = [pair_scores[q, h] for h in range(parts) for q in range(planes - 1, -1, -1)]

    with jax.named_scope("scores"):
        linear, hits = pl.pallas_call(
            functools.partial(linear_kernel, total, planes, cap, user_states.shape[0]),
            out_shape=(
                jax.ShapeDtypeStruct((total, half), jnp.float32),
                jax.ShapeDtypeStruct((planes * rows, total * half), jnp.bfloat16),
            ),
            in_specs=[vmem] * (2 * total + len(items)),
            out_specs=(vmem, vmem),
            scratch_shapes=[
                pltpu.VMEM((total * slots, width), jnp.bfloat16),
                pltpu.VMEM((planes * rows, 3 * total * slots), jnp.bfloat16),
            ],
            compiler_params=params,
            cost_estimate=pl.CostEstimate(flops=2 * 64 * 256 * width, bytes_accessed=2 * 1024 * 1024, transcendentals=0),
        )(*states, *items, *users_near)
        outs = pl.pallas_call(
            functools.partial(score_kernel, total, planes, parts),
            out_shape=[jax.ShapeDtypeStruct((1, half), jnp.float32)] * total,
            in_specs=[vmem] * (planes * parts + 2),
            out_specs=[vmem] * total,
            compiler_params=params,
            cost_estimate=pl.CostEstimate(flops=2 * 16 * 256 * 512, bytes_accessed=512 * 1024, transcendentals=0),
        )(*pair_scores, linear, hits)

    with jax.named_scope("back"):
        result = outs[0]
        for j in range(1, total):
            result = result + shift(outs[j], "shard", -j)
    return result.reshape(half)


def solution(mesh):
    return jax.shard_map(
        body,
        mesh=mesh,
        in_specs=(
            P(("groups", "shard", "cache", "pair")),
            P(("groups", "shard", "cache", "pair")),
            P(("shard", "cache"), None),
            P(("groups", "shard"), None),
            P("pair", None, None),
            P("pair", None),
        ),
        out_specs=P(("groups", "shard", "cache", "pair")),
        check_vma=False,
    )
```

```python
import functools

import jax
import jax.numpy as jnp
from jax import lax
from jax.experimental import pallas as pl
from jax.experimental.pallas import tpu as pltpu
from jax.sharding import PartitionSpec as P

K = 64
LANES = 128
PITCH = 72
CODE_BITS = 7
VMEM_LIMIT = 40 * 1024 * 1024
NT = (((1,), (1,)), ((), ()))
NN = (((1,), (0,)), ((), ()))


def dot(a, b, dims, **kw):
    return lax.dot_general(a, b, dims, preferred_element_type=jnp.float32, **kw)


def iota(shape, dim):
    return lax.broadcasted_iota(jnp.int32, shape, dim)


def ring(index, size):
    return lax.rem(index + size, size)


def pick_kernel(total, cap, *refs):
    users, (digits, states, out) = refs[:total], refs[total:]
    own_rows, width = states.shape
    slots = out.shape[0]
    readers = users[0].shape[1]
    me = lax.axis_index("shard")
    first = me * own_rows
    across = iota((readers, readers), 1)
    down = iota((readers, readers), 0)
    chosen = jnp.zeros((slots, own_rows), jnp.float32)
    for j in range(total):
        row = users[j][...]
        column = jnp.sum(jnp.where(across == down, row, 0), axis=1, keepdims=True)
        mine = (column >= first) & (column < first + own_rows)
        rank = jnp.sum(jnp.where((down < across) & mine, 1, 0), axis=0, keepdims=True)
        held = (row >= first) & (row < first + own_rows)
        slot = jnp.where(held, ring(me - j, total) * cap + rank, -1)
        to_slot = (iota((slots, readers), 0) == slot).astype(jnp.float32).astype(jnp.bfloat16)
        from_row = (iota((readers, own_rows), 1) + first == column).astype(jnp.float32).astype(jnp.bfloat16)
        chosen = chosen + dot(to_slot, from_row, NN)
    out[:, width:] = digits[...]
    out[:, :width] = dot(chosen.astype(jnp.bfloat16), states[...], NN).astype(jnp.bfloat16)


def turn_kernel(items_hbm, mats_hbm, states_hbm, ids_hbm, cands_hbm, rows32, rows16, mats, states, ids, digits, items, cands, sems):
    chunks = sems.shape[0] - 4
    wide = items.shape[1] // chunks
    item_fetches = [
        pltpu.make_async_copy(items_hbm.at[:, pl.ds(t * wide, wide)], items.at[:, pl.ds(t * wide, wide)], sems.at[t])
        for t in range(chunks)
    ]
    mats_fetch = pltpu.make_async_copy(mats_hbm, mats, sems.at[chunks])
    states_fetch = pltpu.make_async_copy(states_hbm, states, sems.at[chunks + 1])
    ids_fetch = pltpu.make_async_copy(ids_hbm, ids, sems.at[chunks + 2])
    cands_fetch = pltpu.make_async_copy(cands_hbm, cands, sems.at[chunks + 3])
    for copy in item_fetches + [mats_fetch, states_fetch, ids_fetch, cands_fetch]:
        copy.start()
    eye = (iota((LANES, LANES), 0) == iota((LANES, LANES), 1)).astype(jnp.bfloat16)
    for t in range(items.shape[1] // LANES):
        if t * LANES % wide == 0:
            item_fetches[t * LANES // wide].wait()
        turned = dot(eye, items[:, t * LANES:(t + 1) * LANES], NT)
        rows32[t * LANES:(t + 1) * LANES, :] = turned
        rows16[t * LANES:(t + 1) * LANES, :] = turned.astype(jnp.bfloat16)
    cands_fetch.wait()
    code = jnp.broadcast_to(cands[...], digits.shape)
    place = iota(digits.shape, 0)
    digit = jnp.where(place == 0, code >> CODE_BITS, jnp.where(place == 1, code & ((1 << CODE_BITS) - 1), 0))
    digits[...] = digit.astype(jnp.float32).astype(jnp.bfloat16)
    ids_fetch.wait()
    mats_fetch.wait()
    states_fetch.wait()


def pair_kernel(total, cap, slots, user_rows, *refs):
    users, (fields_hbm, rows32, rows16, mats, picked, out, places, fields, stacked, sem) = refs[:total], refs[total:]
    del picked
    fields_fetch = pltpu.make_async_copy(fields_hbm, fields, sem)
    fields_fetch.start()
    me = lax.axis_index("shard")
    readers, half = users[0].shape[1], places.shape[1]
    across = iota((readers, readers), 1)
    down = iota((readers, readers), 0)
    asks = (iota((readers, half), 1) // (half // readers) == iota((readers, half), 0)).astype(jnp.float32)
    for j in range(total):
        holder = users[j][...] >> (user_rows.bit_length() - 1)
        column = jnp.sum(jnp.where(across == down, holder, 0), axis=1, keepdims=True)
        rank = jnp.sum(jnp.where((down < across) & (column == holder), 1, 0), axis=0, keepdims=True)
        arrival = jnp.where(holder > me, me - holder + total, me - holder)
        slot = (arrival * slots + ring(me - j, total) * cap + rank).astype(jnp.float32)
        places[j:j + 1, :] = dot(slot, asks, NN, precision=lax.Precision.HIGHEST).astype(jnp.int32)
    pairs = mats.shape[2]
    steps = pairs // 2
    eye = (iota((steps, steps), 0) == iota((steps, steps), 1)).astype(jnp.bfloat16)
    for k in range(0, K, 2):
        sides = [mats[at, :, part * steps:(part + 1) * steps] for at in (k, k + 1) for part in range(2)]
        turned = dot(eye, jnp.concatenate(sides, axis=0), NT)
        stacked[pl.ds(k, steps, stride=PITCH), :] = turned[:, :LANES]
        stacked[pl.ds(k + 1, steps, stride=PITCH), :] = turned[:, LANES:]
    fields_fetch.wait()
    items = rows32.shape[1]
    blank = jnp.zeros((K, items), jnp.bfloat16)

    def two(p, total):
        fields_of = [(pl.multiple_of(fields[0, q] * K, K), pl.multiple_of(fields[1, q] * K, K)) for q in (p, p + steps)]
        left = stacked[pl.ds(pl.multiple_of(p * PITCH, 8), K), :].astype(jnp.bfloat16)
        first, second = [rows16[pl.ds(b, K), :] for _, b in fields_of]
        right = jnp.concatenate(
            [jnp.concatenate([first, blank], axis=1), jnp.concatenate([blank, second], axis=1)], axis=0
        )
        return total + dot(left, right, NN) * jnp.concatenate([rows32[pl.ds(a, K), :] for a, _ in fields_of], axis=1)

    sums = lax.fori_loop(0, steps, two, jnp.zeros((K, 2 * items), jnp.float32), unroll=32)
    line = jnp.sum(sums, axis=0, keepdims=True)
    out[...] = line[:, :items] + line[:, items:]


def thirds(x):
    high = x.astype(jnp.bfloat16)
    rest = x - high.astype(jnp.float32)
    middle = rest.astype(jnp.bfloat16)
    return high, middle, (rest - middle.astype(jnp.float32)).astype(jnp.bfloat16)


def linear_kernel(total, planes, *refs):
    states, refs = refs[:total], refs[total:]
    items, refs = refs[:planes], refs[planes:]
    places, out, hits, wanted, linear = refs
    slots = states[0].shape[0]
    own_rows, width = items[0].shape
    half = out.shape[1]
    me = lax.axis_index("shard")
    plane = lax.axis_index("cache")
    count = total * slots
    cands = []
    for j in range(total):
        wanted[j * slots:(j + 1) * slots, :] = states[j][:, :width]
        digits = states[j][:, width:].astype(jnp.float32)
        place = iota(digits.shape, 0)
        weight = jnp.where(place == 0, float(1 << CODE_BITS), jnp.where(place == 1, 1.0, 0.0))
        cands.append(jnp.sum(digits * weight, axis=0, keepdims=True).astype(jnp.int32))

    for q, rows in enumerate(items):
        for t, part in enumerate(thirds(dot(rows[...], wanted[...], NT))):
            linear[q * own_rows:(q + 1) * own_rows, t * count:(t + 1) * count] = part
    ids = [iota((own_rows, 1), 0) + (me * planes + ring(plane - q, planes)) * own_rows for q in range(planes)]
    item_ids = jnp.concatenate(ids, axis=0)
    for j in range(total):
        spread = (iota((count, half), 0) == places[j:j + 1, :]).astype(jnp.float32).astype(jnp.bfloat16)
        scores = dot(linear[...], jnp.concatenate([spread] * 3, axis=0), NN)
        hit = item_ids == cands[j]
        out[j:j + 1, :] = jnp.sum(jnp.where(hit, scores, 0.0), axis=0, keepdims=True)
        hits[:, j * half:(j + 1) * half] = hit.astype(jnp.float32).astype(jnp.bfloat16)


def score_kernel(total, planes, parts, *refs):
    pairs, (linear, hits), outs = refs[:planes * parts], refs[planes * parts:planes * parts + 2], refs[planes * parts + 2:]
    half = linear.shape[1]
    sums = [sum(pairs[(h + 1) * planes - 1 - q][...] for h in range(parts)) for q in range(planes)]
    row = jnp.concatenate(sums, axis=1)
    pieces = jnp.zeros((16, row.shape[1]), jnp.float32)
    for t, part in enumerate(thirds(row)):
        pieces = jnp.where(iota(pieces.shape, 0) == t, part.astype(jnp.float32), pieces)
    added = jnp.sum(dot(pieces.astype(jnp.bfloat16), hits[...], NN), axis=0, keepdims=True)
    for j in range(total):
        outs[j][...] = linear[j:j + 1, :] + added[:, j * half:(j + 1) * half]


def shift(x, axis, step):
    size = lax.axis_size(axis)
    return lax.ppermute(x, axis, [(s, (s + step) % size) for s in range(size)])


def body(cand_items, reader_users, item_table, user_states, pair_mats, pair_fields):
    total = lax.axis_size("shard")
    planes = lax.axis_size("cache")
    parts = lax.axis_size("pair")
    half = cand_items.shape[0]
    rows, width = item_table.shape
    readers = reader_users.shape[0]
    cap = 2 * ((readers + total - 1) // total)
    slots = -(-total * cap // 16) * 16
    count = pair_mats.shape[0]
    vmem = pl.BlockSpec(memory_space=pltpu.VMEM)
    hbm = pl.BlockSpec(memory_space=pltpu.HBM)
    anywhere = pl.BlockSpec(memory_space=pl.ANY)
    params = pltpu.CompilerParams(vmem_limit_bytes=VMEM_LIMIT)

    def in_hbm(x):
        return pltpu.with_memory_space_constraint(x, pltpu.HBM)

    with jax.named_scope("item_rows"):
        items = [item_table] + [shift(item_table, "cache", q) for q in range(1, planes)]

    with jax.named_scope("ids"):
        users = [shift(reader_users, "shard", j) for j in range(1, total)]

    with jax.named_scope("turn"):
        *turned, states_near, own_ids, digits = pl.pallas_call(
            turn_kernel,
            out_shape=(
                jax.ShapeDtypeStruct((width, rows), jnp.float32),
                jax.ShapeDtypeStruct((width, rows), jnp.bfloat16),
                jax.ShapeDtypeStruct((K, K, count), jnp.bfloat16),
                jax.ShapeDtypeStruct(user_states.shape, jnp.bfloat16),
                jax.ShapeDtypeStruct((1, readers), jnp.int32),
                jax.ShapeDtypeStruct((slots, half), jnp.bfloat16),
            ),
            in_specs=[hbm] * 5,
            out_specs=(vmem,) * 6,
            scratch_shapes=[
                pltpu.VMEM((rows, width), jnp.bfloat16),
                pltpu.VMEM((1, half), jnp.int32),
                pltpu.SemaphoreType.DMA((8,)),
            ],
            compiler_params=params,
            cost_estimate=pl.CostEstimate(flops=2 * rows * rows * width * 16, bytes_accessed=8 * 1024 * 1024, transcendentals=0),
        )(
            in_hbm(item_table),
            in_hbm(jnp.transpose(pair_mats, (1, 2, 0))),
            in_hbm(user_states),
            in_hbm(reader_users.reshape(1, readers)),
            in_hbm(cand_items.reshape(1, half)),
        )

    with jax.named_scope("states"):
        users_near = [own_ids] + [ids.reshape(1, readers) for ids in users]
        picked = pl.pallas_call(
            functools.partial(pick_kernel, total, cap),
            out_shape=jax.ShapeDtypeStruct((slots, width + half), jnp.bfloat16),
            in_specs=[vmem] * (total + 2),
            out_specs=vmem,
            compiler_params=params,
            cost_estimate=pl.CostEstimate(flops=2 * slots * rows * width, bytes_accessed=1024 * 1024, transcendentals=0),
        )(*users_near, digits, states_near)
        states = [picked] + [shift(picked, "shard", j) for j in range(1, total)]

    with jax.named_scope("pairs"):
        pair_parts, places = pl.pallas_call(
            functools.partial(pair_kernel, total, cap, slots, user_states.shape[0]),
            out_shape=(
                jax.ShapeDtypeStruct((1, rows), jnp.float32),
                jax.ShapeDtypeStruct((total, half), jnp.int32),
            ),
            in_specs=[vmem] * total + [hbm, vmem, vmem, vmem, anywhere],
            out_specs=(vmem, vmem),
            scratch_shapes=[
                pltpu.SMEM((2, count), jnp.int32),
                pltpu.VMEM((count // 2 * PITCH + K, LANES), jnp.float32),
                pltpu.SemaphoreType.DMA,
            ],
            compiler_params=params,
            cost_estimate=pl.CostEstimate(flops=2 * count * K * K * rows * 16, bytes_accessed=4 * 1024 * 1024, transcendentals=0),
        )(*users_near, in_hbm(pair_fields.T), *turned, picked)
        pair_scores = {(0, 0): pair_parts}
        steps = [(q, h) for q in range(planes - 1, -1, -1) for h in range(parts) if q or h]
        for q, h in steps:
            perm = [
                (c * parts + d, (c + q) % planes * parts + (d + h) % parts) for c in range(planes) for d in range(parts)
            ]
            source, after = pair_parts, {1: 1, 2: 2}.get(len(pair_scores) - 1, 0)
            if after:
                source, states[after] = lax.optimization_barrier((pair_parts, states[after]))
            pair_scores[q, h] = lax.ppermute(source, ("cache", "pair"), perm)
        pair_scores = [pair_scores[q, h] for h in range(parts) for q in range(planes - 1, -1, -1)]

    with jax.named_scope("scores"):
        linear, hits = pl.pallas_call(
            functools.partial(linear_kernel, total, planes),
            out_shape=(
                jax.ShapeDtypeStruct((total, half), jnp.float32),
                jax.ShapeDtypeStruct((planes * rows, total * half), jnp.bfloat16),
            ),
            in_specs=[vmem] * (total + len(items) + 1),
            out_specs=(vmem, vmem),
            scratch_shapes=[
                pltpu.VMEM((total * slots, width), jnp.bfloat16),
                pltpu.VMEM((planes * rows, 3 * total * slots), jnp.bfloat16),
            ],
            compiler_params=params,
            cost_estimate=pl.CostEstimate(flops=2 * 64 * 256 * width, bytes_accessed=2 * 1024 * 1024, transcendentals=0),
        )(*states, *items, places)
        outs = pl.pallas_call(
            functools.partial(score_kernel, total, planes, parts),
            out_shape=[jax.ShapeDtypeStruct((1, half), jnp.float32)] * total,
            in_specs=[vmem] * (planes * parts + 2),
            out_specs=[vmem] * total,
            compiler_params=params,
            cost_estimate=pl.CostEstimate(flops=2 * 16 * 256 * 512, bytes_accessed=512 * 1024, transcendentals=0),
        )(*pair_scores, linear, hits)

    with jax.named_scope("back"):
        result = outs[0]
        for j in range(1, total):
            result = result + shift(outs[j], "shard", -j)
    return result.reshape(half)


def solution(mesh):
    return jax.shard_map(
        body,
        mesh=mesh,
        in_specs=(
            P(("groups", "shard", "cache", "pair")),
            P(("groups", "shard", "cache", "pair")),
            P(("shard", "cache"), None),
            P(("groups", "shard"), None),
            P("pair", None, None),
            P("pair", None),
        ),
        out_specs=P(("groups", "shard", "cache", "pair")),
        check_vma=False,
    )
```

```python
import functools

import jax
import jax.numpy as jnp
from jax import lax
from jax.experimental import pallas as pl
from jax.experimental.pallas import tpu as pltpu
from jax.sharding import PartitionSpec as P

K = 64
LANES = 128
PITCH = 72
CODE_BITS = 7
VMEM_LIMIT = 40 * 1024 * 1024
NT = (((1,), (1,)), ((), ()))
NN = (((1,), (0,)), ((), ()))


def dot(a, b, dims, **kw):
    return lax.dot_general(a, b, dims, preferred_element_type=jnp.float32, **kw)


def iota(shape, dim):
    return lax.broadcasted_iota(jnp.int32, shape, dim)


def ring(index, size):
    return lax.rem(index + size, size)


def pick_kernel(total, cap, *refs):
    users, (digits, states, out) = refs[:total], refs[total:]
    own_rows, width = states.shape
    slots = out.shape[0]
    readers = users[0].shape[1]
    me = lax.axis_index("shard")
    first = me * own_rows
    across = iota((readers, readers), 1)
    down = iota((readers, readers), 0)
    chosen = jnp.zeros((slots, own_rows), jnp.float32)
    for mask in range(total):
        row = users[mask][...]
        column = jnp.sum(jnp.where(across == down, row, 0), axis=1, keepdims=True)
        mine = (column >= first) & (column < first + own_rows)
        rank = jnp.sum(jnp.where((down < across) & mine, 1, 0), axis=0, keepdims=True)
        held = (row >= first) & (row < first + own_rows)
        slot = jnp.where(held, (me ^ mask) * cap + rank, -1)
        to_slot = (iota((slots, readers), 0) == slot).astype(jnp.float32).astype(jnp.bfloat16)
        from_row = (iota((readers, own_rows), 1) + first == column).astype(jnp.float32).astype(jnp.bfloat16)
        chosen = chosen + dot(to_slot, from_row, NN)
    out[:, width:] = digits[...]
    out[:, :width] = dot(chosen.astype(jnp.bfloat16), states[...], NN).astype(jnp.bfloat16)


def turn_kernel(items_hbm, mats_hbm, states_hbm, ids_hbm, cands_hbm, rows32, rows16, mats, states, ids, digits, items, cands, sems):
    chunks = sems.shape[0] - 4
    wide = items.shape[1] // chunks
    item_fetches = [
        pltpu.make_async_copy(items_hbm.at[:, pl.ds(t * wide, wide)], items.at[:, pl.ds(t * wide, wide)], sems.at[t])
        for t in range(chunks)
    ]
    mats_fetch = pltpu.make_async_copy(mats_hbm, mats, sems.at[chunks])
    states_fetch = pltpu.make_async_copy(states_hbm, states, sems.at[chunks + 1])
    ids_fetch = pltpu.make_async_copy(ids_hbm, ids, sems.at[chunks + 2])
    cands_fetch = pltpu.make_async_copy(cands_hbm, cands, sems.at[chunks + 3])
    for copy in item_fetches + [mats_fetch, states_fetch, ids_fetch, cands_fetch]:
        copy.start()
    eye = (iota((LANES, LANES), 0) == iota((LANES, LANES), 1)).astype(jnp.bfloat16)
    for t in range(items.shape[1] // LANES):
        if t * LANES % wide == 0:
            item_fetches[t * LANES // wide].wait()
        turned = dot(eye, items[:, t * LANES:(t + 1) * LANES], NT)
        rows32[t * LANES:(t + 1) * LANES, :] = turned
        rows16[t * LANES:(t + 1) * LANES, :] = turned.astype(jnp.bfloat16)
    cands_fetch.wait()
    code = jnp.broadcast_to(cands[...], digits.shape)
    place = iota(digits.shape, 0)
    digit = jnp.where(place == 0, code >> CODE_BITS, jnp.where(place == 1, code & ((1 << CODE_BITS) - 1), 0))
    digits[...] = digit.astype(jnp.float32).astype(jnp.bfloat16)
    ids_fetch.wait()
    mats_fetch.wait()
    states_fetch.wait()


def pair_kernel(total, cap, slots, user_rows, *refs):
    users, (fields_hbm, rows32, rows16, mats, picked, out, places, fields, stacked, sem) = refs[:total], refs[total:]
    del picked
    fields_fetch = pltpu.make_async_copy(fields_hbm, fields, sem)
    fields_fetch.start()
    me = lax.axis_index("shard")
    readers, half = users[0].shape[1], places.shape[1]
    across = iota((readers, readers), 1)
    down = iota((readers, readers), 0)
    asks = (iota((readers, half), 1) // (half // readers) == iota((readers, half), 0)).astype(jnp.float32)
    for mask in range(total):
        holder = users[mask][...] >> (user_rows.bit_length() - 1)
        column = jnp.sum(jnp.where(across == down, holder, 0), axis=1, keepdims=True)
        rank = jnp.sum(jnp.where((down < across) & (column == holder), 1, 0), axis=0, keepdims=True)
        arrival = jnp.where(holder > me, me - holder + total, me - holder)
        slot = (arrival * slots + (me ^ mask) * cap + rank).astype(jnp.float32)
        row = dot(slot, asks, NN, precision=lax.Precision.HIGHEST).astype(jnp.int32)
        places[pl.ds(ring(me - (me ^ mask), total), 1), :] = row
    pairs = mats.shape[2]
    steps = pairs // 2
    eye = (iota((steps, steps), 0) == iota((steps, steps), 1)).astype(jnp.bfloat16)
    for k in range(0, K, 2):
        sides = [mats[at, :, part * steps:(part + 1) * steps] for at in (k, k + 1) for part in range(2)]
        turned = dot(eye, jnp.concatenate(sides, axis=0), NT)
        stacked[pl.ds(k, steps, stride=PITCH), :] = turned[:, :LANES]
        stacked[pl.ds(k + 1, steps, stride=PITCH), :] = turned[:, LANES:]
    fields_fetch.wait()
    items = rows32.shape[1]
    blank = jnp.zeros((K, items), jnp.bfloat16)

    def two(p, total):
        fields_of = [(pl.multiple_of(fields[0, q] * K, K), pl.multiple_of(fields[1, q] * K, K)) for q in (p, p + steps)]
        left = stacked[pl.ds(pl.multiple_of(p * PITCH, 8), K), :].astype(jnp.bfloat16)
        first, second = [rows16[pl.ds(b, K), :] for _, b in fields_of]
        right = jnp.concatenate(
            [jnp.concatenate([first, blank], axis=1), jnp.concatenate([blank, second], axis=1)], axis=0
        )
        return total + dot(left, right, NN) * jnp.concatenate([rows32[pl.ds(a, K), :] for a, _ in fields_of], axis=1)

    sums = lax.fori_loop(0, steps, two, jnp.zeros((K, 2 * items), jnp.float32), unroll=32)
    line = jnp.sum(sums, axis=0, keepdims=True)
    out[...] = line[:, :items] + line[:, items:]


def thirds(x):
    high = x.astype(jnp.bfloat16)
    rest = x - high.astype(jnp.float32)
    middle = rest.astype(jnp.bfloat16)
    return high, middle, (rest - middle.astype(jnp.float32)).astype(jnp.bfloat16)


def linear_kernel(total, planes, *refs):
    states, refs = refs[:total], refs[total:]
    items, refs = refs[:planes], refs[planes:]
    places, out, hits, wanted, linear = refs
    slots = states[0].shape[0]
    own_rows, width = items[0].shape
    half = out.shape[1]
    me = lax.axis_index("shard")
    plane = lax.axis_index("cache")
    count = total * slots
    cands = []
    for j in range(total):
        wanted[j * slots:(j + 1) * slots, :] = states[j][:, :width]
        digits = states[j][:, width:].astype(jnp.float32)
        place = iota(digits.shape, 0)
        weight = jnp.where(place == 0, float(1 << CODE_BITS), jnp.where(place == 1, 1.0, 0.0))
        cands.append(jnp.sum(digits * weight, axis=0, keepdims=True).astype(jnp.int32))

    for q, rows in enumerate(items):
        for t, part in enumerate(thirds(dot(rows[...], wanted[...], NT))):
            linear[q * own_rows:(q + 1) * own_rows, t * count:(t + 1) * count] = part
    ids = [iota((own_rows, 1), 0) + (me * planes + ring(plane - q, planes)) * own_rows for q in range(planes)]
    item_ids = jnp.concatenate(ids, axis=0)
    for j in range(total):
        spread = (iota((count, half), 0) == places[j:j + 1, :]).astype(jnp.float32).astype(jnp.bfloat16)
        scores = dot(linear[...], jnp.concatenate([spread] * 3, axis=0), NN)
        hit = item_ids == cands[j]
        out[j:j + 1, :] = jnp.sum(jnp.where(hit, scores, 0.0), axis=0, keepdims=True)
        hits[:, j * half:(j + 1) * half] = hit.astype(jnp.float32).astype(jnp.bfloat16)


def score_kernel(total, planes, parts, *refs):
    pairs, (linear, hits), outs = refs[:planes * parts], refs[planes * parts:planes * parts + 2], refs[planes * parts + 2:]
    half = linear.shape[1]
    sums = [sum(pairs[(h + 1) * planes - 1 - q][...] for h in range(parts)) for q in range(planes)]
    row = jnp.concatenate(sums, axis=1)
    pieces = jnp.zeros((16, row.shape[1]), jnp.float32)
    for t, part in enumerate(thirds(row)):
        pieces = jnp.where(iota(pieces.shape, 0) == t, part.astype(jnp.float32), pieces)
    added = jnp.sum(dot(pieces.astype(jnp.bfloat16), hits[...], NN), axis=0, keepdims=True)
    for j in range(total):
        outs[j][...] = linear[j:j + 1, :] + added[:, j * half:(j + 1) * half]


def shift(x, axis, step):
    size = lax.axis_size(axis)
    return lax.ppermute(x, axis, [(s, (s + step) % size) for s in range(size)])


def swap(x, axis, mask):
    return lax.ppermute(x, axis, [(s, s ^ mask) for s in range(lax.axis_size(axis))])


def body(cand_items, reader_users, item_table, user_states, pair_mats, pair_fields):
    total = lax.axis_size("shard")
    planes = lax.axis_size("cache")
    parts = lax.axis_size("pair")
    half = cand_items.shape[0]
    rows, width = item_table.shape
    readers = reader_users.shape[0]
    cap = 2 * ((readers + total - 1) // total)
    slots = -(-total * cap // 16) * 16
    count = pair_mats.shape[0]
    vmem = pl.BlockSpec(memory_space=pltpu.VMEM)
    hbm = pl.BlockSpec(memory_space=pltpu.HBM)
    anywhere = pl.BlockSpec(memory_space=pl.ANY)
    params = pltpu.CompilerParams(vmem_limit_bytes=VMEM_LIMIT)

    def in_hbm(x):
        return pltpu.with_memory_space_constraint(x, pltpu.HBM)

    with jax.named_scope("item_rows"):
        items = [item_table] + [shift(item_table, "cache", q) for q in range(1, planes)]

    with jax.named_scope("ids"):
        users = [swap(reader_users, "shard", mask) for mask in range(total - 1, 0, -1)]

    with jax.named_scope("turn"):
        *turned, states_near, own_ids, digits = pl.pallas_call(
            turn_kernel,
            out_shape=(
                jax.ShapeDtypeStruct((width, rows), jnp.float32),
                jax.ShapeDtypeStruct((width, rows), jnp.bfloat16),
                jax.ShapeDtypeStruct((K, K, count), jnp.bfloat16),
                jax.ShapeDtypeStruct(user_states.shape, jnp.bfloat16),
                jax.ShapeDtypeStruct((1, readers), jnp.int32),
                jax.ShapeDtypeStruct((slots, half), jnp.bfloat16),
            ),
            in_specs=[hbm] * 5,
            out_specs=(vmem,) * 6,
            scratch_shapes=[
                pltpu.VMEM((rows, width), jnp.bfloat16),
                pltpu.VMEM((1, half), jnp.int32),
                pltpu.SemaphoreType.DMA((8,)),
            ],
            compiler_params=params,
            cost_estimate=pl.CostEstimate(flops=2 * rows * rows * width * 16, bytes_accessed=8 * 1024 * 1024, transcendentals=0),
        )(
            in_hbm(item_table),
            in_hbm(jnp.transpose(pair_mats, (1, 2, 0))),
            in_hbm(user_states),
            in_hbm(reader_users.reshape(1, readers)),
            in_hbm(cand_items.reshape(1, half)),
        )

    with jax.named_scope("states"):
        users_near = [own_ids] + [ids.reshape(1, readers) for ids in users[::-1]]
        picked = pl.pallas_call(
            functools.partial(pick_kernel, total, cap),
            out_shape=jax.ShapeDtypeStruct((slots, width + half), jnp.bfloat16),
            in_specs=[vmem] * (total + 2),
            out_specs=vmem,
            compiler_params=params,
            cost_estimate=pl.CostEstimate(flops=2 * slots * rows * width, bytes_accessed=1024 * 1024, transcendentals=0),
        )(*users_near, digits, states_near)
        states = [picked] + [shift(picked, "shard", j) for j in range(1, total)]

    with jax.named_scope("pairs"):
        pair_parts, places = pl.pallas_call(
            functools.partial(pair_kernel, total, cap, slots, user_states.shape[0]),
            out_shape=(
                jax.ShapeDtypeStruct((1, rows), jnp.float32),
                jax.ShapeDtypeStruct((total, half), jnp.int32),
            ),
            in_specs=[vmem] * total + [hbm, vmem, vmem, vmem, anywhere],
            out_specs=(vmem, vmem),
            scratch_shapes=[
                pltpu.SMEM((2, count), jnp.int32),
                pltpu.VMEM((count // 2 * PITCH + K, LANES), jnp.float32),
                pltpu.SemaphoreType.DMA,
            ],
            compiler_params=params,
            cost_estimate=pl.CostEstimate(flops=2 * count * K * K * rows * 16, bytes_accessed=4 * 1024 * 1024, transcendentals=0),
        )(*users_near, in_hbm(pair_fields.T), *turned, picked)
        pair_scores = {(0, 0): pair_parts}
        steps = [(q, h) for q in range(planes - 1, -1, -1) for h in range(parts) if q or h]
        for q, h in steps:
            perm = [
                (c * parts + d, (c + q) % planes * parts + (d + h) % parts) for c in range(planes) for d in range(parts)
            ]
            source, after = pair_parts, {1: 1, 2: 2}.get(len(pair_scores) - 1, 0)
            if after:
                source, states[after] = lax.optimization_barrier((pair_parts, states[after]))
            pair_scores[q, h] = lax.ppermute(source, ("cache", "pair"), perm)
        pair_scores = [pair_scores[q, h] for h in range(parts) for q in range(planes - 1, -1, -1)]

    with jax.named_scope("scores"):
        linear, hits = pl.pallas_call(
            functools.partial(linear_kernel, total, planes),
            out_shape=(
                jax.ShapeDtypeStruct((total, half), jnp.float32),
                jax.ShapeDtypeStruct((planes * rows, total * half), jnp.bfloat16),
            ),
            in_specs=[vmem] * (total + len(items) + 1),
            out_specs=(vmem, vmem),
            scratch_shapes=[
                pltpu.VMEM((total * slots, width), jnp.bfloat16),
                pltpu.VMEM((planes * rows, 3 * total * slots), jnp.bfloat16),
            ],
            compiler_params=params,
            cost_estimate=pl.CostEstimate(flops=2 * 64 * 256 * width, bytes_accessed=2 * 1024 * 1024, transcendentals=0),
        )(*states, *items, places)
        outs = pl.pallas_call(
            functools.partial(score_kernel, total, planes, parts),
            out_shape=[jax.ShapeDtypeStruct((1, half), jnp.float32)] * total,
            in_specs=[vmem] * (planes * parts + 2),
            out_specs=[vmem] * total,
            compiler_params=params,
            cost_estimate=pl.CostEstimate(flops=2 * 16 * 256 * 512, bytes_accessed=512 * 1024, transcendentals=0),
        )(*pair_scores, linear, hits)

    with jax.named_scope("back"):
        result = outs[0]
        for j in range(1, total):
            result = result + shift(outs[j], "shard", -j)
    return result.reshape(half)


def solution(mesh):
    return jax.shard_map(
        body,
        mesh=mesh,
        in_specs=(
            P(("groups", "shard", "cache", "pair")),
            P(("groups", "shard", "cache", "pair")),
            P(("shard", "cache"), None),
            P(("groups", "shard"), None),
            P("pair", None, None),
            P("pair", None),
        ),
        out_specs=P(("groups", "shard", "cache", "pair")),
        check_vma=False,
    )
```

```python
import functools

import jax
import jax.numpy as jnp
from jax import lax
from jax.experimental import pallas as pl
from jax.experimental.pallas import tpu as pltpu
from jax.sharding import PartitionSpec as P

K = 64
LANES = 128
PITCH = 72
CODE_BITS = 7
VMEM_LIMIT = 40 * 1024 * 1024
NT = (((1,), (1,)), ((), ()))
NN = (((1,), (0,)), ((), ()))


def dot(a, b, dims, **kw):
    return lax.dot_general(a, b, dims, preferred_element_type=jnp.float32, **kw)


def iota(shape, dim):
    return lax.broadcasted_iota(jnp.int32, shape, dim)


def ring(index, size):
    return lax.rem(index + size, size)


def pick_kernel(total, cap, *refs):
    users, (digits, states, out) = refs[:total], refs[total:]
    own_rows, width = states.shape
    slots = out.shape[0]
    readers = users[0].shape[1]
    me = lax.axis_index("shard")
    first = me * own_rows
    across = iota((readers, readers), 1)
    down = iota((readers, readers), 0)
    chosen = jnp.zeros((slots, own_rows), jnp.float32)
    for mask in range(total):
        row = users[-mask % total][...]
        column = jnp.sum(jnp.where(across == down, row, 0), axis=1, keepdims=True)
        mine = (column >= first) & (column < first + own_rows)
        rank = jnp.sum(jnp.where((down < across) & mine, 1, 0), axis=0, keepdims=True)
        held = (row >= first) & (row < first + own_rows)
        slot = jnp.where(held, (me ^ mask) * cap + rank, -1)
        to_slot = (iota((slots, readers), 0) == slot).astype(jnp.float32).astype(jnp.bfloat16)
        from_row = (iota((readers, own_rows), 1) + first == column).astype(jnp.float32).astype(jnp.bfloat16)
        chosen = chosen + dot(to_slot, from_row, NN)
    out[:, width:] = digits[...]
    out[:, :width] = dot(chosen.astype(jnp.bfloat16), states[...], NN).astype(jnp.bfloat16)


def turn_kernel(items_hbm, mats_hbm, states_hbm, ids_hbm, cands_hbm, rows32, rows16, mats, states, ids, digits, items, cands, sems):
    chunks = sems.shape[0] - 4
    wide = items.shape[1] // chunks
    item_fetches = [
        pltpu.make_async_copy(items_hbm.at[:, pl.ds(t * wide, wide)], items.at[:, pl.ds(t * wide, wide)], sems.at[t])
        for t in range(chunks)
    ]
    mats_fetch = pltpu.make_async_copy(mats_hbm, mats, sems.at[chunks])
    states_fetch = pltpu.make_async_copy(states_hbm, states, sems.at[chunks + 1])
    ids_fetch = pltpu.make_async_copy(ids_hbm, ids, sems.at[chunks + 2])
    cands_fetch = pltpu.make_async_copy(cands_hbm, cands, sems.at[chunks + 3])
    for copy in item_fetches + [mats_fetch, states_fetch, ids_fetch, cands_fetch]:
        copy.start()
    eye = (iota((LANES, LANES), 0) == iota((LANES, LANES), 1)).astype(jnp.bfloat16)
    for t in range(items.shape[1] // LANES):
        if t * LANES % wide == 0:
            item_fetches[t * LANES // wide].wait()
        turned = dot(eye, items[:, t * LANES:(t + 1) * LANES], NT)
        rows32[t * LANES:(t + 1) * LANES, :] = turned
        rows16[t * LANES:(t + 1) * LANES, :] = turned.astype(jnp.bfloat16)
    cands_fetch.wait()
    code = jnp.broadcast_to(cands[...], digits.shape)
    place = iota(digits.shape, 0)
    digit = jnp.where(place == 0, code >> CODE_BITS, jnp.where(place == 1, code & ((1 << CODE_BITS) - 1), 0))
    digits[...] = digit.astype(jnp.float32).astype(jnp.bfloat16)
    ids_fetch.wait()
    mats_fetch.wait()
    states_fetch.wait()


def pair_kernel(total, cap, slots, user_rows, *refs):
    users, (fields_hbm, rows32, rows16, mats, picked, out, places, fields, stacked, sem) = refs[:total], refs[total:]
    del picked
    fields_fetch = pltpu.make_async_copy(fields_hbm, fields, sem)
    fields_fetch.start()
    me = lax.axis_index("shard")
    readers, half = users[0].shape[1], places.shape[1]
    across = iota((readers, readers), 1)
    down = iota((readers, readers), 0)
    asks = (iota((readers, half), 1) // (half // readers) == iota((readers, half), 0)).astype(jnp.float32)
    for mask in range(total):
        holder = users[-mask % total][...] >> (user_rows.bit_length() - 1)
        column = jnp.sum(jnp.where(across == down, holder, 0), axis=1, keepdims=True)
        rank = jnp.sum(jnp.where((down < across) & (column == holder), 1, 0), axis=0, keepdims=True)
        arrival = jnp.where(holder > me, me - holder + total, me - holder)
        slot = (arrival * slots + (me ^ mask) * cap + rank).astype(jnp.float32)
        row = dot(slot, asks, NN, precision=lax.Precision.HIGHEST).astype(jnp.int32)
        places[pl.ds(ring(me - (me ^ mask), total), 1), :] = row
    pairs = mats.shape[2]
    steps = pairs // 2
    eye = (iota((steps, steps), 0) == iota((steps, steps), 1)).astype(jnp.bfloat16)
    for k in range(0, K, 2):
        sides = [mats[at, :, part * steps:(part + 1) * steps] for at in (k, k + 1) for part in range(2)]
        turned = dot(eye, jnp.concatenate(sides, axis=0), NT)
        stacked[pl.ds(k, steps, stride=PITCH), :] = turned[:, :LANES]
        stacked[pl.ds(k + 1, steps, stride=PITCH), :] = turned[:, LANES:]
    fields_fetch.wait()
    items = rows32.shape[1]
    blank = jnp.zeros((K, items), jnp.bfloat16)

    def two(p, total):
        fields_of = [(pl.multiple_of(fields[0, q] * K, K), pl.multiple_of(fields[1, q] * K, K)) for q in (p, p + steps)]
        left = stacked[pl.ds(pl.multiple_of(p * PITCH, 8), K), :].astype(jnp.bfloat16)
        first, second = [rows16[pl.ds(b, K), :] for _, b in fields_of]
        right = jnp.concatenate(
            [jnp.concatenate([first, blank], axis=1), jnp.concatenate([blank, second], axis=1)], axis=0
        )
        return total + dot(left, right, NN) * jnp.concatenate([rows32[pl.ds(a, K), :] for a, _ in fields_of], axis=1)

    sums = lax.fori_loop(0, steps, two, jnp.zeros((K, 2 * items), jnp.float32), unroll=32)
    line = jnp.sum(sums, axis=0, keepdims=True)
    out[...] = line[:, :items] + line[:, items:]


def thirds(x):
    high = x.astype(jnp.bfloat16)
    rest = x - high.astype(jnp.float32)
    middle = rest.astype(jnp.bfloat16)
    return high, middle, (rest - middle.astype(jnp.float32)).astype(jnp.bfloat16)


def linear_kernel(total, planes, *refs):
    states, refs = refs[:total], refs[total:]
    items, refs = refs[:planes], refs[planes:]
    places, out, hits, wanted, linear = refs
    slots = states[0].shape[0]
    own_rows, width = items[0].shape
    half = out.shape[1]
    me = lax.axis_index("shard")
    plane = lax.axis_index("cache")
    count = total * slots
    cands = []
    for j in range(total):
        wanted[j * slots:(j + 1) * slots, :] = states[j][:, :width]
        digits = states[j][:, width:].astype(jnp.float32)
        place = iota(digits.shape, 0)
        weight = jnp.where(place == 0, float(1 << CODE_BITS), jnp.where(place == 1, 1.0, 0.0))
        cands.append(jnp.sum(digits * weight, axis=0, keepdims=True).astype(jnp.int32))

    for q, rows in enumerate(items):
        for t, part in enumerate(thirds(dot(rows[...], wanted[...], NT))):
            linear[q * own_rows:(q + 1) * own_rows, t * count:(t + 1) * count] = part
    ids = [iota((own_rows, 1), 0) + (me * planes + ring(plane - q, planes)) * own_rows for q in range(planes)]
    item_ids = jnp.concatenate(ids, axis=0)
    for j in range(total):
        spread = (iota((count, half), 0) == places[j:j + 1, :]).astype(jnp.float32).astype(jnp.bfloat16)
        scores = dot(linear[...], jnp.concatenate([spread] * 3, axis=0), NN)
        hit = item_ids == cands[j]
        out[j:j + 1, :] = jnp.sum(jnp.where(hit, scores, 0.0), axis=0, keepdims=True)
        hits[:, j * half:(j + 1) * half] = hit.astype(jnp.float32).astype(jnp.bfloat16)


def score_kernel(total, planes, parts, *refs):
    pairs, (linear, hits), outs = refs[:planes * parts], refs[planes * parts:planes * parts + 2], refs[planes * parts + 2:]
    half = linear.shape[1]
    sums = [sum(pairs[(h + 1) * planes - 1 - q][...] for h in range(parts)) for q in range(planes)]
    row = jnp.concatenate(sums, axis=1)
    pieces = jnp.zeros((16, row.shape[1]), jnp.float32)
    for t, part in enumerate(thirds(row)):
        pieces = jnp.where(iota(pieces.shape, 0) == t, part.astype(jnp.float32), pieces)
    added = jnp.sum(dot(pieces.astype(jnp.bfloat16), hits[...], NN), axis=0, keepdims=True)
    for j in range(total):
        outs[j][...] = linear[j:j + 1, :] + added[:, j * half:(j + 1) * half]


def shift(x, axis, step):
    size = lax.axis_size(axis)
    return lax.ppermute(x, axis, [(s, (s + step) % size) for s in range(size)])


def swap(x, axis, mask):
    return lax.ppermute(x, axis, [(s, s ^ mask) for s in range(lax.axis_size(axis))])


def body(cand_items, reader_users, item_table, user_states, pair_mats, pair_fields):
    total = lax.axis_size("shard")
    planes = lax.axis_size("cache")
    parts = lax.axis_size("pair")
    half = cand_items.shape[0]
    rows, width = item_table.shape
    readers = reader_users.shape[0]
    cap = 2 * ((readers + total - 1) // total)
    slots = -(-total * cap // 16) * 16
    count = pair_mats.shape[0]
    vmem = pl.BlockSpec(memory_space=pltpu.VMEM)
    hbm = pl.BlockSpec(memory_space=pltpu.HBM)
    anywhere = pl.BlockSpec(memory_space=pl.ANY)
    params = pltpu.CompilerParams(vmem_limit_bytes=VMEM_LIMIT)

    def in_hbm(x):
        return pltpu.with_memory_space_constraint(x, pltpu.HBM)

    with jax.named_scope("item_rows"):
        items = [item_table] + [shift(item_table, "cache", q) for q in range(1, planes)]

    with jax.named_scope("ids"):
        users = [swap(reader_users, "shard", mask) for mask in range(total - 1, 0, -1)]

    with jax.named_scope("turn"):
        *turned, states_near, own_ids, digits = pl.pallas_call(
            turn_kernel,
            out_shape=(
                jax.ShapeDtypeStruct((width, rows), jnp.float32),
                jax.ShapeDtypeStruct((width, rows), jnp.bfloat16),
                jax.ShapeDtypeStruct((K, K, count), jnp.bfloat16),
                jax.ShapeDtypeStruct(user_states.shape, jnp.bfloat16),
                jax.ShapeDtypeStruct((1, readers), jnp.int32),
                jax.ShapeDtypeStruct((slots, half), jnp.bfloat16),
            ),
            in_specs=[hbm] * 5,
            out_specs=(vmem,) * 6,
            scratch_shapes=[
                pltpu.VMEM((rows, width), jnp.bfloat16),
                pltpu.VMEM((1, half), jnp.int32),
                pltpu.SemaphoreType.DMA((8,)),
            ],
            compiler_params=params,
            cost_estimate=pl.CostEstimate(flops=2 * rows * rows * width * 16, bytes_accessed=8 * 1024 * 1024, transcendentals=0),
        )(
            in_hbm(item_table),
            in_hbm(jnp.transpose(pair_mats, (1, 2, 0))),
            in_hbm(user_states),
            in_hbm(reader_users.reshape(1, readers)),
            in_hbm(cand_items.reshape(1, half)),
        )

    with jax.named_scope("states"):
        users_near = [own_ids] + [ids.reshape(1, readers) for ids in users]
        picked = pl.pallas_call(
            functools.partial(pick_kernel, total, cap),
            out_shape=jax.ShapeDtypeStruct((slots, width + half), jnp.bfloat16),
            in_specs=[vmem] * (total + 2),
            out_specs=vmem,
            compiler_params=params,
            cost_estimate=pl.CostEstimate(flops=2 * slots * rows * width, bytes_accessed=1024 * 1024, transcendentals=0),
        )(*users_near, digits, states_near)
        states = [picked] + [shift(picked, "shard", j) for j in range(1, total)]

    with jax.named_scope("pairs"):
        pair_parts, places = pl.pallas_call(
            functools.partial(pair_kernel, total, cap, slots, user_states.shape[0]),
            out_shape=(
                jax.ShapeDtypeStruct((1, rows), jnp.float32),
                jax.ShapeDtypeStruct((total, half), jnp.int32),
            ),
            in_specs=[vmem] * total + [hbm, vmem, vmem, vmem, anywhere],
            out_specs=(vmem, vmem),
            scratch_shapes=[
                pltpu.SMEM((2, count), jnp.int32),
                pltpu.VMEM((count // 2 * PITCH + K, LANES), jnp.float32),
                pltpu.SemaphoreType.DMA,
            ],
            compiler_params=params,
            cost_estimate=pl.CostEstimate(flops=2 * count * K * K * rows * 16, bytes_accessed=4 * 1024 * 1024, transcendentals=0),
        )(*users_near, in_hbm(pair_fields.T), *turned, picked)
        pair_scores = {(0, 0): pair_parts}
        steps = [(q, h) for q in range(planes - 1, -1, -1) for h in range(parts) if q or h]
        for q, h in steps:
            perm = [
                (c * parts + d, (c + q) % planes * parts + (d + h) % parts) for c in range(planes) for d in range(parts)
            ]
            source, after = pair_parts, {1: 1, 2: 2}.get(len(pair_scores) - 1, 0)
            if after:
                source, states[after] = lax.optimization_barrier((pair_parts, states[after]))
            pair_scores[q, h] = lax.ppermute(source, ("cache", "pair"), perm)
        pair_scores = [pair_scores[q, h] for h in range(parts) for q in range(planes - 1, -1, -1)]

    with jax.named_scope("scores"):
        linear, hits = pl.pallas_call(
            functools.partial(linear_kernel, total, planes),
            out_shape=(
                jax.ShapeDtypeStruct((total, half), jnp.float32),
                jax.ShapeDtypeStruct((planes * rows, total * half), jnp.bfloat16),
            ),
            in_specs=[vmem] * (total + len(items) + 1),
            out_specs=(vmem, vmem),
            scratch_shapes=[
                pltpu.VMEM((total * slots, width), jnp.bfloat16),
                pltpu.VMEM((planes * rows, 3 * total * slots), jnp.bfloat16),
            ],
            compiler_params=params,
            cost_estimate=pl.CostEstimate(flops=2 * 64 * 256 * width, bytes_accessed=2 * 1024 * 1024, transcendentals=0),
        )(*states, *items, places)
        outs = pl.pallas_call(
            functools.partial(score_kernel, total, planes, parts),
            out_shape=[jax.ShapeDtypeStruct((1, half), jnp.float32)] * total,
            in_specs=[vmem] * (planes * parts + 2),
            out_specs=[vmem] * total,
            compiler_params=params,
            cost_estimate=pl.CostEstimate(flops=2 * 16 * 256 * 512, bytes_accessed=512 * 1024, transcendentals=0),
        )(*pair_scores, linear, hits)

    with jax.named_scope("back"):
        result = outs[0]
        for j in range(1, total):
            result = result + shift(outs[j], "shard", -j)
    return result.reshape(half)


def solution(mesh):
    return jax.shard_map(
        body,
        mesh=mesh,
        in_specs=(
            P(("groups", "shard", "cache", "pair")),
            P(("groups", "shard", "cache", "pair")),
            P(("shard", "cache"), None),
            P(("groups", "shard"), None),
            P("pair", None, None),
            P("pair", None),
        ),
        out_specs=P(("groups", "shard", "cache", "pair")),
        check_vma=False,
    )
```

```python
import functools

import jax
import jax.numpy as jnp
from jax import lax
from jax.experimental import pallas as pl
from jax.experimental.pallas import tpu as pltpu
from jax.sharding import PartitionSpec as P

K = 64
LANES = 128
PITCH = 72
CODE_BITS = 7
VMEM_LIMIT = 40 * 1024 * 1024
NT = (((1,), (1,)), ((), ()))
NN = (((1,), (0,)), ((), ()))


def dot(a, b, dims, **kw):
    return lax.dot_general(a, b, dims, preferred_element_type=jnp.float32, **kw)


def iota(shape, dim):
    return lax.broadcasted_iota(jnp.int32, shape, dim)


def ring(index, size):
    return lax.rem(index + size, size)


def pick_kernel(total, cap, *refs):
    users, (digits, states, out) = refs[:total], refs[total:]
    own_rows, width = states.shape
    slots = out.shape[0]
    readers = users[0].shape[1]
    me = lax.axis_index("shard")
    first = me * own_rows
    across = iota((readers, readers), 1)
    down = iota((readers, readers), 0)
    chosen = jnp.zeros((slots, own_rows), jnp.float32)
    for j in range(total):
        row = users[j][...]
        column = jnp.sum(jnp.where(across == down, row, 0), axis=1, keepdims=True)
        mine = (column >= first) & (column < first + own_rows)
        rank = jnp.sum(jnp.where((down < across) & mine, 1, 0), axis=0, keepdims=True)
        held = (row >= first) & (row < first + own_rows)
        slot = jnp.where(held, ring(me - j, total) * cap + rank, -1)
        to_slot = (iota((slots, readers), 0) == slot).astype(jnp.float32).astype(jnp.bfloat16)
        from_row = (iota((readers, own_rows), 1) + first == column).astype(jnp.float32).astype(jnp.bfloat16)
        chosen = chosen + dot(to_slot, from_row, NN)
    out[:, width:] = digits[...]
    out[:, :width] = dot(chosen.astype(jnp.bfloat16), states[...], NN).astype(jnp.bfloat16)


def turn_kernel(items_hbm, mats_hbm, states_hbm, ids_hbm, cands_hbm, rows32, rows16, mats, states, ids, digits, items, cands, sems):
    chunks = sems.shape[0] - 4
    wide = items.shape[1] // chunks
    item_fetches = [
        pltpu.make_async_copy(items_hbm.at[:, pl.ds(t * wide, wide)], items.at[:, pl.ds(t * wide, wide)], sems.at[t])
        for t in range(chunks)
    ]
    mats_fetch = pltpu.make_async_copy(mats_hbm, mats, sems.at[chunks])
    states_fetch = pltpu.make_async_copy(states_hbm, states, sems.at[chunks + 1])
    ids_fetch = pltpu.make_async_copy(ids_hbm, ids, sems.at[chunks + 2])
    cands_fetch = pltpu.make_async_copy(cands_hbm, cands, sems.at[chunks + 3])
    for copy in item_fetches + [mats_fetch, states_fetch, ids_fetch, cands_fetch]:
        copy.start()
    eye = (iota((LANES, LANES), 0) == iota((LANES, LANES), 1)).astype(jnp.bfloat16)
    for t in range(items.shape[1] // LANES):
        if t * LANES % wide == 0:
            item_fetches[t * LANES // wide].wait()
        turned = dot(eye, items[:, t * LANES:(t + 1) * LANES], NT)
        rows32[t * LANES:(t + 1) * LANES, :] = turned
        rows16[t * LANES:(t + 1) * LANES, :] = turned.astype(jnp.bfloat16)
    cands_fetch.wait()
    code = jnp.broadcast_to(cands[...], digits.shape)
    place = iota(digits.shape, 0)
    digit = jnp.where(place == 0, code >> CODE_BITS, jnp.where(place == 1, code & ((1 << CODE_BITS) - 1), 0))
    digits[...] = digit.astype(jnp.float32).astype(jnp.bfloat16)
    ids_fetch.wait()
    mats_fetch.wait()
    states_fetch.wait()


def pair_kernel(total, cap, slots, user_rows, *refs):
    users, (fields_hbm, rows32, rows16, mats, picked, out, places, fields, stacked, sem) = refs[:total], refs[total:]
    del picked
    fields_fetch = pltpu.make_async_copy(fields_hbm, fields, sem)
    fields_fetch.start()
    me = lax.axis_index("shard")
    readers, half = users[0].shape[1], places.shape[1]
    across = iota((readers, readers), 1)
    down = iota((readers, readers), 0)
    asks = (iota((readers, half), 1) // (half // readers) == iota((readers, half), 0)).astype(jnp.float32)
    for j in range(total):
        holder = users[j][...] >> (user_rows.bit_length() - 1)
        column = jnp.sum(jnp.where(across == down, holder, 0), axis=1, keepdims=True)
        rank = jnp.sum(jnp.where((down < across) & (column == holder), 1, 0), axis=0, keepdims=True)
        arrival = jnp.where(holder > me, me - holder + total, me - holder)
        slot = (arrival * slots + ring(me - j, total) * cap + rank).astype(jnp.float32)
        places[j:j + 1, :] = dot(slot, asks, NN, precision=lax.Precision.HIGHEST).astype(jnp.int32)
    pairs = mats.shape[2]
    steps = pairs // 2
    eye = (iota((steps, steps), 0) == iota((steps, steps), 1)).astype(jnp.bfloat16)
    for k in range(0, K, 2):
        sides = [mats[at, :, part * steps:(part + 1) * steps] for at in (k, k + 1) for part in range(2)]
        turned = dot(eye, jnp.concatenate(sides, axis=0), NT)
        stacked[pl.ds(k, steps, stride=PITCH), :] = turned[:, :LANES]
        stacked[pl.ds(k + 1, steps, stride=PITCH), :] = turned[:, LANES:]
    fields_fetch.wait()
    items = rows32.shape[1]
    blank = jnp.zeros((K, items), jnp.bfloat16)

    def two(p, total):
        fields_of = [(pl.multiple_of(fields[0, q] * K, K), pl.multiple_of(fields[1, q] * K, K)) for q in (p, p + steps)]
        left = stacked[pl.ds(pl.multiple_of(p * PITCH, 8), K), :].astype(jnp.bfloat16)
        first, second = [rows16[pl.ds(b, K), :] for _, b in fields_of]
        right = jnp.concatenate(
            [jnp.concatenate([first, blank], axis=1), jnp.concatenate([blank, second], axis=1)], axis=0
        )
        return total + dot(left, right, NN) * jnp.concatenate([rows32[pl.ds(a, K), :] for a, _ in fields_of], axis=1)

    sums = lax.fori_loop(0, steps, two, jnp.zeros((K, 2 * items), jnp.float32), unroll=32)
    line = jnp.sum(sums, axis=0, keepdims=True)
    out[...] = line[:, :items] + line[:, items:]


def thirds(x):
    high = x.astype(jnp.bfloat16)
    rest = x - high.astype(jnp.float32)
    middle = rest.astype(jnp.bfloat16)
    return high, middle, (rest - middle.astype(jnp.float32)).astype(jnp.bfloat16)


def linear_kernel(total, planes, *refs):
    states, refs = refs[:total], refs[total:]
    items, refs = refs[:planes], refs[planes:]
    places, out, hits, wanted, linear = refs
    slots = states[0].shape[0]
    own_rows, width = items[0].shape
    half = out.shape[1]
    me = lax.axis_index("shard")
    plane = lax.axis_index("cache")
    count = total * slots
    cands = []
    for j in range(total):
        wanted[j * slots:(j + 1) * slots, :] = states[j][:, :width]
        digits = states[j][:, width:].astype(jnp.float32)
        place = iota(digits.shape, 0)
        weight = jnp.where(place == 0, float(1 << CODE_BITS), jnp.where(place == 1, 1.0, 0.0))
        cands.append(jnp.sum(digits * weight, axis=0, keepdims=True).astype(jnp.int32))

    for q, rows in enumerate(items):
        for t, part in enumerate(thirds(dot(rows[...], wanted[...], NT))):
            linear[q * own_rows:(q + 1) * own_rows, t * count:(t + 1) * count] = part
    ids = [iota((own_rows, 1), 0) + (me * planes + ring(plane - q, planes)) * own_rows for q in range(planes)]
    item_ids = jnp.concatenate(ids, axis=0)
    for j in range(total):
        spread = (iota((count, half), 0) == places[j:j + 1, :]).astype(jnp.float32).astype(jnp.bfloat16)
        scores = dot(linear[...], jnp.concatenate([spread] * 3, axis=0), NN)
        hit = item_ids == cands[j]
        out[j:j + 1, :] = jnp.sum(jnp.where(hit, scores, 0.0), axis=0, keepdims=True)
        hits[:, j * half:(j + 1) * half] = hit.astype(jnp.float32).astype(jnp.bfloat16)


def score_kernel(total, planes, parts, *refs):
    pairs, (linear, hits), outs = refs[:planes * parts], refs[planes * parts:planes * parts + 2], refs[planes * parts + 2:]
    half = linear.shape[1]
    sums = [sum(pairs[(h + 1) * planes - 1 - q][...] for h in range(parts)) for q in range(planes)]
    row = jnp.concatenate(sums, axis=1)
    pieces = jnp.zeros((16, row.shape[1]), jnp.float32)
    for t, part in enumerate(thirds(row)):
        pieces = jnp.where(iota(pieces.shape, 0) == t, part.astype(jnp.float32), pieces)
    added = jnp.sum(dot(pieces.astype(jnp.bfloat16), hits[...], NN), axis=0, keepdims=True)
    for j in range(total):
        outs[j][...] = linear[j:j + 1, :] + added[:, j * half:(j + 1) * half]


def shift(x, axis, step):
    size = lax.axis_size(axis)
    return lax.ppermute(x, axis, [(s, (s + step) % size) for s in range(size)])


def body(cand_items, reader_users, item_table, user_states, pair_mats, pair_fields):
    total = lax.axis_size("shard")
    planes = lax.axis_size("cache")
    parts = lax.axis_size("pair")
    half = cand_items.shape[0]
    rows, width = item_table.shape
    readers = reader_users.shape[0]
    cap = 2 * ((readers + total - 1) // total)
    slots = -(-total * cap // 16) * 16
    count = pair_mats.shape[0]
    vmem = pl.BlockSpec(memory_space=pltpu.VMEM)
    hbm = pl.BlockSpec(memory_space=pltpu.HBM)
    anywhere = pl.BlockSpec(memory_space=pl.ANY)
    params = pltpu.CompilerParams(vmem_limit_bytes=VMEM_LIMIT)

    def in_hbm(x):
        return pltpu.with_memory_space_constraint(x, pltpu.HBM)

    with jax.named_scope("item_rows"):
        items = [item_table] + [shift(item_table, "cache", q) for q in range(1, planes)]

    with jax.named_scope("ids"):
        users = [shift(reader_users, "shard", j) for j in range(1, total)]

    with jax.named_scope("turn"):
        *turned, states_near, own_ids, digits = pl.pallas_call(
            turn_kernel,
            out_shape=(
                jax.ShapeDtypeStruct((width, rows), jnp.float32),
                jax.ShapeDtypeStruct((width, rows), jnp.bfloat16),
                jax.ShapeDtypeStruct((K, K, count), jnp.bfloat16),
                jax.ShapeDtypeStruct(user_states.shape, jnp.bfloat16),
                jax.ShapeDtypeStruct((1, readers), jnp.int32),
                jax.ShapeDtypeStruct((slots, half), jnp.bfloat16),
            ),
            in_specs=[hbm] * 5,
            out_specs=(vmem,) * 6,
            scratch_shapes=[
                pltpu.VMEM((rows, width), jnp.bfloat16),
                pltpu.VMEM((1, half), jnp.int32),
                pltpu.SemaphoreType.DMA((8,)),
            ],
            compiler_params=params,
            cost_estimate=pl.CostEstimate(flops=2 * rows * rows * width * 16, bytes_accessed=8 * 1024 * 1024, transcendentals=0),
        )(
            in_hbm(item_table),
            in_hbm(jnp.transpose(pair_mats, (1, 2, 0))),
            in_hbm(user_states),
            in_hbm(reader_users.reshape(1, readers)),
            in_hbm(cand_items.reshape(1, half)),
        )

    with jax.named_scope("states"):
        users_near = [own_ids] + [ids.reshape(1, readers) for ids in users]
        picked = pl.pallas_call(
            functools.partial(pick_kernel, total, cap),
            out_shape=jax.ShapeDtypeStruct((slots, width + half), jnp.bfloat16),
            in_specs=[vmem] * (total + 2),
            out_specs=vmem,
            compiler_params=params,
            cost_estimate=pl.CostEstimate(flops=2 * slots * rows * width, bytes_accessed=1024 * 1024, transcendentals=0),
        )(*users_near, digits, states_near)
        states = [picked] + [shift(picked, "shard", j) for j in range(1, total)]

    with jax.named_scope("pairs"):
        pair_parts, places = pl.pallas_call(
            functools.partial(pair_kernel, total, cap, slots, user_states.shape[0]),
            out_shape=(
                jax.ShapeDtypeStruct((1, rows), jnp.float32),
                jax.ShapeDtypeStruct((total, half), jnp.int32),
            ),
            in_specs=[vmem] * total + [hbm, vmem, vmem, vmem, anywhere],
            out_specs=(vmem, vmem),
            scratch_shapes=[
                pltpu.SMEM((2, count), jnp.int32),
                pltpu.VMEM((count // 2 * PITCH + K, LANES), jnp.float32),
                pltpu.SemaphoreType.DMA,
            ],
            compiler_params=params,
            cost_estimate=pl.CostEstimate(flops=2 * count * K * K * rows * 16, bytes_accessed=4 * 1024 * 1024, transcendentals=0),
        )(*users_near, in_hbm(pair_fields.T), *turned, picked)
        pair_scores = {(0, 0): pair_parts}
        steps = [(q, h) for q in range(planes - 1, -1, -1) for h in range(parts) if q or h]
        for q, h in steps:
            perm = [
                (c * parts + d, (c + q) % planes * parts + (d + h) % parts) for c in range(planes) for d in range(parts)
            ]
            source, after = pair_parts, {1: 1, 2: 2}.get(len(pair_scores) - 1, 0)
            if after:
                source, states[after] = lax.optimization_barrier((pair_parts, states[after]))
            pair_scores[q, h] = lax.ppermute(source, ("cache", "pair"), perm)
        pair_scores = [pair_scores[q, h] for h in range(parts) for q in range(planes - 1, -1, -1)]

    with jax.named_scope("scores"):
        linear, hits = pl.pallas_call(
            functools.partial(linear_kernel, total, planes),
            out_shape=(
                jax.ShapeDtypeStruct((total, half), jnp.float32),
                jax.ShapeDtypeStruct((planes * rows, total * half), jnp.bfloat16),
            ),
            in_specs=[vmem] * (total + len(items) + 1),
            out_specs=(vmem, vmem),
            scratch_shapes=[
                pltpu.VMEM((total * slots, width), jnp.bfloat16),
                pltpu.VMEM((planes * rows, 3 * total * slots), jnp.bfloat16),
            ],
            compiler_params=params,
            cost_estimate=pl.CostEstimate(flops=2 * 64 * 256 * width, bytes_accessed=2 * 1024 * 1024, transcendentals=0),
        )(*states, *items, places)
        outs = pl.pallas_call(
            functools.partial(score_kernel, total, planes, parts),
            out_shape=[jax.ShapeDtypeStruct((1, half), jnp.float32)] * total,
            in_specs=[vmem] * (planes * parts + 2),
            out_specs=[vmem] * total,
            compiler_params=params,
            cost_estimate=pl.CostEstimate(flops=2 * 16 * 256 * 512, bytes_accessed=512 * 1024, transcendentals=0),
        )(*pair_scores, linear, hits)

    with jax.named_scope("back"):
        result = outs[0]
        for j in sorted(range(1, total), key=lambda step: step == total // 2):
            result = result + shift(outs[j], "shard", -j)
    return result.reshape(half)


def solution(mesh):
    return jax.shard_map(
        body,
        mesh=mesh,
        in_specs=(
            P(("groups", "shard", "cache", "pair")),
            P(("groups", "shard", "cache", "pair")),
            P(("shard", "cache"), None),
            P(("groups", "shard"), None),
            P("pair", None, None),
            P("pair", None),
        ),
        out_specs=P(("groups", "shard", "cache", "pair")),
        check_vma=False,
    )
```

```python
import functools

import jax
import jax.numpy as jnp
from jax import lax
from jax.experimental import pallas as pl
from jax.experimental.pallas import tpu as pltpu
from jax.sharding import PartitionSpec as P

K = 64
LANES = 128
PITCH = 72
CODE_BITS = 7
VMEM_LIMIT = 40 * 1024 * 1024
NT = (((1,), (1,)), ((), ()))
NN = (((1,), (0,)), ((), ()))


def dot(a, b, dims, **kw):
    return lax.dot_general(a, b, dims, preferred_element_type=jnp.float32, **kw)


def iota(shape, dim):
    return lax.broadcasted_iota(jnp.int32, shape, dim)


def ring(index, size):
    return lax.rem(index + size, size)


def pick_kernel(total, cap, *refs):
    users, (digits, states, out) = refs[:total], refs[total:]
    own_rows, width = states.shape
    slots = out.shape[0]
    readers = users[0].shape[1]
    me = lax.axis_index("shard")
    first = me * own_rows
    across = iota((readers, readers), 1)
    down = iota((readers, readers), 0)
    chosen = jnp.zeros((slots, own_rows), jnp.float32)
    for j in range(total):
        row = users[j][...]
        column = jnp.sum(jnp.where(across == down, row, 0), axis=1, keepdims=True)
        mine = (column >= first) & (column < first + own_rows)
        rank = jnp.sum(jnp.where((down < across) & mine, 1, 0), axis=0, keepdims=True)
        held = (row >= first) & (row < first + own_rows)
        slot = jnp.where(held, ring(me - j, total) * cap + rank, -1)
        to_slot = (iota((slots, readers), 0) == slot).astype(jnp.float32).astype(jnp.bfloat16)
        from_row = (iota((readers, own_rows), 1) + first == column).astype(jnp.float32).astype(jnp.bfloat16)
        chosen = chosen + dot(to_slot, from_row, NN)
    out[:, width:] = digits[...]
    out[:, :width] = dot(chosen.astype(jnp.bfloat16), states[...], NN).astype(jnp.bfloat16)


def turn_kernel(items_hbm, mats_hbm, states_hbm, ids_hbm, cands_hbm, rows32, rows16, mats, states, ids, digits, items, cands, sems):
    chunks = sems.shape[0] - 4
    wide = items.shape[1] // chunks
    item_fetches = [
        pltpu.make_async_copy(items_hbm.at[:, pl.ds(t * wide, wide)], items.at[:, pl.ds(t * wide, wide)], sems.at[t])
        for t in range(chunks)
    ]
    mats_fetch = pltpu.make_async_copy(mats_hbm, mats, sems.at[chunks])
    states_fetch = pltpu.make_async_copy(states_hbm, states, sems.at[chunks + 1])
    ids_fetch = pltpu.make_async_copy(ids_hbm, ids, sems.at[chunks + 2])
    cands_fetch = pltpu.make_async_copy(cands_hbm, cands, sems.at[chunks + 3])
    for copy in item_fetches + [mats_fetch, states_fetch, ids_fetch, cands_fetch]:
        copy.start()
    eye = (iota((LANES, LANES), 0) == iota((LANES, LANES), 1)).astype(jnp.bfloat16)
    for t in range(items.shape[1] // LANES):
        if t * LANES % wide == 0:
            item_fetches[t * LANES // wide].wait()
        turned = dot(eye, items[:, t * LANES:(t + 1) * LANES], NT)
        rows32[t * LANES:(t + 1) * LANES, :] = turned
        rows16[t * LANES:(t + 1) * LANES, :] = turned.astype(jnp.bfloat16)
    cands_fetch.wait()
    code = jnp.broadcast_to(cands[...], digits.shape)
    place = iota(digits.shape, 0)
    digit = jnp.where(place == 0, code >> CODE_BITS, jnp.where(place == 1, code & ((1 << CODE_BITS) - 1), 0))
    digits[...] = digit.astype(jnp.float32).astype(jnp.bfloat16)
    ids_fetch.wait()
    mats_fetch.wait()
    states_fetch.wait()


def pair_kernel(total, cap, slots, user_rows, *refs):
    users, (fields_hbm, rows32, rows16, mats, picked, out, places, fields, stacked, sem) = refs[:total], refs[total:]
    del picked
    fields_fetch = pltpu.make_async_copy(fields_hbm, fields, sem)
    fields_fetch.start()
    me = lax.axis_index("shard")
    readers, half = users[0].shape[1], places.shape[1]
    across = iota((readers, readers), 1)
    down = iota((readers, readers), 0)
    asks = (iota((readers, half), 1) // (half // readers) == iota((readers, half), 0)).astype(jnp.float32)
    for j in range(total):
        holder = users[j][...] >> (user_rows.bit_length() - 1)
        column = jnp.sum(jnp.where(across == down, holder, 0), axis=1, keepdims=True)
        rank = jnp.sum(jnp.where((down < across) & (column == holder), 1, 0), axis=0, keepdims=True)
        arrival = jnp.where(holder > me, me - holder + total, me - holder)
        slot = (arrival * slots + ring(me - j, total) * cap + rank).astype(jnp.float32)
        places[j:j + 1, :] = dot(slot, asks, NN, precision=lax.Precision.HIGHEST).astype(jnp.int32)
    pairs = mats.shape[2]
    steps = pairs // 2
    eye = (iota((steps, steps), 0) == iota((steps, steps), 1)).astype(jnp.bfloat16)
    for k in range(0, K, 2):
        sides = [mats[at, :, part * steps:(part + 1) * steps] for at in (k, k + 1) for part in range(2)]
        turned = dot(eye, jnp.concatenate(sides, axis=0), NT)
        stacked[pl.ds(k, steps, stride=PITCH), :] = turned[:, :LANES]
        stacked[pl.ds(k + 1, steps, stride=PITCH), :] = turned[:, LANES:]
    fields_fetch.wait()
    items = rows32.shape[1]
    blank = jnp.zeros((K, items), jnp.bfloat16)

    def two(p, total):
        fields_of = [(pl.multiple_of(fields[0, q] * K, K), pl.multiple_of(fields[1, q] * K, K)) for q in (p, p + steps)]
        left = stacked[pl.ds(pl.multiple_of(p * PITCH, 8), K), :].astype(jnp.bfloat16)
        first, second = [rows16[pl.ds(b, K), :] for _, b in fields_of]
        right = jnp.concatenate(
            [jnp.concatenate([first, blank], axis=1), jnp.concatenate([blank, second], axis=1)], axis=0
        )
        return total + dot(left, right, NN) * jnp.concatenate([rows32[pl.ds(a, K), :] for a, _ in fields_of], axis=1)

    sums = lax.fori_loop(0, steps, two, jnp.zeros((K, 2 * items), jnp.float32), unroll=32)
    line = jnp.sum(sums, axis=0, keepdims=True)
    out[...] = line[:, :items] + line[:, items:]


def thirds(x):
    high = x.astype(jnp.bfloat16)
    rest = x - high.astype(jnp.float32)
    middle = rest.astype(jnp.bfloat16)
    return high, middle, (rest - middle.astype(jnp.float32)).astype(jnp.bfloat16)


def linear_kernel(total, planes, *refs):
    states, refs = refs[:total], refs[total:]
    items, refs = refs[:planes], refs[planes:]
    places, out, hits, wanted, linear = refs
    slots = states[0].shape[0]
    own_rows, width = items[0].shape
    half = out.shape[1]
    me = lax.axis_index("shard")
    plane = lax.axis_index("cache")
    count = total * slots
    cands = []
    for j in range(total):
        wanted[j * slots:(j + 1) * slots, :] = states[j][:, :width]
        digits = states[j][:, width:].astype(jnp.float32)
        place = iota(digits.shape, 0)
        weight = jnp.where(place == 0, float(1 << CODE_BITS), jnp.where(place == 1, 1.0, 0.0))
        cands.append(jnp.sum(digits * weight, axis=0, keepdims=True).astype(jnp.int32))

    for q, rows in enumerate(items):
        for t, part in enumerate(thirds(dot(rows[...], wanted[...], NT))):
            linear[q * own_rows:(q + 1) * own_rows, t * count:(t + 1) * count] = part
    ids = [iota((own_rows, 1), 0) + (me * planes + ring(plane - q, planes)) * own_rows for q in range(planes)]
    item_ids = jnp.concatenate(ids, axis=0)
    for j in range(total):
        spread = (iota((count, half), 0) == places[j:j + 1, :]).astype(jnp.float32).astype(jnp.bfloat16)
        scores = dot(linear[...], jnp.concatenate([spread] * 3, axis=0), NN)
        hit = item_ids == cands[j]
        out[j:j + 1, :] = jnp.sum(jnp.where(hit, scores, 0.0), axis=0, keepdims=True)
        hits[:, j * half:(j + 1) * half] = hit.astype(jnp.float32).astype(jnp.bfloat16)


def score_kernel(total, planes, parts, *refs):
    pairs, (linear, hits), outs = refs[:planes * parts], refs[planes * parts:planes * parts + 2], refs[planes * parts + 2:]
    half = linear.shape[1]
    sums = [sum(pairs[(h + 1) * planes - 1 - q][...] for h in range(parts)) for q in range(planes)]
    row = jnp.concatenate(sums, axis=1)
    pieces = jnp.zeros((16, row.shape[1]), jnp.float32)
    for t, part in enumerate(thirds(row)):
        pieces = jnp.where(iota(pieces.shape, 0) == t, part.astype(jnp.float32), pieces)
    added = jnp.sum(dot(pieces.astype(jnp.bfloat16), hits[...], NN), axis=0, keepdims=True)
    for j in range(total):
        outs[j][...] = linear[j:j + 1, :] + added[:, j * half:(j + 1) * half]


def shift(x, axis, step):
    size = lax.axis_size(axis)
    return lax.ppermute(x, axis, [(s, (s + step) % size) for s in range(size)])


def body(cand_items, reader_users, item_table, user_states, pair_mats, pair_fields):
    total = lax.axis_size("shard")
    planes = lax.axis_size("cache")
    parts = lax.axis_size("pair")
    half = cand_items.shape[0]
    rows, width = item_table.shape
    readers = reader_users.shape[0]
    cap = 2 * ((readers + total - 1) // total)
    slots = -(-total * cap // 16) * 16
    count = pair_mats.shape[0]
    vmem = pl.BlockSpec(memory_space=pltpu.VMEM)
    hbm = pl.BlockSpec(memory_space=pltpu.HBM)
    anywhere = pl.BlockSpec(memory_space=pl.ANY)
    params = pltpu.CompilerParams(vmem_limit_bytes=VMEM_LIMIT)

    def in_hbm(x):
        return pltpu.with_memory_space_constraint(x, pltpu.HBM)

    with jax.named_scope("item_rows"):
        items = [item_table] + [shift(item_table, "cache", q) for q in range(1, planes)]

    with jax.named_scope("ids"):
        users = [shift(reader_users, "shard", j) for j in range(1, total)]

    with jax.named_scope("turn"):
        *turned, states_near, own_ids, digits = pl.pallas_call(
            turn_kernel,
            out_shape=(
                jax.ShapeDtypeStruct((width, rows), jnp.float32),
                jax.ShapeDtypeStruct((width, rows), jnp.bfloat16),
                jax.ShapeDtypeStruct((K, K, count), jnp.bfloat16),
                jax.ShapeDtypeStruct(user_states.shape, jnp.bfloat16),
                jax.ShapeDtypeStruct((1, readers), jnp.int32),
                jax.ShapeDtypeStruct((slots, half), jnp.bfloat16),
            ),
            in_specs=[hbm] * 5,
            out_specs=(vmem,) * 6,
            scratch_shapes=[
                pltpu.VMEM((rows, width), jnp.bfloat16),
                pltpu.VMEM((1, half), jnp.int32),
                pltpu.SemaphoreType.DMA((8,)),
            ],
            compiler_params=params,
            cost_estimate=pl.CostEstimate(flops=2 * rows * rows * width * 16, bytes_accessed=8 * 1024 * 1024, transcendentals=0),
        )(
            in_hbm(item_table),
            in_hbm(jnp.transpose(pair_mats, (1, 2, 0))),
            in_hbm(user_states),
            in_hbm(reader_users.reshape(1, readers)),
            in_hbm(cand_items.reshape(1, half)),
        )

    with jax.named_scope("states"):
        users_near = [own_ids] + [ids.reshape(1, readers) for ids in users]
        picked = pl.pallas_call(
            functools.partial(pick_kernel, total, cap),
            out_shape=jax.ShapeDtypeStruct((slots, width + half), jnp.bfloat16),
            in_specs=[vmem] * (total + 2),
            out_specs=vmem,
            compiler_params=params,
            cost_estimate=pl.CostEstimate(flops=2 * slots * rows * width, bytes_accessed=1024 * 1024, transcendentals=0),
        )(*users_near, digits, states_near)
        states = [picked] + [shift(picked, "shard", j) for j in range(1, total)]

    with jax.named_scope("pairs"):
        pair_parts, places = pl.pallas_call(
            functools.partial(pair_kernel, total, cap, slots, user_states.shape[0]),
            out_shape=(
                jax.ShapeDtypeStruct((1, rows), jnp.float32),
                jax.ShapeDtypeStruct((total, half), jnp.int32),
            ),
            in_specs=[vmem] * total + [hbm, vmem, vmem, vmem, anywhere],
            out_specs=(vmem, vmem),
            scratch_shapes=[
                pltpu.SMEM((2, count), jnp.int32),
                pltpu.VMEM((count // 2 * PITCH + K, LANES), jnp.float32),
                pltpu.SemaphoreType.DMA,
            ],
            compiler_params=params,
            cost_estimate=pl.CostEstimate(flops=2 * count * K * K * rows * 16, bytes_accessed=4 * 1024 * 1024, transcendentals=0),
        )(*users_near, in_hbm(pair_fields.T), *turned, picked)
        pair_scores = {(0, 0): pair_parts}
        steps = [(q, h) for q in range(planes - 1, -1, -1) for h in range(parts) if q or h]
        for q, h in steps:
            perm = [
                (c * parts + d, (c + q) % planes * parts + (d + h) % parts) for c in range(planes) for d in range(parts)
            ]
            source, after = pair_parts, {1: 2, 2: 1}.get(len(pair_scores) - 1, 0)
            if after:
                source, states[after] = lax.optimization_barrier((pair_parts, states[after]))
            pair_scores[q, h] = lax.ppermute(source, ("cache", "pair"), perm)
        pair_scores = [pair_scores[q, h] for h in range(parts) for q in range(planes - 1, -1, -1)]

    with jax.named_scope("scores"):
        linear, hits = pl.pallas_call(
            functools.partial(linear_kernel, total, planes),
            out_shape=(
                jax.ShapeDtypeStruct((total, half), jnp.float32),
                jax.ShapeDtypeStruct((planes * rows, total * half), jnp.bfloat16),
            ),
            in_specs=[vmem] * (total + len(items) + 1),
            out_specs=(vmem, vmem),
            scratch_shapes=[
                pltpu.VMEM((total * slots, width), jnp.bfloat16),
                pltpu.VMEM((planes * rows, 3 * total * slots), jnp.bfloat16),
            ],
            compiler_params=params,
            cost_estimate=pl.CostEstimate(flops=2 * 64 * 256 * width, bytes_accessed=2 * 1024 * 1024, transcendentals=0),
        )(*states, *items, places)
        outs = pl.pallas_call(
            functools.partial(score_kernel, total, planes, parts),
            out_shape=[jax.ShapeDtypeStruct((1, half), jnp.float32)] * total,
            in_specs=[vmem] * (planes * parts + 2),
            out_specs=[vmem] * total,
            compiler_params=params,
            cost_estimate=pl.CostEstimate(flops=2 * 16 * 256 * 512, bytes_accessed=512 * 1024, transcendentals=0),
        )(*pair_scores, linear, hits)

    with jax.named_scope("back"):
        result = outs[0]
        for j in range(1, total):
            result = result + shift(outs[j], "shard", -j)
    return result.reshape(half)


def solution(mesh):
    return jax.shard_map(
        body,
        mesh=mesh,
        in_specs=(
            P(("groups", "shard", "cache", "pair")),
            P(("groups", "shard", "cache", "pair")),
            P(("shard", "cache"), None),
            P(("groups", "shard"), None),
            P("pair", None, None),
            P("pair", None),
        ),
        out_specs=P(("groups", "shard", "cache", "pair")),
        check_vma=False,
    )
```

```python
import functools

import jax
import jax.numpy as jnp
from jax import lax
from jax.experimental import pallas as pl
from jax.experimental.pallas import tpu as pltpu
from jax.sharding import PartitionSpec as P

K = 64
LANES = 128
PITCH = 72
CODE_BITS = 7
VMEM_LIMIT = 40 * 1024 * 1024
NT = (((1,), (1,)), ((), ()))
NN = (((1,), (0,)), ((), ()))


def dot(a, b, dims, **kw):
    return lax.dot_general(a, b, dims, preferred_element_type=jnp.float32, **kw)


def iota(shape, dim):
    return lax.broadcasted_iota(jnp.int32, shape, dim)


def ring(index, size):
    return lax.rem(index + size, size)


def pick_kernel(total, cap, *refs):
    users, (digits, states, out) = refs[:total], refs[total:]
    own_rows, width = states.shape
    slots = out.shape[0]
    readers = users[0].shape[1]
    me = lax.axis_index("shard")
    first = me * own_rows
    across = iota((readers, readers), 1)
    down = iota((readers, readers), 0)
    chosen = jnp.zeros((slots, own_rows), jnp.float32)
    for j in range(total):
        row = users[j][...]
        column = jnp.sum(jnp.where(across == down, row, 0), axis=1, keepdims=True)
        mine = (column >= first) & (column < first + own_rows)
        rank = jnp.sum(jnp.where((down < across) & mine, 1, 0), axis=0, keepdims=True)
        held = (row >= first) & (row < first + own_rows)
        slot = jnp.where(held, ring(me - j, total) * cap + rank, -1)
        to_slot = (iota((slots, readers), 0) == slot).astype(jnp.float32).astype(jnp.bfloat16)
        from_row = (iota((readers, own_rows), 1) + first == column).astype(jnp.float32).astype(jnp.bfloat16)
        chosen = chosen + dot(to_slot, from_row, NN)
    out[:, width:] = digits[...]
    out[:, :width] = dot(chosen.astype(jnp.bfloat16), states[...], NN).astype(jnp.bfloat16)


def turn_kernel(items_hbm, mats_hbm, states_hbm, ids_hbm, cands_hbm, rows32, rows16, mats, states, ids, digits, items, cands, sems):
    chunks = sems.shape[0] - 4
    wide = items.shape[1] // chunks
    item_fetches = [
        pltpu.make_async_copy(items_hbm.at[:, pl.ds(t * wide, wide)], items.at[:, pl.ds(t * wide, wide)], sems.at[t])
        for t in range(chunks)
    ]
    mats_fetch = pltpu.make_async_copy(mats_hbm, mats, sems.at[chunks])
    states_fetch = pltpu.make_async_copy(states_hbm, states, sems.at[chunks + 1])
    ids_fetch = pltpu.make_async_copy(ids_hbm, ids, sems.at[chunks + 2])
    cands_fetch = pltpu.make_async_copy(cands_hbm, cands, sems.at[chunks + 3])
    for copy in item_fetches + [mats_fetch, states_fetch, ids_fetch, cands_fetch]:
        copy.start()
    eye = (iota((LANES, LANES), 0) == iota((LANES, LANES), 1)).astype(jnp.bfloat16)
    for t in range(items.shape[1] // LANES):
        if t * LANES % wide == 0:
            item_fetches[t * LANES // wide].wait()
        turned = dot(eye, items[:, t * LANES:(t + 1) * LANES], NT)
        rows32[t * LANES:(t + 1) * LANES, :] = turned
        rows16[t * LANES:(t + 1) * LANES, :] = turned.astype(jnp.bfloat16)
    cands_fetch.wait()
    code = jnp.broadcast_to(cands[...], digits.shape)
    place = iota(digits.shape, 0)
    digit = jnp.where(place == 0, code >> CODE_BITS, jnp.where(place == 1, code & ((1 << CODE_BITS) - 1), 0))
    digits[...] = digit.astype(jnp.float32).astype(jnp.bfloat16)
    ids_fetch.wait()
    mats_fetch.wait()
    states_fetch.wait()


def pair_kernel(total, cap, slots, user_rows, *refs):
    users, (fields_hbm, rows32, rows16, mats, picked, out, places, fields, stacked, sem) = refs[:total], refs[total:]
    del picked
    fields_fetch = pltpu.make_async_copy(fields_hbm, fields, sem)
    fields_fetch.start()
    me = lax.axis_index("shard")
    readers, half = users[0].shape[1], places.shape[1]
    across = iota((readers, readers), 1)
    down = iota((readers, readers), 0)
    asks = (iota((readers, half), 1) // (half // readers) == iota((readers, half), 0)).astype(jnp.float32)
    for j in range(total):
        holder = users[j][...] >> (user_rows.bit_length() - 1)
        column = jnp.sum(jnp.where(across == down, holder, 0), axis=1, keepdims=True)
        rank = jnp.sum(jnp.where((down < across) & (column == holder), 1, 0), axis=0, keepdims=True)
        arrival = jnp.where(holder > me, me - holder + total, me - holder)
        slot = (arrival * slots + ring(me - j, total) * cap + rank).astype(jnp.float32)
        places[j:j + 1, :] = dot(slot, asks, NN, precision=lax.Precision.HIGHEST).astype(jnp.int32)
    pairs = mats.shape[2]
    steps = pairs // 2
    eye = (iota((steps, steps), 0) == iota((steps, steps), 1)).astype(jnp.bfloat16)
    for k in range(0, K, 2):
        sides = [mats[at, :, part * steps:(part + 1) * steps] for at in (k, k + 1) for part in range(2)]
        turned = dot(eye, jnp.concatenate(sides, axis=0), NT)
        stacked[pl.ds(k, steps, stride=PITCH), :] = turned[:, :LANES]
        stacked[pl.ds(k + 1, steps, stride=PITCH), :] = turned[:, LANES:]
    fields_fetch.wait()
    items = rows32.shape[1]
    blank = jnp.zeros((K, items), jnp.bfloat16)

    def two(p, total):
        fields_of = [(pl.multiple_of(fields[0, q] * K, K), pl.multiple_of(fields[1, q] * K, K)) for q in (p, p + steps)]
        left = stacked[pl.ds(pl.multiple_of(p * PITCH, 8), K), :].astype(jnp.bfloat16)
        first, second = [rows16[pl.ds(b, K), :] for _, b in fields_of]
        right = jnp.concatenate(
            [jnp.concatenate([first, blank], axis=1), jnp.concatenate([blank, second], axis=1)], axis=0
        )
        return total + dot(left, right, NN) * jnp.concatenate([rows32[pl.ds(a, K), :] for a, _ in fields_of], axis=1)

    sums = lax.fori_loop(0, steps, two, jnp.zeros((K, 2 * items), jnp.float32), unroll=32)
    line = jnp.sum(sums, axis=0, keepdims=True)
    out[...] = line[:, :items] + line[:, items:]


def thirds(x):
    high = x.astype(jnp.bfloat16)
    rest = x - high.astype(jnp.float32)
    middle = rest.astype(jnp.bfloat16)
    return high, middle, (rest - middle.astype(jnp.float32)).astype(jnp.bfloat16)


def linear_kernel(total, planes, *refs):
    states, refs = refs[:total], refs[total:]
    items, refs = refs[:planes], refs[planes:]
    places, out, hits, wanted, linear = refs
    slots = states[0].shape[0]
    own_rows, width = items[0].shape
    half = out.shape[1]
    me = lax.axis_index("shard")
    plane = lax.axis_index("cache")
    count = total * slots
    cands = []
    for j in range(total):
        wanted[j * slots:(j + 1) * slots, :] = states[j][:, :width]
        digits = states[j][:, width:].astype(jnp.float32)
        place = iota(digits.shape, 0)
        weight = jnp.where(place == 0, float(1 << CODE_BITS), jnp.where(place == 1, 1.0, 0.0))
        cands.append(jnp.sum(digits * weight, axis=0, keepdims=True).astype(jnp.int32))

    for q, rows in enumerate(items):
        for t, part in enumerate(thirds(dot(rows[...], wanted[...], NT))):
            linear[q * own_rows:(q + 1) * own_rows, t * count:(t + 1) * count] = part
    ids = [iota((own_rows, 1), 0) + (me * planes + ring(plane - q, planes)) * own_rows for q in range(planes)]
    item_ids = jnp.concatenate(ids, axis=0)
    for j in range(total):
        spread = (iota((count, half), 0) == places[j:j + 1, :]).astype(jnp.float32).astype(jnp.bfloat16)
        scores = dot(linear[...], jnp.concatenate([spread] * 3, axis=0), NN)
        hit = item_ids == cands[j]
        out[j:j + 1, :] = jnp.sum(jnp.where(hit, scores, 0.0), axis=0, keepdims=True)
        hits[:, j * half:(j + 1) * half] = hit.astype(jnp.float32).astype(jnp.bfloat16)


def score_kernel(total, planes, parts, *refs):
    pairs, (linear, hits), refs = refs[:planes * parts], refs[planes * parts:planes * parts + 2], refs[planes * parts + 2:]
    outs, rows = refs[:total], refs[total]
    half = linear.shape[1]
    sums = [sum(pairs[(h + 1) * planes - 1 - q][...] for h in range(parts)) for q in range(planes)]
    row = jnp.concatenate(sums, axis=1)
    pieces = jnp.zeros((16, row.shape[1]), jnp.float32)
    for t, part in enumerate(thirds(row)):
        pieces = jnp.where(iota(pieces.shape, 0) == t, part.astype(jnp.float32), pieces)
    added = jnp.sum(dot(pieces.astype(jnp.bfloat16), hits[...], NN), axis=0, keepdims=True)
    for j in range(total):
        rows[j:j + 1, :] = linear[j:j + 1, :] + added[:, j * half:(j + 1) * half]
    me = lax.axis_index("shard")
    for mask in range(total):
        outs[mask][...] = rows[pl.ds(ring(me - (me ^ mask), total), 1), :]


def shift(x, axis, step):
    size = lax.axis_size(axis)
    return lax.ppermute(x, axis, [(s, (s + step) % size) for s in range(size)])


def swap(x, axis, mask):
    return lax.ppermute(x, axis, [(s, s ^ mask) for s in range(lax.axis_size(axis))])


def body(cand_items, reader_users, item_table, user_states, pair_mats, pair_fields):
    total = lax.axis_size("shard")
    planes = lax.axis_size("cache")
    parts = lax.axis_size("pair")
    half = cand_items.shape[0]
    rows, width = item_table.shape
    readers = reader_users.shape[0]
    cap = 2 * ((readers + total - 1) // total)
    slots = -(-total * cap // 16) * 16
    count = pair_mats.shape[0]
    vmem = pl.BlockSpec(memory_space=pltpu.VMEM)
    hbm = pl.BlockSpec(memory_space=pltpu.HBM)
    anywhere = pl.BlockSpec(memory_space=pl.ANY)
    params = pltpu.CompilerParams(vmem_limit_bytes=VMEM_LIMIT)

    def in_hbm(x):
        return pltpu.with_memory_space_constraint(x, pltpu.HBM)

    with jax.named_scope("item_rows"):
        items = [item_table] + [shift(item_table, "cache", q) for q in range(1, planes)]

    with jax.named_scope("ids"):
        users = [shift(reader_users, "shard", j) for j in range(1, total)]

    with jax.named_scope("turn"):
        *turned, states_near, own_ids, digits = pl.pallas_call(
            turn_kernel,
            out_shape=(
                jax.ShapeDtypeStruct((width, rows), jnp.float32),
                jax.ShapeDtypeStruct((width, rows), jnp.bfloat16),
                jax.ShapeDtypeStruct((K, K, count), jnp.bfloat16),
                jax.ShapeDtypeStruct(user_states.shape, jnp.bfloat16),
                jax.ShapeDtypeStruct((1, readers), jnp.int32),
                jax.ShapeDtypeStruct((slots, half), jnp.bfloat16),
            ),
            in_specs=[hbm] * 5,
            out_specs=(vmem,) * 6,
            scratch_shapes=[
                pltpu.VMEM((rows, width), jnp.bfloat16),
                pltpu.VMEM((1, half), jnp.int32),
                pltpu.SemaphoreType.DMA((8,)),
            ],
            compiler_params=params,
            cost_estimate=pl.CostEstimate(flops=2 * rows * rows * width * 16, bytes_accessed=8 * 1024 * 1024, transcendentals=0),
        )(
            in_hbm(item_table),
            in_hbm(jnp.transpose(pair_mats, (1, 2, 0))),
            in_hbm(user_states),
            in_hbm(reader_users.reshape(1, readers)),
            in_hbm(cand_items.reshape(1, half)),
        )

    with jax.named_scope("states"):
        users_near = [own_ids] + [ids.reshape(1, readers) for ids in users]
        picked = pl.pallas_call(
            functools.partial(pick_kernel, total, cap),
            out_shape=jax.ShapeDtypeStruct((slots, width + half), jnp.bfloat16),
            in_specs=[vmem] * (total + 2),
            out_specs=vmem,
            compiler_params=params,
            cost_estimate=pl.CostEstimate(flops=2 * slots * rows * width, bytes_accessed=1024 * 1024, transcendentals=0),
        )(*users_near, digits, states_near)
        states = [picked] + [shift(picked, "shard", j) for j in range(1, total)]

    with jax.named_scope("pairs"):
        pair_parts, places = pl.pallas_call(
            functools.partial(pair_kernel, total, cap, slots, user_states.shape[0]),
            out_shape=(
                jax.ShapeDtypeStruct((1, rows), jnp.float32),
                jax.ShapeDtypeStruct((total, half), jnp.int32),
            ),
            in_specs=[vmem] * total + [hbm, vmem, vmem, vmem, anywhere],
            out_specs=(vmem, vmem),
            scratch_shapes=[
                pltpu.SMEM((2, count), jnp.int32),
                pltpu.VMEM((count // 2 * PITCH + K, LANES), jnp.float32),
                pltpu.SemaphoreType.DMA,
            ],
            compiler_params=params,
            cost_estimate=pl.CostEstimate(flops=2 * count * K * K * rows * 16, bytes_accessed=4 * 1024 * 1024, transcendentals=0),
        )(*users_near, in_hbm(pair_fields.T), *turned, picked)
        pair_scores = {(0, 0): pair_parts}
        steps = [(q, h) for q in range(planes - 1, -1, -1) for h in range(parts) if q or h]
        for q, h in steps:
            perm = [
                (c * parts + d, (c + q) % planes * parts + (d + h) % parts) for c in range(planes) for d in range(parts)
            ]
            source, after = pair_parts, {1: 1, 2: 2}.get(len(pair_scores) - 1, 0)
            if after:
                source, states[after] = lax.optimization_barrier((pair_parts, states[after]))
            pair_scores[q, h] = lax.ppermute(source, ("cache", "pair"), perm)
        pair_scores = [pair_scores[q, h] for h in range(parts) for q in range(planes - 1, -1, -1)]

    with jax.named_scope("scores"):
        linear, hits = pl.pallas_call(
            functools.partial(linear_kernel, total, planes),
            out_shape=(
                jax.ShapeDtypeStruct((total, half), jnp.float32),
                jax.ShapeDtypeStruct((planes * rows, total * half), jnp.bfloat16),
            ),
            in_specs=[vmem] * (total + len(items) + 1),
            out_specs=(vmem, vmem),
            scratch_shapes=[
                pltpu.VMEM((total * slots, width), jnp.bfloat16),
                pltpu.VMEM((planes * rows, 3 * total * slots), jnp.bfloat16),
            ],
            compiler_params=params,
            cost_estimate=pl.CostEstimate(flops=2 * 64 * 256 * width, bytes_accessed=2 * 1024 * 1024, transcendentals=0),
        )(*states, *items, places)
        outs = pl.pallas_call(
            functools.partial(score_kernel, total, planes, parts),
            out_shape=[jax.ShapeDtypeStruct((1, half), jnp.float32)] * total,
            in_specs=[vmem] * (planes * parts + 2),
            out_specs=[vmem] * total,
            scratch_shapes=[pltpu.VMEM((-(-total // 8) * 8, half), jnp.float32)],
            compiler_params=params,
            cost_estimate=pl.CostEstimate(flops=2 * 16 * 256 * 512, bytes_accessed=512 * 1024, transcendentals=0),
        )(*pair_scores, linear, hits)

    with jax.named_scope("back"):
        result = outs[0]
        for j in range(1, total):
            result = result + swap(outs[j], "shard", j)
    return result.reshape(half)


def solution(mesh):
    return jax.shard_map(
        body,
        mesh=mesh,
        in_specs=(
            P(("groups", "shard", "cache", "pair")),
            P(("groups", "shard", "cache", "pair")),
            P(("shard", "cache"), None),
            P(("groups", "shard"), None),
            P("pair", None, None),
            P("pair", None),
        ),
        out_specs=P(("groups", "shard", "cache", "pair")),
        check_vma=False,
    )
```

```python
import functools

import jax
import jax.numpy as jnp
from jax import lax
from jax.experimental import pallas as pl
from jax.experimental.pallas import tpu as pltpu
from jax.sharding import PartitionSpec as P

K = 64
LANES = 128
PITCH = 72
CODE_BITS = 7
VMEM_LIMIT = 40 * 1024 * 1024
NT = (((1,), (1,)), ((), ()))
NN = (((1,), (0,)), ((), ()))


def dot(a, b, dims, **kw):
    return lax.dot_general(a, b, dims, preferred_element_type=jnp.float32, **kw)


def iota(shape, dim):
    return lax.broadcasted_iota(jnp.int32, shape, dim)


def ring(index, size):
    return lax.rem(index + size, size)


def pick_kernel(total, cap, *refs):
    users, (digits, states, out) = refs[:total], refs[total:]
    own_rows, width = states.shape
    slots = out.shape[0]
    readers = users[0].shape[1]
    me = lax.axis_index("shard")
    first = me * own_rows
    across = iota((readers, readers), 1)
    down = iota((readers, readers), 0)
    chosen = jnp.zeros((slots, own_rows), jnp.float32)
    for j in range(total):
        row = users[j][...]
        column = jnp.sum(jnp.where(across == down, row, 0), axis=1, keepdims=True)
        mine = (column >= first) & (column < first + own_rows)
        rank = jnp.sum(jnp.where((down < across) & mine, 1, 0), axis=0, keepdims=True)
        held = (row >= first) & (row < first + own_rows)
        slot = jnp.where(held, ring(me + j, total) * cap + rank, -1)
        to_slot = (iota((slots, readers), 0) == slot).astype(jnp.float32).astype(jnp.bfloat16)
        from_row = (iota((readers, own_rows), 1) + first == column).astype(jnp.float32).astype(jnp.bfloat16)
        chosen = chosen + dot(to_slot, from_row, NN)
    out[:, width:] = digits[...]
    out[:, :width] = dot(chosen.astype(jnp.bfloat16), states[...], NN).astype(jnp.bfloat16)


def turn_kernel(items_hbm, mats_hbm, states_hbm, ids_hbm, cands_hbm, rows32, rows16, mats, states, ids, digits, items, cands, sems):
    chunks = sems.shape[0] - 4
    wide = items.shape[1] // chunks
    item_fetches = [
        pltpu.make_async_copy(items_hbm.at[:, pl.ds(t * wide, wide)], items.at[:, pl.ds(t * wide, wide)], sems.at[t])
        for t in range(chunks)
    ]
    mats_fetch = pltpu.make_async_copy(mats_hbm, mats, sems.at[chunks])
    states_fetch = pltpu.make_async_copy(states_hbm, states, sems.at[chunks + 1])
    ids_fetch = pltpu.make_async_copy(ids_hbm, ids, sems.at[chunks + 2])
    cands_fetch = pltpu.make_async_copy(cands_hbm, cands, sems.at[chunks + 3])
    for copy in item_fetches + [mats_fetch, states_fetch, ids_fetch, cands_fetch]:
        copy.start()
    eye = (iota((LANES, LANES), 0) == iota((LANES, LANES), 1)).astype(jnp.bfloat16)
    for t in range(items.shape[1] // LANES):
        if t * LANES % wide == 0:
            item_fetches[t * LANES // wide].wait()
        turned = dot(eye, items[:, t * LANES:(t + 1) * LANES], NT)
        rows32[t * LANES:(t + 1) * LANES, :] = turned
        rows16[t * LANES:(t + 1) * LANES, :] = turned.astype(jnp.bfloat16)
    cands_fetch.wait()
    code = jnp.broadcast_to(cands[...], digits.shape)
    place = iota(digits.shape, 0)
    digit = jnp.where(place == 0, code >> CODE_BITS, jnp.where(place == 1, code & ((1 << CODE_BITS) - 1), 0))
    digits[...] = digit.astype(jnp.float32).astype(jnp.bfloat16)
    ids_fetch.wait()
    mats_fetch.wait()
    states_fetch.wait()


def pair_kernel(total, cap, slots, user_rows, *refs):
    users, (fields_hbm, rows32, rows16, mats, picked, out, places, fields, stacked, sem) = refs[:total], refs[total:]
    del picked
    fields_fetch = pltpu.make_async_copy(fields_hbm, fields, sem)
    fields_fetch.start()
    me = lax.axis_index("shard")
    readers, half = users[0].shape[1], places.shape[1]
    across = iota((readers, readers), 1)
    down = iota((readers, readers), 0)
    asks = (iota((readers, half), 1) // (half // readers) == iota((readers, half), 0)).astype(jnp.float32)
    for j in range(total):
        holder = users[j][...] >> (user_rows.bit_length() - 1)
        column = jnp.sum(jnp.where(across == down, holder, 0), axis=1, keepdims=True)
        rank = jnp.sum(jnp.where((down < across) & (column == holder), 1, 0), axis=0, keepdims=True)
        arrival = jnp.where(holder < me, holder - me + total, holder - me)
        slot = (arrival * slots + ring(me + j, total) * cap + rank).astype(jnp.float32)
        places[j:j + 1, :] = dot(slot, asks, NN, precision=lax.Precision.HIGHEST).astype(jnp.int32)
    pairs = mats.shape[2]
    steps = pairs // 2
    eye = (iota((steps, steps), 0) == iota((steps, steps), 1)).astype(jnp.bfloat16)
    for k in range(0, K, 2):
        sides = [mats[at, :, part * steps:(part + 1) * steps] for at in (k, k + 1) for part in range(2)]
        turned = dot(eye, jnp.concatenate(sides, axis=0), NT)
        stacked[pl.ds(k, steps, stride=PITCH), :] = turned[:, :LANES]
        stacked[pl.ds(k + 1, steps, stride=PITCH), :] = turned[:, LANES:]
    fields_fetch.wait()
    items = rows32.shape[1]
    blank = jnp.zeros((K, items), jnp.bfloat16)

    def two(p, total):
        fields_of = [(pl.multiple_of(fields[0, q] * K, K), pl.multiple_of(fields[1, q] * K, K)) for q in (p, p + steps)]
        left = stacked[pl.ds(pl.multiple_of(p * PITCH, 8), K), :].astype(jnp.bfloat16)
        first, second = [rows16[pl.ds(b, K), :] for _, b in fields_of]
        right = jnp.concatenate(
            [jnp.concatenate([first, blank], axis=1), jnp.concatenate([blank, second], axis=1)], axis=0
        )
        return total + dot(left, right, NN) * jnp.concatenate([rows32[pl.ds(a, K), :] for a, _ in fields_of], axis=1)

    sums = lax.fori_loop(0, steps, two, jnp.zeros((K, 2 * items), jnp.float32), unroll=32)
    line = jnp.sum(sums, axis=0, keepdims=True)
    out[...] = line[:, :items] + line[:, items:]


def thirds(x):
    high = x.astype(jnp.bfloat16)
    rest = x - high.astype(jnp.float32)
    middle = rest.astype(jnp.bfloat16)
    return high, middle, (rest - middle.astype(jnp.float32)).astype(jnp.bfloat16)


def linear_kernel(total, planes, *refs):
    states, refs = refs[:total], refs[total:]
    items, refs = refs[:planes], refs[planes:]
    places, out, hits, wanted, linear = refs
    slots = states[0].shape[0]
    own_rows, width = items[0].shape
    half = out.shape[1]
    me = lax.axis_index("shard")
    plane = lax.axis_index("cache")
    count = total * slots
    cands = []
    for j in range(total):
        wanted[j * slots:(j + 1) * slots, :] = states[j][:, :width]
        digits = states[j][:, width:].astype(jnp.float32)
        place = iota(digits.shape, 0)
        weight = jnp.where(place == 0, float(1 << CODE_BITS), jnp.where(place == 1, 1.0, 0.0))
        cands.append(jnp.sum(digits * weight, axis=0, keepdims=True).astype(jnp.int32))

    for q, rows in enumerate(items):
        for t, part in enumerate(thirds(dot(rows[...], wanted[...], NT))):
            linear[q * own_rows:(q + 1) * own_rows, t * count:(t + 1) * count] = part
    ids = [iota((own_rows, 1), 0) + (me * planes + ring(plane - q, planes)) * own_rows for q in range(planes)]
    item_ids = jnp.concatenate(ids, axis=0)
    for j in range(total):
        spread = (iota((count, half), 0) == places[j:j + 1, :]).astype(jnp.float32).astype(jnp.bfloat16)
        scores = dot(linear[...], jnp.concatenate([spread] * 3, axis=0), NN)
        hit = item_ids == cands[j]
        out[j:j + 1, :] = jnp.sum(jnp.where(hit, scores, 0.0), axis=0, keepdims=True)
        hits[:, j * half:(j + 1) * half] = hit.astype(jnp.float32).astype(jnp.bfloat16)


def score_kernel(total, planes, parts, *refs):
    pairs, (linear, hits), outs = refs[:planes * parts], refs[planes * parts:planes * parts + 2], refs[planes * parts + 2:]
    half = linear.shape[1]
    sums = [sum(pairs[(h + 1) * planes - 1 - q][...] for h in range(parts)) for q in range(planes)]
    row = jnp.concatenate(sums, axis=1)
    pieces = jnp.zeros((16, row.shape[1]), jnp.float32)
    for t, part in enumerate(thirds(row)):
        pieces = jnp.where(iota(pieces.shape, 0) == t, part.astype(jnp.float32), pieces)
    added = jnp.sum(dot(pieces.astype(jnp.bfloat16), hits[...], NN), axis=0, keepdims=True)
    for j in range(total):
        outs[j][...] = linear[j:j + 1, :] + added[:, j * half:(j + 1) * half]


def shift(x, axis, step):
    size = lax.axis_size(axis)
    return lax.ppermute(x, axis, [(s, (s + step) % size) for s in range(size)])


def body(cand_items, reader_users, item_table, user_states, pair_mats, pair_fields):
    total = lax.axis_size("shard")
    planes = lax.axis_size("cache")
    parts = lax.axis_size("pair")
    half = cand_items.shape[0]
    rows, width = item_table.shape
    readers = reader_users.shape[0]
    cap = 2 * ((readers + total - 1) // total)
    slots = -(-total * cap // 16) * 16
    count = pair_mats.shape[0]
    vmem = pl.BlockSpec(memory_space=pltpu.VMEM)
    hbm = pl.BlockSpec(memory_space=pltpu.HBM)
    anywhere = pl.BlockSpec(memory_space=pl.ANY)
    params = pltpu.CompilerParams(vmem_limit_bytes=VMEM_LIMIT)

    def in_hbm(x):
        return pltpu.with_memory_space_constraint(x, pltpu.HBM)

    with jax.named_scope("item_rows"):
        items = [item_table] + [shift(item_table, "cache", q) for q in range(1, planes)]

    with jax.named_scope("ids"):
        users = [shift(reader_users, "shard", -j) for j in range(1, total)]

    with jax.named_scope("turn"):
        *turned, states_near, own_ids, digits = pl.pallas_call(
            turn_kernel,
            out_shape=(
                jax.ShapeDtypeStruct((width, rows), jnp.float32),
                jax.ShapeDtypeStruct((width, rows), jnp.bfloat16),
                jax.ShapeDtypeStruct((K, K, count), jnp.bfloat16),
                jax.ShapeDtypeStruct(user_states.shape, jnp.bfloat16),
                jax.ShapeDtypeStruct((1, readers), jnp.int32),
                jax.ShapeDtypeStruct((slots, half), jnp.bfloat16),
            ),
            in_specs=[hbm] * 5,
            out_specs=(vmem,) * 6,
            scratch_shapes=[
                pltpu.VMEM((rows, width), jnp.bfloat16),
                pltpu.VMEM((1, half), jnp.int32),
                pltpu.SemaphoreType.DMA((8,)),
            ],
            compiler_params=params,
            cost_estimate=pl.CostEstimate(flops=2 * rows * rows * width * 16, bytes_accessed=8 * 1024 * 1024, transcendentals=0),
        )(
            in_hbm(item_table),
            in_hbm(jnp.transpose(pair_mats, (1, 2, 0))),
            in_hbm(user_states),
            in_hbm(reader_users.reshape(1, readers)),
            in_hbm(cand_items.reshape(1, half)),
        )

    with jax.named_scope("states"):
        users_near = [own_ids] + [ids.reshape(1, readers) for ids in users]
        picked = pl.pallas_call(
            functools.partial(pick_kernel, total, cap),
            out_shape=jax.ShapeDtypeStruct((slots, width + half), jnp.bfloat16),
            in_specs=[vmem] * (total + 2),
            out_specs=vmem,
            compiler_params=params,
            cost_estimate=pl.CostEstimate(flops=2 * slots * rows * width, bytes_accessed=1024 * 1024, transcendentals=0),
        )(*users_near, digits, states_near)
        states = [picked] + [shift(picked, "shard", -j) for j in range(1, total)]

    with jax.named_scope("pairs"):
        pair_parts, places = pl.pallas_call(
            functools.partial(pair_kernel, total, cap, slots, user_states.shape[0]),
            out_shape=(
                jax.ShapeDtypeStruct((1, rows), jnp.float32),
                jax.ShapeDtypeStruct((total, half), jnp.int32),
            ),
            in_specs=[vmem] * total + [hbm, vmem, vmem, vmem, anywhere],
            out_specs=(vmem, vmem),
            scratch_shapes=[
                pltpu.SMEM((2, count), jnp.int32),
                pltpu.VMEM((count // 2 * PITCH + K, LANES), jnp.float32),
                pltpu.SemaphoreType.DMA,
            ],
            compiler_params=params,
            cost_estimate=pl.CostEstimate(flops=2 * count * K * K * rows * 16, bytes_accessed=4 * 1024 * 1024, transcendentals=0),
        )(*users_near, in_hbm(pair_fields.T), *turned, picked)
        pair_scores = {(0, 0): pair_parts}
        steps = [(q, h) for q in range(planes - 1, -1, -1) for h in range(parts) if q or h]
        for q, h in steps:
            perm = [
                (c * parts + d, (c + q) % planes * parts + (d + h) % parts) for c in range(planes) for d in range(parts)
            ]
            source, after = pair_parts, {1: 1, 2: 2}.get(len(pair_scores) - 1, 0)
            if after:
                source, states[after] = lax.optimization_barrier((pair_parts, states[after]))
            pair_scores[q, h] = lax.ppermute(source, ("cache", "pair"), perm)
        pair_scores = [pair_scores[q, h] for h in range(parts) for q in range(planes - 1, -1, -1)]

    with jax.named_scope("scores"):
        linear, hits = pl.pallas_call(
            functools.partial(linear_kernel, total, planes),
            out_shape=(
                jax.ShapeDtypeStruct((total, half), jnp.float32),
                jax.ShapeDtypeStruct((planes * rows, total * half), jnp.bfloat16),
            ),
            in_specs=[vmem] * (total + len(items) + 1),
            out_specs=(vmem, vmem),
            scratch_shapes=[
                pltpu.VMEM((total * slots, width), jnp.bfloat16),
                pltpu.VMEM((planes * rows, 3 * total * slots), jnp.bfloat16),
            ],
            compiler_params=params,
            cost_estimate=pl.CostEstimate(flops=2 * 64 * 256 * width, bytes_accessed=2 * 1024 * 1024, transcendentals=0),
        )(*states, *items, places)
        outs = pl.pallas_call(
            functools.partial(score_kernel, total, planes, parts),
            out_shape=[jax.ShapeDtypeStruct((1, half), jnp.float32)] * total,
            in_specs=[vmem] * (planes * parts + 2),
            out_specs=[vmem] * total,
            compiler_params=params,
            cost_estimate=pl.CostEstimate(flops=2 * 16 * 256 * 512, bytes_accessed=512 * 1024, transcendentals=0),
        )(*pair_scores, linear, hits)

    with jax.named_scope("back"):
        result = outs[0]
        for j in range(1, total):
            result = result + shift(outs[j], "shard", j)
    return result.reshape(half)


def solution(mesh):
    return jax.shard_map(
        body,
        mesh=mesh,
        in_specs=(
            P(("groups", "shard", "cache", "pair")),
            P(("groups", "shard", "cache", "pair")),
            P(("shard", "cache"), None),
            P(("groups", "shard"), None),
            P("pair", None, None),
            P("pair", None),
        ),
        out_specs=P(("groups", "shard", "cache", "pair")),
        check_vma=False,
    )
```

```python
import functools

import jax
import jax.numpy as jnp
from jax import lax
from jax.experimental import pallas as pl
from jax.experimental.pallas import tpu as pltpu
from jax.sharding import PartitionSpec as P

K = 64
LANES = 128
PITCH = 72
CODE_BITS = 7
VMEM_LIMIT = 40 * 1024 * 1024
NT = (((1,), (1,)), ((), ()))
NN = (((1,), (0,)), ((), ()))


def dot(a, b, dims, **kw):
    return lax.dot_general(a, b, dims, preferred_element_type=jnp.float32, **kw)


def iota(shape, dim):
    return lax.broadcasted_iota(jnp.int32, shape, dim)


def ring(index, size):
    return lax.rem(index + size, size)


def pick_kernel(total, cap, *refs):
    users, (digits, states, out) = refs[:total], refs[total:]
    own_rows, width = states.shape
    slots = out.shape[0]
    readers = users[0].shape[1]
    me = lax.axis_index("shard")
    first = me * own_rows
    across = iota((readers, readers), 1)
    down = iota((readers, readers), 0)
    chosen = jnp.zeros((slots, own_rows), jnp.float32)
    for j in range(total):
        row = users[j][...]
        column = jnp.sum(jnp.where(across == down, row, 0), axis=1, keepdims=True)
        mine = (column >= first) & (column < first + own_rows)
        rank = jnp.sum(jnp.where((down < across) & mine, 1, 0), axis=0, keepdims=True)
        held = (row >= first) & (row < first + own_rows)
        slot = jnp.where(held, ring(me - j, total) * cap + rank, -1)
        to_slot = (iota((slots, readers), 0) == slot).astype(jnp.float32).astype(jnp.bfloat16)
        from_row = (iota((readers, own_rows), 1) + first == column).astype(jnp.float32).astype(jnp.bfloat16)
        chosen = chosen + dot(to_slot, from_row, NN)
    out[:, width:] = digits[...]
    out[:, :width] = dot(chosen.astype(jnp.bfloat16), states[...], NN).astype(jnp.bfloat16)


def turn_kernel(items_hbm, mats_hbm, states_hbm, ids_hbm, cands_hbm, rows32, rows16, mats, states, ids, digits, items, cands, sems):
    chunks = sems.shape[0] - 4
    wide = items.shape[1] // chunks
    item_fetches = [
        pltpu.make_async_copy(items_hbm.at[:, pl.ds(t * wide, wide)], items.at[:, pl.ds(t * wide, wide)], sems.at[t])
        for t in range(chunks)
    ]
    mats_fetch = pltpu.make_async_copy(mats_hbm, mats, sems.at[chunks])
    states_fetch = pltpu.make_async_copy(states_hbm, states, sems.at[chunks + 1])
    ids_fetch = pltpu.make_async_copy(ids_hbm, ids, sems.at[chunks + 2])
    cands_fetch = pltpu.make_async_copy(cands_hbm, cands, sems.at[chunks + 3])
    for copy in item_fetches + [mats_fetch, states_fetch, ids_fetch, cands_fetch]:
        copy.start()
    eye = (iota((LANES, LANES), 0) == iota((LANES, LANES), 1)).astype(jnp.bfloat16)
    for t in range(items.shape[1] // LANES):
        if t * LANES % wide == 0:
            item_fetches[t * LANES // wide].wait()
        turned = dot(eye, items[:, t * LANES:(t + 1) * LANES], NT)
        rows32[t * LANES:(t + 1) * LANES, :] = turned
        rows16[t * LANES:(t + 1) * LANES, :] = turned.astype(jnp.bfloat16)
    cands_fetch.wait()
    code = jnp.broadcast_to(cands[...], digits.shape)
    place = iota(digits.shape, 0)
    digit = jnp.where(place == 0, code >> CODE_BITS, jnp.where(place == 1, code & ((1 << CODE_BITS) - 1), 0))
    digits[...] = digit.astype(jnp.float32).astype(jnp.bfloat16)
    ids_fetch.wait()
    mats_fetch.wait()
    states_fetch.wait()


def pair_kernel(total, cap, slots, user_rows, *refs):
    users, (fields_hbm, rows32, rows16, mats, picked, out, places, fields, stacked, sem) = refs[:total], refs[total:]
    del picked
    fields_fetch = pltpu.make_async_copy(fields_hbm, fields, sem)
    fields_fetch.start()
    me = lax.axis_index("shard")
    readers, half = users[0].shape[1], places.shape[1]
    across = iota((readers, readers), 1)
    down = iota((readers, readers), 0)
    asks = (iota((readers, half), 1) // (half // readers) == iota((readers, half), 0)).astype(jnp.float32)
    for j in range(total):
        holder = users[j][...] >> (user_rows.bit_length() - 1)
        column = jnp.sum(jnp.where(across == down, holder, 0), axis=1, keepdims=True)
        rank = jnp.sum(jnp.where((down < across) & (column == holder), 1, 0), axis=0, keepdims=True)
        arrival = jnp.where(holder > me, me - holder + total, me - holder)
        slot = (arrival * slots + ring(me - j, total) * cap + rank).astype(jnp.float32)
        places[j:j + 1, :] = dot(slot, asks, NN, precision=lax.Precision.HIGHEST).astype(jnp.int32)
    pairs = mats.shape[2]
    steps = pairs // 2
    eye = (iota((steps, steps), 0) == iota((steps, steps), 1)).astype(jnp.bfloat16)
    for k in range(0, K, 2):
        sides = [mats[at, :, part * steps:(part + 1) * steps] for at in (k, k + 1) for part in range(2)]
        turned = dot(eye, jnp.concatenate(sides, axis=0), NT)
        stacked[pl.ds(k, steps, stride=PITCH), :] = turned[:, :LANES]
        stacked[pl.ds(k + 1, steps, stride=PITCH), :] = turned[:, LANES:]
    fields_fetch.wait()
    items = rows32.shape[1]
    blank = jnp.zeros((K, items), jnp.bfloat16)

    def two(p, total):
        fields_of = [(pl.multiple_of(fields[0, q] * K, K), pl.multiple_of(fields[1, q] * K, K)) for q in (p, p + steps)]
        left = stacked[pl.ds(pl.multiple_of(p * PITCH, 8), K), :].astype(jnp.bfloat16)
        first, second = [rows16[pl.ds(b, K), :] for _, b in fields_of]
        right = jnp.concatenate(
            [jnp.concatenate([first, blank], axis=1), jnp.concatenate([blank, second], axis=1)], axis=0
        )
        return total + dot(left, right, NN) * jnp.concatenate([rows32[pl.ds(a, K), :] for a, _ in fields_of], axis=1)

    sums = lax.fori_loop(0, steps, two, jnp.zeros((K, 2 * items), jnp.float32), unroll=32)
    line = jnp.sum(sums, axis=0, keepdims=True)
    out[...] = line[:, :items] + line[:, items:]


def thirds(x):
    high = x.astype(jnp.bfloat16)
    rest = x - high.astype(jnp.float32)
    middle = rest.astype(jnp.bfloat16)
    return high, middle, (rest - middle.astype(jnp.float32)).astype(jnp.bfloat16)


def linear_kernel(total, planes, *refs):
    states, refs = refs[:total], refs[total:]
    items, refs = refs[:planes], refs[planes:]
    places, out, hits, wanted, linear = refs
    slots = states[0].shape[0]
    own_rows, width = items[0].shape
    half = out.shape[1]
    me = lax.axis_index("shard")
    plane = lax.axis_index("cache")
    count = total * slots
    cands = []
    for j in range(total):
        wanted[j * slots:(j + 1) * slots, :] = states[j][:, :width]
        digits = states[j][:, width:].astype(jnp.float32)
        place = iota(digits.shape, 0)
        weight = jnp.where(place == 0, float(1 << CODE_BITS), jnp.where(place == 1, 1.0, 0.0))
        cands.append(jnp.sum(digits * weight, axis=0, keepdims=True).astype(jnp.int32))

    for q, rows in enumerate(items):
        for t, part in enumerate(thirds(dot(rows[...], wanted[...], NT))):
            linear[q * own_rows:(q + 1) * own_rows, t * count:(t + 1) * count] = part
    ids = [iota((own_rows, 1), 0) + (me * planes + ring(plane - q, planes)) * own_rows for q in range(planes)]
    item_ids = jnp.concatenate(ids, axis=0)
    for j in range(total):
        spread = (iota((count, half), 0) == places[j:j + 1, :]).astype(jnp.float32).astype(jnp.bfloat16)
        scores = dot(linear[...], jnp.concatenate([spread] * 3, axis=0), NN)
        hit = item_ids == cands[j]
        out[j:j + 1, :] = jnp.sum(jnp.where(hit, scores, 0.0), axis=0, keepdims=True)
        hits[:, j * half:(j + 1) * half] = hit.astype(jnp.float32).astype(jnp.bfloat16)


def score_kernel(total, planes, parts, *refs):
    pairs, (linear, hits), outs = refs[:planes * parts], refs[planes * parts:planes * parts + 2], refs[planes * parts + 2:]
    half = linear.shape[1]
    sums = [sum(pairs[(h + 1) * planes - 1 - q][...] for h in range(parts)) for q in range(planes)]
    row = jnp.concatenate(sums, axis=1)
    pieces = jnp.zeros((16, row.shape[1]), jnp.float32)
    for t, part in enumerate(thirds(row)):
        pieces = jnp.where(iota(pieces.shape, 0) == t, part.astype(jnp.float32), pieces)
    added = jnp.sum(dot(pieces.astype(jnp.bfloat16), hits[...], NN), axis=0, keepdims=True)
    for j in range(total):
        outs[j][...] = linear[j:j + 1, :] + added[:, j * half:(j + 1) * half]


def shift(x, axis, step):
    size = lax.axis_size(axis)
    return lax.ppermute(x, axis, [(s, (s + step) % size) for s in range(size)])


def body(cand_items, reader_users, item_table, user_states, pair_mats, pair_fields):
    total = lax.axis_size("shard")
    planes = lax.axis_size("cache")
    parts = lax.axis_size("pair")
    half = cand_items.shape[0]
    rows, width = item_table.shape
    readers = reader_users.shape[0]
    cap = 2 * ((readers + total - 1) // total)
    slots = -(-total * cap // 16) * 16
    count = pair_mats.shape[0]
    vmem = pl.BlockSpec(memory_space=pltpu.VMEM)
    hbm = pl.BlockSpec(memory_space=pltpu.HBM)
    anywhere = pl.BlockSpec(memory_space=pl.ANY)
    params = pltpu.CompilerParams(vmem_limit_bytes=VMEM_LIMIT)

    def in_hbm(x):
        return pltpu.with_memory_space_constraint(x, pltpu.HBM)

    with jax.named_scope("item_rows"):
        items = [item_table] + [shift(item_table, "cache", q) for q in range(1, planes)]

    with jax.named_scope("ids"):
        users = [shift(reader_users, "shard", j) for j in range(1, total)]

    with jax.named_scope("turn"):
        *turned, states_near, own_ids, digits = pl.pallas_call(
            turn_kernel,
            out_shape=(
                jax.ShapeDtypeStruct((width, rows), jnp.float32),
                jax.ShapeDtypeStruct((width, rows), jnp.bfloat16),
                jax.ShapeDtypeStruct((K, K, count), jnp.bfloat16),
                jax.ShapeDtypeStruct(user_states.shape, jnp.bfloat16),
                jax.ShapeDtypeStruct((1, readers), jnp.int32),
                jax.ShapeDtypeStruct((slots, half), jnp.bfloat16),
            ),
            in_specs=[hbm] * 5,
            out_specs=(vmem,) * 6,
            scratch_shapes=[
                pltpu.VMEM((rows, width), jnp.bfloat16),
                pltpu.VMEM((1, half), jnp.int32),
                pltpu.SemaphoreType.DMA((8,)),
            ],
            compiler_params=params,
            cost_estimate=pl.CostEstimate(flops=2 * rows * rows * width * 16, bytes_accessed=8 * 1024 * 1024, transcendentals=0),
        )(
            in_hbm(item_table),
            in_hbm(jnp.transpose(pair_mats, (1, 2, 0))),
            in_hbm(user_states),
            in_hbm(reader_users.reshape(1, readers)),
            in_hbm(cand_items.reshape(1, half)),
        )

    with jax.named_scope("states"):
        users_near = [own_ids] + [ids.reshape(1, readers) for ids in users]
        picked = pl.pallas_call(
            functools.partial(pick_kernel, total, cap),
            out_shape=jax.ShapeDtypeStruct((slots, width + half), jnp.bfloat16),
            in_specs=[vmem] * (total + 2),
            out_specs=vmem,
            compiler_params=params,
            cost_estimate=pl.CostEstimate(flops=2 * slots * rows * width, bytes_accessed=1024 * 1024, transcendentals=0),
        )(*users_near, digits, states_near)
        states = [picked] + [shift(picked, "shard", j) for j in range(1, total)]

    with jax.named_scope("pairs"):
        pair_parts, places = pl.pallas_call(
            functools.partial(pair_kernel, total, cap, slots, user_states.shape[0]),
            out_shape=(
                jax.ShapeDtypeStruct((1, rows), jnp.float32),
                jax.ShapeDtypeStruct((total, half), jnp.int32),
            ),
            in_specs=[vmem] * total + [hbm, vmem, vmem, vmem, anywhere],
            out_specs=(vmem, vmem),
            scratch_shapes=[
                pltpu.SMEM((2, count), jnp.int32),
                pltpu.VMEM((count // 2 * PITCH + K, LANES), jnp.float32),
                pltpu.SemaphoreType.DMA,
            ],
            compiler_params=params,
            cost_estimate=pl.CostEstimate(flops=2 * count * K * K * rows * 16, bytes_accessed=4 * 1024 * 1024, transcendentals=0),
        )(*users_near, in_hbm(pair_fields.T), *turned, picked)
        pair_scores = {(0, 0): pair_parts}
        steps = [(q, h) for q in range(planes - 1, -1, -1) for h in range(parts) if q or h]
        for q, h in steps:
            perm = [
                (c * parts + d, (c + q) % planes * parts + (d + h) % parts) for c in range(planes) for d in range(parts)
            ]
            source, after = pair_parts, {1: 1, 2: 2}.get(len(pair_scores) - 1, 0)
            if after:
                source, states[after] = lax.optimization_barrier((pair_parts, states[after]))
            pair_scores[q, h] = lax.ppermute(source, ("cache", "pair"), perm)
        pair_scores = [pair_scores[q, h] for h in range(parts) for q in range(planes - 1, -1, -1)]

    with jax.named_scope("scores"):
        linear, hits = pl.pallas_call(
            functools.partial(linear_kernel, total, planes),
            out_shape=(
                jax.ShapeDtypeStruct((total, half), jnp.float32),
                jax.ShapeDtypeStruct((planes * rows, total * half), jnp.bfloat16),
            ),
            in_specs=[vmem] * (total + len(items) + 1),
            out_specs=(vmem, vmem),
            scratch_shapes=[
                pltpu.VMEM((total * slots, width), jnp.bfloat16),
                pltpu.VMEM((planes * rows, 3 * total * slots), jnp.bfloat16),
            ],
            compiler_params=params,
            cost_estimate=pl.CostEstimate(flops=2 * 64 * 256 * width, bytes_accessed=2 * 1024 * 1024, transcendentals=0),
        )(*states, *items, places)
        outs = pl.pallas_call(
            functools.partial(score_kernel, total, planes, parts),
            out_shape=[jax.ShapeDtypeStruct((1, half), jnp.float32)] * total,
            in_specs=[vmem] * (planes * parts + 2),
            out_specs=[vmem] * total,
            compiler_params=params,
            cost_estimate=pl.CostEstimate(flops=2 * 16 * 256 * 512, bytes_accessed=512 * 1024, transcendentals=0),
        )(*pair_scores, linear, hits)

    with jax.named_scope("back"):
        result = outs[0]
        for j in sorted(range(1, total), key=lambda step: (step > total // 2, -step)):
            result = result + shift(outs[j], "shard", -j)
    return result.reshape(half)


def solution(mesh):
    return jax.shard_map(
        body,
        mesh=mesh,
        in_specs=(
            P(("groups", "shard", "cache", "pair")),
            P(("groups", "shard", "cache", "pair")),
            P(("shard", "cache"), None),
            P(("groups", "shard"), None),
            P("pair", None, None),
            P("pair", None),
        ),
        out_specs=P(("groups", "shard", "cache", "pair")),
        check_vma=False,
    )
```

```python
import functools

import jax
import jax.numpy as jnp
from jax import lax
from jax.experimental import pallas as pl
from jax.experimental.pallas import tpu as pltpu
from jax.sharding import PartitionSpec as P

K = 64
LANES = 128
PITCH = 72
CODE_BITS = 7
VMEM_LIMIT = 40 * 1024 * 1024
NT = (((1,), (1,)), ((), ()))
NN = (((1,), (0,)), ((), ()))


def dot(a, b, dims, **kw):
    return lax.dot_general(a, b, dims, preferred_element_type=jnp.float32, **kw)


def iota(shape, dim):
    return lax.broadcasted_iota(jnp.int32, shape, dim)


def ring(index, size):
    return lax.rem(index + size, size)


def pick_kernel(total, cap, *refs):
    users, (digits, states, out) = refs[:total], refs[total:]
    own_rows, width = states.shape
    slots = out.shape[0]
    readers = users[0].shape[1]
    me = lax.axis_index("shard")
    first = me * own_rows
    across = iota((readers, readers), 1)
    down = iota((readers, readers), 0)
    chosen = jnp.zeros((slots, own_rows), jnp.float32)
    for j in range(total):
        row = users[j][...]
        column = jnp.sum(jnp.where(across == down, row, 0), axis=1, keepdims=True)
        mine = (column >= first) & (column < first + own_rows)
        rank = jnp.sum(jnp.where((down < across) & mine, 1, 0), axis=0, keepdims=True)
        held = (row >= first) & (row < first + own_rows)
        slot = jnp.where(held, ring(me - j, total) * cap + rank, -1)
        to_slot = (iota((slots, readers), 0) == slot).astype(jnp.float32).astype(jnp.bfloat16)
        from_row = (iota((readers, own_rows), 1) + first == column).astype(jnp.float32).astype(jnp.bfloat16)
        chosen = chosen + dot(to_slot, from_row, NN)
    out[:, width:] = digits[...]
    out[:, :width] = dot(chosen.astype(jnp.bfloat16), states[...], NN).astype(jnp.bfloat16)


def turn_kernel(items_hbm, mats_hbm, states_hbm, ids_hbm, cands_hbm, rows32, rows16, mats, states, ids, digits, items, cands, sems):
    chunks = sems.shape[0] - 4
    wide = items.shape[1] // chunks
    item_fetches = [
        pltpu.make_async_copy(items_hbm.at[:, pl.ds(t * wide, wide)], items.at[:, pl.ds(t * wide, wide)], sems.at[t])
        for t in range(chunks)
    ]
    mats_fetch = pltpu.make_async_copy(mats_hbm, mats, sems.at[chunks])
    states_fetch = pltpu.make_async_copy(states_hbm, states, sems.at[chunks + 1])
    ids_fetch = pltpu.make_async_copy(ids_hbm, ids, sems.at[chunks + 2])
    cands_fetch = pltpu.make_async_copy(cands_hbm, cands, sems.at[chunks + 3])
    for copy in item_fetches + [mats_fetch, states_fetch, ids_fetch, cands_fetch]:
        copy.start()
    eye = (iota((LANES, LANES), 0) == iota((LANES, LANES), 1)).astype(jnp.bfloat16)
    for t in range(items.shape[1] // LANES):
        if t * LANES % wide == 0:
            item_fetches[t * LANES // wide].wait()
        turned = dot(eye, items[:, t * LANES:(t + 1) * LANES], NT)
        rows32[t * LANES:(t + 1) * LANES, :] = turned
        rows16[t * LANES:(t + 1) * LANES, :] = turned.astype(jnp.bfloat16)
    cands_fetch.wait()
    code = jnp.broadcast_to(cands[...], digits.shape)
    place = iota(digits.shape, 0)
    digit = jnp.where(place == 0, code >> CODE_BITS, jnp.where(place == 1, code & ((1 << CODE_BITS) - 1), 0))
    digits[...] = digit.astype(jnp.float32).astype(jnp.bfloat16)
    ids_fetch.wait()
    mats_fetch.wait()
    states_fetch.wait()


def pair_kernel(total, cap, slots, user_rows, *refs):
    users, (fields_hbm, rows32, rows16, mats, picked, out, places, fields, stacked, sem) = refs[:total], refs[total:]
    del picked
    fields_fetch = pltpu.make_async_copy(fields_hbm, fields, sem)
    fields_fetch.start()
    me = lax.axis_index("shard")
    readers, half = users[0].shape[1], places.shape[1]
    across = iota((readers, readers), 1)
    down = iota((readers, readers), 0)
    asks = (iota((readers, half), 1) // (half // readers) == iota((readers, half), 0)).astype(jnp.float32)
    for j in range(total):
        holder = users[j][...] >> (user_rows.bit_length() - 1)
        column = jnp.sum(jnp.where(across == down, holder, 0), axis=1, keepdims=True)
        rank = jnp.sum(jnp.where((down < across) & (column == holder), 1, 0), axis=0, keepdims=True)
        arrival = jnp.where(holder > me, me - holder + total, me - holder)
        slot = (arrival * slots + ring(me - j, total) * cap + rank).astype(jnp.float32)
        places[j:j + 1, :] = dot(slot, asks, NN, precision=lax.Precision.HIGHEST).astype(jnp.int32)
    pairs = mats.shape[2]
    steps = pairs // 2
    eye = (iota((steps, steps), 0) == iota((steps, steps), 1)).astype(jnp.bfloat16)
    for k in range(0, K, 2):
        sides = [mats[at, :, part * steps:(part + 1) * steps] for at in (k, k + 1) for part in range(2)]
        turned = dot(eye, jnp.concatenate(sides, axis=0), NT)
        stacked[pl.ds(k, steps, stride=PITCH), :] = turned[:, :LANES]
        stacked[pl.ds(k + 1, steps, stride=PITCH), :] = turned[:, LANES:]
    fields_fetch.wait()
    items = rows32.shape[1]
    blank = jnp.zeros((K, items), jnp.bfloat16)

    def two(p, total):
        fields_of = [(pl.multiple_of(fields[0, q] * K, K), pl.multiple_of(fields[1, q] * K, K)) for q in (p, p + steps)]
        left = stacked[pl.ds(pl.multiple_of(p * PITCH, 8), K), :].astype(jnp.bfloat16)
        first, second = [rows16[pl.ds(b, K), :] for _, b in fields_of]
        right = jnp.concatenate(
            [jnp.concatenate([first, blank], axis=1), jnp.concatenate([blank, second], axis=1)], axis=0
        )
        return total + dot(left, right, NN) * jnp.concatenate([rows32[pl.ds(a, K), :] for a, _ in fields_of], axis=1)

    sums = lax.fori_loop(0, steps, two, jnp.zeros((K, 2 * items), jnp.float32), unroll=64)
    line = jnp.sum(sums, axis=0, keepdims=True)
    out[...] = line[:, :items] + line[:, items:]


def thirds(x):
    high = x.astype(jnp.bfloat16)
    rest = x - high.astype(jnp.float32)
    middle = rest.astype(jnp.bfloat16)
    return high, middle, (rest - middle.astype(jnp.float32)).astype(jnp.bfloat16)


def linear_kernel(total, planes, *refs):
    states, refs = refs[:total], refs[total:]
    items, refs = refs[:planes], refs[planes:]
    places, out, hits, wanted, linear = refs
    slots = states[0].shape[0]
    own_rows, width = items[0].shape
    half = out.shape[1]
    me = lax.axis_index("shard")
    plane = lax.axis_index("cache")
    count = total * slots
    cands = []
    for j in range(total):
        wanted[j * slots:(j + 1) * slots, :] = states[j][:, :width]
        digits = states[j][:, width:].astype(jnp.float32)
        place = iota(digits.shape, 0)
        weight = jnp.where(place == 0, float(1 << CODE_BITS), jnp.where(place == 1, 1.0, 0.0))
        cands.append(jnp.sum(digits * weight, axis=0, keepdims=True).astype(jnp.int32))

    for q, rows in enumerate(items):
        for t, part in enumerate(thirds(dot(rows[...], wanted[...], NT))):
            linear[q * own_rows:(q + 1) * own_rows, t * count:(t + 1) * count] = part
    ids = [iota((own_rows, 1), 0) + (me * planes + ring(plane - q, planes)) * own_rows for q in range(planes)]
    item_ids = jnp.concatenate(ids, axis=0)
    for j in range(total):
        spread = (iota((count, half), 0) == places[j:j + 1, :]).astype(jnp.float32).astype(jnp.bfloat16)
        scores = dot(linear[...], jnp.concatenate([spread] * 3, axis=0), NN)
        hit = item_ids == cands[j]
        out[j:j + 1, :] = jnp.sum(jnp.where(hit, scores, 0.0), axis=0, keepdims=True)
        hits[:, j * half:(j + 1) * half] = hit.astype(jnp.float32).astype(jnp.bfloat16)


def score_kernel(total, planes, parts, *refs):
    pairs, (linear, hits), outs = refs[:planes * parts], refs[planes * parts:planes * parts + 2], refs[planes * parts + 2:]
    half = linear.shape[1]
    sums = [sum(pairs[(h + 1) * planes - 1 - q][...] for h in range(parts)) for q in range(planes)]
    row = jnp.concatenate(sums, axis=1)
    pieces = jnp.zeros((16, row.shape[1]), jnp.float32)
    for t, part in enumerate(thirds(row)):
        pieces = jnp.where(iota(pieces.shape, 0) == t, part.astype(jnp.float32), pieces)
    added = jnp.sum(dot(pieces.astype(jnp.bfloat16), hits[...], NN), axis=0, keepdims=True)
    for j in range(total):
        outs[j][...] = linear[j:j + 1, :] + added[:, j * half:(j + 1) * half]


def shift(x, axis, step):
    size = lax.axis_size(axis)
    return lax.ppermute(x, axis, [(s, (s + step) % size) for s in range(size)])


def body(cand_items, reader_users, item_table, user_states, pair_mats, pair_fields):
    total = lax.axis_size("shard")
    planes = lax.axis_size("cache")
    parts = lax.axis_size("pair")
    half = cand_items.shape[0]
    rows, width = item_table.shape
    readers = reader_users.shape[0]
    cap = 2 * ((readers + total - 1) // total)
    slots = -(-total * cap // 16) * 16
    count = pair_mats.shape[0]
    vmem = pl.BlockSpec(memory_space=pltpu.VMEM)
    hbm = pl.BlockSpec(memory_space=pltpu.HBM)
    anywhere = pl.BlockSpec(memory_space=pl.ANY)
    params = pltpu.CompilerParams(vmem_limit_bytes=VMEM_LIMIT)

    def in_hbm(x):
        return pltpu.with_memory_space_constraint(x, pltpu.HBM)

    with jax.named_scope("item_rows"):
        items = [item_table] + [shift(item_table, "cache", q) for q in range(1, planes)]

    with jax.named_scope("ids"):
        users = [shift(reader_users, "shard", j) for j in range(1, total)]

    with jax.named_scope("turn"):
        *turned, states_near, own_ids, digits = pl.pallas_call(
            turn_kernel,
            out_shape=(
                jax.ShapeDtypeStruct((width, rows), jnp.float32),
                jax.ShapeDtypeStruct((width, rows), jnp.bfloat16),
                jax.ShapeDtypeStruct((K, K, count), jnp.bfloat16),
                jax.ShapeDtypeStruct(user_states.shape, jnp.bfloat16),
                jax.ShapeDtypeStruct((1, readers), jnp.int32),
                jax.ShapeDtypeStruct((slots, half), jnp.bfloat16),
            ),
            in_specs=[hbm] * 5,
            out_specs=(vmem,) * 6,
            scratch_shapes=[
                pltpu.VMEM((rows, width), jnp.bfloat16),
                pltpu.VMEM((1, half), jnp.int32),
                pltpu.SemaphoreType.DMA((8,)),
            ],
            compiler_params=params,
            cost_estimate=pl.CostEstimate(flops=2 * rows * rows * width * 16, bytes_accessed=8 * 1024 * 1024, transcendentals=0),
        )(
            in_hbm(item_table),
            in_hbm(jnp.transpose(pair_mats, (1, 2, 0))),
            in_hbm(user_states),
            in_hbm(reader_users.reshape(1, readers)),
            in_hbm(cand_items.reshape(1, half)),
        )

    with jax.named_scope("states"):
        users_near = [own_ids] + [ids.reshape(1, readers) for ids in users]
        picked = pl.pallas_call(
            functools.partial(pick_kernel, total, cap),
            out_shape=jax.ShapeDtypeStruct((slots, width + half), jnp.bfloat16),
            in_specs=[vmem] * (total + 2),
            out_specs=vmem,
            compiler_params=params,
            cost_estimate=pl.CostEstimate(flops=2 * slots * rows * width, bytes_accessed=1024 * 1024, transcendentals=0),
        )(*users_near, digits, states_near)
        states = [picked] + [shift(picked, "shard", j) for j in range(1, total)]

    with jax.named_scope("pairs"):
        pair_parts, places = pl.pallas_call(
            functools.partial(pair_kernel, total, cap, slots, user_states.shape[0]),
            out_shape=(
                jax.ShapeDtypeStruct((1, rows), jnp.float32),
                jax.ShapeDtypeStruct((total, half), jnp.int32),
            ),
            in_specs=[vmem] * total + [hbm, vmem, vmem, vmem, anywhere],
            out_specs=(vmem, vmem),
            scratch_shapes=[
                pltpu.SMEM((2, count), jnp.int32),
                pltpu.VMEM((count // 2 * PITCH + K, LANES), jnp.float32),
                pltpu.SemaphoreType.DMA,
            ],
            compiler_params=params,
            cost_estimate=pl.CostEstimate(flops=2 * count * K * K * rows * 16, bytes_accessed=4 * 1024 * 1024, transcendentals=0),
        )(*users_near, in_hbm(pair_fields.T), *turned, picked)
        pair_scores = {(0, 0): pair_parts}
        steps = [(q, h) for q in range(planes - 1, -1, -1) for h in range(parts) if q or h]
        for q, h in steps:
            perm = [
                (c * parts + d, (c + q) % planes * parts + (d + h) % parts) for c in range(planes) for d in range(parts)
            ]
            source, after = pair_parts, {1: 1, 2: 2}.get(len(pair_scores) - 1, 0)
            if after:
                source, states[after] = lax.optimization_barrier((pair_parts, states[after]))
            pair_scores[q, h] = lax.ppermute(source, ("cache", "pair"), perm)
        pair_scores = [pair_scores[q, h] for h in range(parts) for q in range(planes - 1, -1, -1)]

    with jax.named_scope("scores"):
        linear, hits = pl.pallas_call(
            functools.partial(linear_kernel, total, planes),
            out_shape=(
                jax.ShapeDtypeStruct((total, half), jnp.float32),
                jax.ShapeDtypeStruct((planes * rows, total * half), jnp.bfloat16),
            ),
            in_specs=[vmem] * (total + len(items) + 1),
            out_specs=(vmem, vmem),
            scratch_shapes=[
                pltpu.VMEM((total * slots, width), jnp.bfloat16),
                pltpu.VMEM((planes * rows, 3 * total * slots), jnp.bfloat16),
            ],
            compiler_params=params,
            cost_estimate=pl.CostEstimate(flops=2 * 64 * 256 * width, bytes_accessed=2 * 1024 * 1024, transcendentals=0),
        )(*states, *items, places)
        outs = pl.pallas_call(
            functools.partial(score_kernel, total, planes, parts),
            out_shape=[jax.ShapeDtypeStruct((1, half), jnp.float32)] * total,
            in_specs=[vmem] * (planes * parts + 2),
            out_specs=[vmem] * total,
            compiler_params=params,
            cost_estimate=pl.CostEstimate(flops=2 * 16 * 256 * 512, bytes_accessed=512 * 1024, transcendentals=0),
        )(*pair_scores, linear, hits)

    with jax.named_scope("back"):
        result = outs[0]
        for j in range(1, total):
            result = result + shift(outs[j], "shard", -j)
    return result.reshape(half)


def solution(mesh):
    return jax.shard_map(
        body,
        mesh=mesh,
        in_specs=(
            P(("groups", "shard", "cache", "pair")),
            P(("groups", "shard", "cache", "pair")),
            P(("shard", "cache"), None),
            P(("groups", "shard"), None),
            P("pair", None, None),
            P("pair", None),
        ),
        out_specs=P(("groups", "shard", "cache", "pair")),
        check_vma=False,
    )
```

```python
import functools

import jax
import jax.numpy as jnp
from jax import lax
from jax.experimental import pallas as pl
from jax.experimental.pallas import tpu as pltpu
from jax.sharding import PartitionSpec as P

K = 64
LANES = 128
PITCH = 72
CODE_BITS = 7
VMEM_LIMIT = 40 * 1024 * 1024
NT = (((1,), (1,)), ((), ()))
NN = (((1,), (0,)), ((), ()))


def dot(a, b, dims, **kw):
    return lax.dot_general(a, b, dims, preferred_element_type=jnp.float32, **kw)


def iota(shape, dim):
    return lax.broadcasted_iota(jnp.int32, shape, dim)


def ring(index, size):
    return lax.rem(index + size, size)


def pick_kernel(total, cap, *refs):
    users, (digits, states, out) = refs[:total], refs[total:]
    own_rows, width = states.shape
    slots = out.shape[0]
    readers = users[0].shape[1]
    me = lax.axis_index("shard")
    first = me * own_rows
    across = iota((readers, readers), 1)
    down = iota((readers, readers), 0)
    chosen = jnp.zeros((slots, own_rows), jnp.float32)
    for j in range(total):
        row = users[j][...]
        column = jnp.sum(jnp.where(across == down, row, 0), axis=1, keepdims=True)
        mine = (column >= first) & (column < first + own_rows)
        rank = jnp.sum(jnp.where((down < across) & mine, 1, 0), axis=0, keepdims=True)
        held = (row >= first) & (row < first + own_rows)
        slot = jnp.where(held, ring(me - j, total) * cap + rank, -1)
        to_slot = (iota((slots, readers), 0) == slot).astype(jnp.float32).astype(jnp.bfloat16)
        from_row = (iota((readers, own_rows), 1) + first == column).astype(jnp.float32).astype(jnp.bfloat16)
        chosen = chosen + dot(to_slot, from_row, NN)
    out[:, width:] = digits[...]
    out[:, :width] = dot(chosen.astype(jnp.bfloat16), states[...], NN).astype(jnp.bfloat16)


def turn_kernel(items_hbm, mats_hbm, states_hbm, ids_hbm, cands_hbm, rows32, rows16, mats, states, ids, digits, items, cands, sems):
    chunks = sems.shape[0] - 4
    wide = items.shape[1] // chunks
    item_fetches = [
        pltpu.make_async_copy(items_hbm.at[:, pl.ds(t * wide, wide)], items.at[:, pl.ds(t * wide, wide)], sems.at[t])
        for t in range(chunks)
    ]
    mats_fetch = pltpu.make_async_copy(mats_hbm, mats, sems.at[chunks])
    states_fetch = pltpu.make_async_copy(states_hbm, states, sems.at[chunks + 1])
    ids_fetch = pltpu.make_async_copy(ids_hbm, ids, sems.at[chunks + 2])
    cands_fetch = pltpu.make_async_copy(cands_hbm, cands, sems.at[chunks + 3])
    for copy in item_fetches + [mats_fetch, states_fetch, ids_fetch, cands_fetch]:
        copy.start()
    eye = (iota((LANES, LANES), 0) == iota((LANES, LANES), 1)).astype(jnp.bfloat16)
    for t in range(items.shape[1] // LANES):
        if t * LANES % wide == 0:
            item_fetches[t * LANES // wide].wait()
        turned = dot(eye, items[:, t * LANES:(t + 1) * LANES], NT)
        rows32[t * LANES:(t + 1) * LANES, :] = turned
        rows16[t * LANES:(t + 1) * LANES, :] = turned.astype(jnp.bfloat16)
    cands_fetch.wait()
    code = jnp.broadcast_to(cands[...], digits.shape)
    place = iota(digits.shape, 0)
    digit = jnp.where(place == 0, code >> CODE_BITS, jnp.where(place == 1, code & ((1 << CODE_BITS) - 1), 0))
    digits[...] = digit.astype(jnp.float32).astype(jnp.bfloat16)
    ids_fetch.wait()
    mats_fetch.wait()
    states_fetch.wait()


def pair_kernel(total, cap, slots, user_rows, *refs):
    users, (fields_hbm, rows32, rows16, mats, picked, out, places, fields, stacked, sem) = refs[:total], refs[total:]
    del picked
    fields_fetch = pltpu.make_async_copy(fields_hbm, fields, sem)
    fields_fetch.start()
    me = lax.axis_index("shard")
    readers, half = users[0].shape[1], places.shape[1]
    across = iota((readers, readers), 1)
    down = iota((readers, readers), 0)
    asks = (iota((readers, half), 1) // (half // readers) == iota((readers, half), 0)).astype(jnp.float32)
    for j in range(total):
        holder = users[j][...] >> (user_rows.bit_length() - 1)
        column = jnp.sum(jnp.where(across == down, holder, 0), axis=1, keepdims=True)
        rank = jnp.sum(jnp.where((down < across) & (column == holder), 1, 0), axis=0, keepdims=True)
        arrival = jnp.where(holder > me, me - holder + total, me - holder)
        slot = (arrival * slots + ring(me - j, total) * cap + rank).astype(jnp.float32)
        places[j:j + 1, :] = dot(slot, asks, NN, precision=lax.Precision.HIGHEST).astype(jnp.int32)
    pairs = mats.shape[2]
    steps = pairs // 2
    eye = (iota((steps, steps), 0) == iota((steps, steps), 1)).astype(jnp.bfloat16)
    for k in range(0, K, 2):
        sides = [mats[at, :, part * steps:(part + 1) * steps] for at in (k, k + 1) for part in range(2)]
        turned = dot(eye, jnp.concatenate(sides, axis=0), NT)
        stacked[pl.ds(k, steps, stride=PITCH), :] = turned[:, :LANES]
        stacked[pl.ds(k + 1, steps, stride=PITCH), :] = turned[:, LANES:]
    fields_fetch.wait()
    items = rows32.shape[1]
    blank = jnp.zeros((K, items), jnp.bfloat16)

    def two(p, total):
        fields_of = [(pl.multiple_of(fields[0, q] * K, K), pl.multiple_of(fields[1, q] * K, K)) for q in (p, p + steps)]
        left = stacked[pl.ds(pl.multiple_of(p * PITCH, 8), K), :].astype(jnp.bfloat16)
        first, second = [rows16[pl.ds(b, K), :] for _, b in fields_of]
        right = jnp.concatenate(
            [jnp.concatenate([first, blank], axis=1), jnp.concatenate([blank, second], axis=1)], axis=0
        )
        return total + dot(left, right, NN) * jnp.concatenate([rows32[pl.ds(a, K), :] for a, _ in fields_of], axis=1)

    sums = lax.fori_loop(0, steps, two, jnp.zeros((K, 2 * items), jnp.float32), unroll=64)
    line = jnp.sum(sums, axis=0, keepdims=True)
    out[...] = line[:, :items] + line[:, items:]


def thirds(x):
    high = x.astype(jnp.bfloat16)
    rest = x - high.astype(jnp.float32)
    middle = rest.astype(jnp.bfloat16)
    return high, middle, (rest - middle.astype(jnp.float32)).astype(jnp.bfloat16)


def linear_kernel(total, planes, *refs):
    states, refs = refs[:total], refs[total:]
    items, refs = refs[:planes], refs[planes:]
    places, out, hits, wanted, linear = refs
    slots = states[0].shape[0]
    own_rows, width = items[0].shape
    half = out.shape[1]
    me = lax.axis_index("shard")
    plane = lax.axis_index("cache")
    count = total * slots
    cands = []
    for j in range(total):
        wanted[j * slots:(j + 1) * slots, :] = states[j][:, :width]
        digits = states[j][:, width:].astype(jnp.float32)
        place = iota(digits.shape, 0)
        weight = jnp.where(place == 0, float(1 << CODE_BITS), jnp.where(place == 1, 1.0, 0.0))
        cands.append(jnp.sum(digits * weight, axis=0, keepdims=True).astype(jnp.int32))

    for q, rows in enumerate(items):
        for t, part in enumerate(thirds(dot(rows[...], wanted[...], NT))):
            linear[q * own_rows:(q + 1) * own_rows, t * count:(t + 1) * count] = part
    ids = [iota((own_rows, 1), 0) + (me * planes + ring(plane - q, planes)) * own_rows for q in range(planes)]
    item_ids = jnp.concatenate(ids, axis=0)
    for j in range(total):
        spread = (iota((count, half), 0) == places[j:j + 1, :]).astype(jnp.float32).astype(jnp.bfloat16)
        scores = dot(linear[...], jnp.concatenate([spread] * 3, axis=0), NN)
        hit = item_ids == cands[j]
        out[j:j + 1, :] = jnp.sum(jnp.where(hit, scores, 0.0), axis=0, keepdims=True)
        hits[:, j * half:(j + 1) * half] = hit.astype(jnp.float32).astype(jnp.bfloat16)


def score_kernel(total, planes, parts, *refs):
    pairs, (linear, hits), outs = refs[:planes * parts], refs[planes * parts:planes * parts + 2], refs[planes * parts + 2:]
    half = linear.shape[1]
    sums = [sum(pairs[(h + 1) * planes - 1 - q][...] for h in range(parts)) for q in range(planes)]
    row = jnp.concatenate(sums, axis=1)
    pieces = jnp.zeros((16, row.shape[1]), jnp.float32)
    for t, part in enumerate(thirds(row)):
        pieces = jnp.where(iota(pieces.shape, 0) == t, part.astype(jnp.float32), pieces)
    added = jnp.sum(dot(pieces.astype(jnp.bfloat16), hits[...], NN), axis=0, keepdims=True)
    for j in range(total):
        outs[j][...] = linear[j:j + 1, :] + added[:, j * half:(j + 1) * half]


def shift(x, axis, step):
    size = lax.axis_size(axis)
    return lax.ppermute(x, axis, [(s, (s + step) % size) for s in range(size)])


def body(cand_items, reader_users, item_table, user_states, pair_mats, pair_fields):
    total = lax.axis_size("shard")
    planes = lax.axis_size("cache")
    parts = lax.axis_size("pair")
    half = cand_items.shape[0]
    rows, width = item_table.shape
    readers = reader_users.shape[0]
    cap = 2 * ((readers + total - 1) // total)
    slots = -(-total * cap // 16) * 16
    count = pair_mats.shape[0]
    vmem = pl.BlockSpec(memory_space=pltpu.VMEM)
    hbm = pl.BlockSpec(memory_space=pltpu.HBM)
    anywhere = pl.BlockSpec(memory_space=pl.ANY)
    params = pltpu.CompilerParams(vmem_limit_bytes=VMEM_LIMIT)

    def in_hbm(x):
        return pltpu.with_memory_space_constraint(x, pltpu.HBM)

    with jax.named_scope("item_rows"):
        items = [item_table] + [shift(item_table, "cache", q) for q in range(1, planes)]

    with jax.named_scope("ids"):
        users = [shift(reader_users, "shard", j) for j in range(1, total)]

    with jax.named_scope("turn"):
        *turned, states_near, own_ids, digits = pl.pallas_call(
            turn_kernel,
            out_shape=(
                jax.ShapeDtypeStruct((width, rows), jnp.float32),
                jax.ShapeDtypeStruct((width, rows), jnp.bfloat16),
                jax.ShapeDtypeStruct((K, K, count), jnp.bfloat16),
                jax.ShapeDtypeStruct(user_states.shape, jnp.bfloat16),
                jax.ShapeDtypeStruct((1, readers), jnp.int32),
                jax.ShapeDtypeStruct((slots, half), jnp.bfloat16),
            ),
            in_specs=[hbm] * 5,
            out_specs=(vmem,) * 6,
            scratch_shapes=[
                pltpu.VMEM((rows, width), jnp.bfloat16),
                pltpu.VMEM((1, half), jnp.int32),
                pltpu.SemaphoreType.DMA((8,)),
            ],
            compiler_params=params,
            cost_estimate=pl.CostEstimate(flops=2 * rows * rows * width * 16, bytes_accessed=8 * 1024 * 1024, transcendentals=0),
        )(
            in_hbm(item_table),
            in_hbm(jnp.transpose(pair_mats, (1, 2, 0))),
            in_hbm(user_states),
            in_hbm(reader_users.reshape(1, readers)),
            in_hbm(cand_items.reshape(1, half)),
        )

    with jax.named_scope("states"):
        users_near = [own_ids] + [ids.reshape(1, readers) for ids in users]
        picked = pl.pallas_call(
            functools.partial(pick_kernel, total, cap),
            out_shape=jax.ShapeDtypeStruct((slots, width + half), jnp.bfloat16),
            in_specs=[vmem] * (total + 2),
            out_specs=vmem,
            compiler_params=params,
            cost_estimate=pl.CostEstimate(flops=2 * slots * rows * width, bytes_accessed=1024 * 1024, transcendentals=0),
        )(*users_near, digits, states_near)
        states = [picked] + [shift(picked, "shard", j) for j in range(1, total)]

    with jax.named_scope("pairs"):
        pair_parts, places = pl.pallas_call(
            functools.partial(pair_kernel, total, cap, slots, user_states.shape[0]),
            out_shape=(
                jax.ShapeDtypeStruct((1, rows), jnp.float32),
                jax.ShapeDtypeStruct((total, half), jnp.int32),
            ),
            in_specs=[vmem] * total + [hbm, vmem, vmem, vmem, anywhere],
            out_specs=(vmem, vmem),
            scratch_shapes=[
                pltpu.SMEM((2, count), jnp.int32),
                pltpu.VMEM((count // 2 * PITCH + K, LANES), jnp.float32),
                pltpu.SemaphoreType.DMA,
            ],
            compiler_params=params,
            cost_estimate=pl.CostEstimate(flops=2 * count * K * K * rows * 16, bytes_accessed=4 * 1024 * 1024, transcendentals=0),
        )(*users_near, in_hbm(pair_fields.T), *turned, picked)
        pair_scores = {(0, 0): pair_parts}
        steps = [(q, h) for q in range(planes - 1, -1, -1) for h in range(parts) if q or h]
        for q, h in steps:
            perm = [
                (c * parts + d, (c + q) % planes * parts + (d + h) % parts) for c in range(planes) for d in range(parts)
            ]
            source, after = pair_parts, {1: 1, 2: 2}.get(len(pair_scores) - 1, 0)
            if after:
                source, states[after] = lax.optimization_barrier((pair_parts, states[after]))
            pair_scores[q, h] = lax.ppermute(source, ("cache", "pair"), perm)
        pair_scores = [pair_scores[q, h] for h in range(parts) for q in range(planes - 1, -1, -1)]

    with jax.named_scope("scores"):
        linear, hits = pl.pallas_call(
            functools.partial(linear_kernel, total, planes),
            out_shape=(
                jax.ShapeDtypeStruct((total, half), jnp.float32),
                jax.ShapeDtypeStruct((planes * rows, total * half), jnp.bfloat16),
            ),
            in_specs=[vmem] * (total + len(items) + 1),
            out_specs=(vmem, vmem),
            scratch_shapes=[
                pltpu.VMEM((total * slots, width), jnp.bfloat16),
                pltpu.VMEM((planes * rows, 3 * total * slots), jnp.bfloat16),
            ],
            compiler_params=params,
            cost_estimate=pl.CostEstimate(flops=2 * 64 * 256 * width, bytes_accessed=2 * 1024 * 1024, transcendentals=0),
        )(*states, *items, places)
        outs = pl.pallas_call(
            functools.partial(score_kernel, total, planes, parts),
            out_shape=[jax.ShapeDtypeStruct((1, half), jnp.float32)] * total,
            in_specs=[vmem] * (planes * parts + 2),
            out_specs=[vmem] * total,
            compiler_params=params,
            cost_estimate=pl.CostEstimate(flops=2 * 16 * 256 * 512, bytes_accessed=512 * 1024, transcendentals=0),
        )(*pair_scores, linear, hits)

    with jax.named_scope("back"):
        result = outs[0]
        for j in sorted(range(1, total), key=lambda step: (step == 1, step)):
            result = result + shift(outs[j], "shard", -j)
    return result.reshape(half)


def solution(mesh):
    return jax.shard_map(
        body,
        mesh=mesh,
        in_specs=(
            P(("groups", "shard", "cache", "pair")),
            P(("groups", "shard", "cache", "pair")),
            P(("shard", "cache"), None),
            P(("groups", "shard"), None),
            P("pair", None, None),
            P("pair", None),
        ),
        out_specs=P(("groups", "shard", "cache", "pair")),
        check_vma=False,
    )
```

```python
import functools

import jax
import jax.numpy as jnp
from jax import lax
from jax.experimental import pallas as pl
from jax.experimental.pallas import tpu as pltpu
from jax.sharding import PartitionSpec as P

K = 64
LANES = 128
PITCH = 72
CODE_BITS = 7
VMEM_LIMIT = 40 * 1024 * 1024
NT = (((1,), (1,)), ((), ()))
NN = (((1,), (0,)), ((), ()))


def dot(a, b, dims, **kw):
    return lax.dot_general(a, b, dims, preferred_element_type=jnp.float32, **kw)


def iota(shape, dim):
    return lax.broadcasted_iota(jnp.int32, shape, dim)


def ring(index, size):
    return lax.rem(index + size, size)


def pick_kernel(total, cap, *refs):
    users, (digits, states, out) = refs[:total], refs[total:]
    own_rows, width = states.shape
    slots = out.shape[0]
    readers = users[0].shape[1]
    me = lax.axis_index("shard")
    first = me * own_rows
    across = iota((readers, readers), 1)
    down = iota((readers, readers), 0)
    chosen = jnp.zeros((slots, own_rows), jnp.float32)
    for j in range(total):
        row = users[j][...]
        column = jnp.sum(jnp.where(across == down, row, 0), axis=1, keepdims=True)
        mine = (column >= first) & (column < first + own_rows)
        rank = jnp.sum(jnp.where((down < across) & mine, 1, 0), axis=0, keepdims=True)
        held = (row >= first) & (row < first + own_rows)
        slot = jnp.where(held, ring(me - j, total) * cap + rank, -1)
        to_slot = (iota((slots, readers), 0) == slot).astype(jnp.float32).astype(jnp.bfloat16)
        from_row = (iota((readers, own_rows), 1) + first == column).astype(jnp.float32).astype(jnp.bfloat16)
        chosen = chosen + dot(to_slot, from_row, NN)
    out[:, width:] = digits[...]
    out[:, :width] = dot(chosen.astype(jnp.bfloat16), states[...], NN).astype(jnp.bfloat16)


def turn_kernel(items_hbm, mats_hbm, states_hbm, ids_hbm, cands_hbm, rows32, rows16, mats, states, ids, digits, items, cands, sems):
    chunks = sems.shape[0] - 4
    wide = items.shape[1] // chunks
    item_fetches = [
        pltpu.make_async_copy(items_hbm.at[:, pl.ds(t * wide, wide)], items.at[:, pl.ds(t * wide, wide)], sems.at[t])
        for t in range(chunks)
    ]
    mats_fetch = pltpu.make_async_copy(mats_hbm, mats, sems.at[chunks])
    states_fetch = pltpu.make_async_copy(states_hbm, states, sems.at[chunks + 1])
    ids_fetch = pltpu.make_async_copy(ids_hbm, ids, sems.at[chunks + 2])
    cands_fetch = pltpu.make_async_copy(cands_hbm, cands, sems.at[chunks + 3])
    for copy in item_fetches + [mats_fetch, states_fetch, ids_fetch, cands_fetch]:
        copy.start()
    eye = (iota((LANES, LANES), 0) == iota((LANES, LANES), 1)).astype(jnp.bfloat16)
    for t in range(items.shape[1] // LANES):
        if t * LANES % wide == 0:
            item_fetches[t * LANES // wide].wait()
        turned = dot(eye, items[:, t * LANES:(t + 1) * LANES], NT)
        rows32[t * LANES:(t + 1) * LANES, :] = turned
        rows16[t * LANES:(t + 1) * LANES, :] = turned.astype(jnp.bfloat16)
    cands_fetch.wait()
    code = jnp.broadcast_to(cands[...], digits.shape)
    place = iota(digits.shape, 0)
    digit = jnp.where(place == 0, code >> CODE_BITS, jnp.where(place == 1, code & ((1 << CODE_BITS) - 1), 0))
    digits[...] = digit.astype(jnp.float32).astype(jnp.bfloat16)
    ids_fetch.wait()
    mats_fetch.wait()
    states_fetch.wait()


def pair_kernel(total, cap, slots, user_rows, *refs):
    users, (fields_hbm, rows32, rows16, mats, picked, out, places, fields, stacked, sem) = refs[:total], refs[total:]
    del picked
    fields_fetch = pltpu.make_async_copy(fields_hbm, fields, sem)
    fields_fetch.start()
    me = lax.axis_index("shard")
    readers, half = users[0].shape[1], places.shape[1]
    across = iota((readers, readers), 1)
    down = iota((readers, readers), 0)
    asks = (iota((readers, half), 1) // (half // readers) == iota((readers, half), 0)).astype(jnp.float32)
    for j in range(total):
        holder = users[j][...] >> (user_rows.bit_length() - 1)
        column = jnp.sum(jnp.where(across == down, holder, 0), axis=1, keepdims=True)
        rank = jnp.sum(jnp.where((down < across) & (column == holder), 1, 0), axis=0, keepdims=True)
        arrival = jnp.where(holder > me, me - holder + total, me - holder)
        slot = (arrival * slots + ring(me - j, total) * cap + rank).astype(jnp.float32)
        places[j:j + 1, :] = dot(slot, asks, NN, precision=lax.Precision.HIGHEST).astype(jnp.int32)
    pairs = mats.shape[2]
    steps = pairs // 2
    eye = (iota((steps, steps), 0) == iota((steps, steps), 1)).astype(jnp.bfloat16)
    for k in range(0, K, 2):
        sides = [mats[at, :, part * steps:(part + 1) * steps] for at in (k, k + 1) for part in range(2)]
        turned = dot(eye, jnp.concatenate(sides, axis=0), NT)
        stacked[pl.ds(k, steps, stride=PITCH), :] = turned[:, :LANES]
        stacked[pl.ds(k + 1, steps, stride=PITCH), :] = turned[:, LANES:]
    fields_fetch.wait()
    items = rows32.shape[1]
    blank = jnp.zeros((K, items), jnp.bfloat16)

    def two(p, total):
        fields_of = [(pl.multiple_of(fields[0, q] * K, K), pl.multiple_of(fields[1, q] * K, K)) for q in (p, p + steps)]
        left = stacked[pl.ds(pl.multiple_of(p * PITCH, 8), K), :].astype(jnp.bfloat16)
        first, second = [rows16[pl.ds(b, K), :] for _, b in fields_of]
        right = jnp.concatenate(
            [jnp.concatenate([first, blank], axis=1), jnp.concatenate([blank, second], axis=1)], axis=0
        )
        return total + dot(left, right, NN) * jnp.concatenate([rows32[pl.ds(a, K), :] for a, _ in fields_of], axis=1)

    sums = lax.fori_loop(0, steps, two, jnp.zeros((K, 2 * items), jnp.float32), unroll=64)
    line = jnp.sum(sums, axis=0, keepdims=True)
    out[...] = line[:, :items] + line[:, items:]


def thirds(x):
    high = x.astype(jnp.bfloat16)
    rest = x - high.astype(jnp.float32)
    middle = rest.astype(jnp.bfloat16)
    return high, middle, (rest - middle.astype(jnp.float32)).astype(jnp.bfloat16)


def linear_kernel(total, planes, *refs):
    states, refs = refs[:total], refs[total:]
    items, refs = refs[:planes], refs[planes:]
    places, out, hits, wanted, linear = refs
    slots = states[0].shape[0]
    own_rows, width = items[0].shape
    half = out.shape[1]
    me = lax.axis_index("shard")
    plane = lax.axis_index("cache")
    count = total * slots
    cands = []
    for j in range(total):
        wanted[j * slots:(j + 1) * slots, :] = states[j][:, :width]
        digits = states[j][:, width:].astype(jnp.float32)
        place = iota(digits.shape, 0)
        weight = jnp.where(place == 0, float(1 << CODE_BITS), jnp.where(place == 1, 1.0, 0.0))
        cands.append(jnp.sum(digits * weight, axis=0, keepdims=True).astype(jnp.int32))

    for q, rows in enumerate(items):
        for t, part in enumerate(thirds(dot(rows[...], wanted[...], NT))):
            linear[q * own_rows:(q + 1) * own_rows, t * count:(t + 1) * count] = part
    ids = [iota((own_rows, 1), 0) + (me * planes + ring(plane - q, planes)) * own_rows for q in range(planes)]
    item_ids = jnp.concatenate(ids, axis=0)
    for j in range(total):
        spread = (iota((count, half), 0) == places[j:j + 1, :]).astype(jnp.float32).astype(jnp.bfloat16)
        scores = dot(linear[...], jnp.concatenate([spread] * 3, axis=0), NN)
        hit = item_ids == cands[j]
        out[j:j + 1, :] = jnp.sum(jnp.where(hit, scores, 0.0), axis=0, keepdims=True)
        hits[:, j * half:(j + 1) * half] = hit.astype(jnp.float32).astype(jnp.bfloat16)


def score_kernel(total, planes, parts, *refs):
    pairs, (linear, hits), outs = refs[:planes * parts], refs[planes * parts:planes * parts + 2], refs[planes * parts + 2:]
    half = linear.shape[1]
    sums = [sum(pairs[(h + 1) * planes - 1 - q][...] for h in range(parts)) for q in range(planes)]
    row = jnp.concatenate(sums, axis=1)
    pieces = jnp.zeros((16, row.shape[1]), jnp.float32)
    for t, part in enumerate(thirds(row)):
        pieces = jnp.where(iota(pieces.shape, 0) == t, part.astype(jnp.float32), pieces)
    added = jnp.sum(dot(pieces.astype(jnp.bfloat16), hits[...], NN), axis=0, keepdims=True)
    for j in range(total):
        outs[j][...] = linear[j:j + 1, :] + added[:, j * half:(j + 1) * half]


def shift(x, axis, step):
    size = lax.axis_size(axis)
    return lax.ppermute(x, axis, [(s, (s + step) % size) for s in range(size)])


def body(cand_items, reader_users, item_table, user_states, pair_mats, pair_fields):
    total = lax.axis_size("shard")
    planes = lax.axis_size("cache")
    parts = lax.axis_size("pair")
    half = cand_items.shape[0]
    rows, width = item_table.shape
    readers = reader_users.shape[0]
    cap = 2 * ((readers + total - 1) // total)
    slots = -(-total * cap // 16) * 16
    count = pair_mats.shape[0]
    vmem = pl.BlockSpec(memory_space=pltpu.VMEM)
    hbm = pl.BlockSpec(memory_space=pltpu.HBM)
    anywhere = pl.BlockSpec(memory_space=pl.ANY)
    params = pltpu.CompilerParams(vmem_limit_bytes=VMEM_LIMIT)

    def in_hbm(x):
        return pltpu.with_memory_space_constraint(x, pltpu.HBM)

    with jax.named_scope("item_rows"):
        items = [item_table] + [shift(item_table, "cache", q) for q in range(1, planes)]

    with jax.named_scope("ids"):
        users = [shift(reader_users, "shard", j) for j in range(1, total)]

    with jax.named_scope("turn"):
        *turned, states_near, own_ids, digits = pl.pallas_call(
            turn_kernel,
            out_shape=(
                jax.ShapeDtypeStruct((width, rows), jnp.float32),
                jax.ShapeDtypeStruct((width, rows), jnp.bfloat16),
                jax.ShapeDtypeStruct((K, K, count), jnp.bfloat16),
                jax.ShapeDtypeStruct(user_states.shape, jnp.bfloat16),
                jax.ShapeDtypeStruct((1, readers), jnp.int32),
                jax.ShapeDtypeStruct((slots, half), jnp.bfloat16),
            ),
            in_specs=[hbm] * 5,
            out_specs=(vmem,) * 6,
            scratch_shapes=[
                pltpu.VMEM((rows, width), jnp.bfloat16),
                pltpu.VMEM((1, half), jnp.int32),
                pltpu.SemaphoreType.DMA((8,)),
            ],
            compiler_params=params,
            cost_estimate=pl.CostEstimate(flops=2 * rows * rows * width * 16, bytes_accessed=8 * 1024 * 1024, transcendentals=0),
        )(
            in_hbm(item_table),
            in_hbm(jnp.transpose(pair_mats, (1, 2, 0))),
            in_hbm(user_states),
            in_hbm(reader_users.reshape(1, readers)),
            in_hbm(cand_items.reshape(1, half)),
        )

    with jax.named_scope("states"):
        users_near = [own_ids] + [ids.reshape(1, readers) for ids in users]
        picked = pl.pallas_call(
            functools.partial(pick_kernel, total, cap),
            out_shape=jax.ShapeDtypeStruct((slots, width + half), jnp.bfloat16),
            in_specs=[vmem] * (total + 2),
            out_specs=vmem,
            compiler_params=params,
            cost_estimate=pl.CostEstimate(flops=2 * slots * rows * width, bytes_accessed=1024 * 1024, transcendentals=0),
        )(*users_near, digits, states_near)
        states = [picked] + [shift(picked, "shard", j) for j in range(1, total)]

    with jax.named_scope("pairs"):
        pair_parts, places = pl.pallas_call(
            functools.partial(pair_kernel, total, cap, slots, user_states.shape[0]),
            out_shape=(
                jax.ShapeDtypeStruct((1, rows), jnp.float32),
                jax.ShapeDtypeStruct((total, half), jnp.int32),
            ),
            in_specs=[vmem] * total + [hbm, vmem, vmem, vmem, anywhere],
            out_specs=(vmem, vmem),
            scratch_shapes=[
                pltpu.SMEM((2, count), jnp.int32),
                pltpu.VMEM((count // 2 * PITCH + K, LANES), jnp.float32),
                pltpu.SemaphoreType.DMA,
            ],
            compiler_params=params,
            cost_estimate=pl.CostEstimate(flops=2 * count * K * K * rows * 16, bytes_accessed=4 * 1024 * 1024, transcendentals=0),
        )(*users_near, in_hbm(pair_fields.T), *turned, picked)
        pair_scores = {(0, 0): pair_parts}
        steps = [(q, h) for q in range(planes - 1, -1, -1) for h in range(parts) if q or h]
        for q, h in steps:
            perm = [
                (c * parts + d, (c + q) % planes * parts + (d + h) % parts) for c in range(planes) for d in range(parts)
            ]
            source, after = pair_parts, {1: 2, 2: 1}.get(len(pair_scores) - 1, 0)
            if after:
                source, states[after] = lax.optimization_barrier((pair_parts, states[after]))
            pair_scores[q, h] = lax.ppermute(source, ("cache", "pair"), perm)
        pair_scores = [pair_scores[q, h] for h in range(parts) for q in range(planes - 1, -1, -1)]

    with jax.named_scope("scores"):
        linear, hits = pl.pallas_call(
            functools.partial(linear_kernel, total, planes),
            out_shape=(
                jax.ShapeDtypeStruct((total, half), jnp.float32),
                jax.ShapeDtypeStruct((planes * rows, total * half), jnp.bfloat16),
            ),
            in_specs=[vmem] * (total + len(items) + 1),
            out_specs=(vmem, vmem),
            scratch_shapes=[
                pltpu.VMEM((total * slots, width), jnp.bfloat16),
                pltpu.VMEM((planes * rows, 3 * total * slots), jnp.bfloat16),
            ],
            compiler_params=params,
            cost_estimate=pl.CostEstimate(flops=2 * 64 * 256 * width, bytes_accessed=2 * 1024 * 1024, transcendentals=0),
        )(*states, *items, places)
        outs = pl.pallas_call(
            functools.partial(score_kernel, total, planes, parts),
            out_shape=[jax.ShapeDtypeStruct((1, half), jnp.float32)] * total,
            in_specs=[vmem] * (planes * parts + 2),
            out_specs=[vmem] * total,
            compiler_params=params,
            cost_estimate=pl.CostEstimate(flops=2 * 16 * 256 * 512, bytes_accessed=512 * 1024, transcendentals=0),
        )(*pair_scores, linear, hits)

    with jax.named_scope("back"):
        result = outs[0]
        for j in range(1, total):
            result = result + shift(outs[j], "shard", -j)
    return result.reshape(half)


def solution(mesh):
    return jax.shard_map(
        body,
        mesh=mesh,
        in_specs=(
            P(("groups", "shard", "cache", "pair")),
            P(("groups", "shard", "cache", "pair")),
            P(("shard", "cache"), None),
            P(("groups", "shard"), None),
            P("pair", None, None),
            P("pair", None),
        ),
        out_specs=P(("groups", "shard", "cache", "pair")),
        check_vma=False,
    )
```

```python
import functools

import jax
import jax.numpy as jnp
from jax import lax
from jax.experimental import pallas as pl
from jax.experimental.pallas import tpu as pltpu
from jax.sharding import PartitionSpec as P

K = 64
LANES = 128
PITCH = 72
CODE_BITS = 7
VMEM_LIMIT = 40 * 1024 * 1024
NT = (((1,), (1,)), ((), ()))
NN = (((1,), (0,)), ((), ()))


def dot(a, b, dims, **kw):
    return lax.dot_general(a, b, dims, preferred_element_type=jnp.float32, **kw)


def iota(shape, dim):
    return lax.broadcasted_iota(jnp.int32, shape, dim)


def ring(index, size):
    return lax.rem(index + size, size)


def pick_kernel(total, cap, *refs):
    users, (digits, states, out) = refs[:total], refs[total:]
    own_rows, width = states.shape
    slots = out.shape[0]
    readers = users[0].shape[1]
    me = lax.axis_index("shard")
    first = me * own_rows
    across = iota((readers, readers), 1)
    down = iota((readers, readers), 0)
    chosen = jnp.zeros((slots, own_rows), jnp.float32)
    for j in range(total):
        row = users[j][...]
        column = jnp.sum(jnp.where(across == down, row, 0), axis=1, keepdims=True)
        mine = (column >= first) & (column < first + own_rows)
        rank = jnp.sum(jnp.where((down < across) & mine, 1, 0), axis=0, keepdims=True)
        held = (row >= first) & (row < first + own_rows)
        slot = jnp.where(held, ring(me - j, total) * cap + rank, -1)
        to_slot = (iota((slots, readers), 0) == slot).astype(jnp.float32).astype(jnp.bfloat16)
        from_row = (iota((readers, own_rows), 1) + first == column).astype(jnp.float32).astype(jnp.bfloat16)
        chosen = chosen + dot(to_slot, from_row, NN)
    out[:, width:] = digits[...]
    out[:, :width] = dot(chosen.astype(jnp.bfloat16), states[...], NN).astype(jnp.bfloat16)


def turn_kernel(items_hbm, mats_hbm, states_hbm, ids_hbm, cands_hbm, rows32, rows16, mats, states, ids, digits, items, cands, sems):
    chunks = sems.shape[0] - 4
    wide = items.shape[1] // chunks
    item_fetches = [
        pltpu.make_async_copy(items_hbm.at[:, pl.ds(t * wide, wide)], items.at[:, pl.ds(t * wide, wide)], sems.at[t])
        for t in range(chunks)
    ]
    mats_fetch = pltpu.make_async_copy(mats_hbm, mats, sems.at[chunks])
    states_fetch = pltpu.make_async_copy(states_hbm, states, sems.at[chunks + 1])
    ids_fetch = pltpu.make_async_copy(ids_hbm, ids, sems.at[chunks + 2])
    cands_fetch = pltpu.make_async_copy(cands_hbm, cands, sems.at[chunks + 3])
    for copy in item_fetches + [mats_fetch, states_fetch, ids_fetch, cands_fetch]:
        copy.start()
    eye = (iota((LANES, LANES), 0) == iota((LANES, LANES), 1)).astype(jnp.bfloat16)
    for t in range(items.shape[1] // LANES):
        if t * LANES % wide == 0:
            item_fetches[t * LANES // wide].wait()
        turned = dot(eye, items[:, t * LANES:(t + 1) * LANES], NT)
        rows32[t * LANES:(t + 1) * LANES, :] = turned
        rows16[t * LANES:(t + 1) * LANES, :] = turned.astype(jnp.bfloat16)
    cands_fetch.wait()
    code = jnp.broadcast_to(cands[...], digits.shape)
    place = iota(digits.shape, 0)
    digit = jnp.where(place == 0, code >> CODE_BITS, jnp.where(place == 1, code & ((1 << CODE_BITS) - 1), 0))
    digits[...] = digit.astype(jnp.float32).astype(jnp.bfloat16)
    ids_fetch.wait()
    mats_fetch.wait()
    states_fetch.wait()


def pair_kernel(fields_hbm, rows32, rows16, mats, picked, out, fields, stacked, sem):
    del picked
    fields_fetch = pltpu.make_async_copy(fields_hbm, fields, sem)
    fields_fetch.start()
    pairs = mats.shape[2]
    steps = pairs // 2
    eye = (iota((steps, steps), 0) == iota((steps, steps), 1)).astype(jnp.bfloat16)
    for k in range(0, K, 2):
        sides = [mats[at, :, part * steps:(part + 1) * steps] for at in (k, k + 1) for part in range(2)]
        turned = dot(eye, jnp.concatenate(sides, axis=0), NT)
        stacked[pl.ds(k, steps, stride=PITCH), :] = turned[:, :LANES]
        stacked[pl.ds(k + 1, steps, stride=PITCH), :] = turned[:, LANES:]
    fields_fetch.wait()
    items = rows32.shape[1]
    blank = jnp.zeros((K, items), jnp.bfloat16)

    def two(p, total):
        fields_of = [(pl.multiple_of(fields[0, q] * K, K), pl.multiple_of(fields[1, q] * K, K)) for q in (p, p + steps)]
        left = stacked[pl.ds(pl.multiple_of(p * PITCH, 8), K), :].astype(jnp.bfloat16)
        first, second = [rows16[pl.ds(b, K), :] for _, b in fields_of]
        right = jnp.concatenate(
            [jnp.concatenate([first, blank], axis=1), jnp.concatenate([blank, second], axis=1)], axis=0
        )
        return total + dot(left, right, NN) * jnp.concatenate([rows32[pl.ds(a, K), :] for a, _ in fields_of], axis=1)

    sums = lax.fori_loop(0, steps, two, jnp.zeros((K, 2 * items), jnp.float32), unroll=64)
    line = jnp.sum(sums, axis=0, keepdims=True)
    out[...] = line[:, :items] + line[:, items:]


def thirds(x):
    high = x.astype(jnp.bfloat16)
    rest = x - high.astype(jnp.float32)
    middle = rest.astype(jnp.bfloat16)
    return high, middle, (rest - middle.astype(jnp.float32)).astype(jnp.bfloat16)


def linear_kernel(total, planes, cap, user_rows, *refs):
    states, refs = refs[:total], refs[total:]
    items, refs = refs[:planes], refs[planes:]
    users, (out, hits, wanted, linear) = refs[:total], refs[total:]
    slots = states[0].shape[0]
    own_rows, width = items[0].shape
    half = out.shape[1]
    me = lax.axis_index("shard")
    plane = lax.axis_index("cache")
    count = total * slots
    cands = []
    for j in range(total):
        wanted[j * slots:(j + 1) * slots, :] = states[j][:, :width]
        digits = states[j][:, width:].astype(jnp.float32)
        place = iota(digits.shape, 0)
        weight = jnp.where(place == 0, float(1 << CODE_BITS), jnp.where(place == 1, 1.0, 0.0))
        cands.append(jnp.sum(digits * weight, axis=0, keepdims=True).astype(jnp.int32))

    for q, rows in enumerate(items):
        for t, part in enumerate(thirds(dot(rows[...], wanted[...], NT))):
            linear[q * own_rows:(q + 1) * own_rows, t * count:(t + 1) * count] = part
    ids = [iota((own_rows, 1), 0) + (me * planes + ring(plane - q, planes)) * own_rows for q in range(planes)]
    item_ids = jnp.concatenate(ids, axis=0)
    readers = users[0].shape[1]
    across = iota((readers, readers), 1)
    down = iota((readers, readers), 0)
    asks = (iota((readers, half), 1) // (half // readers) == iota((readers, half), 0)).astype(jnp.float32).astype(jnp.bfloat16)
    for j in range(total):
        holder = users[j][...] >> (user_rows.bit_length() - 1)
        column = jnp.sum(jnp.where(across == down, holder, 0), axis=1, keepdims=True)
        rank = jnp.sum(jnp.where((down < across) & (column == holder), 1, 0), axis=0, keepdims=True)
        arrival = jnp.where(holder > me, me - holder + total, me - holder)
        slot = arrival * slots + ring(me - j, total) * cap + rank
        at_slot = (iota((count, readers), 0) == slot).astype(jnp.float32).astype(jnp.bfloat16)
        spread = dot(at_slot, asks, NN).astype(jnp.bfloat16)
        scores = dot(linear[...], jnp.concatenate([spread] * 3, axis=0), NN)
        hit = item_ids == cands[j]
        out[j:j + 1, :] = jnp.sum(jnp.where(hit, scores, 0.0), axis=0, keepdims=True)
        hits[:, j * half:(j + 1) * half] = hit.astype(jnp.float32).astype(jnp.bfloat16)


def score_kernel(total, planes, parts, *refs):
    pairs, (linear, hits), outs = refs[:planes * parts], refs[planes * parts:planes * parts + 2], refs[planes * parts + 2:]
    half = linear.shape[1]
    sums = [sum(pairs[(h + 1) * planes - 1 - q][...] for h in range(parts)) for q in range(planes)]
    row = jnp.concatenate(sums, axis=1)
    pieces = jnp.zeros((16, row.shape[1]), jnp.float32)
    for t, part in enumerate(thirds(row)):
        pieces = jnp.where(iota(pieces.shape, 0) == t, part.astype(jnp.float32), pieces)
    added = jnp.sum(dot(pieces.astype(jnp.bfloat16), hits[...], NN), axis=0, keepdims=True)
    for j in range(total):
        outs[j][...] = linear[j:j + 1, :] + added[:, j * half:(j + 1) * half]


def shift(x, axis, step):
    size = lax.axis_size(axis)
    return lax.ppermute(x, axis, [(s, (s + step) % size) for s in range(size)])


def body(cand_items, reader_users, item_table, user_states, pair_mats, pair_fields):
    total = lax.axis_size("shard")
    planes = lax.axis_size("cache")
    parts = lax.axis_size("pair")
    half = cand_items.shape[0]
    rows, width = item_table.shape
    readers = reader_users.shape[0]
    cap = 2 * ((readers + total - 1) // total)
    slots = -(-total * cap // 16) * 16
    count = pair_mats.shape[0]
    vmem = pl.BlockSpec(memory_space=pltpu.VMEM)
    hbm = pl.BlockSpec(memory_space=pltpu.HBM)
    anywhere = pl.BlockSpec(memory_space=pl.ANY)
    params = pltpu.CompilerParams(vmem_limit_bytes=VMEM_LIMIT)

    def in_hbm(x):
        return pltpu.with_memory_space_constraint(x, pltpu.HBM)

    with jax.named_scope("item_rows"):
        items = [item_table] + [shift(item_table, "cache", q) for q in range(1, planes)]

    with jax.named_scope("ids"):
        users = [shift(reader_users, "shard", j) for j in range(1, total)]

    with jax.named_scope("turn"):
        *turned, states_near, own_ids, digits = pl.pallas_call(
            turn_kernel,
            out_shape=(
                jax.ShapeDtypeStruct((width, rows), jnp.float32),
                jax.ShapeDtypeStruct((width, rows), jnp.bfloat16),
                jax.ShapeDtypeStruct((K, K, count), jnp.bfloat16),
                jax.ShapeDtypeStruct(user_states.shape, jnp.bfloat16),
                jax.ShapeDtypeStruct((1, readers), jnp.int32),
                jax.ShapeDtypeStruct((slots, half), jnp.bfloat16),
            ),
            in_specs=[hbm] * 5,
            out_specs=(vmem,) * 6,
            scratch_shapes=[
                pltpu.VMEM((rows, width), jnp.bfloat16),
                pltpu.VMEM((1, half), jnp.int32),
                pltpu.SemaphoreType.DMA((8,)),
            ],
            compiler_params=params,
            cost_estimate=pl.CostEstimate(flops=2 * rows * rows * width * 16, bytes_accessed=8 * 1024 * 1024, transcendentals=0),
        )(
            in_hbm(item_table),
            in_hbm(jnp.transpose(pair_mats, (1, 2, 0))),
            in_hbm(user_states),
            in_hbm(reader_users.reshape(1, readers)),
            in_hbm(cand_items.reshape(1, half)),
        )

    with jax.named_scope("states"):
        users_near = [own_ids] + [ids.reshape(1, readers) for ids in users]
        picked = pl.pallas_call(
            functools.partial(pick_kernel, total, cap),
            out_shape=jax.ShapeDtypeStruct((slots, width + half), jnp.bfloat16),
            in_specs=[vmem] * (total + 2),
            out_specs=vmem,
            compiler_params=params,
            cost_estimate=pl.CostEstimate(flops=2 * slots * rows * width, bytes_accessed=1024 * 1024, transcendentals=0),
        )(*users_near, digits, states_near)
        states = [picked] + [shift(picked, "shard", j) for j in range(1, total)]

    with jax.named_scope("pairs"):
        pair_parts = pl.pallas_call(
            pair_kernel,
            out_shape=jax.ShapeDtypeStruct((1, rows), jnp.float32),
            in_specs=[hbm, vmem, vmem, vmem, anywhere],
            out_specs=vmem,
            scratch_shapes=[
                pltpu.SMEM((2, count), jnp.int32),
                pltpu.VMEM((count // 2 * PITCH + K, LANES), jnp.float32),
                pltpu.SemaphoreType.DMA,
            ],
            compiler_params=params,
            cost_estimate=pl.CostEstimate(flops=2 * count * K * K * rows * 16, bytes_accessed=4 * 1024 * 1024, transcendentals=0),
        )(in_hbm(pair_fields.T), *turned, picked)
        pair_scores = {(0, 0): pair_parts}
        steps = [(q, h) for q in range(planes - 1, -1, -1) for h in range(parts) if q or h]
        for q, h in steps:
            perm = [
                (c * parts + d, (c + q) % planes * parts + (d + h) % parts) for c in range(planes) for d in range(parts)
            ]
            source, after = pair_parts, {1: 2, 2: 1}.get(len(pair_scores) - 1, 0)
            if after:
                source, states[after] = lax.optimization_barrier((pair_parts, states[after]))
            pair_scores[q, h] = lax.ppermute(source, ("cache", "pair"), perm)
        pair_scores = [pair_scores[q, h] for h in range(parts) for q in range(planes - 1, -1, -1)]

    with jax.named_scope("scores"):
        linear, hits = pl.pallas_call(
            functools.partial(linear_kernel, total, planes, cap, user_states.shape[0]),
            out_shape=(
                jax.ShapeDtypeStruct((total, half), jnp.float32),
                jax.ShapeDtypeStruct((planes * rows, total * half), jnp.bfloat16),
            ),
            in_specs=[vmem] * (2 * total + len(items)),
            out_specs=(vmem, vmem),
            scratch_shapes=[
                pltpu.VMEM((total * slots, width), jnp.bfloat16),
                pltpu.VMEM((planes * rows, 3 * total * slots), jnp.bfloat16),
            ],
            compiler_params=params,
            cost_estimate=pl.CostEstimate(flops=2 * 64 * 256 * width, bytes_accessed=2 * 1024 * 1024, transcendentals=0),
        )(*states, *items, *users_near)
        outs = pl.pallas_call(
            functools.partial(score_kernel, total, planes, parts),
            out_shape=[jax.ShapeDtypeStruct((1, half), jnp.float32)] * total,
            in_specs=[vmem] * (planes * parts + 2),
            out_specs=[vmem] * total,
            compiler_params=params,
            cost_estimate=pl.CostEstimate(flops=2 * 16 * 256 * 512, bytes_accessed=512 * 1024, transcendentals=0),
        )(*pair_scores, linear, hits)

    with jax.named_scope("back"):
        result = outs[0]
        for j in range(1, total):
            result = result + shift(outs[j], "shard", -j)
    return result.reshape(half)


def solution(mesh):
    return jax.shard_map(
        body,
        mesh=mesh,
        in_specs=(
            P(("groups", "shard", "cache", "pair")),
            P(("groups", "shard", "cache", "pair")),
            P(("shard", "cache"), None),
            P(("groups", "shard"), None),
            P("pair", None, None),
            P("pair", None),
        ),
        out_specs=P(("groups", "shard", "cache", "pair")),
        check_vma=False,
    )
```

```python
import functools

import jax
import jax.numpy as jnp
from jax import lax
from jax.experimental import pallas as pl
from jax.experimental.pallas import tpu as pltpu
from jax.sharding import PartitionSpec as P

K = 64
LANES = 128
PITCH = 72
CODE_BITS = 7
VMEM_LIMIT = 40 * 1024 * 1024
NT = (((1,), (1,)), ((), ()))
NN = (((1,), (0,)), ((), ()))


def dot(a, b, dims, **kw):
    return lax.dot_general(a, b, dims, preferred_element_type=jnp.float32, **kw)


def iota(shape, dim):
    return lax.broadcasted_iota(jnp.int32, shape, dim)


def ring(index, size):
    return lax.rem(index + size, size)


def pick_kernel(total, cap, *refs):
    users, (digits, states, out) = refs[:total], refs[total:]
    own_rows, width = states.shape
    slots = out.shape[0]
    readers = users[0].shape[1]
    me = lax.axis_index("shard")
    first = me * own_rows
    across = iota((readers, readers), 1)
    down = iota((readers, readers), 0)
    chosen = jnp.zeros((slots, own_rows), jnp.float32)
    for j in range(total):
        row = users[j][...]
        column = jnp.sum(jnp.where(across == down, row, 0), axis=1, keepdims=True)
        mine = (column >= first) & (column < first + own_rows)
        rank = jnp.sum(jnp.where((down < across) & mine, 1, 0), axis=0, keepdims=True)
        held = (row >= first) & (row < first + own_rows)
        slot = jnp.where(held, ring(me - j, total) * cap + rank, -1)
        to_slot = (iota((slots, readers), 0) == slot).astype(jnp.float32).astype(jnp.bfloat16)
        from_row = (iota((readers, own_rows), 1) + first == column).astype(jnp.float32).astype(jnp.bfloat16)
        chosen = chosen + dot(to_slot, from_row, NN)
    out[:, width:] = digits[...]
    out[:, :width] = dot(chosen.astype(jnp.bfloat16), states[...], NN).astype(jnp.bfloat16)


def turn_kernel(items_hbm, mats_hbm, states_hbm, ids_hbm, cands_hbm, rows32, rows16, mats, states, ids, digits, items, cands, sems):
    chunks = sems.shape[0] - 4
    wide = items.shape[1] // chunks
    item_fetches = [
        pltpu.make_async_copy(items_hbm.at[:, pl.ds(t * wide, wide)], items.at[:, pl.ds(t * wide, wide)], sems.at[t])
        for t in range(chunks)
    ]
    mats_fetch = pltpu.make_async_copy(mats_hbm, mats, sems.at[chunks])
    states_fetch = pltpu.make_async_copy(states_hbm, states, sems.at[chunks + 1])
    ids_fetch = pltpu.make_async_copy(ids_hbm, ids, sems.at[chunks + 2])
    cands_fetch = pltpu.make_async_copy(cands_hbm, cands, sems.at[chunks + 3])
    for copy in item_fetches + [mats_fetch, states_fetch, ids_fetch, cands_fetch]:
        copy.start()
    eye = (iota((LANES, LANES), 0) == iota((LANES, LANES), 1)).astype(jnp.bfloat16)
    for t in range(items.shape[1] // LANES):
        if t * LANES % wide == 0:
            item_fetches[t * LANES // wide].wait()
        turned = dot(eye, items[:, t * LANES:(t + 1) * LANES], NT)
        rows32[t * LANES:(t + 1) * LANES, :] = turned
        rows16[t * LANES:(t + 1) * LANES, :] = turned.astype(jnp.bfloat16)
    cands_fetch.wait()
    code = jnp.broadcast_to(cands[...], digits.shape)
    place = iota(digits.shape, 0)
    digit = jnp.where(place == 0, code >> CODE_BITS, jnp.where(place == 1, code & ((1 << CODE_BITS) - 1), 0))
    digits[...] = digit.astype(jnp.float32).astype(jnp.bfloat16)
    ids_fetch.wait()
    mats_fetch.wait()
    states_fetch.wait()


def pair_kernel(total, cap, slots, user_rows, *refs):
    users, (fields_hbm, rows32, rows16, mats, picked, out, places, fields, stacked, sem) = refs[:total], refs[total:]
    del picked
    fields_fetch = pltpu.make_async_copy(fields_hbm, fields, sem)
    fields_fetch.start()
    me = lax.axis_index("shard")
    readers, half = users[0].shape[1], places.shape[1]
    across = iota((readers, readers), 1)
    down = iota((readers, readers), 0)
    asks = (iota((readers, half), 1) // (half // readers) == iota((readers, half), 0)).astype(jnp.float32)
    for j in range(total):
        holder = users[j][...] >> (user_rows.bit_length() - 1)
        column = jnp.sum(jnp.where(across == down, holder, 0), axis=1, keepdims=True)
        rank = jnp.sum(jnp.where((down < across) & (column == holder), 1, 0), axis=0, keepdims=True)
        arrival = jnp.where(holder > me, me - holder + total, me - holder)
        slot = (arrival * slots + ring(me - j, total) * cap + rank).astype(jnp.float32)
        places[j:j + 1, :] = dot(slot, asks, NN, precision=lax.Precision.HIGHEST).astype(jnp.int32)
    pairs = mats.shape[2]
    steps = pairs // 2
    eye = (iota((steps, steps), 0) == iota((steps, steps), 1)).astype(jnp.bfloat16)
    for k in range(0, K, 2):
        sides = [mats[at, :, part * steps:(part + 1) * steps] for at in (k, k + 1) for part in range(2)]
        turned = dot(eye, jnp.concatenate(sides, axis=0), NT)
        stacked[pl.ds(k, steps, stride=PITCH), :] = turned[:, :LANES]
        stacked[pl.ds(k + 1, steps, stride=PITCH), :] = turned[:, LANES:]
    fields_fetch.wait()
    items = rows32.shape[1]
    blank = jnp.zeros((K, items), jnp.bfloat16)

    def two(p, total):
        fields_of = [(pl.multiple_of(fields[0, q] * K, K), pl.multiple_of(fields[1, q] * K, K)) for q in (p, p + steps)]
        left = stacked[pl.ds(pl.multiple_of(p * PITCH, 8), K), :].astype(jnp.bfloat16)
        first, second = [rows16[pl.ds(b, K), :] for _, b in fields_of]
        right = jnp.concatenate(
            [jnp.concatenate([first, blank], axis=1), jnp.concatenate([blank, second], axis=1)], axis=0
        )
        return total + dot(left, right, NN) * jnp.concatenate([rows32[pl.ds(a, K), :] for a, _ in fields_of], axis=1)

    sums = lax.fori_loop(0, steps, two, jnp.zeros((K, 2 * items), jnp.float32), unroll=64)
    line = jnp.sum(sums, axis=0, keepdims=True)
    out[...] = line[:, :items] + line[:, items:]


def thirds(x):
    high = x.astype(jnp.bfloat16)
    rest = x - high.astype(jnp.float32)
    middle = rest.astype(jnp.bfloat16)
    return high, middle, (rest - middle.astype(jnp.float32)).astype(jnp.bfloat16)


def linear_kernel(total, planes, *refs):
    states, refs = refs[:total], refs[total:]
    items, refs = refs[:planes], refs[planes:]
    places, out, hits, wanted, linear = refs
    slots = states[0].shape[0]
    own_rows, width = items[0].shape
    half = out.shape[1]
    me = lax.axis_index("shard")
    plane = lax.axis_index("cache")
    count = total * slots
    cands = []
    for j in range(total):
        wanted[j * slots:(j + 1) * slots, :] = states[j][:, :width]
        digits = states[j][:, width:].astype(jnp.float32)
        place = iota(digits.shape, 0)
        weight = jnp.where(place == 0, float(1 << CODE_BITS), jnp.where(place == 1, 1.0, 0.0))
        cands.append(jnp.sum(digits * weight, axis=0, keepdims=True).astype(jnp.int32))

    for q, rows in enumerate(items):
        for t, part in enumerate(thirds(dot(rows[...], wanted[...], NT))):
            linear[q * own_rows:(q + 1) * own_rows, t * count:(t + 1) * count] = part
    ids = [iota((own_rows, 1), 0) + (me * planes + ring(plane - q, planes)) * own_rows for q in range(planes)]
    item_ids = jnp.concatenate(ids, axis=0)
    for j in range(total):
        spread = (iota((count, half), 0) == places[j:j + 1, :]).astype(jnp.float32).astype(jnp.bfloat16)
        scores = dot(linear[...], jnp.concatenate([spread] * 3, axis=0), NN)
        hit = item_ids == cands[j]
        out[j:j + 1, :] = jnp.sum(jnp.where(hit, scores, 0.0), axis=0, keepdims=True)
        hits[:, j * half:(j + 1) * half] = hit.astype(jnp.float32).astype(jnp.bfloat16)


def score_kernel(total, planes, parts, *refs):
    pairs, (linear, hits), outs = refs[:planes * parts], refs[planes * parts:planes * parts + 2], refs[planes * parts + 2:]
    half = linear.shape[1]
    sums = [sum(pairs[(h + 1) * planes - 1 - q][...] for h in range(parts)) for q in range(planes)]
    row = jnp.concatenate(sums, axis=1)
    pieces = jnp.zeros((16, row.shape[1]), jnp.float32)
    for t, part in enumerate(thirds(row)):
        pieces = jnp.where(iota(pieces.shape, 0) == t, part.astype(jnp.float32), pieces)
    added = jnp.sum(dot(pieces.astype(jnp.bfloat16), hits[...], NN), axis=0, keepdims=True)
    for j in range(total):
        outs[j][...] = linear[j:j + 1, :] + added[:, j * half:(j + 1) * half]


def shift(x, axis, step):
    size = lax.axis_size(axis)
    return lax.ppermute(x, axis, [(s, (s + step) % size) for s in range(size)])


def body(cand_items, reader_users, item_table, user_states, pair_mats, pair_fields):
    total = lax.axis_size("shard")
    planes = lax.axis_size("cache")
    parts = lax.axis_size("pair")
    half = cand_items.shape[0]
    rows, width = item_table.shape
    readers = reader_users.shape[0]
    cap = 2 * ((readers + total - 1) // total)
    slots = -(-total * cap // 16) * 16
    count = pair_mats.shape[0]
    vmem = pl.BlockSpec(memory_space=pltpu.VMEM)
    hbm = pl.BlockSpec(memory_space=pltpu.HBM)
    anywhere = pl.BlockSpec(memory_space=pl.ANY)
    params = pltpu.CompilerParams(vmem_limit_bytes=VMEM_LIMIT)

    def in_hbm(x):
        return pltpu.with_memory_space_constraint(x, pltpu.HBM)

    with jax.named_scope("item_rows"):
        items = [item_table] + [shift(item_table, "cache", q) for q in range(1, planes)]

    with jax.named_scope("ids"):
        users = [shift(reader_users, "shard", j) for j in range(1, total)]

    with jax.named_scope("turn"):
        *turned, states_near, own_ids, digits = pl.pallas_call(
            turn_kernel,
            out_shape=(
                jax.ShapeDtypeStruct((width, rows), jnp.float32),
                jax.ShapeDtypeStruct((width, rows), jnp.bfloat16),
                jax.ShapeDtypeStruct((K, K, count), jnp.bfloat16),
                jax.ShapeDtypeStruct(user_states.shape, jnp.bfloat16),
                jax.ShapeDtypeStruct((1, readers), jnp.int32),
                jax.ShapeDtypeStruct((slots, half), jnp.bfloat16),
            ),
            in_specs=[hbm] * 5,
            out_specs=(vmem,) * 6,
            scratch_shapes=[
                pltpu.VMEM((rows, width), jnp.bfloat16),
                pltpu.VMEM((1, half), jnp.int32),
                pltpu.SemaphoreType.DMA((8,)),
            ],
            compiler_params=params,
            cost_estimate=pl.CostEstimate(flops=2 * rows * rows * width * 16, bytes_accessed=8 * 1024 * 1024, transcendentals=0),
        )(
            in_hbm(item_table),
            in_hbm(jnp.transpose(pair_mats, (1, 2, 0))),
            in_hbm(user_states),
            in_hbm(reader_users.reshape(1, readers)),
            in_hbm(cand_items.reshape(1, half)),
        )

    with jax.named_scope("states"):
        users_near = [own_ids] + [ids.reshape(1, readers) for ids in users]
        picked = pl.pallas_call(
            functools.partial(pick_kernel, total, cap),
            out_shape=jax.ShapeDtypeStruct((slots, width + half), jnp.bfloat16),
            in_specs=[vmem] * (total + 2),
            out_specs=vmem,
            compiler_params=params,
            cost_estimate=pl.CostEstimate(flops=2 * slots * rows * width, bytes_accessed=1024 * 1024, transcendentals=0),
        )(*users_near, digits, states_near)
        states = [picked] + [shift(picked, "shard", j) for j in range(1, total)]

    with jax.named_scope("pairs"):
        pair_parts, places = pl.pallas_call(
            functools.partial(pair_kernel, total, cap, slots, user_states.shape[0]),
            out_shape=(
                jax.ShapeDtypeStruct((1, rows), jnp.float32),
                jax.ShapeDtypeStruct((total, half), jnp.int32),
            ),
            in_specs=[vmem] * total + [hbm, vmem, vmem, vmem, anywhere],
            out_specs=(vmem, vmem),
            scratch_shapes=[
                pltpu.SMEM((2, count), jnp.int32),
                pltpu.VMEM((count // 2 * PITCH + K, LANES), jnp.float32),
                pltpu.SemaphoreType.DMA,
            ],
            compiler_params=params,
            cost_estimate=pl.CostEstimate(flops=2 * count * K * K * rows * 16, bytes_accessed=4 * 1024 * 1024, transcendentals=0),
        )(*users_near, in_hbm(pair_fields.T), *turned, picked)
        pair_scores = {(0, 0): pair_parts}
        steps = [(q, h) for q in range(planes - 1, -1, -1) for h in range(parts) if q or h]
        for q, h in steps:
            perm = [
                (c * parts + d, (c + q) % planes * parts + (d + h) % parts) for c in range(planes) for d in range(parts)
            ]
            source, after = pair_parts, {1: 1, 2: 2}.get(len(pair_scores) - 1, 0)
            if after:
                source, states[after] = lax.optimization_barrier((pair_parts, states[after]))
            pair_scores[q, h] = lax.ppermute(source, ("cache", "pair"), perm)
        pair_scores = [pair_scores[q, h] for h in range(parts) for q in range(planes - 1, -1, -1)]

    with jax.named_scope("scores"):
        linear, hits = pl.pallas_call(
            functools.partial(linear_kernel, total, planes),
            out_shape=(
                jax.ShapeDtypeStruct((total, half), jnp.float32),
                jax.ShapeDtypeStruct((planes * rows, total * half), jnp.bfloat16),
            ),
            in_specs=[vmem] * (total + len(items) + 1),
            out_specs=(vmem, vmem),
            scratch_shapes=[
                pltpu.VMEM((total * slots, width), jnp.bfloat16),
                pltpu.VMEM((planes * rows, 3 * total * slots), jnp.bfloat16),
            ],
            compiler_params=params,
            cost_estimate=pl.CostEstimate(flops=2 * 64 * 256 * width, bytes_accessed=2 * 1024 * 1024, transcendentals=0),
        )(*states, *items, places)
        outs = pl.pallas_call(
            functools.partial(score_kernel, total, planes, parts),
            out_shape=[jax.ShapeDtypeStruct((1, half), jnp.float32)] * total,
            in_specs=[vmem] * (planes * parts + 2),
            out_specs=[vmem] * total,
            compiler_params=params,
            cost_estimate=pl.CostEstimate(flops=2 * 16 * 256 * 512, bytes_accessed=512 * 1024, transcendentals=0),
        )(*pair_scores, linear, hits)

    with jax.named_scope("back"):
        result = outs[0]
        for j in sorted(range(1, total), key=lambda step: (step + 1) % total):
            result = result + shift(outs[j], "shard", -j)
    return result.reshape(half)


def solution(mesh):
    return jax.shard_map(
        body,
        mesh=mesh,
        in_specs=(
            P(("groups", "shard", "cache", "pair")),
            P(("groups", "shard", "cache", "pair")),
            P(("shard", "cache"), None),
            P(("groups", "shard"), None),
            P("pair", None, None),
            P("pair", None),
        ),
        out_specs=P(("groups", "shard", "cache", "pair")),
        check_vma=False,
    )
```

```python
import functools

import jax
import jax.numpy as jnp
from jax import lax
from jax.experimental import pallas as pl
from jax.experimental.pallas import tpu as pltpu
from jax.sharding import PartitionSpec as P

K = 64
LANES = 128
PITCH = 72
CODE_BITS = 7
VMEM_LIMIT = 40 * 1024 * 1024
NT = (((1,), (1,)), ((), ()))
NN = (((1,), (0,)), ((), ()))


def dot(a, b, dims, **kw):
    return lax.dot_general(a, b, dims, preferred_element_type=jnp.float32, **kw)


def iota(shape, dim):
    return lax.broadcasted_iota(jnp.int32, shape, dim)


def ring(index, size):
    return lax.rem(index + size, size)


def pick_kernel(total, cap, *refs):
    users, (digits, states, out) = refs[:total], refs[total:]
    own_rows, width = states.shape
    slots = out.shape[0]
    readers = users[0].shape[1]
    me = lax.axis_index("shard")
    first = me * own_rows
    across = iota((readers, readers), 1)
    down = iota((readers, readers), 0)
    chosen = jnp.zeros((slots, own_rows), jnp.float32)
    for j in range(total):
        row = users[j][...]
        column = jnp.sum(jnp.where(across == down, row, 0), axis=1, keepdims=True)
        mine = (column >= first) & (column < first + own_rows)
        rank = jnp.sum(jnp.where((down < across) & mine, 1, 0), axis=0, keepdims=True)
        held = (row >= first) & (row < first + own_rows)
        slot = jnp.where(held, ring(me - j, total) * cap + rank, -1)
        to_slot = (iota((slots, readers), 0) == slot).astype(jnp.float32).astype(jnp.bfloat16)
        from_row = (iota((readers, own_rows), 1) + first == column).astype(jnp.float32).astype(jnp.bfloat16)
        chosen = chosen + dot(to_slot, from_row, NN)
    out[:, width:] = digits[...]
    out[:, :width] = dot(chosen.astype(jnp.bfloat16), states[...], NN).astype(jnp.bfloat16)


def turn_kernel(items_hbm, mats_hbm, states_hbm, ids_hbm, cands_hbm, rows32, rows16, mats, states, ids, digits, items, cands, sems):
    chunks = sems.shape[0] - 4
    wide = items.shape[1] // chunks
    item_fetches = [
        pltpu.make_async_copy(items_hbm.at[:, pl.ds(t * wide, wide)], items.at[:, pl.ds(t * wide, wide)], sems.at[t])
        for t in range(chunks)
    ]
    mats_fetch = pltpu.make_async_copy(mats_hbm, mats, sems.at[chunks])
    states_fetch = pltpu.make_async_copy(states_hbm, states, sems.at[chunks + 1])
    ids_fetch = pltpu.make_async_copy(ids_hbm, ids, sems.at[chunks + 2])
    cands_fetch = pltpu.make_async_copy(cands_hbm, cands, sems.at[chunks + 3])
    for copy in item_fetches + [mats_fetch, states_fetch, ids_fetch, cands_fetch]:
        copy.start()
    eye = (iota((LANES, LANES), 0) == iota((LANES, LANES), 1)).astype(jnp.bfloat16)
    for t in range(items.shape[1] // LANES):
        if t * LANES % wide == 0:
            item_fetches[t * LANES // wide].wait()
        turned = dot(eye, items[:, t * LANES:(t + 1) * LANES], NT)
        rows32[t * LANES:(t + 1) * LANES, :] = turned
        rows16[t * LANES:(t + 1) * LANES, :] = turned.astype(jnp.bfloat16)
    cands_fetch.wait()
    code = jnp.broadcast_to(cands[...], digits.shape)
    place = iota(digits.shape, 0)
    digit = jnp.where(place == 0, code >> CODE_BITS, jnp.where(place == 1, code & ((1 << CODE_BITS) - 1), 0))
    digits[...] = digit.astype(jnp.float32).astype(jnp.bfloat16)
    ids_fetch.wait()
    mats_fetch.wait()
    states_fetch.wait()


def pair_kernel(total, cap, slots, user_rows, *refs):
    users, (fields_hbm, rows32, rows16, mats, picked, out, places, fields, stacked, sem) = refs[:total], refs[total:]
    del picked
    fields_fetch = pltpu.make_async_copy(fields_hbm, fields, sem)
    fields_fetch.start()
    me = lax.axis_index("shard")
    readers, half = users[0].shape[1], places.shape[1]
    across = iota((readers, readers), 1)
    down = iota((readers, readers), 0)
    asks = (iota((readers, half), 1) // (half // readers) == iota((readers, half), 0)).astype(jnp.float32)
    for j in range(total):
        holder = users[j][...] >> (user_rows.bit_length() - 1)
        column = jnp.sum(jnp.where(across == down, holder, 0), axis=1, keepdims=True)
        rank = jnp.sum(jnp.where((down < across) & (column == holder), 1, 0), axis=0, keepdims=True)
        arrival = jnp.where(holder > me, me - holder + total, me - holder)
        slot = (arrival * slots + ring(me - j, total) * cap + rank).astype(jnp.float32)
        places[j:j + 1, :] = dot(slot, asks, NN, precision=lax.Precision.HIGHEST).astype(jnp.int32)
    pairs = mats.shape[2]
    steps = pairs // 2
    eye = (iota((steps, steps), 0) == iota((steps, steps), 1)).astype(jnp.bfloat16)
    for k in range(0, K, 2):
        sides = [mats[at, :, part * steps:(part + 1) * steps] for at in (k, k + 1) for part in range(2)]
        turned = dot(eye, jnp.concatenate(sides, axis=0), NT)
        stacked[pl.ds(k, steps, stride=PITCH), :] = turned[:, :LANES]
        stacked[pl.ds(k + 1, steps, stride=PITCH), :] = turned[:, LANES:]
    fields_fetch.wait()
    items = rows32.shape[1]
    blank = jnp.zeros((K, items), jnp.bfloat16)

    def two(p, total):
        fields_of = [(pl.multiple_of(fields[0, q] * K, K), pl.multiple_of(fields[1, q] * K, K)) for q in (p, p + steps)]
        left = stacked[pl.ds(pl.multiple_of(p * PITCH, 8), K), :].astype(jnp.bfloat16)
        first, second = [rows16[pl.ds(b, K), :] for _, b in fields_of]
        right = jnp.concatenate(
            [jnp.concatenate([first, blank], axis=1), jnp.concatenate([blank, second], axis=1)], axis=0
        )
        return total + dot(left, right, NN) * jnp.concatenate([rows32[pl.ds(a, K), :] for a, _ in fields_of], axis=1)

    sums = lax.fori_loop(0, steps, two, jnp.zeros((K, 2 * items), jnp.float32), unroll=128)
    line = jnp.sum(sums, axis=0, keepdims=True)
    out[...] = line[:, :items] + line[:, items:]


def thirds(x):
    high = x.astype(jnp.bfloat16)
    rest = x - high.astype(jnp.float32)
    middle = rest.astype(jnp.bfloat16)
    return high, middle, (rest - middle.astype(jnp.float32)).astype(jnp.bfloat16)


def linear_kernel(total, planes, *refs):
    states, refs = refs[:total], refs[total:]
    items, refs = refs[:planes], refs[planes:]
    places, out, hits, wanted, linear = refs
    slots = states[0].shape[0]
    own_rows, width = items[0].shape
    half = out.shape[1]
    me = lax.axis_index("shard")
    plane = lax.axis_index("cache")
    count = total * slots
    cands = []
    for j in range(total):
        wanted[j * slots:(j + 1) * slots, :] = states[j][:, :width]
        digits = states[j][:, width:].astype(jnp.float32)
        place = iota(digits.shape, 0)
        weight = jnp.where(place == 0, float(1 << CODE_BITS), jnp.where(place == 1, 1.0, 0.0))
        cands.append(jnp.sum(digits * weight, axis=0, keepdims=True).astype(jnp.int32))

    for q, rows in enumerate(items):
        for t, part in enumerate(thirds(dot(rows[...], wanted[...], NT))):
            linear[q * own_rows:(q + 1) * own_rows, t * count:(t + 1) * count] = part
    ids = [iota((own_rows, 1), 0) + (me * planes + ring(plane - q, planes)) * own_rows for q in range(planes)]
    item_ids = jnp.concatenate(ids, axis=0)
    for j in range(total):
        spread = (iota((count, half), 0) == places[j:j + 1, :]).astype(jnp.float32).astype(jnp.bfloat16)
        scores = dot(linear[...], jnp.concatenate([spread] * 3, axis=0), NN)
        hit = item_ids == cands[j]
        out[j:j + 1, :] = jnp.sum(jnp.where(hit, scores, 0.0), axis=0, keepdims=True)
        hits[:, j * half:(j + 1) * half] = hit.astype(jnp.float32).astype(jnp.bfloat16)


def score_kernel(total, planes, parts, *refs):
    pairs, (linear, hits), outs = refs[:planes * parts], refs[planes * parts:planes * parts + 2], refs[planes * parts + 2:]
    half = linear.shape[1]
    sums = [sum(pairs[(h + 1) * planes - 1 - q][...] for h in range(parts)) for q in range(planes)]
    row = jnp.concatenate(sums, axis=1)
    pieces = jnp.zeros((16, row.shape[1]), jnp.float32)
    for t, part in enumerate(thirds(row)):
        pieces = jnp.where(iota(pieces.shape, 0) == t, part.astype(jnp.float32), pieces)
    added = jnp.sum(dot(pieces.astype(jnp.bfloat16), hits[...], NN), axis=0, keepdims=True)
    for j in range(total):
        outs[j][...] = linear[j:j + 1, :] + added[:, j * half:(j + 1) * half]


def shift(x, axis, step):
    size = lax.axis_size(axis)
    return lax.ppermute(x, axis, [(s, (s + step) % size) for s in range(size)])


def body(cand_items, reader_users, item_table, user_states, pair_mats, pair_fields):
    total = lax.axis_size("shard")
    planes = lax.axis_size("cache")
    parts = lax.axis_size("pair")
    half = cand_items.shape[0]
    rows, width = item_table.shape
    readers = reader_users.shape[0]
    cap = 2 * ((readers + total - 1) // total)
    slots = -(-total * cap // 16) * 16
    count = pair_mats.shape[0]
    vmem = pl.BlockSpec(memory_space=pltpu.VMEM)
    hbm = pl.BlockSpec(memory_space=pltpu.HBM)
    anywhere = pl.BlockSpec(memory_space=pl.ANY)
    params = pltpu.CompilerParams(vmem_limit_bytes=VMEM_LIMIT)

    def in_hbm(x):
        return pltpu.with_memory_space_constraint(x, pltpu.HBM)

    with jax.named_scope("item_rows"):
        items = [item_table] + [shift(item_table, "cache", q) for q in range(1, planes)]

    with jax.named_scope("ids"):
        users = [shift(reader_users, "shard", j) for j in range(1, total)]

    with jax.named_scope("turn"):
        *turned, states_near, own_ids, digits = pl.pallas_call(
            turn_kernel,
            out_shape=(
                jax.ShapeDtypeStruct((width, rows), jnp.float32),
                jax.ShapeDtypeStruct((width, rows), jnp.bfloat16),
                jax.ShapeDtypeStruct((K, K, count), jnp.bfloat16),
                jax.ShapeDtypeStruct(user_states.shape, jnp.bfloat16),
                jax.ShapeDtypeStruct((1, readers), jnp.int32),
                jax.ShapeDtypeStruct((slots, half), jnp.bfloat16),
            ),
            in_specs=[hbm] * 5,
            out_specs=(vmem,) * 6,
            scratch_shapes=[
                pltpu.VMEM((rows, width), jnp.bfloat16),
                pltpu.VMEM((1, half), jnp.int32),
                pltpu.SemaphoreType.DMA((8,)),
            ],
            compiler_params=params,
            cost_estimate=pl.CostEstimate(flops=2 * rows * rows * width * 16, bytes_accessed=8 * 1024 * 1024, transcendentals=0),
        )(
            in_hbm(item_table),
            in_hbm(jnp.transpose(pair_mats, (1, 2, 0))),
            in_hbm(user_states),
            in_hbm(reader_users.reshape(1, readers)),
            in_hbm(cand_items.reshape(1, half)),
        )

    with jax.named_scope("states"):
        users_near = [own_ids] + [ids.reshape(1, readers) for ids in users]
        picked = pl.pallas_call(
            functools.partial(pick_kernel, total, cap),
            out_shape=jax.ShapeDtypeStruct((slots, width + half), jnp.bfloat16),
            in_specs=[vmem] * (total + 2),
            out_specs=vmem,
            compiler_params=params,
            cost_estimate=pl.CostEstimate(flops=2 * slots * rows * width, bytes_accessed=1024 * 1024, transcendentals=0),
        )(*users_near, digits, states_near)
        states = [picked] + [shift(picked, "shard", j) for j in range(1, total)]

    with jax.named_scope("pairs"):
        pair_parts, places = pl.pallas_call(
            functools.partial(pair_kernel, total, cap, slots, user_states.shape[0]),
            out_shape=(
                jax.ShapeDtypeStruct((1, rows), jnp.float32),
                jax.ShapeDtypeStruct((total, half), jnp.int32),
            ),
            in_specs=[vmem] * total + [hbm, vmem, vmem, vmem, anywhere],
            out_specs=(vmem, vmem),
            scratch_shapes=[
                pltpu.SMEM((2, count), jnp.int32),
                pltpu.VMEM((count // 2 * PITCH + K, LANES), jnp.float32),
                pltpu.SemaphoreType.DMA,
            ],
            compiler_params=params,
            cost_estimate=pl.CostEstimate(flops=2 * count * K * K * rows * 16, bytes_accessed=4 * 1024 * 1024, transcendentals=0),
        )(*users_near, in_hbm(pair_fields.T), *turned, picked)
        pair_scores = {(0, 0): pair_parts}
        steps = [(q, h) for q in range(planes - 1, -1, -1) for h in range(parts) if q or h]
        for q, h in steps:
            perm = [
                (c * parts + d, (c + q) % planes * parts + (d + h) % parts) for c in range(planes) for d in range(parts)
            ]
            source, after = pair_parts, {1: 2, 2: 1}.get(len(pair_scores) - 1, 0)
            if after:
                source, states[after] = lax.optimization_barrier((pair_parts, states[after]))
            pair_scores[q, h] = lax.ppermute(source, ("cache", "pair"), perm)
        pair_scores = [pair_scores[q, h] for h in range(parts) for q in range(planes - 1, -1, -1)]

    with jax.named_scope("scores"):
        linear, hits = pl.pallas_call(
            functools.partial(linear_kernel, total, planes),
            out_shape=(
                jax.ShapeDtypeStruct((total, half), jnp.float32),
                jax.ShapeDtypeStruct((planes * rows, total * half), jnp.bfloat16),
            ),
            in_specs=[vmem] * (total + len(items) + 1),
            out_specs=(vmem, vmem),
            scratch_shapes=[
                pltpu.VMEM((total * slots, width), jnp.bfloat16),
                pltpu.VMEM((planes * rows, 3 * total * slots), jnp.bfloat16),
            ],
            compiler_params=params,
            cost_estimate=pl.CostEstimate(flops=2 * 64 * 256 * width, bytes_accessed=2 * 1024 * 1024, transcendentals=0),
        )(*states, *items, places)
        outs = pl.pallas_call(
            functools.partial(score_kernel, total, planes, parts),
            out_shape=[jax.ShapeDtypeStruct((1, half), jnp.float32)] * total,
            in_specs=[vmem] * (planes * parts + 2),
            out_specs=[vmem] * total,
            compiler_params=params,
            cost_estimate=pl.CostEstimate(flops=2 * 16 * 256 * 512, bytes_accessed=512 * 1024, transcendentals=0),
        )(*pair_scores, linear, hits)

    with jax.named_scope("back"):
        result = outs[0]
        for j in range(1, total):
            result = result + shift(outs[j], "shard", -j)
    return result.reshape(half)


def solution(mesh):
    return jax.shard_map(
        body,
        mesh=mesh,
        in_specs=(
            P(("groups", "shard", "cache", "pair")),
            P(("groups", "shard", "cache", "pair")),
            P(("shard", "cache"), None),
            P(("groups", "shard"), None),
            P("pair", None, None),
            P("pair", None),
        ),
        out_specs=P(("groups", "shard", "cache", "pair")),
        check_vma=False,
    )
```
